32 devices in a mesh: groups: 2 (over y), dp: 4 (over z), seq: 2 (over x), head: 2 (over core).
Axes of the slice: x: 2, y: 2, z: 4, core: 2. Of those that a mesh axis runs over, the one named last changes fastest.
Arguments:
- tokens: bfloat16 [8, 768, 6144], P(('groups', 'dp'), 'seq'), parts along dimension 0, may hold values from -8 to 8
- ln_gain: float32 [6144], replicated, may hold values from 0.1 to 1.9
- qkv_weight: bfloat16 [6144, 24, 384], P('dp', ('seq', 'head')), may hold values from -8 to 8
Outputs:
- attended: bfloat16 [8, 768, 3072], P(('groups', 'dp'), 'seq', 'head'), parts along dimension 0
The draws below stay inside these ranges and needn't reach their ends.
There are 2 independent parts, one for each index of `groups`. The reference program is written for one: setup_inputs(seed, part) draws one part's arguments, and reference() takes and returns one part's arrays. A program takes and returns all parts, laid end to end along the dimension named above; an argument that names none is the same for every part. Nothing has to cross between parts.
All inputs are finite; a program needn't handle non-finite values.
Results may differ from the reference program's by a relative error of at most 0.012.
Values may be sent and summed in bfloat16 or wider, within the bound.
No kernel may reach another device: no remote copies, remote signals or barrier semaphores. Data moves between devices by JAX's collectives and lax.ppermute only.
A program may use at most 128 MiB of HBM per device.

```python
import math
import jax
import jax.numpy as jnp
from jax import lax

D = 6144
HD = 128
HEADS = 24
TOK = 768
IMAGES = 4
HEADS_DEV = 6
N_SEQ = 2
N_HEAD = 2


def draw_tokens(key, part):
    key = jax.random.fold_in(key, 5)
    first = jax.random.fold_in(key, 0)
    shape = (IMAGES, TOK, D)
    return jnp.clip(jax.random.normal(first, shape, jnp.float32), -6.0, 6.0).astype(jnp.bfloat16)


def draw_qkv_weight(key, part):
    key = jax.random.fold_in(key, 11)
    first = jax.random.fold_in(key, 0)
    shape = (D, HEADS, 3 * HD)
    query_scale = math.sqrt(2.0 / D)
    value_scale = math.sqrt(1.0 / D)
    noise = jnp.clip(jax.random.normal(first, shape, jnp.float32), -6.0, 6.0)
    column_scale = jnp.concatenate([jnp.full((2 * HD,), query_scale, jnp.float32), jnp.full((HD,), value_scale, jnp.float32)])
    return (noise * column_scale).astype(jnp.bfloat16)


def setup_inputs(seed: int = 0, part: int = 0) -> dict:
    splits = jax.random.split(jax.random.key(seed), 4)
    part_keys = jax.random.split(jax.random.fold_in(splits[3], part), 4)
    tokens = draw_tokens(jax.random.fold_in(jax.random.fold_in(splits[3], part), 71), part)
    ln_gain = jnp.clip(1.0 + 0.18 * jax.random.normal(splits[1], (D,), jnp.float32), 0.1, 1.9)
    qkv_weight = draw_qkv_weight(jax.random.fold_in(splits[3], 71), part)
    return {"tokens": tokens, "ln_gain": ln_gain, "qkv_weight": qkv_weight}


def normalize(array, gain):
    widened = array.astype(jnp.float32)
    centered = widened - lax.optimization_barrier(jnp.mean(widened, axis=-1, keepdims=True))
    variance = lax.optimization_barrier(jnp.mean(centered * centered, axis=-1, keepdims=True))
    return (centered * lax.rsqrt(variance + 1e-06) * gain).astype(jnp.bfloat16)

def attend(projected):
    width = projected.shape[2] // 3
    queries = projected[:, :, :width].astype(jnp.float32)
    key_rows = projected[:, :, width:2 * width].astype(jnp.float32)
    value_rows = projected[:, :, 2 * width:].astype(jnp.float32)
    scores = jnp.einsum('qhd,khd->hqk', queries, key_rows) * (1.0 / math.sqrt(width))
    highest = lax.optimization_barrier(jnp.max(scores, axis=-1, keepdims=True))
    expo = jnp.exp(scores - highest)
    probs = (expo / lax.optimization_barrier(jnp.sum(expo, axis=-1, keepdims=True))).astype(jnp.bfloat16)
    mixed = jnp.einsum('hqk,khd->qhd', probs.astype(jnp.float32), value_rows)
    return mixed.astype(jnp.bfloat16).reshape(projected.shape[0], -1)

def reference(tokens, ln_gain, qkv_weight):
    flat_weight = qkv_weight.reshape(D, HEADS * 3 * HD)

    def one_image(image):
        normed = normalize(image, ln_gain)
        projected = jnp.dot(normed, flat_weight, preferred_element_type=jnp.float32)
        projected = projected.astype(jnp.bfloat16).reshape(TOK, HEADS, 3 * HD)
        return attend(projected)
    mixed = lax.map(one_image, tokens)
    ordered = mixed.reshape(IMAGES, TOK, N_SEQ, N_HEAD, HEADS_DEV, HD)
    ordered = ordered.transpose(0, 1, 3, 2, 4, 5)
    return ordered.reshape(IMAGES, TOK, HEADS * HD)
```

```python
import math

import jax
import jax.numpy as jnp
from jax import lax
from jax.sharding import PartitionSpec as P


def normalize(array, gain):
    widened = array.astype(jnp.float32)
    centered = widened - jnp.mean(widened, axis=-1, keepdims=True)
    variance = jnp.mean(centered * centered, axis=-1, keepdims=True)
    return (centered * lax.rsqrt(variance + 1e-06) * gain).astype(jnp.bfloat16)


def attend(projected):
    width = projected.shape[2] // 3
    queries = projected[:, :, :width]
    key_rows = projected[:, :, width : 2 * width]
    value_rows = projected[:, :, 2 * width :]
    scores = jnp.einsum("qhd,khd->hqk", queries, key_rows, preferred_element_type=jnp.float32) * (
        1.0 / math.sqrt(width)
    )
    highest = jnp.max(scores, axis=-1, keepdims=True)
    expo = jnp.exp(scores - highest)
    probs = (expo / jnp.sum(expo, axis=-1, keepdims=True)).astype(jnp.bfloat16)
    mixed = jnp.einsum("hqk,khd->qhd", probs, value_rows, preferred_element_type=jnp.float32)
    return mixed.astype(jnp.bfloat16).reshape(projected.shape[0], -1)


def plain(tokens, ln_gain, qkv_weight):
    images = tokens.shape[0]
    width = tokens.shape[2]
    heads_here = qkv_weight.shape[1]
    columns = heads_here * qkv_weight.shape[2]
    source = normalize(tokens, ln_gain)
    half_width = width // lax.axis_size("head")
    core_index = lax.axis_index("head")
    own_half = lax.dynamic_slice_in_dim(source, core_index * half_width, half_width, 2)
    fetched = lax.all_gather(own_half, "seq", axis=1, tiled=True)
    gathered = lax.all_gather(fetched, "head", axis=2, tiled=True)
    full_tokens = gathered.shape[1]
    features = gathered.reshape(images * full_tokens, width)
    piece = lax.all_gather(qkv_weight, "dp", axis=0, tiled=True)
    projected = jnp.dot(
        features, piece.reshape(piece.shape[0], columns), preferred_element_type=jnp.float32
    )
    projected = projected.astype(jnp.bfloat16).reshape(
        images, full_tokens, heads_here, qkv_weight.shape[2]
    )
    mixed = lax.map(attend, projected)
    return lax.all_to_all(mixed, "seq", split_axis=1, concat_axis=2, tiled=True)


def shared(tokens, ln_gain, qkv_weight):
    groups, seqs, cores = (lax.axis_size(a) for a in ("groups", "seq", "head"))
    _, rows, width = tokens.shape
    heads, head_cols = qkv_weight.shape[1] // groups, qkv_weight.shape[2]
    depth = head_cols // 3
    part = rows // cores
    own = lax.dynamic_slice_in_dim(tokens[0], lax.axis_index("head") * part, part, 0)
    normed = normalize(own, ln_gain)
    features = lax.all_gather(normed, ("groups", "seq", "head"), axis=0, tiled=True)
    first = lax.axis_index("groups") * heads
    mixed = []
    for j in range(heads):
        piece = lax.dynamic_slice_in_dim(qkv_weight, first + j, 1, 1)[:, 0]
        weight = lax.all_gather(piece, "dp", axis=0, tiled=True)
        projected = jnp.dot(features, weight, preferred_element_type=jnp.float32)
        projected = projected.astype(jnp.bfloat16).reshape(groups, seqs * rows, 1, head_cols)
        mixed.append(jnp.stack([attend(projected[g]) for g in range(groups)]))
    out = jnp.concatenate(mixed, axis=-1).reshape(groups * seqs, rows, heads * depth)
    out = lax.all_to_all(out, ("groups", "seq"), split_axis=0, concat_axis=0, tiled=True)
    out = out.reshape(groups, seqs, rows, heads * depth).transpose(2, 1, 0, 3)
    return out.reshape(1, rows, seqs * groups * heads * depth)


def per_device(tokens, ln_gain, qkv_weight):
    groups, cores = lax.axis_size("groups"), lax.axis_size("head")
    if tokens.shape[0] == 1 and qkv_weight.shape[1] % groups == 0 and tokens.shape[1] % cores == 0:
        return shared(tokens, ln_gain, qkv_weight)
    return plain(tokens, ln_gain, qkv_weight)


def solution(mesh):
    return jax.shard_map(
        per_device,
        mesh=mesh,
        in_specs=(P(("groups", "dp"), "seq", None), P(), P("dp", ("seq", "head"), None)),
        out_specs=P(("groups", "dp"), "seq", "head"),
        check_vma=False,
    )
```

```python
import math

import jax
import jax.numpy as jnp
from jax import lax
from jax.experimental import pallas as pl
from jax.experimental.pallas import tpu as pltpu
from jax.sharding import PartitionSpec as P


def normalize(array, gain):
    widened = array.astype(jnp.float32)
    centered = widened - jnp.mean(widened, axis=-1, keepdims=True)
    variance = jnp.mean(centered * centered, axis=-1, keepdims=True)
    return (centered * lax.rsqrt(variance + 1e-06) * gain).astype(jnp.bfloat16)


def attend(projected):
    width = projected.shape[2] // 3
    queries = projected[:, :, :width]
    key_rows = projected[:, :, width : 2 * width]
    value_rows = projected[:, :, 2 * width :]
    scores = jnp.einsum("qhd,khd->hqk", queries, key_rows, preferred_element_type=jnp.float32) * (
        1.0 / math.sqrt(width)
    )
    highest = jnp.max(scores, axis=-1, keepdims=True)
    expo = jnp.exp(scores - highest)
    probs = (expo / jnp.sum(expo, axis=-1, keepdims=True)).astype(jnp.bfloat16)
    mixed = jnp.einsum("hqk,khd->qhd", probs, value_rows, preferred_element_type=jnp.float32)
    return mixed.astype(jnp.bfloat16).reshape(projected.shape[0], -1)


def plain(tokens, ln_gain, qkv_weight):
    images = tokens.shape[0]
    width = tokens.shape[2]
    heads_here = qkv_weight.shape[1]
    columns = heads_here * qkv_weight.shape[2]
    source = normalize(tokens, ln_gain)
    half_width = width // lax.axis_size("head")
    core_index = lax.axis_index("head")
    own_half = lax.dynamic_slice_in_dim(source, core_index * half_width, half_width, 2)
    fetched = lax.all_gather(own_half, "seq", axis=1, tiled=True)
    gathered = lax.all_gather(fetched, "head", axis=2, tiled=True)
    full_tokens = gathered.shape[1]
    features = gathered.reshape(images * full_tokens, width)
    piece = lax.all_gather(qkv_weight, "dp", axis=0, tiled=True)
    projected = jnp.dot(
        features, piece.reshape(piece.shape[0], columns), preferred_element_type=jnp.float32
    )
    projected = projected.astype(jnp.bfloat16).reshape(
        images, full_tokens, heads_here, qkv_weight.shape[2]
    )
    mixed = lax.map(attend, projected)
    return lax.all_to_all(mixed, "seq", split_axis=1, concat_axis=2, tiled=True)


def attend_kernel(projected_ref, mixed_ref):
    tokens, columns = projected_ref.shape
    width = columns // 3
    step = 256 if tokens % 256 == 0 else tokens
    key_rows = projected_ref[:, width : 2 * width]
    value_rows = projected_ref[:, 2 * width :]
    for begin in range(0, tokens, step):
        queries = projected_ref[begin : begin + step, :width]
        scores = lax.dot_general(
            queries, key_rows, (((1,), (1,)), ((), ())), preferred_element_type=jnp.float32
        ) * (1.0 / math.sqrt(width))
        expo = jnp.exp(scores - jnp.max(scores, axis=-1, keepdims=True))
        probs = (expo / jnp.sum(expo, axis=-1, keepdims=True)).astype(jnp.bfloat16)
        mixed = jnp.dot(probs, value_rows, preferred_element_type=jnp.float32)
        mixed_ref[begin : begin + step, :] = mixed.astype(jnp.bfloat16)


def attend_images(projected, images):
    tokens, columns = projected.shape[0] // images, projected.shape[1]
    width = columns // 3
    return pl.pallas_call(
        attend_kernel,
        grid=(images,),
        out_shape=jax.ShapeDtypeStruct((images * tokens, width), jnp.bfloat16),
        in_specs=[pl.BlockSpec((tokens, columns), lambda i: (i, 0))],
        out_specs=pl.BlockSpec((tokens, width), lambda i: (i, 0)),
        compiler_params=pltpu.CompilerParams(vmem_limit_bytes=32 << 20),
        cost_estimate=pl.CostEstimate(
            flops=4 * images * tokens * tokens * width,
            bytes_accessed=2 * images * tokens * (columns + width),
            transcendentals=images * tokens * tokens,
        ),
    )(projected)


def shared(tokens, ln_gain, qkv_weight):
    groups, seqs, cores = (lax.axis_size(a) for a in ("groups", "seq", "head"))
    group, seq, core, plane = (lax.axis_index(a) for a in ("groups", "seq", "head", "dp"))
    _, rows, width = tokens.shape
    heads, head_cols = qkv_weight.shape[1] // groups, qkv_weight.shape[2]
    depth = head_cols // 3
    slab = qkv_weight.shape[0]
    inner = (plane == 1) | (plane == 2)

    order = (plane, plane ^ 1, 2 - plane // 2, 3 - 3 * (plane // 2))
    part = rows // cores
    own = lax.dynamic_slice_in_dim(tokens[0], core * part, part, 0)
    normed = normalize(own, ln_gain)
    normed = jnp.concatenate(
        [lax.dynamic_slice_in_dim(normed, k * slab, slab, 1) for k in order], axis=1
    )
    features = lax.all_gather(normed, ("groups", "seq", "head"), axis=0, tiled=True)

    pairs = [(0, 1), (1, 0), (2, 3), (3, 2)]
    middle = [(1, 2), (2, 1)]
    ends = [(1, 0), (2, 3)]
    pieces, after = [], None
    for j in range(heads):
        piece = lax.dynamic_slice_in_dim(qkv_weight, group * heads + j, 1, 1)[:, 0]
        if after is not None:
            piece, after = lax.optimization_barrier((piece, after))
        near = lax.ppermute(piece, "dp", pairs)
        over = lax.ppermute(piece, "dp", middle)
        far = lax.ppermute(near, "dp", middle)
        over_end = lax.ppermute(over, "dp", ends)
        far_end = lax.ppermute(far, "dp", ends)
        after = over
        pieces.append((piece, near, jnp.where(inner, over, over_end), jnp.where(inner, far, far_end)))

    received = []
    for j in range(heads):
        total = None
        for i, weight in enumerate(pieces[j]):
            term = jnp.dot(
                features[:, i * slab : (i + 1) * slab], weight, preferred_element_type=jnp.float32
            )
            total = term if total is None else total + term
        mixed = attend_images(total.astype(jnp.bfloat16), groups)
        mixed = mixed.reshape(groups, seqs, rows, depth)
        got = []
        for a in range(groups):
            for b in range(seqs):
                to_group, to_seq = (group + a) % groups, (seq + b) % seqs
                sent = lax.dynamic_slice(
                    mixed, (to_group, to_seq, 0, 0), (1, 1, rows, depth)
                )[0, 0]
                if a or b:
                    sent = lax.ppermute(
                        sent,
                        ("groups", "seq"),
                        [
                            (g * seqs + s, (g + a) % groups * seqs + (s + b) % seqs)
                            for g in range(groups)
                            for s in range(seqs)
                        ],
                    )
                got.append(sent)
        received.append(jnp.stack(got))
    received = jnp.stack(received)
    blocks = []
    for s in range(seqs):
        for g in range(groups):
            index = (group - g) % groups * seqs + (seq - s) % seqs
            chosen = lax.dynamic_index_in_dim(received, index, 1, keepdims=False)
            blocks.extend(chosen[j] for j in range(heads))
    return jnp.concatenate(blocks, axis=1)[None]


def per_device(tokens, ln_gain, qkv_weight):
    groups, cores = lax.axis_size("groups"), lax.axis_size("head")
    fits = tokens.shape[0] == 1 and qkv_weight.shape[1] % groups == 0
    if fits and tokens.shape[1] % cores == 0 and lax.axis_size("dp") == 4:
        return shared(tokens, ln_gain, qkv_weight)
    return plain(tokens, ln_gain, qkv_weight)


def solution(mesh):
    return jax.shard_map(
        per_device,
        mesh=mesh,
        in_specs=(P(("groups", "dp"), "seq", None), P(), P("dp", ("seq", "head"), None)),
        out_specs=P(("groups", "dp"), "seq", "head"),
        check_vma=False,
    )
```

```python
import math

import jax
import jax.numpy as jnp
from jax import lax
from jax.experimental import pallas as pl
from jax.experimental.pallas import tpu as pltpu
from jax.sharding import PartitionSpec as P


def normalize(array, gain):
    widened = array.astype(jnp.float32)
    centered = widened - jnp.mean(widened, axis=-1, keepdims=True)
    variance = jnp.mean(centered * centered, axis=-1, keepdims=True)
    return (centered * lax.rsqrt(variance + 1e-06) * gain).astype(jnp.bfloat16)


def attend(projected):
    width = projected.shape[2] // 3
    queries = projected[:, :, :width]
    key_rows = projected[:, :, width : 2 * width]
    value_rows = projected[:, :, 2 * width :]
    scores = jnp.einsum("qhd,khd->hqk", queries, key_rows, preferred_element_type=jnp.float32) * (
        1.0 / math.sqrt(width)
    )
    highest = jnp.max(scores, axis=-1, keepdims=True)
    expo = jnp.exp(scores - highest)
    probs = (expo / jnp.sum(expo, axis=-1, keepdims=True)).astype(jnp.bfloat16)
    mixed = jnp.einsum("hqk,khd->qhd", probs, value_rows, preferred_element_type=jnp.float32)
    return mixed.astype(jnp.bfloat16).reshape(projected.shape[0], -1)


def plain(tokens, ln_gain, qkv_weight):
    images = tokens.shape[0]
    width = tokens.shape[2]
    heads_here = qkv_weight.shape[1]
    columns = heads_here * qkv_weight.shape[2]
    source = normalize(tokens, ln_gain)
    half_width = width // lax.axis_size("head")
    core_index = lax.axis_index("head")
    own_half = lax.dynamic_slice_in_dim(source, core_index * half_width, half_width, 2)
    fetched = lax.all_gather(own_half, "seq", axis=1, tiled=True)
    gathered = lax.all_gather(fetched, "head", axis=2, tiled=True)
    full_tokens = gathered.shape[1]
    features = gathered.reshape(images * full_tokens, width)
    piece = lax.all_gather(qkv_weight, "dp", axis=0, tiled=True)
    projected = jnp.dot(
        features, piece.reshape(piece.shape[0], columns), preferred_element_type=jnp.float32
    )
    projected = projected.astype(jnp.bfloat16).reshape(
        images, full_tokens, heads_here, qkv_weight.shape[2]
    )
    mixed = lax.map(attend, projected)
    return lax.all_to_all(mixed, "seq", split_axis=1, concat_axis=2, tiled=True)


def normalize_kernel(place_ref, tokens_ref, gain_ref, *normed_refs):
    widened = tokens_ref[0].astype(jnp.float32)
    mean = jnp.mean(widened, axis=-1, keepdims=True)
    centered = widened - mean
    scale = lax.rsqrt(jnp.mean(centered * centered, axis=-1, keepdims=True) + 1e-06)
    slab = normed_refs[0].shape[1] // 2
    for i in range(4):
        columns = pl.ds(pl.multiple_of(place_ref[i + 1] * slab, 128), slab)
        part = (tokens_ref[0, :, columns].astype(jnp.float32) - mean) * scale * gain_ref[:, columns]
        begin = (i % 2) * slab
        normed_refs[i // 2][:, begin : begin + slab] = part.astype(jnp.bfloat16)


def normalize_part(tokens, ln_gain, cores, core, order):
    _, rows, width = tokens.shape
    part = rows // cores
    step = 32 if part % 32 == 0 else part
    steps = part // step
    place = jnp.stack([jnp.asarray(v, jnp.int32) for v in (core, *order)])
    half = jax.ShapeDtypeStruct((part, width // 2), jnp.bfloat16)
    return pl.pallas_call(
        normalize_kernel,
        out_shape=(half, half),
        grid_spec=pltpu.PrefetchScalarGridSpec(
            num_scalar_prefetch=1,
            grid=(steps,),
            in_specs=[
                pl.BlockSpec((1, step, width), lambda i, place: (0, place[0] * steps + i, 0)),
                pl.BlockSpec((1, width), lambda i, place: (0, 0)),
            ],
            out_specs=(
                pl.BlockSpec((step, width // 2), lambda i, place: (i, 0)),
                pl.BlockSpec((step, width // 2), lambda i, place: (i, 0)),
            ),
        ),
        compiler_params=pltpu.CompilerParams(vmem_limit_bytes=32 << 20),
        cost_estimate=pl.CostEstimate(
            flops=8 * part * width, bytes_accessed=4 * part * width, transcendentals=part
        ),
    )(place, tokens, ln_gain[None])


def attend_kernel(projected_ref, mixed_ref):
    tokens, columns = projected_ref.shape
    width = columns // 3
    step = 256 if tokens % 256 == 0 else tokens
    key_rows = projected_ref[:, width : 2 * width]
    value_rows = projected_ref[:, 2 * width :]
    for begin in range(0, tokens, step):
        queries = projected_ref[begin : begin + step, :width]
        scores = lax.dot_general(
            queries, key_rows, (((1,), (1,)), ((), ())), preferred_element_type=jnp.float32
        ) * (1.0 / math.sqrt(width))
        expo = jnp.exp(scores - jnp.max(scores, axis=-1, keepdims=True))
        probs = (expo / jnp.sum(expo, axis=-1, keepdims=True)).astype(jnp.bfloat16)
        mixed = jnp.dot(probs, value_rows, preferred_element_type=jnp.float32)
        mixed_ref[begin : begin + step, :] = mixed.astype(jnp.bfloat16)


def attend_images(projected, images):
    tokens, columns = projected.shape[0] // images, projected.shape[1]
    width = columns // 3
    return pl.pallas_call(
        attend_kernel,
        grid=(images,),
        out_shape=jax.ShapeDtypeStruct((images * tokens, width), jnp.bfloat16),
        in_specs=[pl.BlockSpec((tokens, columns), lambda i: (i, 0))],
        out_specs=pl.BlockSpec((tokens, width), lambda i: (i, 0)),
        compiler_params=pltpu.CompilerParams(vmem_limit_bytes=32 << 20),
        cost_estimate=pl.CostEstimate(
            flops=4 * images * tokens * tokens * width,
            bytes_accessed=2 * images * tokens * (columns + width),
            transcendentals=images * tokens * tokens,
        ),
    )(projected)


def lent_kernel(core_ref, *refs):
    count = len(refs) - 9
    pieces, weights, mixed_ref = refs[:count], refs[count : count + 4], refs[count + 4]
    halves, projected_ref, sems = refs[count + 5 : count + 7], refs[count + 7], refs[count + 8]
    core, part = core_ref[0], pieces[0].shape[0]
    slab = weights[0].shape[0]
    copies = []
    for i, piece in enumerate(pieces):
        place, owner, half = i // 4, (i // 2) % 2, i % 2
        row = (2 * place + (1 - core if owner else core)) * part
        target = halves[half].at[pl.ds(pl.multiple_of(row, 32), part)]
        copies.append(pltpu.make_async_copy(piece, target, sems.at[i]))
    for copy in copies:
        copy.start()
    for copy in copies:
        copy.wait()

    step = 256

    @pl.loop(0, projected_ref.shape[0] // step)
    def _(i):
        rows = pl.ds(pl.multiple_of(i * step, step), step)
        total = jnp.zeros((step, projected_ref.shape[1]), jnp.float32)
        for k in range(4):
            total += jnp.dot(
                halves[k // 2][rows, (k % 2) * slab : (k % 2 + 1) * slab],
                weights[k][...],
                preferred_element_type=jnp.float32,
            )
        projected_ref[rows, :] = total.astype(jnp.bfloat16)

    attend_kernel(projected_ref, mixed_ref)


def attend_lent(pieces, weights, core):
    part, half = pieces[0].shape
    head_cols = weights[0].shape[1]
    tokens, width = part * len(pieces) // 2, head_cols // 3
    anywhere, vmem = pl.BlockSpec(memory_space=pl.ANY), pl.BlockSpec(memory_space=pltpu.VMEM)
    return pl.pallas_call(
        lent_kernel,
        out_shape=jax.ShapeDtypeStruct((tokens, width), jnp.bfloat16),
        in_specs=[pl.BlockSpec(memory_space=pltpu.SMEM)]
        + [anywhere] * len(pieces)
        + [vmem] * len(weights),
        out_specs=vmem,
        scratch_shapes=[
            pltpu.VMEM((tokens, half), jnp.bfloat16),
            pltpu.VMEM((tokens, half), jnp.bfloat16),
            pltpu.VMEM((tokens, head_cols), jnp.bfloat16),
            pltpu.SemaphoreType.DMA((len(pieces),)),
        ],
        compiler_params=pltpu.CompilerParams(vmem_limit_bytes=40 << 20),
        cost_estimate=pl.CostEstimate(
            flops=4 * tokens * half * head_cols + 4 * tokens * tokens * width,
            bytes_accessed=4 * tokens * half + 4 * half * head_cols,
            transcendentals=tokens * tokens,
        ),
    )(jnp.asarray(core, jnp.int32)[None], *pieces, *weights)


def project(slabs, weights):
    total = None
    for slab, weight in zip(slabs, weights):
        term = jnp.dot(slab, weight, preferred_element_type=jnp.float32)
        total = term if total is None else total + term
    return total.astype(jnp.bfloat16)


def shared(tokens, ln_gain, qkv_weight):
    groups, planes, seqs, cores = (lax.axis_size(a) for a in ("groups", "dp", "seq", "head"))
    group, plane, seq, core = (lax.axis_index(a) for a in ("groups", "dp", "seq", "head"))
    _, rows, width = tokens.shape
    heads, head_cols = qkv_weight.shape[1] // groups, qkv_weight.shape[2]
    depth = head_cols // 3
    slab = qkv_weight.shape[0]
    inner = (plane == 1) | (plane == 2)
    outward, inward, middle = [(1, 0), (2, 3)], [(0, 1), (3, 2)], [(1, 2), (2, 1)]
    swap = [(0, 1), (1, 0)]

    def dp_move(value, pairs):
        return lax.ppermute(value, "dp", pairs)

    own = [
        lax.dynamic_slice_in_dim(qkv_weight, group * heads + j, 1, 1)[:, 0] for j in range(heads)
    ]
    order = (plane, plane ^ 1, 2 - plane // 2, 3 - 3 * (plane // 2))
    normed = normalize_part(tokens, ln_gain, cores, core, order)
    *own, first_half, second_half = lax.optimization_barrier((*own, *normed))

    def plane_gather(half):
        return lax.all_gather(half, ("groups", "seq", "head"), axis=0, tiled=True)

    features = (plane_gather(first_half), plane_gather(second_half))

    def beside(value):
        return lax.ppermute(value, "seq", swap)

    def across(value):
        return lax.ppermute(value, "groups", swap)

    def other_core(value):
        return lax.ppermute(value, "head", swap)

    wait = lax.optimization_barrier
    out_own0, mid_own0 = dp_move(own[0], outward), dp_move(own[0], middle)
    lent0 = dp_move(first_half, inward)

    out_own0, mid_own0, lent0, own1, second_half = wait(
        (out_own0, mid_own0, lent0, own[1], second_half)
    )
    out_mid0, mid_own1 = dp_move(mid_own0, outward), dp_move(own1, middle)
    lent1 = dp_move(second_half, inward)

    out_mid0, mid_own1, lent0, lent1, own0, own1, own2 = wait(
        (out_mid0, mid_own1, lent0, lent1, own[0], own1, own[2])
    )
    out_own1, mid_own2 = dp_move(own1, outward), dp_move(own2, middle)
    in_own0 = dp_move(own0, inward)
    beside0, across0 = beside(lent0), across(lent0)

    out_own1, mid_own2, in_own0, mid_own1, own1, lent0, lent1 = wait(
        (out_own1, mid_own2, in_own0, mid_own1, own1, lent0, lent1)
    )
    out_mid1, mid_in0 = dp_move(mid_own1, outward), dp_move(in_own0, middle)
    in_own1 = dp_move(own1, inward)
    beside1, across1 = beside(lent1), across(lent1)
    lent_other = (other_core(lent0), other_core(lent1))

    out_mid1, mid_in0, in_own1, own2, beside0, across0, features = wait(
        (out_mid1, mid_in0, in_own1, own2, beside0, across0, features)
    )
    out_in0, mid_in1 = dp_move(mid_in0, outward), dp_move(in_own1, middle)
    in_own2 = dp_move(own2, inward)
    beside0_other, across0_other = other_core(beside0), other_core(across0)

    out_in0, mid_in1, in_own2, beside1, across1 = wait(
        (out_in0, mid_in1, in_own2, beside1, across1)
    )
    out_in1, mid_in2 = dp_move(mid_in1, outward), dp_move(in_own2, middle)
    corner = (beside(across0), across(beside1))
    beside1_other, across1_other = other_core(beside1), other_core(across1)
    in_own = (in_own0, in_own1, in_own2)
    slabs = [half[:, i * slab : (i + 1) * slab] for half in features for i in range(2)]
    both = (
        (lent0, lent1, *lent_other, beside0, beside1, beside0_other, beside1_other),
        (across0, across1, across0_other, across1_other, *corner, *map(other_core, corner)),
    )

    def exchange(mixed):
        mixed = mixed.reshape(groups, seqs, rows, depth)
        got = []
        for a in range(groups):
            for b in range(seqs):
                to_group, to_seq = (group + a) % groups, (seq + b) % seqs
                sent = lax.dynamic_slice(mixed, (to_group, to_seq, 0, 0), (1, 1, rows, depth))[0, 0]
                if a or b:
                    pairs = [
                        (g * seqs + s, (g + a) % groups * seqs + (s + b) % seqs)
                        for g in range(groups)
                        for s in range(seqs)
                    ]
                    sent = lax.ppermute(sent, ("groups", "seq"), pairs)
                got.append(sent)
        return got

    def hand_back(mixed):
        got = []
        for a in range(groups):
            for b in range(seqs):
                pairs = [
                    (
                        (g * planes + z) * seqs + s,
                        ((g + a) % groups * planes + (z ^ 1)) * seqs + (s + b) % seqs,
                    )
                    for g in range(groups)
                    for z in (1, 2)
                    for s in range(seqs)
                ]
                sent = mixed[a][b * rows : (b + 1) * rows]
                got.append(lax.ppermute(sent, ("groups", "dp", "seq"), pairs))
        return got

    def pick(for_inner, for_ends):
        return jnp.where(inner, for_inner, for_ends)

    first = exchange(attend_images(
        project(
            slabs,
            (own[0], pick(in_own[0], out_own0), pick(mid_own0, out_mid0), pick(mid_in0, out_in0)),
        ),
        groups,
    ))
    second = exchange(attend_images(
        project(slabs, (own[1], in_own[1], mid_own1, mid_in1)), groups
    ))
    third = exchange(attend_images(
        project(
            slabs,
            (
                pick(own[2], own[1]),
                pick(in_own[2], out_own1),
                pick(mid_own2, out_mid1),
                pick(mid_in2, out_in1),
            ),
        ),
        groups,
    ))
    lent_weights = (in_own[2], own[2], mid_own2, mid_in2)
    lent_mixed = [attend_lent(pieces, lent_weights, core) for pieces in both]
    lent_back = hand_back(lent_mixed)

    received = [
        first,
        [pick(x, y) for x, y in zip(second, third)],
        [pick(x, y) for x, y in zip(third, lent_back)],
    ]
    received = jnp.stack([jnp.concatenate(parts, axis=1) for parts in zip(*received)])
    blocks = []
    for s in range(seqs):
        for g in range(groups):
            index = (group - g) % groups * seqs + (seq - s) % seqs
            blocks.append(lax.dynamic_index_in_dim(received, index, 0, keepdims=False))
    return jnp.concatenate(blocks, axis=1)[None]


def per_device(tokens, ln_gain, qkv_weight):
    groups, planes, seqs, cores = (lax.axis_size(a) for a in ("groups", "dp", "seq", "head"))
    line = (groups, planes, seqs) == (2, 4, 2)
    if line and tokens.shape[0] == 1 and qkv_weight.shape[1] == 3 * groups:
        if tokens.shape[1] % cores == 0:
            return shared(tokens, ln_gain, qkv_weight)
    return plain(tokens, ln_gain, qkv_weight)


def solution(mesh):
    return jax.shard_map(
        per_device,
        mesh=mesh,
        in_specs=(P(("groups", "dp"), "seq", None), P(), P("dp", ("seq", "head"), None)),
        out_specs=P(("groups", "dp"), "seq", "head"),
        check_vma=False,
    )
```

```python
import functools
import math

import jax
import jax.numpy as jnp
from jax import lax
from jax.experimental import pallas as pl
from jax.experimental.pallas import tpu as pltpu
from jax.sharding import PartitionSpec as P


def normalize(array, gain):
    widened = array.astype(jnp.float32)
    centered = widened - jnp.mean(widened, axis=-1, keepdims=True)
    variance = jnp.mean(centered * centered, axis=-1, keepdims=True)
    return (centered * lax.rsqrt(variance + 1e-06) * gain).astype(jnp.bfloat16)


def attend(projected):
    width = projected.shape[2] // 3
    queries = projected[:, :, :width]
    key_rows = projected[:, :, width : 2 * width]
    value_rows = projected[:, :, 2 * width :]
    scores = jnp.einsum("qhd,khd->hqk", queries, key_rows, preferred_element_type=jnp.float32) * (
        1.0 / math.sqrt(width)
    )
    highest = jnp.max(scores, axis=-1, keepdims=True)
    expo = jnp.exp(scores - highest)
    probs = (expo / jnp.sum(expo, axis=-1, keepdims=True)).astype(jnp.bfloat16)
    mixed = jnp.einsum("hqk,khd->qhd", probs, value_rows, preferred_element_type=jnp.float32)
    return mixed.astype(jnp.bfloat16).reshape(projected.shape[0], -1)


def plain(tokens, ln_gain, qkv_weight):
    images = tokens.shape[0]
    width = tokens.shape[2]
    heads_here = qkv_weight.shape[1]
    columns = heads_here * qkv_weight.shape[2]
    source = normalize(tokens, ln_gain)
    half_width = width // lax.axis_size("head")
    core_index = lax.axis_index("head")
    own_half = lax.dynamic_slice_in_dim(source, core_index * half_width, half_width, 2)
    fetched = lax.all_gather(own_half, "seq", axis=1, tiled=True)
    gathered = lax.all_gather(fetched, "head", axis=2, tiled=True)
    full_tokens = gathered.shape[1]
    features = gathered.reshape(images * full_tokens, width)
    piece = lax.all_gather(qkv_weight, "dp", axis=0, tiled=True)
    projected = jnp.dot(
        features, piece.reshape(piece.shape[0], columns), preferred_element_type=jnp.float32
    )
    projected = projected.astype(jnp.bfloat16).reshape(
        images, full_tokens, heads_here, qkv_weight.shape[2]
    )
    mixed = lax.map(attend, projected)
    return lax.all_to_all(mixed, "seq", split_axis=1, concat_axis=2, tiled=True)


CHAINS = 1


def normalize_kernel(place_ref, tokens_ref, gain_ref, *normed_refs):
    widened = tokens_ref[0].astype(jnp.float32)
    mean = jnp.mean(widened, axis=-1, keepdims=True)
    centered = widened - mean
    scale = lax.rsqrt(jnp.mean(centered * centered, axis=-1, keepdims=True) + 1e-06)
    slab = widened.shape[1] // 4
    span = normed_refs[0].shape[1]
    for i in range(4):
        columns = pl.ds(pl.multiple_of(place_ref[i + 1] * slab, 128), slab)
        part = (tokens_ref[0, :, columns].astype(jnp.float32) - mean) * scale * gain_ref[:, columns]
        begin = i * slab % span
        normed_refs[i * slab // span][:, begin : begin + slab] = part.astype(jnp.bfloat16)


def normalize_part(tokens, ln_gain, part, core, order):
    width = tokens.shape[2]
    step, count = 32, 2 * CHAINS
    steps = part // step
    place = jnp.stack([jnp.asarray(v, jnp.int32) for v in (core, *order)])
    return pl.pallas_call(
        normalize_kernel,
        out_shape=[jax.ShapeDtypeStruct((part, width // count), jnp.bfloat16)] * count,
        grid_spec=pltpu.PrefetchScalarGridSpec(
            num_scalar_prefetch=1,
            grid=(steps,),
            in_specs=[
                pl.BlockSpec((1, step, width), lambda i, place: (0, place[0] * steps + i, 0)),
                pl.BlockSpec((1, width), lambda i, place: (0, 0)),
            ],
            out_specs=[pl.BlockSpec((step, width // count), lambda i, place: (i, 0))] * count,
        ),
        compiler_params=pltpu.CompilerParams(vmem_limit_bytes=56 << 20),
        cost_estimate=pl.CostEstimate(
            flops=8 * part * width, bytes_accessed=4 * part * width, transcendentals=part
        ),
    )(place, tokens, ln_gain[None])


def attend_rows(projected_ref, mixed_ref, base):
    tokens, columns = projected_ref.shape
    width = columns // 3
    step = 256
    key_rows = projected_ref[:, width : 2 * width]
    value_rows = projected_ref[:, 2 * width :]
    for begin in range(0, tokens, step):
        queries = projected_ref[begin : begin + step, :width]
        scores = lax.dot_general(
            queries, key_rows, (((1,), (1,)), ((), ())), preferred_element_type=jnp.float32
        ) * (1.0 / math.sqrt(width))
        expo = jnp.exp(scores - jnp.max(scores, axis=-1, keepdims=True))
        probs = (expo / jnp.sum(expo, axis=-1, keepdims=True)).astype(jnp.bfloat16)
        mixed = jnp.dot(probs, value_rows, preferred_element_type=jnp.float32)
        mixed_ref[base + begin : base + begin + step, :] = mixed.astype(jnp.bfloat16)


def job_kernel(images, slots, finish, add, role_ref, *refs):
    count = 2 * CHAINS
    refs = list(refs)
    take = lambda n: [refs.pop(0) for _ in range(n)]
    pieces = [[[take(count) for _ in range(2)] for _ in range(2)] for _ in range(images)]
    weights = [(take(CHAINS), take(CHAINS)) for _ in slots]
    partial_ref = refs.pop(0) if add else None
    out_ref, features_ref, weight_ref, total_ref, projected_ref, sems, weight_sems = take(7)
    core, inner = role_ref[0], role_ref[1]
    part, span = pieces[0][0][0][0].shape
    columns = weight_ref.shape[1]
    slab = weight_ref.shape[0] // len(slots)
    tokens = 4 * part
    blocks = span // columns

    def token_copies(image, n):
        begin = slots[n] * slab
        for place in range(2):
            for owner in range(2):
                row = image * tokens + (2 * place + (1 - core if owner else core)) * part
                yield pltpu.make_async_copy(
                    pieces[image][place][owner][begin // span].at[:, pl.ds(begin % span, slab)],
                    features_ref.at[pl.ds(pl.multiple_of(row, 32), part), pl.ds(n * slab, slab)],
                    sems.at[(image * len(slots) + n) * 4 + place * 2 + owner],
                )

    def weight_copies(n, role):
        for i in range(CHAINS):
            for b in range(blocks):
                row = n * slab + (i * blocks + b) * part
                yield pltpu.make_async_copy(
                    weights[n][role][i].at[:, pl.ds(b * columns, columns)],
                    weight_ref.at[pl.ds(row, part)],
                    weight_sems.at[(n * CHAINS + i) * blocks + b],
                )

    for n in range(len(slots)):

        @pl.when(inner == 1)
        def _():
            for copy in weight_copies(n, 0):
                copy.start()

        @pl.when(inner != 1)
        def _():
            for copy in weight_copies(n, 1):
                copy.start()

        for copy in token_copies(0, n):
            copy.start()
    for image in range(1, images):
        for n in range(len(slots)):
            for copy in token_copies(image, n):
                copy.start()

    step = 256
    for image in range(images):
        for n in range(len(slots)):
            if image == 0:
                for copy in weight_copies(n, 0):
                    copy.wait()
            for copy in token_copies(image, n):
                copy.wait()

            @pl.loop(0, tokens // step)
            def _(i):
                rows = pl.ds(pl.multiple_of(i * step, step), step)
                from_rows = pl.ds(pl.multiple_of(image * tokens + i * step, step), step)
                term = jnp.dot(
                    features_ref[from_rows, n * slab : (n + 1) * slab],
                    weight_ref[n * slab : (n + 1) * slab, :],
                    preferred_element_type=jnp.float32,
                )
                if n:
                    term += total_ref[rows, :]
                elif add:
                    term += partial_ref[from_rows, :]
                if n < len(slots) - 1:
                    total_ref[rows, :] = term
                elif finish:
                    projected_ref[rows, :] = term.astype(jnp.bfloat16)
                else:
                    out_ref[from_rows, :] = term

        if finish:
            attend_rows(projected_ref, out_ref, image * tokens)


def run_job(core, inner, columns, images, weights, slots=(0, 1, 2, 3), partial=None, finish=True):
    part, span = images[0][0][0][0].shape
    slab = span * CHAINS // 2
    tokens = 4 * part
    total = len(images) * tokens
    width = columns // 3
    anywhere, vmem = pl.BlockSpec(memory_space=pl.ANY), pl.BlockSpec(memory_space=pltpu.VMEM)
    pieces = [x for image in images for place in image for owner in place for x in owner]
    pieces += [x for slot in slots for role in weights[slot] for x in role]
    operands = pieces + ([partial] if partial is not None else [])
    depth = len(slots) * slab
    shape = (total, width) if finish else (total, columns)
    return pl.pallas_call(
        functools.partial(job_kernel, len(images), slots, finish, partial is not None),
        out_shape=jax.ShapeDtypeStruct(shape, jnp.bfloat16 if finish else jnp.float32),
        in_specs=[pl.BlockSpec(memory_space=pltpu.SMEM)]
        + [anywhere] * len(pieces)
        + [vmem] * (len(operands) - len(pieces)),
        out_specs=vmem,
        scratch_shapes=[
            pltpu.VMEM((total, depth), jnp.bfloat16),
            pltpu.VMEM((depth, columns), jnp.bfloat16),
            pltpu.VMEM((tokens, columns), jnp.float32),
            pltpu.VMEM((tokens, columns), jnp.bfloat16),
            pltpu.SemaphoreType.DMA((len(images) * len(slots) * 4,)),
            pltpu.SemaphoreType.DMA((depth // part,)),
        ],
        compiler_params=pltpu.CompilerParams(vmem_limit_bytes=56 << 20),
        cost_estimate=pl.CostEstimate(
            flops=2 * total * depth * columns + (4 * total * tokens * width if finish else 0),
            bytes_accessed=2 * total * depth + 2 * depth * columns,
            transcendentals=total * tokens if finish else 0,
        ),
    )(jnp.stack([core, inner]).astype(jnp.int32), *operands)


def shared(tokens, ln_gain, qkv_weight):
    groups, planes, seqs, cores = (lax.axis_size(a) for a in ("groups", "dp", "seq", "head"))
    group, plane, seq, core = (lax.axis_index(a) for a in ("groups", "dp", "seq", "head"))
    _, rows, width = tokens.shape
    slab, heads, columns = qkv_weight.shape
    heads, part, depth = heads // groups, rows // cores, columns // 3
    inner = (plane == 1) | (plane == 2)
    chains = range(CHAINS)
    wait = lax.optimization_barrier

    def fold(piece):
        piece = piece.reshape(-1, part, columns).transpose(1, 0, 2)
        return piece.reshape(part, -1)

    own = []
    for j in range(heads):
        piece = lax.dynamic_slice_in_dim(qkv_weight, group * heads + j, 1, 1)[:, 0]
        own.append([fold(p) for p in jnp.split(piece, CHAINS)])

    order = (plane, plane ^ 1, 2 - plane // 2, 3 - 3 * (plane // 2))
    normed = normalize_part(tokens, ln_gain, part, core, order)

    def pick(for_inner, for_ends):
        return jnp.where(inner, for_inner, for_ends)

    def pair(value):
        return lax.ppermute(value, "dp", [(0, 1), (1, 0), (2, 3), (3, 2)])

    def outward(value):
        return lax.ppermute(value, "dp", [(1, 0), (2, 3)])

    def middle(value):
        return lax.ppermute(value, "dp", [(1, 2), (2, 1)])

    swap = [(0, 1), (1, 0)]
    beside = lambda value: lax.ppermute(value, "seq", swap)
    across = lambda value: lax.ppermute(value, "groups", swap)
    other = lambda value: lax.ppermute(value, "head", swap)

    pairs, middles, xs, ys = [], [], [], []
    tokens_later = tokens
    for t in range(6):
        now = []
        for i in chains:
            give = {
                0: lambda: pick(own[0][i], normed[i]),
                1: lambda: pick(middles[0][i], normed[CHAINS + i]),
                2: lambda: pick(own[1][i], own[0][i]),
                3: lambda: pick(middles[1][i], own[1][i]),
                4: lambda: pick(middles[3][i], own[2][i]),
                5: lambda: middles[4][i],
            }[t]()
            give_middle = own[t][i] if t < 3 else pairs[t - 1][i]
            if t < 2:
                give_x = give_y = normed[t * CHAINS + i]
            elif t == 2:
                give_x, give_y = ys[0][i], xs[1][i]
            elif t < 5:
                give_x = give_y = pairs[t - 3][i]
            else:
                give_x, give_y = ys[3][i], xs[4][i]
            now.append((give, give_middle, give_x, give_y))
        got = [
            (pair(a) if t < 5 else outward(a), middle(b), beside(c), across(d))
            for a, b, c, d in now
        ]
        if t < 5:
            got, own, normed, tokens_later = wait((got, own, normed, tokens_later))
        pairs.append([g[0] for g in got])
        middles.append([g[1] for g in got])
        xs.append([g[2] for g in got])
        ys.append([g[3] for g in got])
        if t == 0:
            normed_other = normalize_part(tokens_later, ln_gain, part, 1 - core, order)

    def with_other(values):
        return (values, [other(v) for v in values])

    own_images = (
        ((normed, normed_other), with_other(xs[0] + xs[1])),
        (with_other(ys[0] + ys[1]), with_other(xs[2] + ys[2])),
    )
    lent_images = (
        (with_other(pairs[0] + pairs[1]), with_other(xs[3] + xs[4])),
        (with_other(ys[3] + ys[4]), with_other(xs[5] + ys[5])),
    )

    def exchange(mixed):
        got = []
        for a in range(groups):
            for b in range(seqs):
                sent = mixed[(a * seqs + b) * rows : (a * seqs + b + 1) * rows]
                if a or b:
                    steps = [
                        (g * seqs + s, (g + a) % groups * seqs + (s + b) % seqs)
                        for g in range(groups)
                        for s in range(seqs)
                    ]
                    sent = lax.ppermute(sent, ("groups", "seq"), steps)
                got.append(sent)
        return got

    def hand_back(mixed):
        got = []
        for a in range(groups):
            for b in range(seqs):
                steps = [
                    (
                        (g * planes + z) * seqs + s,
                        ((g + a) % groups * planes + (z ^ 1)) * seqs + (s + b) % seqs,
                    )
                    for g in range(groups)
                    for z in (1, 2)
                    for s in range(seqs)
                ]
                sent = mixed[(a * seqs + b) * rows : (a * seqs + b + 1) * rows]
                got.append(lax.ppermute(sent, ("groups", "dp", "seq"), steps))
        return got

    inner_heads = (
        (own[0], pairs[2], middles[0], middles[3]),
        (own[1], pairs[3], middles[1], middles[4]),
        (own[2], pairs[4], middles[2], middles[5]),
    )
    end_heads = (
        (own[0], pairs[0], pairs[1], pairs[4]),
        (own[1], pairs[2], pairs[3], pairs[5]),
    )
    jobs = (
        tuple(zip(inner_heads[0], inner_heads[0])),
        tuple(zip(inner_heads[1], end_heads[0])),
        tuple(zip(inner_heads[2], end_heads[1])),
    )
    lent = inner_heads[2]
    lent = tuple((w, w) for w in (lent[1], lent[0], lent[2], lent[3]))

    results = [exchange(run_job(core, inner, columns, own_images, job)) for job in jobs]
    results.append(hand_back(run_job(core, inner, columns, lent_images, lent)))
    results = wait(results)

    received = jnp.stack([
        jnp.concatenate(
            [pick(results[j][i], results[j + 1][i]) for j in range(heads)], axis=1
        )
        for i in range(groups * seqs)
    ])
    blocks = []
    for s in range(seqs):
        for g in range(groups):
            index = (group - g) % groups * seqs + (seq - s) % seqs
            blocks.append(lax.dynamic_index_in_dim(received, index, 0, keepdims=False))
    return jnp.concatenate(blocks, axis=1)[None]


def per_device(tokens, ln_gain, qkv_weight):
    groups, planes, seqs, cores = (lax.axis_size(a) for a in ("groups", "dp", "seq", "head"))
    images, rows, width = tokens.shape
    slab, heads, _ = qkv_weight.shape
    if (groups, planes, seqs, cores) == (2, 4, 2, 2) and images == 1 and heads == 3 * groups:
        part = rows // cores
        if rows % (32 * cores) == 0 and slab % part == 0 and 2 * slab == qkv_weight.shape[2] * slab // part:
            return shared(tokens, ln_gain, qkv_weight)
    return plain(tokens, ln_gain, qkv_weight)


def solution(mesh):
    return jax.shard_map(
        per_device,
        mesh=mesh,
        in_specs=(P(("groups", "dp"), "seq", None), P(), P("dp", ("seq", "head"), None)),
        out_specs=P(("groups", "dp"), "seq", "head"),
        check_vma=False,
    )
```

```python
import functools
import math

import jax
import jax.numpy as jnp
from jax import lax
from jax.experimental import pallas as pl
from jax.experimental.pallas import tpu as pltpu
from jax.sharding import PartitionSpec as P


def normalize(array, gain):
    widened = array.astype(jnp.float32)
    centered = widened - jnp.mean(widened, axis=-1, keepdims=True)
    variance = jnp.mean(centered * centered, axis=-1, keepdims=True)
    return (centered * lax.rsqrt(variance + 1e-06) * gain).astype(jnp.bfloat16)


def attend(projected):
    width = projected.shape[2] // 3
    queries = projected[:, :, :width]
    key_rows = projected[:, :, width : 2 * width]
    value_rows = projected[:, :, 2 * width :]
    scores = jnp.einsum("qhd,khd->hqk", queries, key_rows, preferred_element_type=jnp.float32) * (
        1.0 / math.sqrt(width)
    )
    highest = jnp.max(scores, axis=-1, keepdims=True)
    expo = jnp.exp(scores - highest)
    probs = (expo / jnp.sum(expo, axis=-1, keepdims=True)).astype(jnp.bfloat16)
    mixed = jnp.einsum("hqk,khd->qhd", probs, value_rows, preferred_element_type=jnp.float32)
    return mixed.astype(jnp.bfloat16).reshape(projected.shape[0], -1)


def plain(tokens, ln_gain, qkv_weight):
    images = tokens.shape[0]
    width = tokens.shape[2]
    heads_here = qkv_weight.shape[1]
    columns = heads_here * qkv_weight.shape[2]
    source = normalize(tokens, ln_gain)
    half_width = width // lax.axis_size("head")
    core_index = lax.axis_index("head")
    own_half = lax.dynamic_slice_in_dim(source, core_index * half_width, half_width, 2)
    fetched = lax.all_gather(own_half, "seq", axis=1, tiled=True)
    gathered = lax.all_gather(fetched, "head", axis=2, tiled=True)
    full_tokens = gathered.shape[1]
    features = gathered.reshape(images * full_tokens, width)
    piece = lax.all_gather(qkv_weight, "dp", axis=0, tiled=True)
    projected = jnp.dot(
        features, piece.reshape(piece.shape[0], columns), preferred_element_type=jnp.float32
    )
    projected = projected.astype(jnp.bfloat16).reshape(
        images, full_tokens, heads_here, qkv_weight.shape[2]
    )
    mixed = lax.map(attend, projected)
    return lax.all_to_all(mixed, "seq", split_axis=1, concat_axis=2, tiled=True)


CHAINS = 1


def normalize_kernel(place_ref, tokens_ref, gain_ref, *normed_refs):
    widened = tokens_ref[0].astype(jnp.float32)
    mean = jnp.mean(widened, axis=-1, keepdims=True)
    centered = widened - mean
    scale = lax.rsqrt(jnp.mean(centered * centered, axis=-1, keepdims=True) + 1e-06)
    slab = widened.shape[1] // 4
    span = normed_refs[0].shape[1]
    for i in range(4):
        columns = pl.ds(pl.multiple_of(place_ref[i + 1] * slab, 128), slab)
        part = (tokens_ref[0, :, columns].astype(jnp.float32) - mean) * scale * gain_ref[:, columns]
        begin = i * slab % span
        normed_refs[i * slab // span][:, begin : begin + slab] = part.astype(jnp.bfloat16)


def normalize_part(tokens, ln_gain, part, core, order):
    width = tokens.shape[2]
    step, count = 32, 2 * CHAINS
    steps = part // step
    place = jnp.stack([jnp.asarray(v, jnp.int32) for v in (core, *order)])
    return pl.pallas_call(
        normalize_kernel,
        out_shape=[jax.ShapeDtypeStruct((part, width // count), jnp.bfloat16)] * count,
        grid_spec=pltpu.PrefetchScalarGridSpec(
            num_scalar_prefetch=1,
            grid=(steps,),
            in_specs=[
                pl.BlockSpec((1, step, width), lambda i, place: (0, place[0] * steps + i, 0)),
                pl.BlockSpec((1, width), lambda i, place: (0, 0)),
            ],
            out_specs=[pl.BlockSpec((step, width // count), lambda i, place: (i, 0))] * count,
        ),
        compiler_params=pltpu.CompilerParams(vmem_limit_bytes=56 << 20),
        cost_estimate=pl.CostEstimate(
            flops=8 * part * width, bytes_accessed=4 * part * width, transcendentals=part
        ),
    )(place, tokens, ln_gain[None])


def attend_rows(projected_ref, mixed_ref, base):
    tokens, columns = projected_ref.shape
    width = columns // 3
    step = 256
    key_rows = projected_ref[:, width : 2 * width]
    value_rows = projected_ref[:, 2 * width :]
    for begin in range(0, tokens, step):
        queries = projected_ref[begin : begin + step, :width]
        scores = lax.dot_general(
            queries, key_rows, (((1,), (1,)), ((), ())), preferred_element_type=jnp.float32
        ) * (1.0 / math.sqrt(width))
        expo = jnp.exp(scores - jnp.max(scores, axis=-1, keepdims=True))
        probs = (expo / jnp.sum(expo, axis=-1, keepdims=True)).astype(jnp.bfloat16)
        mixed = jnp.dot(probs, value_rows, preferred_element_type=jnp.float32)
        mixed_ref[base + begin : base + begin + step, :] = mixed.astype(jnp.bfloat16)


def job_kernel(layout, slots, finish, add, role_ref, *refs):
    count = 2 * CHAINS
    refs = list(refs)
    take = lambda n: [refs.pop(0) for _ in range(n)]
    images = len(layout)
    pieces = [[[take(count) for _ in range(n)] for n in places] for places in layout]
    weights = [(take(CHAINS), take(CHAINS)) for _ in slots]
    partial_refs = take(images) if add else None
    out_ref, features_ref, weight_ref, total_ref, projected_ref, sems, weight_sems = take(7)
    core, inner = role_ref[0], role_ref[1]
    span = pieces[0][0][0][0].shape[1]
    columns = weight_ref.shape[1]
    slab = weight_ref.shape[0] // len(slots)
    tokens = projected_ref.shape[0]
    part = tokens // 4
    blocks = span // columns

    def token_copies(image, n):
        begin = slots[n] * slab
        for place in range(2):
            split = layout[image][place]
            for owner in range(split):
                row = image * tokens + 2 * place * part
                if split == 2:
                    row += (1 - core if owner else core) * part
                yield pltpu.make_async_copy(
                    pieces[image][place][owner][begin // span].at[:, pl.ds(begin % span, slab)],
                    features_ref.at[
                        pl.ds(pl.multiple_of(row, 32), 2 * part // split), pl.ds(n * slab, slab)
                    ],
                    sems.at[(image * len(slots) + n) * 4 + place * 2 + owner],
                )

    def weight_copies(n, role):
        for i in range(CHAINS):
            for b in range(blocks):
                row = n * slab + (i * blocks + b) * part
                yield pltpu.make_async_copy(
                    weights[n][role][i].at[:, pl.ds(b * columns, columns)],
                    weight_ref.at[pl.ds(row, part)],
                    weight_sems.at[(n * CHAINS + i) * blocks + b],
                )

    for n in range(len(slots)):

        @pl.when(inner == 1)
        def _():
            for copy in weight_copies(n, 0):
                copy.start()

        @pl.when(inner != 1)
        def _():
            for copy in weight_copies(n, 1):
                copy.start()

        for copy in token_copies(0, n):
            copy.start()

    for image in range(images):
        for n in range(len(slots)):
            if image == 0:
                for copy in weight_copies(n, 0):
                    copy.wait()
            for copy in token_copies(image, n):
                copy.wait()

            if n == 0 and image + 1 < images:
                for later in range(len(slots)):
                    for copy in token_copies(image + 1, later):
                        copy.start()
            rows = pl.ds(image * tokens, tokens)
            term = jnp.dot(
                features_ref[rows, n * slab : (n + 1) * slab],
                weight_ref[n * slab : (n + 1) * slab, :],
                preferred_element_type=jnp.float32,
            )
            if n:
                term += total_ref[...]
            elif add:
                term += partial_refs[image][...]
            if n < len(slots) - 1:
                total_ref[...] = term
            elif finish:
                projected_ref[...] = term.astype(jnp.bfloat16)
            else:
                out_ref[rows, :] = term

        if finish:
            attend_rows(projected_ref, out_ref, image * tokens)


def run_job(core, inner, columns, images, weights, slots, partials=None, finish=True):
    layout = [[len(place) for place in image] for image in images]
    pieces = [x for image in images for place in image for owner in place for x in owner]
    slab = pieces[0].shape[1] * CHAINS // 2
    tokens = sum(owner[0].shape[0] for place in images[0] for owner in place)
    total, width, depth = len(images) * tokens, columns // 3, len(slots) * slab
    pieces += [x for pair in weights for role in pair for x in role]
    partials = list(partials or ())
    anywhere, vmem = pl.BlockSpec(memory_space=pl.ANY), pl.BlockSpec(memory_space=pltpu.VMEM)
    shape = (total, width) if finish else (total, columns)
    return pl.pallas_call(
        functools.partial(job_kernel, layout, slots, finish, bool(partials)),
        out_shape=jax.ShapeDtypeStruct(shape, jnp.bfloat16 if finish else jnp.float32),
        in_specs=[pl.BlockSpec(memory_space=pltpu.SMEM)]
        + [anywhere] * len(pieces)
        + [vmem] * len(partials),
        out_specs=vmem,
        scratch_shapes=[
            pltpu.VMEM((total, depth), jnp.bfloat16),
            pltpu.VMEM((depth, columns), jnp.bfloat16),
            pltpu.VMEM((tokens, columns), jnp.float32),
            pltpu.VMEM((tokens, columns), jnp.bfloat16),
            pltpu.SemaphoreType.DMA((len(images) * len(slots) * 4,)),
            pltpu.SemaphoreType.DMA((4 * depth // tokens,)),
        ],
        compiler_params=pltpu.CompilerParams(vmem_limit_bytes=56 << 20),
        cost_estimate=pl.CostEstimate(
            flops=2 * total * depth * columns + (4 * total * tokens * width if finish else 0),
            bytes_accessed=2 * total * depth + 2 * depth * columns,
            transcendentals=total * tokens if finish else 0,
        ),
    )(jnp.stack([core, inner]).astype(jnp.int32), *pieces, *partials)


def shared(tokens, ln_gain, qkv_weight):
    groups, planes, seqs, cores = (lax.axis_size(a) for a in ("groups", "dp", "seq", "head"))
    group, plane, seq, core = (lax.axis_index(a) for a in ("groups", "dp", "seq", "head"))
    _, rows, width = tokens.shape
    slab, heads, columns = qkv_weight.shape
    heads, part, depth = heads // groups, rows // cores, columns // 3
    inner = (plane == 1) | (plane == 2)
    wait = lax.optimization_barrier

    def fold(piece):
        piece = piece.reshape(-1, part, columns).transpose(1, 0, 2)
        return piece.reshape(part, -1)

    def weight_piece(weight, j):
        piece = lax.dynamic_slice_in_dim(weight, group * heads + j, 1, 1)[:, 0]
        return [fold(p) for p in jnp.split(piece, CHAINS)]

    def pick(for_inner, for_ends):
        return jnp.where(inner, for_inner, for_ends)

    def pair(values):
        return [lax.ppermute(v, "dp", [(0, 1), (1, 0), (2, 3), (3, 2)]) for v in values]

    def outward(values):
        return [lax.ppermute(v, "dp", [(1, 0), (2, 3)]) for v in values]

    def middle(values):
        return [lax.ppermute(v, "dp", [(1, 2), (2, 1)]) for v in values]

    swap = [(0, 1), (1, 0)]

    def beside(values):
        return [lax.ppermute(v, "seq", swap) for v in values]

    def across(values):
        return [lax.ppermute(v, "groups", swap) for v in values]

    def with_other(values):
        return (values, [lax.ppermute(v, "head", swap) for v in values])

    def both_cores(values):
        return ([lax.all_gather(v, "head", axis=0, tiled=True) for v in values],)

    def select(for_inner, for_ends):
        return [pick(a, b) for a, b in zip(for_inner, for_ends)]

    order = (plane, plane ^ 1, 2 - plane // 2, 3 - 3 * (plane // 2))

    own0 = weight_piece(qkv_weight, 0)
    pair1, middle1 = pair(own0), middle(own0)
    tokens, own0 = wait((tokens, own0))
    normed = normalize_part(tokens, ln_gain, part, core, order)
    normed, qkv_weight = wait((normed, qkv_weight))
    cut0, cut1 = normed[:CHAINS], normed[CHAINS:]
    beside1, across1 = beside(cut0), across(cut0)
    own1, own2 = weight_piece(qkv_weight, 1), weight_piece(qkv_weight, 2)
    pair1, middle1, beside1, across1, own1, own2, cut0, cut1, tokens = wait(
        (pair1, middle1, beside1, across1, own1, own2, cut0, cut1, tokens)
    )

    pair2, middle2 = pair(select(middle1, cut0)), middle(own1)
    beside2, across2 = beside(cut1), across(cut1)
    normed_other = normalize_part(tokens, ln_gain, part, 1 - core, order)
    pair2, middle2, beside2, across2, across1, cut1, normed_other = wait(
        (pair2, middle2, beside2, across2, across1, cut1, normed_other)
    )

    pair3, middle3 = pair(select(own1, cut1)), middle(own2)
    beside3, across3 = beside(across1), across(beside2)
    pair3, middle3, beside3, across3, middle2, pair1, pair2 = wait(
        (pair3, middle3, beside3, across3, middle2, pair1, pair2)
    )

    def job(images, inner_weights, end_weights, slots, partials=None, finish=True):
        weights = list(zip(inner_weights, end_weights))
        return run_job(core, inner, columns, images, weights, slots, partials, finish)

    pair4, middle4 = pair(select(middle2, own1)), middle(pair1)
    beside4, across4 = beside(pair2), across(pair2)
    own_images = [((normed, normed_other), both_cores(beside1 + beside2))]
    part1 = [job(own_images, (own0, middle1), (own0, middle1), (0, 2), finish=False)]
    part2 = [job(own_images, (own1, middle2), (own0, pair2), (0, 2), finish=False)]
    pair4, middle4, beside4, across4, own2, pair3, part1, part2 = wait(
        (pair4, middle4, beside4, across4, own2, pair3, part1, part2)
    )

    pair5, middle5 = pair(select(middle4, own2)), middle(pair4)
    beside5, across5 = beside(pair3), across(pair3)
    own_images.append((both_cores(across1 + across2), both_cores(beside3 + across3)))
    part1.append(job(own_images[1:], (own0, middle1), (own0, middle1), (0, 2), finish=False))
    part2.append(job(own_images[1:], (own1, middle2), (own0, pair2), (0, 2), finish=False))
    mixed1 = job(own_images, (pair1, middle4), (pair1, middle4), (1, 3), part1)
    part3 = [
        job([image], (own2, middle3), (own1, pair4), (0, 2), finish=False) for image in own_images
    ]
    pair5, middle5, beside5, across5, across4, mixed1, part2, part3 = wait(
        (pair5, middle5, beside5, across5, across4, mixed1, part2, part3)
    )

    pair6, middle6 = outward(middle5), middle(pair5)
    beside6, across6 = beside(across4), across(beside5)
    lent_images = [(both_cores(pair2 + pair3), both_cores(beside4 + beside5))]
    mixed2 = job(own_images, (pair4, middle5), (pair1, pair5), (1, 3), part2)
    part3 = [
        job([image], (pair5,), (pair3,), (1,), [part], finish=False)
        for image, part in zip(own_images, part3)
    ]
    lent_weights = (pair5, own2, middle3)
    part4 = job(lent_images, lent_weights, lent_weights, (0, 1, 2), finish=False)
    pair6, middle6, mixed2, part3, part4 = wait((pair6, middle6, mixed2, part3, part4))

    mixed3 = job(own_images, (middle6,), (pair6,), (3,), part3)
    mixed4 = [job(lent_images, (middle6,), (middle6,), (3,), [part4])]
    lent_images = [(both_cores(across4 + across5), with_other(beside6 + across6))]
    lent_weights = (*lent_weights, middle6)
    mixed4.append(job(lent_images, lent_weights, lent_weights, (0, 1, 2, 3)))

    def exchange(mixed):
        got = []
        for a in range(groups):
            for b in range(seqs):
                sent = mixed[(a * seqs + b) * rows : (a * seqs + b + 1) * rows]
                if a or b:
                    steps = [
                        (g * seqs + s, (g + a) % groups * seqs + (s + b) % seqs)
                        for g in range(groups)
                        for s in range(seqs)
                    ]
                    sent = lax.ppermute(sent, ("groups", "seq"), steps)
                got.append(sent)
        return got

    def hand_back(mixed):
        got = []
        for a in range(groups):
            for b in range(seqs):
                steps = [
                    (
                        (g * planes + z) * seqs + s,
                        ((g + a) % groups * planes + (z ^ 1)) * seqs + (s + b) % seqs,
                    )
                    for g in range(groups)
                    for z in (1, 2)
                    for s in range(seqs)
                ]
                sent = mixed[a][b * rows : (b + 1) * rows]
                got.append(lax.ppermute(sent, ("groups", "dp", "seq"), steps))
        return got

    results = [exchange(mixed) for mixed in (mixed1, mixed2, mixed3)]
    results.append(hand_back(mixed4))
    results = wait(results)

    received = jnp.stack([
        jnp.concatenate(
            [pick(results[j][i], results[j + 1][i]) for j in range(heads)], axis=1
        )
        for i in range(groups * seqs)
    ])
    blocks = []
    for s in range(seqs):
        for g in range(groups):
            index = (group - g) % groups * seqs + (seq - s) % seqs
            blocks.append(lax.dynamic_index_in_dim(received, index, 0, keepdims=False))
    return jnp.concatenate(blocks, axis=1)[None]


def per_device(tokens, ln_gain, qkv_weight):
    groups, planes, seqs, cores = (lax.axis_size(a) for a in ("groups", "dp", "seq", "head"))
    images, rows, width = tokens.shape
    slab, heads, _ = qkv_weight.shape
    if (groups, planes, seqs, cores) == (2, 4, 2, 2) and images == 1 and heads == 3 * groups:
        part = rows // cores
        if rows % (32 * cores) == 0 and slab % part == 0 and 2 * slab == qkv_weight.shape[2] * slab // part:
            return shared(tokens, ln_gain, qkv_weight)
    return plain(tokens, ln_gain, qkv_weight)


def solution(mesh):
    return jax.shard_map(
        per_device,
        mesh=mesh,
        in_specs=(P(("groups", "dp"), "seq", None), P(), P("dp", ("seq", "head"), None)),
        out_specs=P(("groups", "dp"), "seq", "head"),
        check_vma=False,
    )
```

```python
import functools
import math

import jax
import jax.numpy as jnp
from jax import lax
from jax.experimental import pallas as pl
from jax.experimental.pallas import tpu as pltpu
from jax.sharding import PartitionSpec as P


def normalize(array, gain):
    widened = array.astype(jnp.float32)
    centered = widened - jnp.mean(widened, axis=-1, keepdims=True)
    variance = jnp.mean(centered * centered, axis=-1, keepdims=True)
    return (centered * lax.rsqrt(variance + 1e-06) * gain).astype(jnp.bfloat16)


def attend(projected):
    width = projected.shape[2] // 3
    queries = projected[:, :, :width]
    key_rows = projected[:, :, width : 2 * width]
    value_rows = projected[:, :, 2 * width :]
    scores = jnp.einsum("qhd,khd->hqk", queries, key_rows, preferred_element_type=jnp.float32) * (
        1.0 / math.sqrt(width)
    )
    highest = jnp.max(scores, axis=-1, keepdims=True)
    expo = jnp.exp(scores - highest)
    probs = (expo / jnp.sum(expo, axis=-1, keepdims=True)).astype(jnp.bfloat16)
    mixed = jnp.einsum("hqk,khd->qhd", probs, value_rows, preferred_element_type=jnp.float32)
    return mixed.astype(jnp.bfloat16).reshape(projected.shape[0], -1)


def plain(tokens, ln_gain, qkv_weight):
    images = tokens.shape[0]
    width = tokens.shape[2]
    heads_here = qkv_weight.shape[1]
    columns = heads_here * qkv_weight.shape[2]
    source = normalize(tokens, ln_gain)
    half_width = width // lax.axis_size("head")
    core_index = lax.axis_index("head")
    own_half = lax.dynamic_slice_in_dim(source, core_index * half_width, half_width, 2)
    fetched = lax.all_gather(own_half, "seq", axis=1, tiled=True)
    gathered = lax.all_gather(fetched, "head", axis=2, tiled=True)
    full_tokens = gathered.shape[1]
    features = gathered.reshape(images * full_tokens, width)
    piece = lax.all_gather(qkv_weight, "dp", axis=0, tiled=True)
    projected = jnp.dot(
        features, piece.reshape(piece.shape[0], columns), preferred_element_type=jnp.float32
    )
    projected = projected.astype(jnp.bfloat16).reshape(
        images, full_tokens, heads_here, qkv_weight.shape[2]
    )
    mixed = lax.map(attend, projected)
    return lax.all_to_all(mixed, "seq", split_axis=1, concat_axis=2, tiled=True)


def normalize_kernel(place_ref, tokens_ref, gain_ref, *normed_refs):
    widened = tokens_ref[0].astype(jnp.float32)
    mean = jnp.mean(widened, axis=-1, keepdims=True)
    centered = widened - mean
    scale = lax.rsqrt(jnp.mean(centered * centered, axis=-1, keepdims=True) + 1e-06)
    slab = widened.shape[1] // 4
    span = normed_refs[0].shape[1]
    for i in range(4):
        columns = pl.ds(pl.multiple_of(place_ref[i + 1] * slab, 128), slab)
        part = (tokens_ref[0, :, columns].astype(jnp.float32) - mean) * scale * gain_ref[:, columns]
        begin = i * slab % span
        normed_refs[i * slab // span][:, begin : begin + slab] = part.astype(jnp.bfloat16)


def normalize_part(tokens, ln_gain, part, core, order):
    width = tokens.shape[2]
    step, count = 32, 2
    steps = part // step
    place = jnp.stack([jnp.asarray(v, jnp.int32) for v in (core, *order)])
    return pl.pallas_call(
        normalize_kernel,
        out_shape=[jax.ShapeDtypeStruct((part, width // count), jnp.bfloat16)] * count,
        grid_spec=pltpu.PrefetchScalarGridSpec(
            num_scalar_prefetch=1,
            grid=(steps,),
            in_specs=[
                pl.BlockSpec((1, step, width), lambda i, place: (0, place[0] * steps + i, 0)),
                pl.BlockSpec((1, width), lambda i, place: (0, 0)),
            ],
            out_specs=[pl.BlockSpec((step, width // count), lambda i, place: (i, 0))] * count,
        ),
        compiler_params=pltpu.CompilerParams(vmem_limit_bytes=56 << 20),
        cost_estimate=pl.CostEstimate(
            flops=8 * part * width, bytes_accessed=4 * part * width, transcendentals=part
        ),
    )(place, tokens, ln_gain[None])


def attend_rows(projected_ref, mixed_ref, base):
    tokens, columns = projected_ref.shape
    width = columns // 3
    step = 256
    key_rows = projected_ref[:, width : 2 * width]
    value_rows = projected_ref[:, 2 * width :]
    for begin in range(0, tokens, step):
        queries = projected_ref[begin : begin + step, :width]
        scores = lax.dot_general(
            queries, key_rows, (((1,), (1,)), ((), ())), preferred_element_type=jnp.float32
        )
        highest = jnp.max(scores, axis=-1, keepdims=True)
        expo = jnp.exp2((scores - highest) * (math.log2(math.e) / math.sqrt(width)))
        mixed = jnp.dot(expo.astype(jnp.bfloat16), value_rows, preferred_element_type=jnp.float32)
        mixed = mixed / jnp.sum(expo, axis=-1, keepdims=True)
        mixed_ref[base + begin : base + begin + step, :] = mixed.astype(jnp.bfloat16)


def job_kernel(layout, slots, counts, same, columns, finished, role_ref, *refs):
    refs = list(refs)
    take = lambda n: [refs.pop(0) for _ in range(n)]
    images, jobs = len(layout), counts[0]
    pieces = [[[take(2) for _ in range(n)] for n in places] for places in layout]
    weights = [[take(1) * 2 if alike else take(2) for alike in row] for row in same]
    partials = [None if at is None else take(1)[0] for at in columns]
    outs = take(jobs)
    features_ref, weight_ref, total_ref, projected_ref, token_sems, weight_sems, sum_sems = take(7)
    core, inner = role_ref[0], role_ref[1]
    span = pieces[0][0][0][0].shape[1]
    slab = span // 2
    tokens, wide = projected_ref.shape
    part = tokens // 4

    def features(image, n):
        return features_ref.at[pl.ds(image * tokens, tokens), pl.ds(n * slab, slab)]

    def weight(n, j):
        return weight_ref.at[pl.ds(n * slab, slab), pl.ds(j * wide, wide)]

    def total(image, j):
        return total_ref.at[pl.ds(image * tokens, tokens), pl.ds(j * wide, wide)]

    def start_tokens(image, n):
        cut, begin = slots[n] // 2, slots[n] % 2 * slab
        for place in range(2):
            split = layout[image][place]
            for owner in range(split):
                row = image * tokens + 2 * place * part
                if split == 2:
                    row += (1 - core if owner else core) * part
                rows = pl.ds(pl.multiple_of(row, 32), 2 * part // split)
                pltpu.make_async_copy(
                    pieces[image][place][owner][cut].at[:, pl.ds(begin, slab)],
                    features_ref.at[rows, pl.ds(n * slab, slab)],
                    token_sems.at[image, n],
                ).start()

    def start_weight(n, j, role):
        source = weights[n][j][role]
        if source.shape[0] == slab:
            pltpu.make_async_copy(source, weight(n, j), weight_sems.at[n, j]).start()
            return
        for b in range(source.shape[1] // wide):
            pltpu.make_async_copy(
                source.at[:, pl.ds(b * wide, wide)],
                weight_ref.at[pl.ds(n * slab + b * part, part), pl.ds(j * wide, wide)],
                weight_sems.at[n, j],
            ).start()

    def start_weights(n):
        for j in range(counts[n]):
            if same[n][j]:
                start_weight(n, j, 0)
                continue

            @pl.when(inner == 1)
            def _():
                start_weight(n, j, 0)

            @pl.when(inner != 1)
            def _():
                start_weight(n, j, 1)

    def partial_copy(image, j):
        source = partials[j].at[pl.ds(image * tokens, tokens), pl.ds(columns[j], wide)]
        return pltpu.make_async_copy(source, total(image, j), sum_sems.at[image, j])

    for n in range(len(slots)):
        start_tokens(0, n)
        start_weights(n)
    for image in range(images):
        for j in range(jobs):
            if columns[j] is not None:
                partial_copy(image, j).start()
        if image:
            for n in range(len(slots)):
                start_tokens(image, n)

    for image in range(images):
        for n in range(len(slots)):
            pltpu.make_async_copy(
                features(image, n), features(image, n), token_sems.at[image, n]
            ).wait()
            if image == 0:
                for j in range(counts[n]):
                    pltpu.make_async_copy(weight(n, j), weight(n, j), weight_sems.at[n, j]).wait()
            term = jnp.dot(
                features(image, n)[...],
                weight_ref[n * slab : (n + 1) * slab, : counts[n] * wide],
                preferred_element_type=jnp.float32,
            )
            for j in range(counts[n]):
                value = term[:, j * wide : (j + 1) * wide]
                if n == 0 and columns[j] is not None:
                    partial_copy(image, j).wait()
                if n or columns[j] is not None:
                    value += total(image, j)[...]
                if n + 1 < len(slots) and j < counts[n + 1]:
                    total(image, j)[...] = value
                elif j < finished:
                    projected_ref[...] = value.astype(jnp.bfloat16)
                    attend_rows(projected_ref, outs[j], image * tokens)
                else:
                    outs[j][image * tokens : (image + 1) * tokens, :] = value


def run_jobs(core, inner, wide, images, slots, weights, partials=None, finished=0):
    layout = [[len(place) for place in image] for image in images]
    operands = [x for image in images for place in image for owner in place for x in owner]
    span = operands[0].shape[1]
    slab = span // 2
    tokens = sum(owner[0].shape[0] for place in images[0] for owner in place)
    total = len(images) * tokens
    counts = [len(row) for row in weights]
    jobs = counts[0]
    same = [[not isinstance(w, tuple) for w in row] for row in weights]
    for row in weights:
        for w in row:
            operands += list(w) if isinstance(w, tuple) else [w]
    partials = partials or [None] * jobs
    columns = [p and p[1] for p in partials]
    operands += [p[0] for p in partials if p]
    vmem = pl.BlockSpec(memory_space=pltpu.VMEM)
    depth = len(slots) * slab
    return pl.pallas_call(
        functools.partial(job_kernel, layout, slots, counts, same, columns, finished),
        out_shape=[
            jax.ShapeDtypeStruct((total, wide // 3), jnp.bfloat16)
            if j < finished
            else jax.ShapeDtypeStruct((total, wide), jnp.float32)
            for j in range(jobs)
        ],
        in_specs=[pl.BlockSpec(memory_space=pltpu.SMEM)]
        + [pl.BlockSpec(memory_space=pl.ANY)] * len(operands),
        out_specs=[vmem] * jobs,
        scratch_shapes=[
            pltpu.VMEM((total, depth), jnp.bfloat16),
            pltpu.VMEM((depth, jobs * wide), jnp.bfloat16),
            pltpu.VMEM((total, jobs * wide), jnp.float32),
            pltpu.VMEM((tokens, wide), jnp.bfloat16),
            pltpu.SemaphoreType.DMA((len(images), len(slots))),
            pltpu.SemaphoreType.DMA((len(slots), jobs)),
            pltpu.SemaphoreType.DMA((len(images), jobs)),
        ],
        compiler_params=pltpu.CompilerParams(vmem_limit_bytes=56 << 20),
        cost_estimate=pl.CostEstimate(
            flops=2 * total * slab * wide * sum(counts), bytes_accessed=0, transcendentals=0
        ),
    )(jnp.stack([core, inner]).astype(jnp.int32), *operands)


def shared(tokens, ln_gain, qkv_weight):
    groups, planes, seqs, cores = (lax.axis_size(a) for a in ("groups", "dp", "seq", "head"))
    group, plane, seq, core = (lax.axis_index(a) for a in ("groups", "dp", "seq", "head"))
    _, rows, _ = tokens.shape
    slab, heads, columns = qkv_weight.shape
    heads, part = heads // groups, rows // cores
    inner = (plane == 1) | (plane == 2)
    wait = lax.optimization_barrier

    def fold(piece):
        piece = piece.reshape(-1, part, columns).transpose(1, 0, 2)
        return piece.reshape(part, -1)

    def weight_piece(weight, j):
        return lax.dynamic_slice_in_dim(weight, group * heads + j, 1, 1)[:, 0]

    def pick(for_inner, for_ends):
        return jnp.where(inner, for_inner, for_ends)

    def pair(value):
        return lax.ppermute(value, "dp", [(0, 1), (1, 0), (2, 3), (3, 2)])

    def outward(value):
        return lax.ppermute(value, "dp", [(1, 0), (2, 3)])

    def middle(value):
        return lax.ppermute(value, "dp", [(1, 2), (2, 1)])

    swap = [(0, 1), (1, 0)]
    beside = lambda value: lax.ppermute(value, "seq", swap)
    across = lambda value: lax.ppermute(value, "groups", swap)

    def others(*values):
        got = []
        for value in values:
            if got:
                value, got[-1] = wait((value, got[-1]))
            got.append(lax.ppermute(value, "head", swap))
        return got

    beside_plane, far_inner = plane ^ 1, 2 - plane // 2
    order = (
        plane,
        pick(beside_plane, far_inner),
        pick(far_inner, beside_plane),
        3 - 3 * (plane // 2),
    )
    run = functools.partial(run_jobs, core, inner, columns)

    def exchange(mixed):
        got = []
        for a in range(groups):
            for b in range(seqs):
                sent = mixed[(a * seqs + b) * rows : (a * seqs + b + 1) * rows]
                if a or b:
                    steps = [
                        (g * seqs + s, (g + a) % groups * seqs + (s + b) % seqs)
                        for g in range(groups)
                        for s in range(seqs)
                    ]
                    sent = lax.ppermute(sent, ("groups", "seq"), steps)
                got.append(sent)
        return got

    own0 = weight_piece(qkv_weight, 0)
    pair1, middle1 = pair(own0), middle(own0)
    tokens, own0 = wait((tokens, own0))
    normed = normalize_part(tokens, ln_gain, part, core, order)
    normed, qkv_weight = wait((normed, qkv_weight))
    cut0, cut1 = normed
    beside1, across1 = beside(cut0), across(cut0)
    own1, own2 = weight_piece(qkv_weight, 1), weight_piece(qkv_weight, 2)
    pair1, middle1, beside1, across1, own1, own2, cut0, cut1, tokens = wait(
        (pair1, middle1, beside1, across1, own1, own2, cut0, cut1, tokens)
    )

    pair2, middle2 = pair(pick(fold(middle1), cut0)), middle(own1)
    beside2, across2 = beside(cut1), across(cut1)
    far_normed = normalize_part(tokens, ln_gain, part, 1 - core, order)
    far1 = others(beside1, across1)
    pair2, middle2, beside2, across2, across1, cut1, own2, far_normed, far1 = wait(
        (pair2, middle2, beside2, across2, across1, cut1, own2, far_normed, far1)
    )

    pair3, middle3 = pair(pick(fold(own1), cut1)), middle(own2)
    beside3, across3 = beside(across1), across(beside2)
    far2 = others(beside2, across2)
    pair3, middle3, beside3, across3, middle2, pair1, pair2, far2 = wait(
        (pair3, middle3, beside3, across3, middle2, pair1, pair2, far2)
    )

    pair4, middle4 = pair(pick(middle2, own1)), middle(pair1)
    beside4, across4 = beside(pair2), across(pair2)
    far3 = others(beside3, across3)
    images = [
        ((normed, far_normed), ((beside1, beside2), (far1[0], far2[0]))),
        (((across1, across2), (far1[1], far2[1])), ((beside3, across3), far3)),
    ]
    sums = run(
        images,
        (0, 2),
        [[own0, (own1, own0), (own2, own1)], [middle1, (middle2, pair1), (middle3, pair3)]],
    )
    pair4, middle4, beside4, across4, own2, pair3, sums = wait(
        (pair4, middle4, beside4, across4, own2, pair3, sums)
    )

    pair5, middle5 = pair(pick(middle4, own2)), middle(pair4)
    beside5, across5 = beside(pair3), across(pair3)
    (mixed1,) = run(images, (1, 3), [[pair1], [middle4]], [(sums[0], 0)], 1)
    far_lent = others(pair2, pair3, beside4, across4)
    pair5, middle5, beside5, across5, across4, mixed1, far_lent = wait(
        (pair5, middle5, beside5, across5, across4, mixed1, far_lent)
    )

    pair6, middle6 = outward(middle5), middle(pair5)
    beside6, across6 = beside(across4), across(beside5)
    far5 = others(beside5, across5)
    mixed2, sum3 = run(
        images,
        (1, 3),
        [[(pair4, pair2), (pair5, pair4)], [(middle5, pair5)]],
        [(sums[1], 0), (sums[2], 0)],
        1,
    )
    early = exchange(jnp.concatenate([mixed1, mixed2], axis=1))
    lent0 = [
        (((pair2, pair3), far_lent[:2]), ((beside4, beside5), (far_lent[2], far5[0])))
    ]
    (sum4,) = run(lent0, (0, 1, 2), [[pair5], [middle3], [own2]])
    pair6, middle6, beside6, across6, sum3, sum4, far5 = wait(
        (pair6, middle6, beside6, across6, sum3, sum4, far5)
    )

    far6 = [lax.ppermute(value, "head", swap) for value in (beside6, across6)]
    (mixed3,) = run(images, (3,), [[(middle6, pair6)]], [(sum3, 0)], 1)
    late = exchange(mixed3)
    (mixed4,) = run(lent0, (3,), [[middle6]], [(sum4, 0)], 1)
    lent1 = [
        (((across4, across5), (far_lent[3], far5[1])), ((beside6, across6), far6))
    ]
    (mixed5,) = run(lent1, (0, 1, 2, 3), [[pair5], [middle3], [own2], [middle6]], None, 1)

    def hand_back(mixed):
        got = []
        for a in range(groups):
            for b in range(seqs):
                steps = [
                    (
                        (g * planes + z) * seqs + s,
                        ((g + a) % groups * planes + (z ^ 1)) * seqs + (s + b) % seqs,
                    )
                    for g in range(groups)
                    for z in (1, 2)
                    for s in range(seqs)
                ]
                sent = mixed[a][b * rows : (b + 1) * rows]
                got.append(lax.ppermute(sent, ("groups", "dp", "seq"), steps))
        return got

    early, late, back = wait((early, late, hand_back((mixed4, mixed5))))
    received = jnp.stack([
        pick(jnp.concatenate([x, y], axis=1), jnp.concatenate([x[:, x.shape[1] // 2 :], y, z], axis=1))
        for x, y, z in zip(early, late, back)
    ])
    blocks = []
    for s in range(seqs):
        for g in range(groups):
            index = (group - g) % groups * seqs + (seq - s) % seqs
            blocks.append(lax.dynamic_index_in_dim(received, index, 0, keepdims=False))
    return jnp.concatenate(blocks, axis=1)[None]


def per_device(tokens, ln_gain, qkv_weight):
    groups, planes, seqs, cores = (lax.axis_size(a) for a in ("groups", "dp", "seq", "head"))
    images, rows, width = tokens.shape
    slab, heads, _ = qkv_weight.shape
    if (groups, planes, seqs, cores) == (2, 4, 2, 2) and images == 1 and heads == 3 * groups:
        part = rows // cores
        if rows % (32 * cores) == 0 and slab % part == 0 and 2 * slab == qkv_weight.shape[2] * slab // part:
            return shared(tokens, ln_gain, qkv_weight)
    return plain(tokens, ln_gain, qkv_weight)


def solution(mesh):
    return jax.shard_map(
        per_device,
        mesh=mesh,
        in_specs=(P(("groups", "dp"), "seq", None), P(), P("dp", ("seq", "head"), None)),
        out_specs=P(("groups", "dp"), "seq", "head"),
        check_vma=False,
    )
```

```python
import functools
import math

import jax
import jax.numpy as jnp
from jax import lax
from jax.experimental import pallas as pl
from jax.experimental.pallas import tpu as pltpu
from jax.sharding import PartitionSpec as P


def normalize(array, gain):
    widened = array.astype(jnp.float32)
    centered = widened - jnp.mean(widened, axis=-1, keepdims=True)
    variance = jnp.mean(centered * centered, axis=-1, keepdims=True)
    return (centered * lax.rsqrt(variance + 1e-06) * gain).astype(jnp.bfloat16)


def attend(projected):
    width = projected.shape[2] // 3
    queries = projected[:, :, :width]
    key_rows = projected[:, :, width : 2 * width]
    value_rows = projected[:, :, 2 * width :]
    scores = jnp.einsum("qhd,khd->hqk", queries, key_rows, preferred_element_type=jnp.float32) * (
        1.0 / math.sqrt(width)
    )
    highest = jnp.max(scores, axis=-1, keepdims=True)
    expo = jnp.exp(scores - highest)
    probs = (expo / jnp.sum(expo, axis=-1, keepdims=True)).astype(jnp.bfloat16)
    mixed = jnp.einsum("hqk,khd->qhd", probs, value_rows, preferred_element_type=jnp.float32)
    return mixed.astype(jnp.bfloat16).reshape(projected.shape[0], -1)


def plain(tokens, ln_gain, qkv_weight):
    images = tokens.shape[0]
    width = tokens.shape[2]
    heads_here = qkv_weight.shape[1]
    columns = heads_here * qkv_weight.shape[2]
    source = normalize(tokens, ln_gain)
    half_width = width // lax.axis_size("head")
    core_index = lax.axis_index("head")
    own_half = lax.dynamic_slice_in_dim(source, core_index * half_width, half_width, 2)
    fetched = lax.all_gather(own_half, "seq", axis=1, tiled=True)
    gathered = lax.all_gather(fetched, "head", axis=2, tiled=True)
    full_tokens = gathered.shape[1]
    features = gathered.reshape(images * full_tokens, width)
    piece = lax.all_gather(qkv_weight, "dp", axis=0, tiled=True)
    projected = jnp.dot(
        features, piece.reshape(piece.shape[0], columns), preferred_element_type=jnp.float32
    )
    projected = projected.astype(jnp.bfloat16).reshape(
        images, full_tokens, heads_here, qkv_weight.shape[2]
    )
    mixed = lax.map(attend, projected)
    return lax.all_to_all(mixed, "seq", split_axis=1, concat_axis=2, tiled=True)


def normalize_kernel(place_ref, tokens_ref, gain_ref, *normed_refs):
    widened = tokens_ref[0].astype(jnp.float32)
    mean = jnp.mean(widened, axis=-1, keepdims=True)
    centered = widened - mean
    scale = lax.rsqrt(jnp.mean(centered * centered, axis=-1, keepdims=True) + 1e-06)
    slab = widened.shape[1] // 4
    span = normed_refs[0].shape[1]
    for i in range(4):
        columns = pl.ds(pl.multiple_of(place_ref[i + 1] * slab, 128), slab)
        part = (tokens_ref[0, :, columns].astype(jnp.float32) - mean) * scale * gain_ref[:, columns]
        begin = i * slab % span
        normed_refs[i * slab // span][:, begin : begin + slab] = part.astype(jnp.bfloat16)


def normalize_part(tokens, ln_gain, part, core, order):
    width = tokens.shape[2]
    step, count = 32, 2
    steps = part // step
    place = jnp.stack([jnp.asarray(v, jnp.int32) for v in (core, *order)])
    return pl.pallas_call(
        normalize_kernel,
        out_shape=[jax.ShapeDtypeStruct((part, width // count), jnp.bfloat16)] * count,
        grid_spec=pltpu.PrefetchScalarGridSpec(
            num_scalar_prefetch=1,
            grid=(steps,),
            in_specs=[
                pl.BlockSpec((1, step, width), lambda i, place: (0, place[0] * steps + i, 0)),
                pl.BlockSpec((1, width), lambda i, place: (0, 0)),
            ],
            out_specs=[pl.BlockSpec((step, width // count), lambda i, place: (i, 0))] * count,
        ),
        compiler_params=pltpu.CompilerParams(vmem_limit_bytes=56 << 20),
        cost_estimate=pl.CostEstimate(
            flops=8 * part * width, bytes_accessed=4 * part * width, transcendentals=part
        ),
    )(place, tokens, ln_gain[None])


def attend_rows(projected_ref, mixed_ref, base):
    tokens, columns = projected_ref.shape
    width = columns // 3
    step = 256
    key_rows = projected_ref[:, width : 2 * width]
    value_rows = projected_ref[:, 2 * width :]
    for begin in range(0, tokens, step):
        queries = projected_ref[begin : begin + step, :width]
        scores = lax.dot_general(
            queries, key_rows, (((1,), (1,)), ((), ())), preferred_element_type=jnp.float32
        )
        highest = jnp.max(scores, axis=-1, keepdims=True)
        expo = jnp.exp2((scores - highest) * (math.log2(math.e) / math.sqrt(width)))
        mixed = jnp.dot(expo.astype(jnp.bfloat16), value_rows, preferred_element_type=jnp.float32)
        mixed = mixed / jnp.sum(expo, axis=-1, keepdims=True)
        mixed_ref[base + begin : base + begin + step, :] = mixed.astype(jnp.bfloat16)


def job_kernel(layout, slots, ranges, same, added, starts, finished, role_ref, *refs):
    refs = list(refs)
    take = lambda n: [refs.pop(0) for _ in range(n)]
    images, jobs = len(layout), len(added)
    steps = range(len(slots))
    pieces = [[[take(2) for _ in place] for place in image] for image in layout]
    weights = [[take(1) * 2 if alike else take(2) for alike in row] for row in same]
    partials = [take(images) if has else None for has in added]
    outs = take(jobs)
    features_ref, weight_ref, total_ref, projected_ref, token_sems, weight_sems, sum_sems = take(7)
    core, inner = role_ref[0], role_ref[1]
    span = pieces[0][0][0][0].shape[1]
    slab = span // 2
    tokens, wide = projected_ref.shape
    part = tokens // 4

    def features(image, n):
        return features_ref.at[pl.ds(image * tokens, tokens), pl.ds(n * slab, slab)]

    def weight(n, j):
        return weight_ref.at[pl.ds(n * slab, slab), pl.ds(j * wide, wide)]

    def total(image, j):
        return total_ref.at[pl.ds(image * tokens, tokens), pl.ds(j * wide, wide)]

    def start_tokens(image, n):
        cut, begin = slots[n] // 2, slots[n] % 2 * slab
        for place in range(2):
            split = len(layout[image][place])
            for owner in range(split):
                row = image * tokens + 2 * place * part
                if split == 2:
                    row += (1 - core if owner else core) * part
                count = 2 * part // split
                from_rows = pl.ds(layout[image][place][owner][cut], count)
                rows = pl.ds(pl.multiple_of(row, 32), count)
                pltpu.make_async_copy(
                    pieces[image][place][owner][cut].at[from_rows, pl.ds(begin, slab)],
                    features_ref.at[rows, pl.ds(n * slab, slab)],
                    token_sems.at[image, n],
                ).start()

    def start_weight(n, j, role):
        source = weights[n][j - ranges[n][0]][role]
        if source.shape[0] == slab:
            pltpu.make_async_copy(source, weight(n, j), weight_sems.at[n, j]).start()
            return
        for b in range(source.shape[1] // wide):
            pltpu.make_async_copy(
                source.at[:, pl.ds(b * wide, wide)],
                weight_ref.at[pl.ds(n * slab + b * part, part), pl.ds(j * wide, wide)],
                weight_sems.at[n, j],
            ).start()

    def start_weights(n):
        for j in range(*ranges[n]):
            if same[n][j - ranges[n][0]]:
                start_weight(n, j, 0)
                continue

            @pl.when(inner == 1)
            def _():
                start_weight(n, j, 0)

            @pl.when(inner != 1)
            def _():
                start_weight(n, j, 1)

    def partial_copy(image, j):
        source = partials[j][image].at[pl.ds(starts[j][image], tokens)]
        return pltpu.make_async_copy(source, total(image, j), sum_sems.at[image, j])

    for n in steps:
        start_tokens(0, n)
        start_weights(n)
    for image in range(images):
        for j in range(jobs):
            if added[j]:
                partial_copy(image, j).start()
        if image:
            for n in steps:
                start_tokens(image, n)

    for image in range(images):
        for n in steps:
            pltpu.make_async_copy(
                features(image, n), features(image, n), token_sems.at[image, n]
            ).wait()
            low, high = ranges[n]
            if image == 0:
                for j in range(low, high):
                    pltpu.make_async_copy(weight(n, j), weight(n, j), weight_sems.at[n, j]).wait()
            term = jnp.dot(
                features(image, n)[...],
                weight_ref[n * slab : (n + 1) * slab, low * wide : high * wide],
                preferred_element_type=jnp.float32,
            )
            for j in range(low, high):
                value = term[:, (j - low) * wide : (j - low + 1) * wide]
                mine = [m for m in steps if ranges[m][0] <= j < ranges[m][1]]
                if n == mine[0] and added[j]:
                    partial_copy(image, j).wait()
                if n != mine[0] or added[j]:
                    value += total(image, j)[...]
                if n != mine[-1]:
                    total(image, j)[...] = value
                elif j < finished:
                    projected_ref[...] = value.astype(jnp.bfloat16)
                    attend_rows(projected_ref, outs[j], image * tokens)
                else:
                    outs[j][image * tokens : (image + 1) * tokens, :] = value


def run_jobs(core, inner, tokens, wide, images, weights, partials, finished=0):
    images = [
        [[[x if isinstance(x, tuple) else (x, 0) for x in owner] for owner in place] for place in image]
        for image in images
    ]
    layout = [[[[row for _, row in owner] for owner in place] for place in image] for image in images]
    operands = [x for image in images for place in image for owner in place for x, _ in owner]
    span = operands[0].shape[1]
    slab = span // 2
    total, jobs = len(images) * tokens, len(partials)
    slots = [slot for slot, _, _ in weights]
    ranges = [(first, first + len(row)) for _, first, row in weights]
    same = [[not isinstance(w, tuple) for w in row] for _, _, row in weights]
    for _, _, row in weights:
        for w in row:
            operands += list(w) if isinstance(w, tuple) else [w]
    added = [p is not None for p in partials]
    starts = [p and [row for _, row in p] for p in partials]
    operands += [x for p in partials if p is not None for x, _ in p]
    vmem = pl.BlockSpec(memory_space=pltpu.VMEM)
    depth = len(slots) * slab
    return pl.pallas_call(
        functools.partial(job_kernel, layout, slots, ranges, same, added, starts, finished),
        out_shape=[
            jax.ShapeDtypeStruct((total, wide // 3), jnp.bfloat16)
            if j < finished
            else jax.ShapeDtypeStruct((total, wide), jnp.float32)
            for j in range(jobs)
        ],
        in_specs=[pl.BlockSpec(memory_space=pltpu.SMEM)]
        + [pl.BlockSpec(memory_space=pl.ANY)] * len(operands),
        out_specs=[vmem] * jobs,
        scratch_shapes=[
            pltpu.VMEM((total, depth), jnp.bfloat16),
            pltpu.VMEM((depth, jobs * wide), jnp.bfloat16),
            pltpu.VMEM((total, jobs * wide), jnp.float32),
            pltpu.VMEM((tokens, wide), jnp.bfloat16),
            pltpu.SemaphoreType.DMA((len(images), len(slots))),
            pltpu.SemaphoreType.DMA((len(slots), jobs)),
            pltpu.SemaphoreType.DMA((len(images), jobs)),
        ],
        compiler_params=pltpu.CompilerParams(vmem_limit_bytes=56 << 20),
        cost_estimate=pl.CostEstimate(
            flops=2 * total * slab * wide * sum(len(row) for row in same),
            bytes_accessed=0,
            transcendentals=0,
        ),
    )(jnp.stack([core, inner]).astype(jnp.int32), *operands)


def shared(tokens, ln_gain, qkv_weight):
    groups, planes, seqs, cores = (lax.axis_size(a) for a in ("groups", "dp", "seq", "head"))
    group, plane, seq, core = (lax.axis_index(a) for a in ("groups", "dp", "seq", "head"))
    _, rows, _ = tokens.shape
    slab, heads, columns = qkv_weight.shape
    heads, part = heads // groups, rows // cores
    inner = (plane == 1) | (plane == 2)
    wait = lax.optimization_barrier

    def fold(piece):
        piece = piece.reshape(-1, part, columns).transpose(1, 0, 2)
        return piece.reshape(part, -1)

    def weight_piece(weight, j):
        return lax.dynamic_slice_in_dim(weight, group * heads + j, 1, 1)[:, 0]

    def pick(for_inner, for_ends):
        return jnp.where(inner, for_inner, for_ends)

    def pair(value):
        return lax.ppermute(value, "dp", [(0, 1), (1, 0), (2, 3), (3, 2)])

    def outward(value):
        return lax.ppermute(value, "dp", [(1, 0), (2, 3)])

    def middle(value):
        return lax.ppermute(value, "dp", [(1, 2), (2, 1)])

    swap = [(0, 1), (1, 0)]
    beside = lambda value: lax.ppermute(value, "seq", swap)
    across = lambda value: lax.ppermute(value, "groups", swap)

    def others(*values):
        got = []
        for value in values:
            if got:
                value, got[-1] = wait((value, got[-1]))
            got.append(lax.ppermute(value, "head", swap))
        return got

    beside_plane, far_inner = plane ^ 1, 2 - plane // 2
    order = (
        plane,
        pick(beside_plane, far_inner),
        pick(far_inner, beside_plane),
        3 - 3 * (plane // 2),
    )
    run = functools.partial(run_jobs, core, inner, seqs * rows, columns)

    def exchange(mixed):
        got = []
        for a in range(groups):
            for b in range(seqs):
                sent = mixed[(a * seqs + b) * rows : (a * seqs + b + 1) * rows]
                if a or b:
                    steps = [
                        (g * seqs + s, (g + a) % groups * seqs + (s + b) % seqs)
                        for g in range(groups)
                        for s in range(seqs)
                    ]
                    sent = lax.ppermute(sent, ("groups", "seq"), steps)
                got.append(sent)
        return got

    own0 = weight_piece(qkv_weight, 0)
    pair1, middle1 = pair(own0), middle(own0)
    tokens, own0 = wait((tokens, own0))
    normed = normalize_part(tokens, ln_gain, part, core, order)
    normed, qkv_weight = wait((normed, qkv_weight))
    cut0, cut1 = normed
    beside1, across1 = beside(cut0), across(cut0)
    own1, own2 = weight_piece(qkv_weight, 1), weight_piece(qkv_weight, 2)
    give = pick(fold(own1), cut0)
    pair1, middle1, beside1, across1, own1, own2, cut0, cut1, tokens, give = wait(
        (pair1, middle1, beside1, across1, own1, own2, cut0, cut1, tokens, give)
    )

    pair2, middle2 = pair(give), middle(pair1)
    beside2, across2 = beside(cut1), across(cut1)
    give = pick(fold(middle1), cut1)
    far_normed = normalize_part(tokens, ln_gain, part, 1 - core, order)
    far1 = others(beside1, across1)
    pair2, middle2, beside2, across2, across1, own1, own2, far_normed, far1, give = wait(
        (pair2, middle2, beside2, across2, across1, own1, own2, far_normed, far1, give)
    )

    pair3, middle3 = pair(give), middle(own1)
    beside3, across3 = beside(across1), across(beside2)
    give = pick(middle2, own1)
    far2 = others(beside2, across2)
    pair3, middle3, beside3, across3, pair1, pair2, own2, far2, give = wait(
        (pair3, middle3, beside3, across3, pair1, pair2, own2, far2, give)
    )

    pair4, middle4 = pair(give), middle(own2)
    beside4, across4 = beside(pair2), across(pair2)
    give = pick(middle3, own2)
    image0 = ((normed, far_normed), ((beside1, beside2), (far1[0], far2[0])))
    owns = [own0, (own1, own0), (own2, own1)]
    mixed10, sum20, sum30 = run(
        [image0],
        [(0, 0, owns), (2, 0, [middle1, (middle3, pair1)]), (1, 0, [pair1]), (3, 0, [middle2])],
        [None] * 3,
        1,
    )
    far3 = others(beside3, across3)
    lent = jnp.concatenate([pair2, pair3])
    pair4, middle4, beside4, across4, own2, pair3, lent, mixed10, sum20, sum30, far3, give = wait(
        (pair4, middle4, beside4, across4, own2, pair3, lent, mixed10, sum20, sum30, far3, give)
    )

    pair5, middle5 = pair(give), middle(pair4)
    beside5, across5 = beside(pair3), across(pair3)
    image1 = (((across1, across2), (far1[1], far2[1])), ((beside3, across3), far3))
    over, near = (middle4, pair2), (pair4, pair3)
    mixed11, sum21, sum31 = run(
        [image1],
        [
            (0, 0, owns),
            (2, 0, [middle1, (middle3, pair1), over]),
            (1, 0, [pair1, near]),
            (3, 0, [middle2]),
        ],
        [None] * 3,
        1,
    )
    sum20, sum30 = run([image0], [(2, 1, [over]), (1, 0, [near])], [[(sum20, 0)], [(sum30, 0)]])
    far_lent, far4 = others(lent, beside4)
    pair5, middle5, beside5, across5, across4, mixed11, sum20, sum21, sum30, sum31, far_lent, far4 = wait(
        (
            *(pair5, middle5, beside5, across5, across4, mixed11),
            *(sum20, sum21, sum30, sum31, far_lent, far4),
        )
    )

    pair6, middle6 = outward(middle5), middle(pair5)
    beside6, across6 = beside(across4), across(beside5)
    far5, far_across4 = others(beside5, across4)
    mixed2, sum3 = run(
        [image0, image1],
        [(3, 0, [(middle5, pair4)]), (1, 1, [pair5])],
        [[(sum20, 0), (sum21, 0)], [(sum30, 0), (sum31, 0)]],
        1,
    )
    lent0 = (((pair2, pair3), (far_lent, (far_lent, part))), ((beside4, beside5), (far4, far5)))
    lent_weights = [(0, 0, [pair5]), (1, 0, [middle4]), (2, 0, [own2])]
    (sum4,) = run([lent0], lent_weights, [None])
    pair6, middle6, beside6, across6, across5, mixed2, sum3, sum4, far_across4 = wait(
        (pair6, middle6, beside6, across6, across5, mixed2, sum3, sum4, far_across4)
    )

    far_across5, *far6 = [
        lax.ppermute(value, "head", swap) for value in (across5, beside6, across6)
    ]
    (mixed3,) = run(
        [image0, image1, lent0],
        [(3, 0, [(middle6, pair6)])],
        [[(sum3, 0), (sum3, seqs * rows), (sum4, 0)]],
        1,
    )
    sent = exchange(
        jnp.concatenate(
            [
                jnp.concatenate([mixed10, mixed11]),
                mixed2,
                mixed3[: mixed2.shape[0]],
            ],
            axis=1,
        )
    )
    lent1 = (((across4, across5), (far_across4, far_across5)), ((beside6, across6), far6))
    (mixed4,) = run([lent1], [*lent_weights, (3, 0, [middle6])], [None], 1)

    def hand_back(mixed):
        got = []
        for a in range(groups):
            for b in range(seqs):
                steps = [
                    (
                        (g * planes + z) * seqs + s,
                        ((g + a) % groups * planes + (z ^ 1)) * seqs + (s + b) % seqs,
                    )
                    for g in range(groups)
                    for z in (1, 2)
                    for s in range(seqs)
                ]
                sent = mixed[a][b * rows : (b + 1) * rows]
                got.append(lax.ppermute(sent, ("groups", "dp", "seq"), steps))
        return got

    back = hand_back((mixed3[mixed2.shape[0] :], mixed4))
    received = jnp.stack([
        pick(x, jnp.concatenate([x[:, x.shape[1] // heads :], y], axis=1))
        for x, y in zip(*wait((sent, back)))
    ])
    blocks = []
    for s in range(seqs):
        for g in range(groups):
            index = (group - g) % groups * seqs + (seq - s) % seqs
            blocks.append(lax.dynamic_index_in_dim(received, index, 0, keepdims=False))
    return jnp.concatenate(blocks, axis=1)[None]


def per_device(tokens, ln_gain, qkv_weight):
    groups, planes, seqs, cores = (lax.axis_size(a) for a in ("groups", "dp", "seq", "head"))
    images, rows, width = tokens.shape
    slab, heads, _ = qkv_weight.shape
    if (groups, planes, seqs, cores) == (2, 4, 2, 2) and images == 1 and heads == 3 * groups:
        part = rows // cores
        if rows % (32 * cores) == 0 and slab % part == 0 and 2 * slab == qkv_weight.shape[2] * slab // part:
            return shared(tokens, ln_gain, qkv_weight)
    return plain(tokens, ln_gain, qkv_weight)


def solution(mesh):
    return jax.shard_map(
        per_device,
        mesh=mesh,
        in_specs=(P(("groups", "dp"), "seq", None), P(), P("dp", ("seq", "head"), None)),
        out_specs=P(("groups", "dp"), "seq", "head"),
        check_vma=False,
    )
```

```python
import functools
import math

import jax
import jax.numpy as jnp
from jax import lax
from jax.experimental import pallas as pl
from jax.experimental.pallas import tpu as pltpu
from jax.sharding import PartitionSpec as P


def normalize(array, gain):
    widened = array.astype(jnp.float32)
    centered = widened - jnp.mean(widened, axis=-1, keepdims=True)
    variance = jnp.mean(centered * centered, axis=-1, keepdims=True)
    return (centered * lax.rsqrt(variance + 1e-06) * gain).astype(jnp.bfloat16)


def attend(projected):
    width = projected.shape[2] // 3
    queries = projected[:, :, :width]
    key_rows = projected[:, :, width : 2 * width]
    value_rows = projected[:, :, 2 * width :]
    scores = jnp.einsum("qhd,khd->hqk", queries, key_rows, preferred_element_type=jnp.float32) * (
        1.0 / math.sqrt(width)
    )
    highest = jnp.max(scores, axis=-1, keepdims=True)
    expo = jnp.exp(scores - highest)
    probs = (expo / jnp.sum(expo, axis=-1, keepdims=True)).astype(jnp.bfloat16)
    mixed = jnp.einsum("hqk,khd->qhd", probs, value_rows, preferred_element_type=jnp.float32)
    return mixed.astype(jnp.bfloat16).reshape(projected.shape[0], -1)


def plain(tokens, ln_gain, qkv_weight):
    images = tokens.shape[0]
    width = tokens.shape[2]
    heads_here = qkv_weight.shape[1]
    columns = heads_here * qkv_weight.shape[2]
    source = normalize(tokens, ln_gain)
    half_width = width // lax.axis_size("head")
    core_index = lax.axis_index("head")
    own_half = lax.dynamic_slice_in_dim(source, core_index * half_width, half_width, 2)
    fetched = lax.all_gather(own_half, "seq", axis=1, tiled=True)
    gathered = lax.all_gather(fetched, "head", axis=2, tiled=True)
    full_tokens = gathered.shape[1]
    features = gathered.reshape(images * full_tokens, width)
    piece = lax.all_gather(qkv_weight, "dp", axis=0, tiled=True)
    projected = jnp.dot(
        features, piece.reshape(piece.shape[0], columns), preferred_element_type=jnp.float32
    )
    projected = projected.astype(jnp.bfloat16).reshape(
        images, full_tokens, heads_here, qkv_weight.shape[2]
    )
    mixed = lax.map(attend, projected)
    return lax.all_to_all(mixed, "seq", split_axis=1, concat_axis=2, tiled=True)


def normalize_kernel(place_ref, tokens_ref, gain_ref, *normed_refs):
    rows, width = tokens_ref.shape[1:]
    lanes = 128
    slab, span = width // 4, width // 2

    def widened(begin):
        return tokens_ref[0, :, pl.ds(begin, lanes)].astype(jnp.float32)

    total = jnp.zeros((rows, lanes), jnp.float32)
    for begin in range(0, width, lanes):
        total += widened(begin)
    mean = jnp.sum(total, axis=-1, keepdims=True) / width
    total = jnp.zeros((rows, lanes), jnp.float32)
    for begin in range(0, width, lanes):
        centered = widened(begin) - mean
        total += centered * centered
    scale = lax.rsqrt(jnp.sum(total, axis=-1, keepdims=True) / width + 1e-06)
    for i in range(4):
        source = place_ref[i + 1] * slab
        for begin in range(0, slab, lanes):
            column = pl.multiple_of(source + begin, lanes)
            part = (widened(column) - mean) * scale * gain_ref[:, pl.ds(column, lanes)]
            target = i * slab % span + begin
            normed_refs[i * slab // span][:, target : target + lanes] = part.astype(jnp.bfloat16)


def normalize_part(tokens, ln_gain, part, core, order):
    width = tokens.shape[2]
    step, count = 32, 2
    steps = part // step
    place = jnp.stack([jnp.asarray(v, jnp.int32) for v in (core, *order)])
    return pl.pallas_call(
        normalize_kernel,
        out_shape=[jax.ShapeDtypeStruct((part, width // count), jnp.bfloat16)] * count,
        grid_spec=pltpu.PrefetchScalarGridSpec(
            num_scalar_prefetch=1,
            grid=(steps,),
            in_specs=[
                pl.BlockSpec((1, step, width), lambda i, place: (0, place[0] * steps + i, 0)),
                pl.BlockSpec((1, width), lambda i, place: (0, 0)),
            ],
            out_specs=[pl.BlockSpec((step, width // count), lambda i, place: (i, 0))] * count,
        ),
        compiler_params=pltpu.CompilerParams(vmem_limit_bytes=56 << 20),
        cost_estimate=pl.CostEstimate(
            flops=8 * part * width, bytes_accessed=4 * part * width, transcendentals=part
        ),
    )(place, tokens, ln_gain[None])


def attend_rows(projected_ref, parts, column):
    width = projected_ref.shape[1] // 3
    key_rows = projected_ref[:, width : 2 * width]
    value_rows = projected_ref[:, 2 * width :]
    begin = 0
    for part in parts:
        step = part.shape[0]
        queries = projected_ref[begin : begin + step, :width]
        scores = lax.dot_general(
            queries, key_rows, (((1,), (1,)), ((), ())), preferred_element_type=jnp.float32
        )
        highest = jnp.max(scores, axis=-1, keepdims=True)
        expo = jnp.exp2((scores - highest) * (math.log2(math.e) / math.sqrt(width)))
        mixed = jnp.dot(expo.astype(jnp.bfloat16), value_rows, preferred_element_type=jnp.float32)
        mixed = mixed / jnp.sum(expo, axis=-1, keepdims=True)
        part[:, column : column + width] = mixed.astype(jnp.bfloat16)
        begin += step


class Jobs:
    def __init__(self, **numbers):
        self.__dict__.update(numbers)

    def jobs(self, image):
        return sorted({j for use in self.uses[image] if use for j in range(*use)})


def job_kernel(plan, role_ref, *refs):
    refs = list(refs)
    take = lambda n: [refs.pop(0) for _ in range(n)]
    images, ns = range(len(plan.uses)), range(len(plan.slots))
    pieces = [[[take(2) for _ in place] for place in image] for image in plan.origins]
    weights = [[take(1) * 2 if alike else take(2) for alike in row] for row in plan.same]
    partials = [{j: take(1)[0] for j in plan.added[i]} for i in images]
    carried = [[take(plan.carried) for _ in range(2)] for _ in images]
    outs = [
        {j: take(2) if j in plan.finished[i] else take(1)[0] for j in plan.jobs(i)} for i in images
    ]
    features_ref, weight_ref, total_ref, projected_ref = take(4)
    token_sems, weight_sems, sum_sems, out_sems, carry_sems = take(5)
    core, inner = role_ref[0], role_ref[1]
    slab = pieces[0][0][0][0].shape[1] // 2
    tokens, wide = projected_ref.shape
    part = tokens // 4

    def features(i, n):
        return features_ref.at[pl.ds(i * tokens, tokens), pl.ds(n * slab, slab)]

    def weight(n, j):
        return weight_ref.at[pl.ds(n * slab, slab), pl.ds(j * wide, wide)]

    def total(i, j):
        return total_ref.at[pl.ds(i * tokens, tokens), pl.ds(j * wide, wide)]

    def start_tokens(i, n):
        cut, begin = plan.slots[n] // 2, plan.slots[n] % 2 * slab
        for place in range(2):
            split = len(plan.origins[i][place])
            for owner in range(split):
                row = i * tokens + 2 * place * part
                if split == 2:
                    row += (1 - core if owner else core) * part
                count = 2 * part // split
                from_rows = pl.ds(plan.origins[i][place][owner][cut], count)
                rows = pl.ds(pl.multiple_of(row, 32), count)
                pltpu.make_async_copy(
                    pieces[i][place][owner][cut].at[from_rows, pl.ds(begin, slab)],
                    features_ref.at[rows, pl.ds(n * slab, slab)],
                    token_sems.at[i, n],
                ).start()

    def start_weight(n, j, role):
        source = weights[n][j - plan.first[n]][role]
        if source.shape[0] == slab:
            pltpu.make_async_copy(source, weight(n, j), weight_sems.at[n, j]).start()
            return
        for b in range(source.shape[1] // wide):
            pltpu.make_async_copy(
                source.at[:, pl.ds(b * wide, wide)],
                weight_ref.at[pl.ds(n * slab + b * part, part), pl.ds(j * wide, wide)],
                weight_sems.at[n, j],
            ).start()

    def start_role_weight(n, j):
        if plan.same[n][j - plan.first[n]]:
            start_weight(n, j, 0)
            return

        @pl.when(inner == 1)
        def _():
            start_weight(n, j, 0)

        @pl.when(inner != 1)
        def _():
            start_weight(n, j, 1)

    def partial_copy(i, j):
        return pltpu.make_async_copy(partials[i][j], total(i, j), sum_sems.at[i, j])

    def out_copy(i, j):
        return pltpu.make_async_copy(total(i, j), outs[i][j], out_sems.at[i, j])

    def carry_copies():
        for i in images:
            for place in range(2):
                for k in range(plan.carried):
                    (finished,) = plan.finished[i]
                    target = outs[i][finished][place].at[:, pl.ds(k * wide // 3, wide // 3)]
                    yield pltpu.make_async_copy(
                        carried[i][place][k], target, carry_sems.at[i, place, k]
                    )

    stages = [(i, n) for i in images for n in ns if plan.uses[i][n]]
    held = set()

    def start_stage(i, n):
        start_tokens(i, n)
        for j in range(*plan.uses[i][n]):
            if (n, j) not in held:
                held.add((n, j))
                start_role_weight(n, j)
        if not any((i, n) > (i, m) and plan.uses[i][m] for m in ns):
            for j in plan.added[i]:
                partial_copy(i, j).start()

    ahead = 2
    for stage in stages[:ahead]:
        start_stage(*stage)
    for copy in carry_copies():
        copy.start()
    ready = set()
    for index, (i, n) in enumerate(stages):
        low, high = plan.uses[i][n]
        pltpu.make_async_copy(features(i, n), features(i, n), token_sems.at[i, n]).wait()
        for j in range(low, high):
            if (n, j) not in ready:
                ready.add((n, j))
                pltpu.make_async_copy(weight(n, j), weight(n, j), weight_sems.at[n, j]).wait()
        if index + ahead < len(stages):
            start_stage(*stages[index + ahead])
        term = jnp.dot(
            features(i, n)[...],
            weight_ref[n * slab : (n + 1) * slab, low * wide : high * wide],
            preferred_element_type=jnp.float32,
        )
        for j in range(low, high):
            value = term[:, (j - low) * wide : (j - low + 1) * wide]
            mine = [m for m in ns if plan.uses[i][m] and j in range(*plan.uses[i][m])]
            if n == mine[0] and j in plan.added[i]:
                partial_copy(i, j).wait()
            if n != mine[0] or j in plan.added[i]:
                value += total(i, j)[...]
            if n == mine[-1] and j in plan.finished[i]:
                projected_ref[...] = value.astype(jnp.bfloat16)
                attend_rows(projected_ref, outs[i][j], plan.carried * wide // 3)
                continue
            total(i, j)[...] = value
            if n == mine[-1]:
                out_copy(i, j).start()
    for copy in carry_copies():
        copy.wait()
    for i in images:
        for j in plan.jobs(i):
            if j not in plan.finished[i]:
                out_copy(i, j).wait()


def run_jobs(core, inner, tokens, wide, images, weights):
    images = [
        dict(
            image,
            pieces=[
                [[x if isinstance(x, tuple) else (x, 0) for x in owner] for owner in place]
                for place in image["pieces"]
            ],
            sums=image.get("sums", {}),
            finish=image.get("finish", ()),
            carry=image.get("carry", ((), ())),
        )
        for image in images
    ]
    plan = Jobs(
        origins=[[[[r for _, r in o] for o in p] for p in image["pieces"]] for image in images],
        slots=[slot for slot, _, _ in weights],
        first=[first for _, first, _ in weights],
        same=[[not isinstance(w, tuple) for w in row] for _, _, row in weights],
        uses=[image["uses"] for image in images],
        added=[tuple(image["sums"]) for image in images],
        finished=[image["finish"] for image in images],
        carried=len(images[0]["carry"][0]),
    )
    operands = [x for i in images for place in i["pieces"] for owner in place for x, _ in owner]
    slab = operands[0].shape[1] // 2
    for _, _, row in weights:
        for w in row:
            operands += list(w) if isinstance(w, tuple) else [w]
    operands += [x for image in images for x in image["sums"].values()]
    operands += [x for image in images for place in image["carry"] for x in place]
    anywhere, vmem = pl.BlockSpec(memory_space=pl.ANY), pl.BlockSpec(memory_space=pltpu.VMEM)
    head = wide // 3
    shapes, specs = [], []
    for i in range(len(images)):
        for j in plan.jobs(i):
            if j in plan.finished[i]:
                shape = (tokens // 2, head * (plan.carried + 1))
                shapes += [jax.ShapeDtypeStruct(shape, jnp.bfloat16)] * 2
                specs += [vmem] * 2
            else:
                shapes.append(jax.ShapeDtypeStruct((tokens, wide), jnp.float32))
                specs.append(anywhere)
    jobs = 1 + max(j for i in range(len(images)) for j in plan.jobs(i))
    count, depth, total = len(images), len(weights) * slab, len(images) * tokens
    added = sum(high - low for uses in plan.uses for low, high in filter(None, uses))
    got = pl.pallas_call(
        functools.partial(job_kernel, plan),
        out_shape=shapes,
        in_specs=[pl.BlockSpec(memory_space=pltpu.SMEM)] + [anywhere] * len(operands),
        out_specs=specs,
        scratch_shapes=[
            pltpu.VMEM((total, depth), jnp.bfloat16),
            pltpu.VMEM((depth, jobs * wide), jnp.bfloat16),
            pltpu.VMEM((total, jobs * wide), jnp.float32),
            pltpu.VMEM((tokens, wide), jnp.bfloat16),
            pltpu.SemaphoreType.DMA((count, len(weights))),
            pltpu.SemaphoreType.DMA((len(weights), jobs)),
            pltpu.SemaphoreType.DMA((count, jobs)),
            pltpu.SemaphoreType.DMA((count, jobs)),
            pltpu.SemaphoreType.DMA((count, 2, max(plan.carried, 1))),
        ],
        compiler_params=pltpu.CompilerParams(vmem_limit_bytes=56 << 20),
        cost_estimate=pl.CostEstimate(
            flops=2 * tokens * slab * wide * added, bytes_accessed=0, transcendentals=0
        ),
    )(jnp.stack([core, inner]).astype(jnp.int32), *operands)
    got = list(got)
    return [
        {
            j: (got.pop(0), got.pop(0)) if j in plan.finished[i] else got.pop(0)
            for j in plan.jobs(i)
        }
        for i in range(count)
    ]


def join_kernel(place_ref, *refs):
    *parts, out_ref, sems = refs
    count = len(parts) // 2
    inner = place_ref[count]
    wide, head = parts[0].shape[1], parts[count].shape[1]

    def copies(i, role):
        begin = pl.multiple_of(place_ref[i] * wide, wide)
        if role:
            yield parts[i], out_ref.at[:, pl.ds(begin, wide)], sems.at[i, 0]
            return
        kept = wide - head
        yield parts[i].at[:, pl.ds(head, kept)], out_ref.at[:, pl.ds(begin, kept)], sems.at[i, 0]
        last = pl.multiple_of(begin + kept, head)
        yield parts[count + i], out_ref.at[:, pl.ds(last, head)], sems.at[i, 1]

    for role in (1, 0):

        @pl.when((inner == 1) == (role == 1))
        def _():
            every = [pltpu.make_async_copy(*c) for i in range(count) for c in copies(i, role)]
            for copy in every:
                copy.start()
            for copy in every:
                copy.wait()


def join(places, inner, parts, back):
    rows, wide = parts[0].shape
    anywhere = pl.BlockSpec(memory_space=pl.ANY)
    return pl.pallas_call(
        join_kernel,
        out_shape=jax.ShapeDtypeStruct((rows, wide * len(parts)), jnp.bfloat16),
        in_specs=[pl.BlockSpec(memory_space=pltpu.SMEM)] + [anywhere] * (2 * len(parts)),
        out_specs=anywhere,
        scratch_shapes=[pltpu.SemaphoreType.DMA((len(parts), 2))],
        cost_estimate=pl.CostEstimate(
            flops=0, bytes_accessed=4 * rows * wide * len(parts), transcendentals=0
        ),
    )(jnp.stack([*places, inner]).astype(jnp.int32), *parts, *back)


def shared(tokens, ln_gain, qkv_weight):
    groups, planes, seqs, cores = (lax.axis_size(a) for a in ("groups", "dp", "seq", "head"))
    group, plane, seq, core = (lax.axis_index(a) for a in ("groups", "dp", "seq", "head"))
    _, rows, _ = tokens.shape
    slab, heads, columns = qkv_weight.shape
    heads, part = heads // groups, rows // cores
    inner = (plane == 1) | (plane == 2)
    wait = lax.optimization_barrier

    def fold(piece):
        piece = piece.reshape(-1, part, columns).transpose(1, 0, 2)
        return piece.reshape(part, -1)

    def weight_piece(weight, j):
        return lax.dynamic_slice_in_dim(weight, group * heads + j, 1, 1)[:, 0]

    def pick(for_inner, for_ends):
        return jnp.where(inner, for_inner, for_ends)

    def pair(value):
        return lax.ppermute(value, "dp", [(0, 1), (1, 0), (2, 3), (3, 2)])

    def outward(value):
        return lax.ppermute(value, "dp", [(1, 0), (2, 3)])

    def middle(value):
        return lax.ppermute(value, "dp", [(1, 2), (2, 1)])

    swap = [(0, 1), (1, 0)]
    beside = lambda value: lax.ppermute(value, "seq", swap)
    across = lambda value: lax.ppermute(value, "groups", swap)

    def others(*values):
        got = []
        for value in values:
            if got:
                value, got[-1] = wait((value, got[-1]))
            got.append(lax.ppermute(value, "head", swap))
        return got

    beside_plane, far_inner = plane ^ 1, 2 - plane // 2
    order = (
        plane,
        pick(beside_plane, far_inner),
        pick(far_inner, beside_plane),
        3 - 3 * (plane // 2),
    )
    run = functools.partial(run_jobs, core, inner, seqs * rows, columns)

    def exchange(mixed):
        got = []
        for a in range(groups):
            for b in range(seqs):
                sent = mixed[a * seqs + b]
                if a or b:
                    steps = [
                        (g * seqs + s, (g + a) % groups * seqs + (s + b) % seqs)
                        for g in range(groups)
                        for s in range(seqs)
                    ]
                    sent = lax.ppermute(sent, ("groups", "seq"), steps)
                got.append(sent)
        return got

    normed = normalize_part(tokens, ln_gain, part, core, order)
    normed, qkv_weight = wait((normed, qkv_weight))
    cut0, cut1 = normed
    beside1, across1 = beside(cut0), across(cut0)
    own0 = weight_piece(qkv_weight, 0)
    pair1, middle1 = pair(own0), middle(own0)
    own1, own2 = weight_piece(qkv_weight, 1), weight_piece(qkv_weight, 2)
    give = pick(fold(own1), cut0)
    pair1, middle1, beside1, across1, own1, own2, cut0, cut1, tokens, give = wait(
        (pair1, middle1, beside1, across1, own1, own2, cut0, cut1, tokens, give)
    )

    pair2, middle2 = pair(give), middle(pair1)
    beside2, across2 = beside(cut1), across(cut1)
    give = pick(fold(middle1), cut1)
    far_normed = normalize_part(tokens, ln_gain, part, 1 - core, order)
    far1 = others(beside1, across1)
    pair2, middle2, beside2, across2, across1, own1, own2, far_normed, far1, give = wait(
        (pair2, middle2, beside2, across2, across1, own1, own2, far_normed, far1, give)
    )

    pair3, middle3 = pair(give), middle(own1)
    beside3, across3 = beside(across1), across(beside2)
    give = pick(middle2, own1)
    far2 = others(beside2, across2)
    pair3, middle3, beside3, across3, pair1, pair2, own2, far2, give = wait(
        (pair3, middle3, beside3, across3, pair1, pair2, own2, far2, give)
    )

    pair4, middle4 = pair(give), middle(own2)
    beside4, across4 = beside(pair2), across(pair2)
    give = pick(middle3, own2)
    pieces0 = ((normed, far_normed), ((beside1, beside2), (far1[0], far2[0])))
    owns = [own0, (own1, own0), (own2, own1)]
    ((head0, sum20, sum30),) = [
        tuple(got.values())
        for got in run(
            [dict(pieces=pieces0, uses=[(0, 3), (0, 2), (0, 1), (0, 1)], finish=(0,))],
            [(0, 0, owns), (2, 0, [middle1, (middle3, pair1)]), (1, 0, [pair1]), (3, 0, [middle2])],
        )
    ]
    far3 = others(beside3, across3)
    lent = jnp.concatenate([pair2, pair3])
    pair4, middle4, beside4, across4, own2, pair3, lent, head0, sum20, sum30, far3, give = wait(
        (pair4, middle4, beside4, across4, own2, pair3, lent, head0, sum20, sum30, far3, give)
    )

    pair5, middle5 = pair(give), middle(pair4)
    beside5, across5 = beside(pair3), across(pair3)
    pieces1 = (((across1, across2), (far1[1], far2[1])), ((beside3, across3), far3))
    image1, image0 = run(
        [
            dict(pieces=pieces1, uses=[(0, 3), (0, 3), (0, 2), (0, 1)], finish=(0,)),
            dict(pieces=pieces0, uses=[None, (2, 3), (1, 2), None], sums={1: sum20, 2: sum30}),
        ],
        [
            (0, 0, owns),
            (2, 0, [middle1, (middle3, pair1), (middle4, pair2)]),
            (1, 0, [pair1, (pair4, pair3)]),
            (3, 0, [middle2]),
        ],
    )
    far_lent, far4 = others(lent, beside4)
    pair5, middle5, beside5, across5, across4, image0, image1, far_lent, far4 = wait(
        (
            *(pair5, middle5, beside5, across5, across4),
            *(image0, image1, far_lent, far4),
        )
    )

    pair6, middle6 = outward(middle5), middle(pair5)
    beside6, across6 = beside(across4), across(beside5)
    far5, far_across4 = others(beside5, across4)
    ahead0, ahead1 = run(
        [
            dict(
                pieces=pieces,
                uses=[(0, 1), (1, 2)],
                sums={0: image[1], 1: image[2]},
                finish=(0,),
            )
            for pieces, image in ((pieces0, image0), (pieces1, image1))
        ],
        [(3, 0, [(middle5, pair4)]), (1, 1, [pair5])],
    )
    lent0 = (((pair2, pair3), (far_lent, (far_lent, part))), ((beside4, beside5), (far4, far5)))
    lent_weights = [(0, 0, [pair5]), (1, 0, [middle4]), (2, 0, [own2])]
    ((sum4,),) = [
        tuple(got.values()) for got in run([dict(pieces=lent0, uses=[(0, 1)] * 3)], lent_weights)
    ]
    pair6, middle6, beside6, across6, across5, ahead0, ahead1, sum4, far_across4 = wait(
        (pair6, middle6, beside6, across6, across5, ahead0, ahead1, sum4, far_across4)
    )

    far_across5, *far6 = [
        lax.ppermute(value, "head", swap) for value in (across5, beside6, across6)
    ]
    done0, done1 = run(
        [
            dict(pieces=p, uses=[(0, 1)], sums={0: x[1]}, finish=(0,), carry=tuple(zip(h, x[0])))
            for p, h, x in ((pieces0, head0, ahead0), (pieces1, image1[0], ahead1))
        ],
        [(3, 0, [(middle6, pair6)])],
    )
    sent = exchange((*done0[0], *done1[0]))
    lent1 = (((across4, across5), (far_across4, far_across5)), ((beside6, across6), far6))
    lent0, lent1 = run(
        [
            dict(pieces=lent0, uses=[None] * 3 + [(0, 1)], sums={0: sum4}, finish=(0,)),
            dict(pieces=lent1, uses=[(0, 1)] * 4, finish=(0,)),
        ],
        [*lent_weights, (3, 0, [middle6])],
    )

    def hand_back(mixed):
        got = []
        for a in range(groups):
            for b in range(seqs):
                steps = [
                    (
                        (g * planes + z) * seqs + s,
                        ((g + a) % groups * planes + (z ^ 1)) * seqs + (s + b) % seqs,
                    )
                    for g in range(groups)
                    for z in (1, 2)
                    for s in range(seqs)
                ]
                sent = mixed[a * seqs + b]
                got.append(lax.ppermute(sent, ("groups", "dp", "seq"), steps))
        return got

    back = hand_back((*lent0[0], *lent1[0]))
    places = [
        (seq - b) % seqs * groups + (group - a) % groups
        for a in range(groups)
        for b in range(seqs)
    ]
    return join(places, inner, sent, back)[None]


def per_device(tokens, ln_gain, qkv_weight):
    groups, planes, seqs, cores = (lax.axis_size(a) for a in ("groups", "dp", "seq", "head"))
    images, rows, width = tokens.shape
    slab, heads, _ = qkv_weight.shape
    if (groups, planes, seqs, cores) == (2, 4, 2, 2) and images == 1 and heads == 3 * groups:
        part = rows // cores
        if rows % (32 * cores) == 0 and slab % part == 0 and 2 * slab == qkv_weight.shape[2] * slab // part:
            return shared(tokens, ln_gain, qkv_weight)
    return plain(tokens, ln_gain, qkv_weight)


def solution(mesh):
    return jax.shard_map(
        per_device,
        mesh=mesh,
        in_specs=(P(("groups", "dp"), "seq", None), P(), P("dp", ("seq", "head"), None)),
        out_specs=P(("groups", "dp"), "seq", "head"),
        check_vma=False,
    )
```

```python
import functools
import math

import jax
import jax.numpy as jnp
from jax import lax
from jax.experimental import pallas as pl
from jax.experimental.pallas import tpu as pltpu
from jax.sharding import PartitionSpec as P


def normalize(array, gain):
    widened = array.astype(jnp.float32)
    centered = widened - jnp.mean(widened, axis=-1, keepdims=True)
    variance = jnp.mean(centered * centered, axis=-1, keepdims=True)
    return (centered * lax.rsqrt(variance + 1e-06) * gain).astype(jnp.bfloat16)


def attend(projected):
    width = projected.shape[2] // 3
    queries = projected[:, :, :width]
    key_rows = projected[:, :, width : 2 * width]
    value_rows = projected[:, :, 2 * width :]
    scores = jnp.einsum("qhd,khd->hqk", queries, key_rows, preferred_element_type=jnp.float32) * (
        1.0 / math.sqrt(width)
    )
    highest = jnp.max(scores, axis=-1, keepdims=True)
    expo = jnp.exp(scores - highest)
    probs = (expo / jnp.sum(expo, axis=-1, keepdims=True)).astype(jnp.bfloat16)
    mixed = jnp.einsum("hqk,khd->qhd", probs, value_rows, preferred_element_type=jnp.float32)
    return mixed.astype(jnp.bfloat16).reshape(projected.shape[0], -1)


def plain(tokens, ln_gain, qkv_weight):
    images = tokens.shape[0]
    width = tokens.shape[2]
    heads_here = qkv_weight.shape[1]
    columns = heads_here * qkv_weight.shape[2]
    source = normalize(tokens, ln_gain)
    half_width = width // lax.axis_size("head")
    core_index = lax.axis_index("head")
    own_half = lax.dynamic_slice_in_dim(source, core_index * half_width, half_width, 2)
    fetched = lax.all_gather(own_half, "seq", axis=1, tiled=True)
    gathered = lax.all_gather(fetched, "head", axis=2, tiled=True)
    full_tokens = gathered.shape[1]
    features = gathered.reshape(images * full_tokens, width)
    piece = lax.all_gather(qkv_weight, "dp", axis=0, tiled=True)
    projected = jnp.dot(
        features, piece.reshape(piece.shape[0], columns), preferred_element_type=jnp.float32
    )
    projected = projected.astype(jnp.bfloat16).reshape(
        images, full_tokens, heads_here, qkv_weight.shape[2]
    )
    mixed = lax.map(attend, projected)
    return lax.all_to_all(mixed, "seq", split_axis=1, concat_axis=2, tiled=True)


def normalize_kernel(place_ref, tokens_ref, gain_ref, *normed_refs):
    rows, width = tokens_ref.shape[1:]
    lanes = 128
    slab, span = width // 4, width // 2

    def widened(begin):
        return tokens_ref[0, :, pl.ds(begin, lanes)].astype(jnp.float32)

    total = jnp.zeros((rows, lanes), jnp.float32)
    for begin in range(0, width, lanes):
        total += widened(begin)
    mean = jnp.sum(total, axis=-1, keepdims=True) / width
    total = jnp.zeros((rows, lanes), jnp.float32)
    for begin in range(0, width, lanes):
        centered = widened(begin) - mean
        total += centered * centered
    scale = lax.rsqrt(jnp.sum(total, axis=-1, keepdims=True) / width + 1e-06)
    for i in range(4):
        source = place_ref[i + 1] * slab
        for begin in range(0, slab, lanes):
            column = pl.multiple_of(source + begin, lanes)
            part = (widened(column) - mean) * scale * gain_ref[:, pl.ds(column, lanes)]
            target = i * slab % span + begin
            normed_refs[i * slab // span][:, target : target + lanes] = part.astype(jnp.bfloat16)


def normalize_part(tokens, ln_gain, part, core, order):
    width = tokens.shape[2]
    step, count = 64 if part % 64 == 0 else 32, 2
    steps = part // step
    place = jnp.stack([jnp.asarray(v, jnp.int32) for v in (core, *order)])
    return pl.pallas_call(
        normalize_kernel,
        out_shape=[jax.ShapeDtypeStruct((part, width // count), jnp.bfloat16)] * count,
        grid_spec=pltpu.PrefetchScalarGridSpec(
            num_scalar_prefetch=1,
            grid=(steps,),
            in_specs=[
                pl.BlockSpec((1, step, width), lambda i, place: (0, place[0] * steps + i, 0)),
                pl.BlockSpec((1, width), lambda i, place: (0, 0)),
            ],
            out_specs=[pl.BlockSpec((step, width // count), lambda i, place: (i, 0))] * count,
        ),
        compiler_params=pltpu.CompilerParams(vmem_limit_bytes=62 << 20),
        cost_estimate=pl.CostEstimate(
            flops=8 * part * width, bytes_accessed=4 * part * width, transcendentals=part
        ),
    )(place, tokens, ln_gain[None])


def attend_rows(projected_ref, parts, column):
    width = projected_ref.shape[1] // 3
    key_rows = projected_ref[:, width : 2 * width]
    value_rows = projected_ref[:, 2 * width :]
    begin = 0
    for part in parts:
        step = part.shape[0]
        queries = projected_ref[begin : begin + step, :width]
        scores = lax.dot_general(
            queries, key_rows, (((1,), (1,)), ((), ())), preferred_element_type=jnp.float32
        )
        highest = jnp.max(scores, axis=-1, keepdims=True)
        expo = jnp.exp2((scores - highest) * (math.log2(math.e) / math.sqrt(width)))
        mixed = jnp.dot(expo.astype(jnp.bfloat16), value_rows, preferred_element_type=jnp.float32)
        mixed = mixed / jnp.sum(expo, axis=-1, keepdims=True)
        part[:, column : column + width] = mixed.astype(jnp.bfloat16)
        begin += step


class Jobs:
    def __init__(self, **numbers):
        self.__dict__.update(numbers)

    def jobs(self, image):
        return sorted({j for use in self.uses[image] if use for j in range(*use)})


def job_kernel(plan, role_ref, *refs):
    refs = list(refs)
    take = lambda n: [refs.pop(0) for _ in range(n)]
    images, ns = range(len(plan.uses)), range(len(plan.slots))
    pieces = [[[take(2) for _ in place] for place in image] for image in plan.origins]
    weights = [[take(1) * 2 if alike else take(2) for alike in row] for row in plan.same]
    partials = [{j: take(1)[0] for j in plan.added[i]} for i in images]
    carried = [[take(plan.carried[i]) for _ in range(2)] for i in images]
    outs = [
        {j: take(2) if j in plan.finished[i] else take(1)[0] for j in plan.jobs(i)} for i in images
    ]
    features_ref, weight_ref, total_ref, projected_ref = take(4)
    token_sems, weight_sems, sum_sems, out_sems, carry_sems = take(5)
    core, inner = role_ref[0], role_ref[1]
    slab = pieces[0][0][0][0].shape[1] // 2
    tokens, wide = projected_ref.shape
    part = tokens // 4

    def features(i, n):
        return features_ref.at[pl.ds(i * tokens, tokens), pl.ds(n * slab, slab)]

    def weight(n, j):
        return weight_ref.at[pl.ds(n * slab, slab), pl.ds(j * wide, wide)]

    def total(i, j):
        return total_ref.at[pl.ds(i * tokens, tokens), pl.ds(j * wide, wide)]

    def start_tokens(i, n):
        cut, begin = plan.slots[n] // 2, plan.slots[n] % 2 * slab
        for place in range(2):
            split = len(plan.origins[i][place])
            for owner in range(split):
                row = i * tokens + 2 * place * part
                if split == 2:
                    row += (1 - core if owner else core) * part
                count = 2 * part // split
                from_rows = pl.ds(plan.origins[i][place][owner][cut], count)
                rows = pl.ds(pl.multiple_of(row, 32), count)
                pltpu.make_async_copy(
                    pieces[i][place][owner][cut].at[from_rows, pl.ds(begin, slab)],
                    features_ref.at[rows, pl.ds(n * slab, slab)],
                    token_sems.at[i, n],
                ).start()

    def start_weight(n, j, role):
        source = weights[n][j - plan.first[n]][role]
        if source.shape[0] == slab:
            pltpu.make_async_copy(source, weight(n, j), weight_sems.at[n, j]).start()
            return
        for b in range(source.shape[1] // wide):
            pltpu.make_async_copy(
                source.at[:, pl.ds(b * wide, wide)],
                weight_ref.at[pl.ds(n * slab + b * part, part), pl.ds(j * wide, wide)],
                weight_sems.at[n, j],
            ).start()

    def start_role_weight(n, j):
        if plan.same[n][j - plan.first[n]]:
            start_weight(n, j, 0)
            return

        @pl.when(inner == 1)
        def _():
            start_weight(n, j, 0)

        @pl.when(inner != 1)
        def _():
            start_weight(n, j, 1)

    def partial_copy(i, j):
        return pltpu.make_async_copy(partials[i][j], total(i, j), sum_sems.at[i, j])

    def out_copy(i, j):
        return pltpu.make_async_copy(total(i, j), outs[i][j], out_sems.at[i, j])

    def carry_copies():
        for i in images:
            for place in range(2):
                for k in range(plan.carried[i]):
                    (finished,) = plan.finished[i]
                    target = outs[i][finished][place].at[:, pl.ds(k * wide // 3, wide // 3)]
                    yield pltpu.make_async_copy(
                        carried[i][place][k], target, carry_sems.at[i, place, k]
                    )

    stages = [(i, n) for i in images for n in ns if plan.uses[i][n]]
    held = set()

    def start_stage(i, n):
        start_tokens(i, n)
        for j in range(*plan.uses[i][n]):
            if (n, j) not in held:
                held.add((n, j))
                start_role_weight(n, j)
        if not any((i, n) > (i, m) and plan.uses[i][m] for m in ns):
            for j in plan.added[i]:
                partial_copy(i, j).start()

    ahead = 2
    for stage in stages[:ahead]:
        start_stage(*stage)
    for copy in carry_copies():
        copy.start()
    ready = set()
    for index, (i, n) in enumerate(stages):
        low, high = plan.uses[i][n]
        pltpu.make_async_copy(features(i, n), features(i, n), token_sems.at[i, n]).wait()
        for j in range(low, high):
            if (n, j) not in ready:
                ready.add((n, j))
                pltpu.make_async_copy(weight(n, j), weight(n, j), weight_sems.at[n, j]).wait()
        if index + ahead < len(stages):
            start_stage(*stages[index + ahead])
        term = jnp.dot(
            features(i, n)[...],
            weight_ref[n * slab : (n + 1) * slab, low * wide : high * wide],
            preferred_element_type=jnp.float32,
        )
        for j in range(low, high):
            value = term[:, (j - low) * wide : (j - low + 1) * wide]
            mine = [m for m in ns if plan.uses[i][m] and j in range(*plan.uses[i][m])]
            if n == mine[0] and j in plan.added[i]:
                partial_copy(i, j).wait()
            if n != mine[0] or j in plan.added[i]:
                value += total(i, j)[...]
            if n == mine[-1] and j in plan.finished[i]:
                projected_ref[...] = value.astype(jnp.bfloat16)
                attend_rows(projected_ref, outs[i][j], plan.carried[i] * wide // 3)
                continue
            total(i, j)[...] = value
            if n == mine[-1]:
                out_copy(i, j).start()
    for copy in carry_copies():
        copy.wait()
    for i in images:
        for j in plan.jobs(i):
            if j not in plan.finished[i]:
                out_copy(i, j).wait()


def run_jobs(core, inner, tokens, wide, images, weights):
    images = [
        dict(
            image,
            pieces=[
                [[x if isinstance(x, tuple) else (x, 0) for x in owner] for owner in place]
                for place in image["pieces"]
            ],
            sums=image.get("sums", {}),
            finish=image.get("finish", ()),
            carry=image.get("carry", ((), ())),
        )
        for image in images
    ]
    plan = Jobs(
        origins=[[[[r for _, r in o] for o in p] for p in image["pieces"]] for image in images],
        slots=[slot for slot, _, _ in weights],
        first=[first for _, first, _ in weights],
        same=[[not isinstance(w, tuple) for w in row] for _, _, row in weights],
        uses=[image["uses"] for image in images],
        added=[tuple(image["sums"]) for image in images],
        finished=[image["finish"] for image in images],
        carried=[len(image["carry"][0]) for image in images],
    )
    operands = [x for i in images for place in i["pieces"] for owner in place for x, _ in owner]
    slab = operands[0].shape[1] // 2
    for _, _, row in weights:
        for w in row:
            operands += list(w) if isinstance(w, tuple) else [w]
    operands += [x for image in images for x in image["sums"].values()]
    operands += [x for image in images for place in image["carry"] for x in place]
    anywhere, vmem = pl.BlockSpec(memory_space=pl.ANY), pl.BlockSpec(memory_space=pltpu.VMEM)
    head = wide // 3
    shapes, specs = [], []
    for i in range(len(images)):
        for j in plan.jobs(i):
            if j in plan.finished[i]:
                shape = (tokens // 2, head * (plan.carried[i] + 1))
                shapes += [jax.ShapeDtypeStruct(shape, jnp.bfloat16)] * 2
                specs += [vmem] * 2
            else:
                shapes.append(jax.ShapeDtypeStruct((tokens, wide), jnp.float32))
                specs.append(anywhere)
    jobs = 1 + max(j for i in range(len(images)) for j in plan.jobs(i))
    count, depth, total = len(images), len(weights) * slab, len(images) * tokens
    added = sum(high - low for uses in plan.uses for low, high in filter(None, uses))
    got = pl.pallas_call(
        functools.partial(job_kernel, plan),
        out_shape=shapes,
        in_specs=[pl.BlockSpec(memory_space=pltpu.SMEM)] + [anywhere] * len(operands),
        out_specs=specs,
        scratch_shapes=[
            pltpu.VMEM((total, depth), jnp.bfloat16),
            pltpu.VMEM((depth, jobs * wide), jnp.bfloat16),
            pltpu.VMEM((total, jobs * wide), jnp.float32),
            pltpu.VMEM((tokens, wide), jnp.bfloat16),
            pltpu.SemaphoreType.DMA((count, len(weights))),
            pltpu.SemaphoreType.DMA((len(weights), jobs)),
            pltpu.SemaphoreType.DMA((count, jobs)),
            pltpu.SemaphoreType.DMA((count, jobs)),
            pltpu.SemaphoreType.DMA((count, 2, max(*plan.carried, 1))),
        ],
        compiler_params=pltpu.CompilerParams(vmem_limit_bytes=62 << 20),
        cost_estimate=pl.CostEstimate(
            flops=2 * tokens * slab * wide * added, bytes_accessed=0, transcendentals=0
        ),
    )(jnp.stack([core, inner]).astype(jnp.int32), *operands)
    got = list(got)
    return [
        {
            j: (got.pop(0), got.pop(0)) if j in plan.finished[i] else got.pop(0)
            for j in plan.jobs(i)
        }
        for i in range(count)
    ]


def join_kernel(place_ref, *refs):
    *parts, out_ref, sems = refs
    count = len(parts) // 2
    inner = place_ref[count]
    wide, head = parts[0].shape[1], parts[count].shape[1]

    def copies(i, role):
        begin = pl.multiple_of(place_ref[i] * wide, wide)
        if role:
            yield parts[i], out_ref.at[:, pl.ds(begin, wide)], sems.at[i, 0]
            return
        kept = wide - head
        yield parts[i].at[:, pl.ds(head, kept)], out_ref.at[:, pl.ds(begin, kept)], sems.at[i, 0]
        last = pl.multiple_of(begin + kept, head)
        yield parts[count + i], out_ref.at[:, pl.ds(last, head)], sems.at[i, 1]

    for role in (1, 0):

        @pl.when((inner == 1) == (role == 1))
        def _():
            every = [pltpu.make_async_copy(*c) for i in range(count) for c in copies(i, role)]
            for copy in every:
                copy.start()
            for copy in every:
                copy.wait()


def join(places, inner, parts, back):
    rows, wide = parts[0].shape
    anywhere = pl.BlockSpec(memory_space=pl.ANY)
    return pl.pallas_call(
        join_kernel,
        out_shape=jax.ShapeDtypeStruct((rows, wide * len(parts)), jnp.bfloat16),
        in_specs=[pl.BlockSpec(memory_space=pltpu.SMEM)] + [anywhere] * (2 * len(parts)),
        out_specs=pl.BlockSpec(memory_space=pltpu.VMEM),
        scratch_shapes=[pltpu.SemaphoreType.DMA((len(parts), 2))],
        cost_estimate=pl.CostEstimate(
            flops=0, bytes_accessed=4 * rows * wide * len(parts), transcendentals=0
        ),
    )(jnp.stack([*places, inner]).astype(jnp.int32), *parts, *back)


def shared(tokens, ln_gain, qkv_weight):
    groups, planes, seqs, cores = (lax.axis_size(a) for a in ("groups", "dp", "seq", "head"))
    group, plane, seq, core = (lax.axis_index(a) for a in ("groups", "dp", "seq", "head"))
    _, rows, _ = tokens.shape
    slab, heads, columns = qkv_weight.shape
    heads, part = heads // groups, rows // cores
    inner = (plane == 1) | (plane == 2)
    wait = lax.optimization_barrier

    def fold(piece):
        piece = piece.reshape(-1, part, columns).transpose(1, 0, 2)
        return piece.reshape(part, -1)

    def weight_piece(weight, j):
        return lax.dynamic_slice_in_dim(weight, group * heads + j, 1, 1)[:, 0]

    def pick(for_inner, for_ends):
        return jnp.where(inner, for_inner, for_ends)

    def pair(value):
        return lax.ppermute(value, "dp", [(0, 1), (1, 0), (2, 3), (3, 2)])

    def outward(value):
        return lax.ppermute(value, "dp", [(1, 0), (2, 3)])

    def middle(value):
        return lax.ppermute(value, "dp", [(1, 2), (2, 1)])

    swap = [(0, 1), (1, 0)]
    beside = lambda value: lax.ppermute(value, "seq", swap)
    across = lambda value: lax.ppermute(value, "groups", swap)

    def others(*values):
        got = []
        for value in values:
            if got:
                value, got[-1] = wait((value, got[-1]))
            got.append(lax.ppermute(value, "head", swap))
        return got

    beside_plane, far_inner = plane ^ 1, 2 - plane // 2
    order = (
        plane,
        pick(beside_plane, far_inner),
        pick(far_inner, beside_plane),
        3 - 3 * (plane // 2),
    )
    run = functools.partial(run_jobs, core, inner, seqs * rows, columns)

    def exchange(mixed):
        got = []
        for a in range(groups):
            for b in range(seqs):
                sent = mixed[a * seqs + b]
                if a or b:
                    steps = [
                        (g * seqs + s, (g + a) % groups * seqs + (s + b) % seqs)
                        for g in range(groups)
                        for s in range(seqs)
                    ]
                    sent = lax.ppermute(sent, ("groups", "seq"), steps)
                got.append(sent)
        return got

    normed = normalize_part(tokens, ln_gain, part, core, order)
    normed, qkv_weight = wait((normed, qkv_weight))
    cut0, cut1 = normed
    beside1, across1 = beside(cut0), across(cut0)
    own0 = weight_piece(qkv_weight, 0)
    pair1, middle1 = pair(own0), middle(own0)
    own1, own2 = weight_piece(qkv_weight, 1), weight_piece(qkv_weight, 2)
    give = pick(fold(own1), cut0)
    pair1, middle1, beside1, across1, own1, own2, cut0, cut1, tokens, give = wait(
        (pair1, middle1, beside1, across1, own1, own2, cut0, cut1, tokens, give)
    )

    pair2, middle2 = pair(give), middle(pair1)
    beside2, across2 = beside(cut1), across(cut1)
    give = pick(fold(middle1), cut1)
    far_normed = normalize_part(tokens, ln_gain, part, 1 - core, order)
    far1 = others(beside1, across1)
    pair2, middle2, beside2, across2, across1, own1, own2, far_normed, far1, give = wait(
        (pair2, middle2, beside2, across2, across1, own1, own2, far_normed, far1, give)
    )

    pair3, middle3 = pair(give), middle(own1)
    beside3, across3 = beside(across1), across(beside2)
    give = pick(middle2, own1)
    far2 = others(beside2, across2)
    pair3, middle3, beside3, across3, pair1, pair2, own2, far2, give = wait(
        (pair3, middle3, beside3, across3, pair1, pair2, own2, far2, give)
    )

    pair4, middle4 = pair(give), middle(own2)
    beside4, across4 = beside(pair2), across(pair2)
    give = pick(middle3, own2)
    pieces0 = ((normed, far_normed), ((beside1, beside2), (far1[0], far2[0])))
    owns = [own0, (own1, own0), (own2, own1)]
    ((head0, sum20, sum30),) = [
        tuple(got.values())
        for got in run(
            [dict(pieces=pieces0, uses=[(0, 3), (0, 2), (0, 1), (0, 1)], finish=(0,))],
            [(0, 0, owns), (2, 0, [middle1, (middle3, pair1)]), (1, 0, [pair1]), (3, 0, [middle2])],
        )
    ]
    far3 = others(beside3, across3)
    lent = jnp.concatenate([pair2, pair3])
    pair4, middle4, beside4, across4, own2, pair3, lent, head0, sum20, sum30, far3, give = wait(
        (pair4, middle4, beside4, across4, own2, pair3, lent, head0, sum20, sum30, far3, give)
    )

    pair5, middle5 = pair(give), middle(pair4)
    beside5, across5 = beside(pair3), across(pair3)
    pieces1 = (((across1, across2), (far1[1], far2[1])), ((beside3, across3), far3))
    image1, image0 = run(
        [
            dict(pieces=pieces1, uses=[(0, 3), (0, 3), (0, 2), (0, 1)], finish=(0,)),
            dict(pieces=pieces0, uses=[None, (2, 3), (1, 2), None], sums={1: sum20, 2: sum30}),
        ],
        [
            (0, 0, owns),
            (2, 0, [middle1, (middle3, pair1), (middle4, pair2)]),
            (1, 0, [pair1, (pair4, pair3)]),
            (3, 0, [middle2]),
        ],
    )
    far_lent, far4 = others(lent, beside4)
    pair5, middle5, beside5, across5, across4, image0, image1, far_lent, far4 = wait(
        (
            *(pair5, middle5, beside5, across5, across4),
            *(image0, image1, far_lent, far4),
        )
    )

    pair6, middle6 = outward(middle5), middle(pair5)
    beside6, across6 = beside(across4), across(beside5)
    far5, far_across4 = others(beside5, across4)
    ahead0, ahead1 = run(
        [
            dict(
                pieces=pieces,
                uses=[(0, 1), (1, 2)],
                sums={0: image[1], 1: image[2]},
                finish=(0,),
            )
            for pieces, image in ((pieces0, image0), (pieces1, image1))
        ],
        [(3, 0, [(middle5, pair4)]), (1, 1, [pair5])],
    )
    lent0 = (((pair2, pair3), (far_lent, (far_lent, part))), ((beside4, beside5), (far4, far5)))
    lent_weights = [(0, 0, [pair5]), (1, 0, [middle4]), (2, 0, [own2])]
    ((sum4,),) = [
        tuple(got.values()) for got in run([dict(pieces=lent0, uses=[(0, 1)] * 3)], lent_weights)
    ]
    pair6, middle6, beside6, across6, across5, ahead0, ahead1, sum4, far_across4 = wait(
        (pair6, middle6, beside6, across6, across5, ahead0, ahead1, sum4, far_across4)
    )

    far_across5, *far6 = [
        lax.ppermute(value, "head", swap) for value in (across5, beside6, across6)
    ]
    done0, done1, lent0 = run(
        [
            dict(pieces=p, uses=[(0, 1)], sums={0: x[1]}, finish=(0,), carry=tuple(zip(h, x[0])))
            for p, h, x in ((pieces0, head0, ahead0), (pieces1, image1[0], ahead1))
        ]
        + [dict(pieces=lent0, uses=[(0, 1)], sums={0: sum4}, finish=(0,))],
        [(3, 0, [(middle6, pair6)])],
    )
    sent = exchange((*done0[0], *done1[0]))
    lent1 = (((across4, across5), (far_across4, far_across5)), ((beside6, across6), far6))
    (lent1,) = run(
        [dict(pieces=lent1, uses=[(0, 1)] * 4, finish=(0,))], [*lent_weights, (3, 0, [middle6])]
    )

    def hand_back(mixed):
        got = []
        for a in range(groups):
            for b in range(seqs):
                steps = [
                    (
                        (g * planes + z) * seqs + s,
                        ((g + a) % groups * planes + (z ^ 1)) * seqs + (s + b) % seqs,
                    )
                    for g in range(groups)
                    for z in (1, 2)
                    for s in range(seqs)
                ]
                sent = mixed[a * seqs + b]
                got.append(lax.ppermute(sent, ("groups", "dp", "seq"), steps))
        return got

    back = hand_back((*lent0[0], *lent1[0]))
    places = [
        (seq - b) % seqs * groups + (group - a) % groups
        for a in range(groups)
        for b in range(seqs)
    ]
    return join(places, inner, sent, back)[None]


def per_device(tokens, ln_gain, qkv_weight):
    groups, planes, seqs, cores = (lax.axis_size(a) for a in ("groups", "dp", "seq", "head"))
    images, rows, width = tokens.shape
    slab, heads, _ = qkv_weight.shape
    if (groups, planes, seqs, cores) == (2, 4, 2, 2) and images == 1 and heads == 3 * groups:
        part = rows // cores
        if rows % (32 * cores) == 0 and slab % part == 0 and 2 * slab == qkv_weight.shape[2] * slab // part:
            return shared(tokens, ln_gain, qkv_weight)
    return plain(tokens, ln_gain, qkv_weight)


def solution(mesh):
    return jax.shard_map(
        per_device,
        mesh=mesh,
        in_specs=(P(("groups", "dp"), "seq", None), P(), P("dp", ("seq", "head"), None)),
        out_specs=P(("groups", "dp"), "seq", "head"),
        check_vma=False,
    )
```

```python
import functools
import math

import jax
import jax.numpy as jnp
from jax import lax
from jax.experimental import pallas as pl
from jax.experimental.pallas import tpu as pltpu
from jax.sharding import PartitionSpec as P


def normalize(array, gain):
    widened = array.astype(jnp.float32)
    centered = widened - jnp.mean(widened, axis=-1, keepdims=True)
    variance = jnp.mean(centered * centered, axis=-1, keepdims=True)
    return (centered * lax.rsqrt(variance + 1e-06) * gain).astype(jnp.bfloat16)


def attend(projected):
    width = projected.shape[2] // 3
    queries = projected[:, :, :width]
    key_rows = projected[:, :, width : 2 * width]
    value_rows = projected[:, :, 2 * width :]
    scores = jnp.einsum("qhd,khd->hqk", queries, key_rows, preferred_element_type=jnp.float32) * (
        1.0 / math.sqrt(width)
    )
    highest = jnp.max(scores, axis=-1, keepdims=True)
    expo = jnp.exp(scores - highest)
    probs = (expo / jnp.sum(expo, axis=-1, keepdims=True)).astype(jnp.bfloat16)
    mixed = jnp.einsum("hqk,khd->qhd", probs, value_rows, preferred_element_type=jnp.float32)
    return mixed.astype(jnp.bfloat16).reshape(projected.shape[0], -1)


def plain(tokens, ln_gain, qkv_weight):
    images = tokens.shape[0]
    width = tokens.shape[2]
    heads_here = qkv_weight.shape[1]
    columns = heads_here * qkv_weight.shape[2]
    source = normalize(tokens, ln_gain)
    half_width = width // lax.axis_size("head")
    core_index = lax.axis_index("head")
    own_half = lax.dynamic_slice_in_dim(source, core_index * half_width, half_width, 2)
    fetched = lax.all_gather(own_half, "seq", axis=1, tiled=True)
    gathered = lax.all_gather(fetched, "head", axis=2, tiled=True)
    full_tokens = gathered.shape[1]
    features = gathered.reshape(images * full_tokens, width)
    piece = lax.all_gather(qkv_weight, "dp", axis=0, tiled=True)
    projected = jnp.dot(
        features, piece.reshape(piece.shape[0], columns), preferred_element_type=jnp.float32
    )
    projected = projected.astype(jnp.bfloat16).reshape(
        images, full_tokens, heads_here, qkv_weight.shape[2]
    )
    mixed = lax.map(attend, projected)
    return lax.all_to_all(mixed, "seq", split_axis=1, concat_axis=2, tiled=True)


def slab_order(plane):
    inner = (plane == 1) | (plane == 2)
    near, far = plane ^ 1, 2 - plane // 2
    return plane, jnp.where(inner, near, far), jnp.where(inner, far, near), 3 - 3 * (plane // 2)


def normalize_kernel(step, other, taken, tokens_ref, gain_ref, weight_ref, *refs):
    refs = list(refs)
    take = lambda n: [refs.pop(0) for _ in range(n)]
    normed_refs, own_refs, (tokens_buf, *normed_bufs) = take(2), take(len(taken)), take(3)
    own_bufs, (in_sems, out_sems, own_sems) = take(len(taken)), take(3)
    part, width = tokens_buf.shape
    lanes = 128
    slab, span = width // 4, width // 2
    core = lax.axis_index("head")
    first = pl.multiple_of((1 - core if other else core) * part, part)
    order = slab_order(lax.axis_index("dp"))
    heads = weight_ref.shape[0] // lax.axis_size("groups")

    def rows_in(i):
        return pltpu.make_async_copy(
            tokens_ref.at[0, pl.ds(pl.multiple_of(first + i * step, step), step)],
            tokens_buf.at[pl.ds(pl.multiple_of(i * step, step), step)],
            in_sems.at[i],
        )

    def rows_out(i):
        rows = pl.ds(pl.multiple_of(i * step, step), step)
        return [
            pltpu.make_async_copy(buf.at[rows], ref.at[rows], out_sems.at[i, cut])
            for cut, (buf, ref) in enumerate(zip(normed_bufs, normed_refs))
        ]

    def own_in(k):
        head = lax.axis_index("groups") * heads + taken[k]
        return pltpu.make_async_copy(weight_ref.at[head], own_bufs[k], own_sems.at[k, 0])

    def own_out(k):
        return pltpu.make_async_copy(own_bufs[k], own_refs[k], own_sems.at[k, 1])

    for i in range(part // step):
        rows_in(i).start()
    for k in range(len(taken)):
        own_in(k).start()

    @pl.loop(0, part // step)
    def _(i):
        rows_in(i).wait()
        rows = pl.ds(pl.multiple_of(i * step, step), step)

        def widened(begin):
            return tokens_buf[rows, pl.ds(begin, lanes)].astype(jnp.float32)

        total = jnp.zeros((step, lanes), jnp.float32)
        for begin in range(0, width, lanes):
            total += widened(begin)
        mean = jnp.sum(total, axis=-1, keepdims=True) / width
        total = jnp.zeros((step, lanes), jnp.float32)
        for begin in range(0, width, lanes):
            centered = widened(begin) - mean
            total += centered * centered
        scale = lax.rsqrt(jnp.sum(total, axis=-1, keepdims=True) / width + 1e-06)
        for k in range(4):
            for begin in range(0, slab, lanes):
                column = pl.multiple_of(order[k] * slab + begin, lanes)
                value = (widened(column) - mean) * scale * gain_ref[:, pl.ds(column, lanes)]
                target = k * slab % span + begin
                normed_bufs[k * slab // span][rows, target : target + lanes] = value.astype(
                    jnp.bfloat16
                )
        for copy in rows_out(i):
            copy.start()

    for k in range(len(taken)):
        own_in(k).wait()
        own_out(k).start()
    for i in range(part // step):
        for copy in rows_out(i):
            copy.wait()
    for k in range(len(taken)):
        own_out(k).wait()


def normalize_part(tokens, ln_gain, weight, part, other, taken=()):
    width = tokens.shape[2]
    piece = weight.shape[1:]
    step = 32
    anywhere = pl.BlockSpec(memory_space=pl.ANY)
    half = jax.ShapeDtypeStruct((part, width // 2), jnp.bfloat16)
    got = pl.pallas_call(
        functools.partial(normalize_kernel, step, other, taken),
        out_shape=[half] * 2 + [jax.ShapeDtypeStruct(piece, jnp.bfloat16)] * len(taken),
        in_specs=[anywhere, pl.BlockSpec(memory_space=pltpu.VMEM), anywhere],
        out_specs=[anywhere] * (2 + len(taken)),
        scratch_shapes=[
            pltpu.VMEM((part, width), jnp.bfloat16),
            *[pltpu.VMEM((part, width // 2), jnp.bfloat16)] * 2,
            *[pltpu.VMEM(piece, jnp.bfloat16)] * len(taken),
            pltpu.SemaphoreType.DMA((part // step,)),
            pltpu.SemaphoreType.DMA((part // step, 2)),
            pltpu.SemaphoreType.DMA((max(len(taken), 1), 2)),
        ],
        compiler_params=pltpu.CompilerParams(vmem_limit_bytes=62 << 20),
        cost_estimate=pl.CostEstimate(
            flops=8 * part * width, bytes_accessed=4 * part * width, transcendentals=part
        ),
    )(tokens, ln_gain[None], weight)
    return got[:2], got[2:]


def attend_rows(projected_ref, parts, column):
    width = projected_ref.shape[1] // 3
    key_rows = projected_ref[:, width : 2 * width]
    value_rows = projected_ref[:, 2 * width :]
    value_rows = jnp.concatenate([value_rows, jnp.ones_like(value_rows)], axis=1)
    begin = 0
    for part in parts:
        step = part.shape[0]
        queries = projected_ref[begin : begin + step, :width]
        scores = lax.dot_general(
            queries, key_rows, (((1,), (1,)), ((), ())), preferred_element_type=jnp.float32
        )
        highest = jnp.max(scores, axis=-1, keepdims=True)
        expo = jnp.exp2((scores - highest) * (math.log2(math.e) / math.sqrt(width)))
        mixed = jnp.dot(expo.astype(jnp.bfloat16), value_rows, preferred_element_type=jnp.float32)
        mixed = mixed[:, :width] / mixed[:, width:]
        part[:, column : column + width] = mixed.astype(jnp.bfloat16)
        begin += step


class Jobs:
    def __init__(self, **numbers):
        self.__dict__.update(numbers)

    def jobs(self, image):
        return sorted({j for use in self.uses[image] if use for j in range(*use)})


def job_kernel(plan, role_ref, *refs):
    refs = list(refs)
    take = lambda n: [refs.pop(0) for _ in range(n)]
    images, ns = range(len(plan.uses)), range(len(plan.slots))
    pieces = [[[take(2) for _ in place] for place in image] for image in plan.origins]
    weights = [[take(1) * 2 if alike else take(2) for alike in row] for row in plan.same]
    partials = [{j: take(1)[0] for j in plan.added[i]} for i in images]
    carried = [[take(plan.carried[i]) for _ in range(2)] for i in images]
    outs = [
        {j: take(2) if j in plan.finished[i] else take(1)[0] for j in plan.jobs(i)} for i in images
    ]
    features_ref, weight_ref, total_ref, projected_ref = take(4)
    token_sems, weight_sems, sum_sems, out_sems, carry_sems = take(5)
    core, inner = role_ref[0], role_ref[1]
    slab = pieces[0][0][0][0].shape[1] // 2
    tokens, wide = projected_ref.shape
    part = tokens // 4

    def features(i, n):
        return features_ref.at[pl.ds(i * tokens, tokens), pl.ds(n * slab, slab)]

    def weight(n, j):
        return weight_ref.at[pl.ds(n * slab, slab), pl.ds(j * wide, wide)]

    def total(i, j):
        return total_ref.at[pl.ds(i * tokens, tokens), pl.ds(j * wide, wide)]

    def start_tokens(i, n):
        cut, begin = plan.slots[n] // 2, plan.slots[n] % 2 * slab
        for place in range(2):
            split = len(plan.origins[i][place])
            for owner in range(split):
                row = i * tokens + 2 * place * part
                if split == 2:
                    row += (1 - core if owner else core) * part
                count = 2 * part // split
                from_rows = pl.ds(plan.origins[i][place][owner][cut], count)
                rows = pl.ds(pl.multiple_of(row, 32), count)
                pltpu.make_async_copy(
                    pieces[i][place][owner][cut].at[from_rows, pl.ds(begin, slab)],
                    features_ref.at[rows, pl.ds(n * slab, slab)],
                    token_sems.at[i, n],
                ).start()

    def start_weight(n, j, role):
        source = weights[n][j - plan.first[n]][role]
        if source.shape[0] == slab:
            pltpu.make_async_copy(source, weight(n, j), weight_sems.at[n, j]).start()
            return
        for b in range(source.shape[1] // wide):
            pltpu.make_async_copy(
                source.at[:, pl.ds(b * wide, wide)],
                weight_ref.at[pl.ds(n * slab + b * part, part), pl.ds(j * wide, wide)],
                weight_sems.at[n, j],
            ).start()

    def start_role_weight(n, j):
        if plan.same[n][j - plan.first[n]]:
            start_weight(n, j, 0)
            return

        @pl.when(inner == 1)
        def _():
            start_weight(n, j, 0)

        @pl.when(inner != 1)
        def _():
            start_weight(n, j, 1)

    def partial_copy(i, j):
        return pltpu.make_async_copy(partials[i][j], total(i, j), sum_sems.at[i, j])

    def out_copy(i, j):
        return pltpu.make_async_copy(total(i, j), outs[i][j], out_sems.at[i, j])

    def carry_copies():
        for i in images:
            for place in range(2):
                for k in range(plan.carried[i]):
                    (finished,) = plan.finished[i]
                    target = outs[i][finished][place].at[:, pl.ds(k * wide // 3, wide // 3)]
                    yield pltpu.make_async_copy(
                        carried[i][place][k], target, carry_sems.at[i, place, k]
                    )

    stages = [(i, n) for i in images for n in ns if plan.uses[i][n]]
    held = set()

    def start_stage(i, n):
        start_tokens(i, n)
        for j in range(*plan.uses[i][n]):
            if (n, j) not in held:
                held.add((n, j))
                start_role_weight(n, j)
        if not any((i, n) > (i, m) and plan.uses[i][m] for m in ns):
            for j in plan.added[i]:
                partial_copy(i, j).start()

    ahead = 2
    for stage in stages[:ahead]:
        start_stage(*stage)
    for copy in carry_copies():
        copy.start()
    ready = set()
    for index, (i, n) in enumerate(stages):
        low, high = plan.uses[i][n]
        pltpu.make_async_copy(features(i, n), features(i, n), token_sems.at[i, n]).wait()
        for j in range(low, high):
            if (n, j) not in ready:
                ready.add((n, j))
                pltpu.make_async_copy(weight(n, j), weight(n, j), weight_sems.at[n, j]).wait()
        if index + ahead < len(stages):
            start_stage(*stages[index + ahead])
        term = jnp.dot(
            features(i, n)[...],
            weight_ref[n * slab : (n + 1) * slab, low * wide : high * wide],
            preferred_element_type=jnp.float32,
        )
        for j in range(low, high):
            value = term[:, (j - low) * wide : (j - low + 1) * wide]
            mine = [m for m in ns if plan.uses[i][m] and j in range(*plan.uses[i][m])]
            if n == mine[0] and j in plan.added[i]:
                partial_copy(i, j).wait()
            if n != mine[0] or j in plan.added[i]:
                value += total(i, j)[...]
            if n == mine[-1] and j in plan.finished[i]:
                projected_ref[...] = value.astype(jnp.bfloat16)
                attend_rows(projected_ref, outs[i][j], plan.carried[i] * wide // 3)
                continue
            total(i, j)[...] = value
            if n == mine[-1]:
                out_copy(i, j).start()
    for copy in carry_copies():
        copy.wait()
    for i in images:
        for j in plan.jobs(i):
            if j not in plan.finished[i]:
                out_copy(i, j).wait()


def run_jobs(core, inner, tokens, wide, images, weights):
    images = [
        dict(
            image,
            pieces=[
                [[x if isinstance(x, tuple) else (x, 0) for x in owner] for owner in place]
                for place in image["pieces"]
            ],
            sums=image.get("sums", {}),
            finish=image.get("finish", ()),
            carry=image.get("carry", ((), ())),
        )
        for image in images
    ]
    plan = Jobs(
        origins=[[[[r for _, r in o] for o in p] for p in image["pieces"]] for image in images],
        slots=[slot for slot, _, _ in weights],
        first=[first for _, first, _ in weights],
        same=[[not isinstance(w, tuple) for w in row] for _, _, row in weights],
        uses=[image["uses"] for image in images],
        added=[tuple(image["sums"]) for image in images],
        finished=[image["finish"] for image in images],
        carried=[len(image["carry"][0]) for image in images],
    )
    operands = [x for i in images for place in i["pieces"] for owner in place for x, _ in owner]
    slab = operands[0].shape[1] // 2
    for _, _, row in weights:
        for w in row:
            operands += list(w) if isinstance(w, tuple) else [w]
    operands += [x for image in images for x in image["sums"].values()]
    operands += [x for image in images for place in image["carry"] for x in place]
    anywhere, vmem = pl.BlockSpec(memory_space=pl.ANY), pl.BlockSpec(memory_space=pltpu.VMEM)
    head = wide // 3
    shapes, specs = [], []
    for i in range(len(images)):
        for j in plan.jobs(i):
            if j in plan.finished[i]:
                shape = (tokens // 2, head * (plan.carried[i] + 1))
                shapes += [jax.ShapeDtypeStruct(shape, jnp.bfloat16)] * 2
                specs += [vmem] * 2
            else:
                shapes.append(jax.ShapeDtypeStruct((tokens, wide), jnp.float32))
                specs.append(anywhere)
    jobs = 1 + max(j for i in range(len(images)) for j in plan.jobs(i))
    count, depth, total = len(images), len(weights) * slab, len(images) * tokens
    added = sum(high - low for uses in plan.uses for low, high in filter(None, uses))
    got = pl.pallas_call(
        functools.partial(job_kernel, plan),
        out_shape=shapes,
        in_specs=[pl.BlockSpec(memory_space=pltpu.SMEM)] + [anywhere] * len(operands),
        out_specs=specs,
        scratch_shapes=[
            pltpu.VMEM((total, depth), jnp.bfloat16),
            pltpu.VMEM((depth, jobs * wide), jnp.bfloat16),
            pltpu.VMEM((total, jobs * wide), jnp.float32),
            pltpu.VMEM((tokens, wide), jnp.bfloat16),
            pltpu.SemaphoreType.DMA((count, len(weights))),
            pltpu.SemaphoreType.DMA((len(weights), jobs)),
            pltpu.SemaphoreType.DMA((count, jobs)),
            pltpu.SemaphoreType.DMA((count, jobs)),
            pltpu.SemaphoreType.DMA((count, 2, max(*plan.carried, 1))),
        ],
        compiler_params=pltpu.CompilerParams(vmem_limit_bytes=62 << 20),
        cost_estimate=pl.CostEstimate(
            flops=2 * tokens * slab * wide * added, bytes_accessed=0, transcendentals=0
        ),
    )(jnp.stack([core, inner]).astype(jnp.int32), *operands)
    got = list(got)
    return [
        {
            j: (got.pop(0), got.pop(0)) if j in plan.finished[i] else got.pop(0)
            for j in plan.jobs(i)
        }
        for i in range(count)
    ]


def join_kernel(place_ref, tick_ref, *refs):
    *parts, out_ref, sems = refs
    count = len(parts) // 2
    inner = place_ref[count]
    wide, head = parts[0].shape[1], parts[count].shape[1]

    def copies(i, role):
        begin = pl.multiple_of(place_ref[i] * wide, wide)
        if role:
            yield parts[i], out_ref.at[:, pl.ds(begin, wide)], sems.at[i, 0]
            return
        kept = wide - head
        yield parts[i].at[:, pl.ds(head, kept)], out_ref.at[:, pl.ds(begin, kept)], sems.at[i, 0]
        last = pl.multiple_of(begin + kept, head)
        yield parts[count + i], out_ref.at[:, pl.ds(last, head)], sems.at[i, 1]

    for role in (1, 0):

        @pl.when((inner == 1) == (role == 1))
        def _():
            every = [pltpu.make_async_copy(*c) for i in range(count) for c in copies(i, role)]
            for copy in every:
                copy.start()
            for copy in every:
                copy.wait()


def join(places, inner, tick, parts, back):
    rows, wide = parts[0].shape
    anywhere = pl.BlockSpec(memory_space=pl.ANY)
    return pl.pallas_call(
        join_kernel,
        out_shape=jax.ShapeDtypeStruct((rows, wide * len(parts)), jnp.bfloat16),
        in_specs=[pl.BlockSpec(memory_space=pltpu.SMEM)] + [anywhere] * (1 + 2 * len(parts)),
        out_specs=pl.BlockSpec(memory_space=pltpu.VMEM),
        scratch_shapes=[pltpu.SemaphoreType.DMA((len(parts), 2))],
        cost_estimate=pl.CostEstimate(
            flops=0, bytes_accessed=4 * rows * wide * len(parts), transcendentals=0
        ),
    )(jnp.stack([*places, inner]).astype(jnp.int32), tick, *parts, *back)


def shared(tokens, ln_gain, qkv_weight):
    groups, planes, seqs, cores = (lax.axis_size(a) for a in ("groups", "dp", "seq", "head"))
    group, plane, seq, core = (lax.axis_index(a) for a in ("groups", "dp", "seq", "head"))
    _, rows, _ = tokens.shape
    slab, heads, columns = qkv_weight.shape
    heads, part = heads // groups, rows // cores
    inner = (plane == 1) | (plane == 2)
    wait = lax.optimization_barrier

    def fold(piece):
        piece = piece.reshape(-1, part, columns).transpose(1, 0, 2)
        return piece.reshape(part, -1)

    def pick(for_inner, for_ends):
        return jnp.where(inner, for_inner, for_ends)

    def pair(value):
        return lax.ppermute(value, "dp", [(0, 1), (1, 0), (2, 3), (3, 2)])

    def outward(value):
        return lax.ppermute(value, "dp", [(1, 0), (2, 3)])

    def middle(value):
        return lax.ppermute(value, "dp", [(1, 2), (2, 1)])

    swap = [(0, 1), (1, 0)]
    beside = lambda value: lax.ppermute(value, "seq", swap)
    across = lambda value: lax.ppermute(value, "groups", swap)

    def others(*values):
        got = []
        for value in values:
            if got:
                value, got[-1] = wait((value, got[-1]))
            got.append(lax.ppermute(value, "head", swap))
        return got

    run = functools.partial(run_jobs, core, inner, seqs * rows, columns)

    def exchange(mixed):
        got = []
        for a in range(groups):
            for b in range(seqs):
                sent = mixed[a * seqs + b]
                if a or b:
                    steps = [
                        (g * seqs + s, (g + a) % groups * seqs + (s + b) % seqs)
                        for g in range(groups)
                        for s in range(seqs)
                    ]
                    sent = lax.ppermute(sent, ("groups", "seq"), steps)
                got.append(sent)
        return got

    tick = jnp.full((8, 128), core, jnp.float32)

    def later(tick, *values):
        tick = tick * 0.5 + 1.0
        return wait((tick, *values))

    weight = qkv_weight.transpose(1, 0, 2)
    own0 = lax.dynamic_index_in_dim(weight, group * heads, 0, keepdims=False)
    pair1, middle1 = pair(own0), middle(own0)
    tokens, own0 = wait((tokens, own0))
    normed, (own1, own2) = normalize_part(tokens, ln_gain, weight, part, False, (1, 2))
    cut0, cut1 = normed
    beside1, across1 = beside(cut0), across(cut0)
    give = pick(fold(own1), cut0)
    pair1, middle1, beside1, across1, own1, own2, cut0, cut1, tokens, give, tick = wait(
        (pair1, middle1, beside1, across1, own1, own2, cut0, cut1, tokens, give, tick)
    )

    pair2, middle2 = pair(give), middle(pair1)
    tick, cut1 = later(tick, cut1)
    beside2, across2 = beside(cut1), across(cut1)
    give = pick(fold(middle1), cut1)
    far_normed, _ = normalize_part(tokens, ln_gain, weight, part, True)
    far1 = others(beside1, across1)
    pair2, middle2, beside2, across2, across1, own1, own2, far_normed, far1, give, tick = wait(
        (pair2, middle2, beside2, across2, across1, own1, own2, far_normed, far1, give, tick)
    )

    pair3, middle3 = pair(give), middle(own1)
    tick, across1, beside2 = later(tick, across1, beside2)
    beside3, across3 = beside(across1), across(beside2)
    give = pick(middle2, own1)
    far2 = others(beside2, across2)
    pair3, middle3, beside3, across3, pair1, pair2, own2, far2, give, tick = wait(
        (pair3, middle3, beside3, across3, pair1, pair2, own2, far2, give, tick)
    )

    pair4, middle4 = pair(give), middle(own2)
    tick, pair2 = later(tick, pair2)
    beside4, across4 = beside(pair2), across(pair2)
    give = pick(middle3, own2)
    pieces0 = ((normed, far_normed), ((beside1, beside2), (far1[0], far2[0])))
    owns = [own0, (own1, own0), (own2, own1)]
    ((head0, sum20, sum30),) = [
        tuple(got.values())
        for got in run(
            [dict(pieces=pieces0, uses=[(0, 3), (0, 2), (0, 1), (0, 1)], finish=(0,))],
            [(0, 0, owns), (2, 0, [middle1, (middle3, pair1)]), (1, 0, [pair1]), (3, 0, [middle2])],
        )
    ]
    far3 = others(beside3, across3)
    lent = jnp.concatenate([pair2, pair3])
    pair4, middle4, beside4, across4, own2, pair3, lent, head0, sum20, sum30, far3, give, tick = wait(
        (pair4, middle4, beside4, across4, own2, pair3, lent, head0, sum20, sum30, far3, give, tick)
    )

    pair5, middle5 = pair(give), middle(pair4)
    tick, pair3 = later(tick, pair3)
    beside5, across5 = beside(pair3), across(pair3)
    pieces1 = (((across1, across2), (far1[1], far2[1])), ((beside3, across3), far3))
    image1, image0 = run(
        [
            dict(pieces=pieces1, uses=[(0, 3), (0, 3), (0, 2), (0, 1)], finish=(0,)),
            dict(pieces=pieces0, uses=[None, (2, 3), (1, 2), None], sums={1: sum20, 2: sum30}),
        ],
        [
            (0, 0, owns),
            (2, 0, [middle1, (middle3, pair1), (middle4, pair2)]),
            (1, 0, [pair1, (pair4, pair3)]),
            (3, 0, [middle2]),
        ],
    )
    far_lent, far4 = others(lent, beside4)
    pair5, middle5, beside5, across5, across4, image0, image1, far_lent, far4, tick = wait(
        (
            *(pair5, middle5, beside5, across5, across4),
            *(image0, image1, far_lent, far4, tick),
        )
    )

    pair6, middle6 = outward(middle5), middle(pair5)
    tick, across4, beside5 = later(tick, across4, beside5)
    beside6, across6 = beside(across4), across(beside5)
    far5, far_across4 = others(beside5, across4)
    ahead0, ahead1 = run(
        [
            dict(
                pieces=pieces,
                uses=[(0, 1), (1, 2)],
                sums={0: image[1], 1: image[2]},
                finish=(0,),
            )
            for pieces, image in ((pieces0, image0), (pieces1, image1))
        ],
        [(3, 0, [(middle5, pair4)]), (1, 1, [pair5])],
    )
    lent0 = (((pair2, pair3), (far_lent, (far_lent, part))), ((beside4, beside5), (far4, far5)))
    lent_weights = [(0, 0, [pair5]), (1, 0, [middle4]), (2, 0, [own2])]
    ((sum4,),) = [
        tuple(got.values()) for got in run([dict(pieces=lent0, uses=[(0, 1)] * 3)], lent_weights)
    ]
    pair6, middle6, beside6, across6, across5, ahead0, ahead1, sum4, far_across4 = wait(
        (pair6, middle6, beside6, across6, across5, ahead0, ahead1, sum4, far_across4)
    )

    far_across5, *far6 = [
        lax.ppermute(value, "head", swap) for value in (across5, beside6, across6)
    ]
    done0, done1, lent0 = run(
        [
            dict(pieces=p, uses=[(0, 1)], sums={0: x[1]}, finish=(0,), carry=tuple(zip(h, x[0])))
            for p, h, x in ((pieces0, head0, ahead0), (pieces1, image1[0], ahead1))
        ]
        + [dict(pieces=lent0, uses=[(0, 1)], sums={0: sum4}, finish=(0,))],
        [(3, 0, [(middle6, pair6)])],
    )
    sent = exchange((*done0[0], *done1[0]))
    lent1 = (((across4, across5), (far_across4, far_across5)), ((beside6, across6), far6))
    (lent1,) = run(
        [dict(pieces=lent1, uses=[(0, 1)] * 4, finish=(0,))], [*lent_weights, (3, 0, [middle6])]
    )

    def hand_back(mixed):
        got = []
        for a in range(groups):
            for b in range(seqs):
                steps = [
                    (
                        (g * planes + z) * seqs + s,
                        ((g + a) % groups * planes + (z ^ 1)) * seqs + (s + b) % seqs,
                    )
                    for g in range(groups)
                    for z in (1, 2)
                    for s in range(seqs)
                ]
                sent = mixed[a * seqs + b]
                got.append(lax.ppermute(sent, ("groups", "dp", "seq"), steps))
        return got

    back = hand_back((*lent0[0], *lent1[0]))
    places = [
        (seq - b) % seqs * groups + (group - a) % groups
        for a in range(groups)
        for b in range(seqs)
    ]
    return join(places, inner, tick, sent, back)[None]


def per_device(tokens, ln_gain, qkv_weight):
    groups, planes, seqs, cores = (lax.axis_size(a) for a in ("groups", "dp", "seq", "head"))
    images, rows, width = tokens.shape
    slab, heads, _ = qkv_weight.shape
    if (groups, planes, seqs, cores) == (2, 4, 2, 2) and images == 1 and heads == 3 * groups:
        part = rows // cores
        if rows % (32 * cores) == 0 and slab % part == 0 and 2 * slab == qkv_weight.shape[2] * slab // part:
            return shared(tokens, ln_gain, qkv_weight)
    return plain(tokens, ln_gain, qkv_weight)


def solution(mesh):
    return jax.shard_map(
        per_device,
        mesh=mesh,
        in_specs=(P(("groups", "dp"), "seq", None), P(), P("dp", ("seq", "head"), None)),
        out_specs=P(("groups", "dp"), "seq", "head"),
        check_vma=False,
    )
```

```python
import functools
import math

import jax
import jax.numpy as jnp
from jax import lax
from jax.experimental import pallas as pl
from jax.experimental.pallas import tpu as pltpu
from jax.sharding import PartitionSpec as P


def normalize(array, gain):
    widened = array.astype(jnp.float32)
    centered = widened - jnp.mean(widened, axis=-1, keepdims=True)
    variance = jnp.mean(centered * centered, axis=-1, keepdims=True)
    return (centered * lax.rsqrt(variance + 1e-06) * gain).astype(jnp.bfloat16)


def attend(projected):
    width = projected.shape[2] // 3
    queries = projected[:, :, :width]
    key_rows = projected[:, :, width : 2 * width]
    value_rows = projected[:, :, 2 * width :]
    scores = jnp.einsum("qhd,khd->hqk", queries, key_rows, preferred_element_type=jnp.float32) * (
        1.0 / math.sqrt(width)
    )
    highest = jnp.max(scores, axis=-1, keepdims=True)
    expo = jnp.exp(scores - highest)
    probs = (expo / jnp.sum(expo, axis=-1, keepdims=True)).astype(jnp.bfloat16)
    mixed = jnp.einsum("hqk,khd->qhd", probs, value_rows, preferred_element_type=jnp.float32)
    return mixed.astype(jnp.bfloat16).reshape(projected.shape[0], -1)


def plain(tokens, ln_gain, qkv_weight):
    images = tokens.shape[0]
    width = tokens.shape[2]
    heads_here = qkv_weight.shape[1]
    columns = heads_here * qkv_weight.shape[2]
    source = normalize(tokens, ln_gain)
    half_width = width // lax.axis_size("head")
    core_index = lax.axis_index("head")
    own_half = lax.dynamic_slice_in_dim(source, core_index * half_width, half_width, 2)
    fetched = lax.all_gather(own_half, "seq", axis=1, tiled=True)
    gathered = lax.all_gather(fetched, "head", axis=2, tiled=True)
    full_tokens = gathered.shape[1]
    features = gathered.reshape(images * full_tokens, width)
    piece = lax.all_gather(qkv_weight, "dp", axis=0, tiled=True)
    projected = jnp.dot(
        features, piece.reshape(piece.shape[0], columns), preferred_element_type=jnp.float32
    )
    projected = projected.astype(jnp.bfloat16).reshape(
        images, full_tokens, heads_here, qkv_weight.shape[2]
    )
    mixed = lax.map(attend, projected)
    return lax.all_to_all(mixed, "seq", split_axis=1, concat_axis=2, tiled=True)


def slab_order(plane):
    inner = (plane == 1) | (plane == 2)
    near, far = plane ^ 1, 2 - plane // 2
    return plane, jnp.where(inner, near, far), jnp.where(inner, far, near), 3 - 3 * (plane // 2)


def normalize_kernel(step, other, taken, tokens_ref, gain_ref, weight_ref, *refs):
    refs = list(refs)
    take = lambda n: [refs.pop(0) for _ in range(n)]
    normed_refs, own_refs, (tokens_buf, *normed_bufs) = take(2), take(len(taken)), take(3)
    own_bufs, (in_sems, out_sems, own_sems) = take(len(taken)), take(3)
    part, width = tokens_buf.shape
    lanes = 128
    slab, span = width // 4, width // 2
    core = lax.axis_index("head")
    first = pl.multiple_of((1 - core if other else core) * part, part)
    order = slab_order(lax.axis_index("dp"))
    heads = weight_ref.shape[0] // lax.axis_size("groups")

    def rows_in(i):
        return pltpu.make_async_copy(
            tokens_ref.at[0, pl.ds(pl.multiple_of(first + i * step, step), step)],
            tokens_buf.at[pl.ds(pl.multiple_of(i * step, step), step)],
            in_sems.at[i],
        )

    def rows_out(i):
        rows = pl.ds(pl.multiple_of(i * step, step), step)
        return [
            pltpu.make_async_copy(buf.at[rows], ref.at[rows], out_sems.at[i, cut])
            for cut, (buf, ref) in enumerate(zip(normed_bufs, normed_refs))
        ]

    def own_in(k):
        head = lax.axis_index("groups") * heads + taken[k]
        return pltpu.make_async_copy(weight_ref.at[head], own_bufs[k], own_sems.at[k, 0])

    def own_out(k):
        return pltpu.make_async_copy(own_bufs[k], own_refs[k], own_sems.at[k, 1])

    for i in range(part // step):
        rows_in(i).start()
    for k in range(len(taken)):
        own_in(k).start()

    @pl.loop(0, part // step)
    def _(i):
        rows_in(i).wait()
        rows = pl.ds(pl.multiple_of(i * step, step), step)

        def widened(begin):
            return tokens_buf[rows, pl.ds(begin, lanes)].astype(jnp.float32)

        total = jnp.zeros((step, lanes), jnp.float32)
        for begin in range(0, width, lanes):
            total += widened(begin)
        mean = jnp.sum(total, axis=-1, keepdims=True) / width
        total = jnp.zeros((step, lanes), jnp.float32)
        for begin in range(0, width, lanes):
            centered = widened(begin) - mean
            total += centered * centered
        scale = lax.rsqrt(jnp.sum(total, axis=-1, keepdims=True) / width + 1e-06)
        for k in range(4):
            for begin in range(0, slab, lanes):
                column = pl.multiple_of(order[k] * slab + begin, lanes)
                value = (widened(column) - mean) * scale * gain_ref[:, pl.ds(column, lanes)]
                target = k * slab % span + begin
                normed_bufs[k * slab // span][rows, target : target + lanes] = value.astype(
                    jnp.bfloat16
                )
        for copy in rows_out(i):
            copy.start()

    for k in range(len(taken)):
        own_in(k).wait()
        own_out(k).start()
    for i in range(part // step):
        for copy in rows_out(i):
            copy.wait()
    for k in range(len(taken)):
        own_out(k).wait()


def normalize_part(tokens, ln_gain, weight, part, other, taken=()):
    width = tokens.shape[2]
    piece = weight.shape[1:]
    step = 32
    anywhere = pl.BlockSpec(memory_space=pl.ANY)
    half = jax.ShapeDtypeStruct((part, width // 2), jnp.bfloat16)
    got = pl.pallas_call(
        functools.partial(normalize_kernel, step, other, taken),
        out_shape=[half] * 2 + [jax.ShapeDtypeStruct(piece, jnp.bfloat16)] * len(taken),
        in_specs=[anywhere, pl.BlockSpec(memory_space=pltpu.VMEM), anywhere],
        out_specs=[anywhere] * (2 + len(taken)),
        scratch_shapes=[
            pltpu.VMEM((part, width), jnp.bfloat16),
            *[pltpu.VMEM((part, width // 2), jnp.bfloat16)] * 2,
            *[pltpu.VMEM(piece, jnp.bfloat16)] * len(taken),
            pltpu.SemaphoreType.DMA((part // step,)),
            pltpu.SemaphoreType.DMA((part // step, 2)),
            pltpu.SemaphoreType.DMA((max(len(taken), 1), 2)),
        ],
        compiler_params=pltpu.CompilerParams(vmem_limit_bytes=62 << 20),
        cost_estimate=pl.CostEstimate(
            flops=8 * part * width, bytes_accessed=4 * part * width, transcendentals=part
        ),
    )(tokens, ln_gain[None], weight)
    return got[:2], got[2:]


def attend_rows(projected_ref, parts, column):
    width = projected_ref.shape[1] // 3
    key_rows = projected_ref[:, width : 2 * width]
    value_rows = projected_ref[:, 2 * width :]
    value_rows = jnp.concatenate([value_rows, jnp.ones_like(value_rows)], axis=1)
    begin = 0
    for part in parts:
        step = part.shape[0]
        queries = projected_ref[begin : begin + step, :width]
        scores = lax.dot_general(
            queries, key_rows, (((1,), (1,)), ((), ())), preferred_element_type=jnp.float32
        )
        highest = jnp.max(scores, axis=-1, keepdims=True)
        expo = jnp.exp2((scores - highest) * (math.log2(math.e) / math.sqrt(width)))
        mixed = jnp.dot(expo.astype(jnp.bfloat16), value_rows, preferred_element_type=jnp.float32)
        mixed = mixed[:, :width] / mixed[:, width:]
        part[:, column : column + width] = mixed.astype(jnp.bfloat16)
        begin += step


class Jobs:
    def __init__(self, **numbers):
        self.__dict__.update(numbers)

    def jobs(self, image):
        return sorted({j for use in self.uses[image] if use for j in range(*use)})


def job_kernel(plan, role_ref, *refs):
    refs = list(refs)
    take = lambda n: [refs.pop(0) for _ in range(n)]
    images, ns = range(len(plan.uses)), range(len(plan.slots))
    pieces = [[[take(2) for _ in place] for place in image] for image in plan.origins]
    weights = [[take(1) * 2 if alike else take(2) for alike in row] for row in plan.same]
    partials = [{j: take(1)[0] for j in plan.added[i]} for i in images]
    carried = [[take(plan.carried[i]) for _ in range(2)] for i in images]
    outs = [
        {j: take(2) if j in plan.finished[i] else take(1)[0] for j in plan.jobs(i)} for i in images
    ]
    features_ref, weight_ref, total_ref, projected_ref = take(4)
    token_sems, weight_sems, sum_sems, out_sems, carry_sems = take(5)
    core, inner = role_ref[0], role_ref[1]
    slab = pieces[0][0][0][0].shape[1] // 2
    tokens, wide = projected_ref.shape
    part = tokens // 4

    def features(i, n):
        return features_ref.at[pl.ds(i * tokens, tokens), pl.ds(n * slab, slab)]

    def weight(n, j):
        return weight_ref.at[pl.ds(n * slab, slab), pl.ds(j * wide, wide)]

    def total(i, j):
        return total_ref.at[pl.ds(i * tokens, tokens), pl.ds(j * wide, wide)]

    def start_tokens(i, n):
        cut, begin = plan.slots[n] // 2, plan.slots[n] % 2 * slab
        for place in range(2):
            split = len(plan.origins[i][place])
            for owner in range(split):
                row = i * tokens + 2 * place * part
                if split == 2:
                    row += (1 - core if owner else core) * part
                count = 2 * part // split
                from_rows = pl.ds(plan.origins[i][place][owner][cut], count)
                rows = pl.ds(pl.multiple_of(row, 32), count)
                pltpu.make_async_copy(
                    pieces[i][place][owner][cut].at[from_rows, pl.ds(begin, slab)],
                    features_ref.at[rows, pl.ds(n * slab, slab)],
                    token_sems.at[i, n],
                ).start()

    def start_weight(n, j, role):
        source = weights[n][j - plan.first[n]][role]
        if source.shape[0] == slab:
            pltpu.make_async_copy(source, weight(n, j), weight_sems.at[n, j]).start()
            return
        for b in range(source.shape[1] // wide):
            pltpu.make_async_copy(
                source.at[:, pl.ds(b * wide, wide)],
                weight_ref.at[pl.ds(n * slab + b * part, part), pl.ds(j * wide, wide)],
                weight_sems.at[n, j],
            ).start()

    def start_role_weight(n, j):
        if plan.same[n][j - plan.first[n]]:
            start_weight(n, j, 0)
            return

        @pl.when(inner == 1)
        def _():
            start_weight(n, j, 0)

        @pl.when(inner != 1)
        def _():
            start_weight(n, j, 1)

    def partial_copy(i, j):
        return pltpu.make_async_copy(partials[i][j], total(i, j), sum_sems.at[i, j])

    def out_copy(i, j):
        return pltpu.make_async_copy(total(i, j), outs[i][j], out_sems.at[i, j])

    def carry_copies():
        for i in images:
            for place in range(2):
                for k in range(plan.carried[i]):
                    (finished,) = plan.finished[i]
                    target = outs[i][finished][place].at[:, pl.ds(k * wide // 3, wide // 3)]
                    yield pltpu.make_async_copy(
                        carried[i][place][k], target, carry_sems.at[i, place, k]
                    )

    stages = [(i, n) for i in images for n in ns if plan.uses[i][n]]
    held = set()

    def start_stage(i, n):
        start_tokens(i, n)
        for j in range(*plan.uses[i][n]):
            if (n, j) not in held:
                held.add((n, j))
                start_role_weight(n, j)
        if not any((i, n) > (i, m) and plan.uses[i][m] for m in ns):
            for j in plan.added[i]:
                partial_copy(i, j).start()

    ahead = 2
    for stage in stages[:ahead]:
        start_stage(*stage)
    for copy in carry_copies():
        copy.start()
    ready = set()
    for index, (i, n) in enumerate(stages):
        low, high = plan.uses[i][n]
        pltpu.make_async_copy(features(i, n), features(i, n), token_sems.at[i, n]).wait()
        for j in range(low, high):
            if (n, j) not in ready:
                ready.add((n, j))
                pltpu.make_async_copy(weight(n, j), weight(n, j), weight_sems.at[n, j]).wait()
        if index + ahead < len(stages):
            start_stage(*stages[index + ahead])
        term = jnp.dot(
            features(i, n)[...],
            weight_ref[n * slab : (n + 1) * slab, low * wide : high * wide],
            preferred_element_type=jnp.float32,
        )
        for j in range(low, high):
            value = term[:, (j - low) * wide : (j - low + 1) * wide]
            mine = [m for m in ns if plan.uses[i][m] and j in range(*plan.uses[i][m])]
            if n == mine[0] and j in plan.added[i]:
                partial_copy(i, j).wait()
            if n != mine[0] or j in plan.added[i]:
                value += total(i, j)[...]
            if n == mine[-1] and j in plan.finished[i]:
                projected_ref[...] = value.astype(jnp.bfloat16)
                attend_rows(projected_ref, outs[i][j], plan.carried[i] * wide // 3)
                continue
            total(i, j)[...] = value
            if n == mine[-1]:
                out_copy(i, j).start()
    for copy in carry_copies():
        copy.wait()
    for i in images:
        for j in plan.jobs(i):
            if j not in plan.finished[i]:
                out_copy(i, j).wait()


def run_jobs(core, inner, tokens, wide, images, weights):
    images = [
        dict(
            image,
            pieces=[
                [[x if isinstance(x, tuple) else (x, 0) for x in owner] for owner in place]
                for place in image["pieces"]
            ],
            sums=image.get("sums", {}),
            finish=image.get("finish", ()),
            carry=image.get("carry", ((), ())),
        )
        for image in images
    ]
    plan = Jobs(
        origins=[[[[r for _, r in o] for o in p] for p in image["pieces"]] for image in images],
        slots=[slot for slot, _, _ in weights],
        first=[first for _, first, _ in weights],
        same=[[not isinstance(w, tuple) for w in row] for _, _, row in weights],
        uses=[image["uses"] for image in images],
        added=[tuple(image["sums"]) for image in images],
        finished=[image["finish"] for image in images],
        carried=[len(image["carry"][0]) for image in images],
    )
    operands = [x for i in images for place in i["pieces"] for owner in place for x, _ in owner]
    slab = operands[0].shape[1] // 2
    for _, _, row in weights:
        for w in row:
            operands += list(w) if isinstance(w, tuple) else [w]
    operands += [x for image in images for x in image["sums"].values()]
    operands += [x for image in images for place in image["carry"] for x in place]
    anywhere, vmem = pl.BlockSpec(memory_space=pl.ANY), pl.BlockSpec(memory_space=pltpu.VMEM)
    head = wide // 3
    shapes, specs = [], []
    for i in range(len(images)):
        for j in plan.jobs(i):
            if j in plan.finished[i]:
                shape = (tokens // 2, head * (plan.carried[i] + 1))
                shapes += [jax.ShapeDtypeStruct(shape, jnp.bfloat16)] * 2
                specs += [vmem] * 2
            else:
                shapes.append(jax.ShapeDtypeStruct((tokens, wide), jnp.float32))
                specs.append(anywhere)
    jobs = 1 + max(j for i in range(len(images)) for j in plan.jobs(i))
    count, depth, total = len(images), len(weights) * slab, len(images) * tokens
    added = sum(high - low for uses in plan.uses for low, high in filter(None, uses))
    got = pl.pallas_call(
        functools.partial(job_kernel, plan),
        out_shape=shapes,
        in_specs=[pl.BlockSpec(memory_space=pltpu.SMEM)] + [anywhere] * len(operands),
        out_specs=specs,
        scratch_shapes=[
            pltpu.VMEM((total, depth), jnp.bfloat16),
            pltpu.VMEM((depth, jobs * wide), jnp.bfloat16),
            pltpu.VMEM((total, jobs * wide), jnp.float32),
            pltpu.VMEM((tokens, wide), jnp.bfloat16),
            pltpu.SemaphoreType.DMA((count, len(weights))),
            pltpu.SemaphoreType.DMA((len(weights), jobs)),
            pltpu.SemaphoreType.DMA((count, jobs)),
            pltpu.SemaphoreType.DMA((count, jobs)),
            pltpu.SemaphoreType.DMA((count, 2, max(*plan.carried, 1))),
        ],
        compiler_params=pltpu.CompilerParams(vmem_limit_bytes=62 << 20),
        cost_estimate=pl.CostEstimate(
            flops=2 * tokens * slab * wide * added, bytes_accessed=0, transcendentals=0
        ),
    )(jnp.stack([core, inner]).astype(jnp.int32), *operands)
    got = list(got)
    return [
        {
            j: (got.pop(0), got.pop(0)) if j in plan.finished[i] else got.pop(0)
            for j in plan.jobs(i)
        }
        for i in range(count)
    ]


def join_kernel(place_ref, tick_ref, *refs):
    *parts, out_ref, wide_buf, head_buf, sems = refs
    count = len(parts) // 2
    inner = place_ref[count]
    wide, head = parts[0].shape[1], parts[count].shape[1]
    kept = wide - head

    def arrive(i):
        return (
            pltpu.make_async_copy(parts[i], wide_buf.at[i], sems.at[i, 0]),
            pltpu.make_async_copy(parts[count + i], head_buf.at[i], sems.at[i, 1]),
        )

    def leave(i, role):
        begin = pl.multiple_of(place_ref[i] * wide, wide)
        if role:
            target = out_ref.at[:, pl.ds(begin, wide)]
            return [pltpu.make_async_copy(wide_buf.at[i], target, sems.at[i, 2])]
        last = pl.multiple_of(begin + kept, head)
        return [
            pltpu.make_async_copy(
                wide_buf.at[i, :, pl.ds(head, kept)],
                out_ref.at[:, pl.ds(begin, kept)],
                sems.at[i, 2],
            ),
            pltpu.make_async_copy(
                head_buf.at[i], out_ref.at[:, pl.ds(last, head)], sems.at[i, 3]
            ),
        ]

    for i in range(count):
        for copy in arrive(i):
            copy.start()
    for i in range(count):
        for copy in arrive(i):
            copy.wait()
        for role in (1, 0):

            @pl.when((inner == 1) == (role == 1))
            def _():
                for copy in leave(i, role):
                    copy.start()

    for role in (1, 0):

        @pl.when((inner == 1) == (role == 1))
        def _():
            for i in range(count):
                for copy in leave(i, role):
                    copy.wait()


def join(places, inner, tick, parts, back):
    rows, wide = parts[0].shape
    anywhere = pl.BlockSpec(memory_space=pl.ANY)
    return pl.pallas_call(
        join_kernel,
        out_shape=jax.ShapeDtypeStruct((rows, wide * len(parts)), jnp.bfloat16),
        in_specs=[pl.BlockSpec(memory_space=pltpu.SMEM)] + [anywhere] * (1 + 2 * len(parts)),
        out_specs=anywhere,
        scratch_shapes=[
            pltpu.VMEM((len(parts), *parts[0].shape), jnp.bfloat16),
            pltpu.VMEM((len(parts), *back[0].shape), jnp.bfloat16),
            pltpu.SemaphoreType.DMA((len(parts), 4)),
        ],
        cost_estimate=pl.CostEstimate(
            flops=0, bytes_accessed=4 * rows * wide * len(parts), transcendentals=0
        ),
    )(jnp.stack([*places, inner]).astype(jnp.int32), tick, *parts, *back)


def shared(tokens, ln_gain, qkv_weight):
    groups, planes, seqs, cores = (lax.axis_size(a) for a in ("groups", "dp", "seq", "head"))
    group, plane, seq, core = (lax.axis_index(a) for a in ("groups", "dp", "seq", "head"))
    _, rows, _ = tokens.shape
    slab, heads, columns = qkv_weight.shape
    heads, part = heads // groups, rows // cores
    inner = (plane == 1) | (plane == 2)
    wait = lax.optimization_barrier

    def fold(piece):
        piece = piece.reshape(-1, part, columns).transpose(1, 0, 2)
        return piece.reshape(part, -1)

    def pick(for_inner, for_ends):
        return jnp.where(inner, for_inner, for_ends)

    def pair(value):
        return lax.ppermute(value, "dp", [(0, 1), (1, 0), (2, 3), (3, 2)])

    def outward(value):
        return lax.ppermute(value, "dp", [(1, 0), (2, 3)])

    def middle(value):
        return lax.ppermute(value, "dp", [(1, 2), (2, 1)])

    swap = [(0, 1), (1, 0)]
    beside = lambda value: lax.ppermute(value, "seq", swap)
    across = lambda value: lax.ppermute(value, "groups", swap)

    def others(*values):
        got = []
        for value in values:
            if got:
                value, got[-1] = wait((value, got[-1]))
            got.append(lax.ppermute(value, "head", swap))
        return got

    run = functools.partial(run_jobs, core, inner, seqs * rows, columns)

    def exchange(mixed):
        got = []
        for a in range(groups):
            for b in range(seqs):
                sent = mixed[a * seqs + b]
                if a or b:
                    steps = [
                        (g * seqs + s, (g + a) % groups * seqs + (s + b) % seqs)
                        for g in range(groups)
                        for s in range(seqs)
                    ]
                    sent = lax.ppermute(sent, ("groups", "seq"), steps)
                got.append(sent)
        return got

    tick = jnp.full((8, 128), core, jnp.float32)

    weight = qkv_weight.transpose(1, 0, 2)
    normed, (own0,) = normalize_part(tokens, ln_gain, weight, part, False, (0,))
    normed, own0, later_weight = wait((normed, own0, weight))
    cut0, cut1 = normed
    pair1, middle1 = pair(own0), middle(own0)
    beside1, across1 = beside(cut0), across(cut0)
    own1, own2 = [
        lax.dynamic_index_in_dim(later_weight, group * heads + j, 0, keepdims=False) for j in (1, 2)
    ]
    give = pick(fold(own1), cut0)
    pair1, middle1, tick = wait((pair1, middle1, tick))
    tick = tick * 0.5 + 1.0
    pair1, middle1, beside1, across1, own1, own2, cut0, cut1, tokens, give, tick = wait(
        (pair1, middle1, beside1, across1, own1, own2, cut0, cut1, tokens, give, tick)
    )

    pair2, middle2 = pair(give), middle(pair1)
    beside2, across2 = beside(cut1), across(cut1)
    give = pick(fold(middle1), cut1)
    far_normed, _ = normalize_part(tokens, ln_gain, weight, part, True)
    far1 = others(beside1, across1)
    pair2, middle2, tick = wait((pair2, middle2, tick))
    tick = tick * 0.5 + 1.0
    pair2, middle2, beside2, across2, across1, own1, own2, far_normed, far1, give, tick = wait(
        (pair2, middle2, beside2, across2, across1, own1, own2, far_normed, far1, give, tick)
    )

    pair3, middle3 = pair(give), middle(own1)
    beside3, across3 = beside(across1), across(beside2)
    give = pick(middle2, own1)
    far2 = others(beside2, across2)
    pair3, middle3, tick = wait((pair3, middle3, tick))
    tick = tick * 0.5 + 1.0
    pair3, middle3, beside3, across3, pair1, pair2, own2, far2, give, tick = wait(
        (pair3, middle3, beside3, across3, pair1, pair2, own2, far2, give, tick)
    )

    pair4, middle4 = pair(give), middle(own2)
    beside4, across4 = beside(pair2), across(pair2)
    give = pick(middle3, own2)
    pieces0 = ((normed, far_normed), ((beside1, beside2), (far1[0], far2[0])))
    owns = [own0, (own1, own0), (own2, own1)]
    ((head0, sum20, sum30),) = [
        tuple(got.values())
        for got in run(
            [dict(pieces=pieces0, uses=[(0, 3), (0, 2), (0, 1), (0, 1)], finish=(0,))],
            [(0, 0, owns), (2, 0, [middle1, (middle3, pair1)]), (1, 0, [pair1]), (3, 0, [middle2])],
        )
    ]
    far3 = others(beside3, across3)
    lent = jnp.concatenate([pair2, pair3])
    pair4, middle4, tick = wait((pair4, middle4, tick))
    tick = tick * 0.5 + 1.0
    pair4, middle4, beside4, across4, own2, pair3, lent, head0, sum20, sum30, far3, give, tick = wait(
        (pair4, middle4, beside4, across4, own2, pair3, lent, head0, sum20, sum30, far3, give, tick)
    )

    pair5, middle5 = pair(give), middle(pair4)
    beside5, across5 = beside(pair3), across(pair3)
    pieces1 = (((across1, across2), (far1[1], far2[1])), ((beside3, across3), far3))
    image1, image0 = run(
        [
            dict(pieces=pieces1, uses=[(0, 3), (0, 3), (0, 2), (0, 1)], finish=(0,)),
            dict(pieces=pieces0, uses=[None, (2, 3), (1, 2), None], sums={1: sum20, 2: sum30}),
        ],
        [
            (0, 0, owns),
            (2, 0, [middle1, (middle3, pair1), (middle4, pair2)]),
            (1, 0, [pair1, (pair4, pair3)]),
            (3, 0, [middle2]),
        ],
    )
    far_lent, far4 = others(lent, beside4)
    pair5, middle5, tick = wait((pair5, middle5, tick))
    tick = tick * 0.5 + 1.0
    pair5, middle5, beside5, across5, across4, image0, image1, far_lent, far4, tick = wait(
        (
            *(pair5, middle5, beside5, across5, across4),
            *(image0, image1, far_lent, far4, tick),
        )
    )

    pair6, middle6 = outward(middle5), middle(pair5)
    beside6, across6 = beside(across4), across(beside5)
    far5, far_across4 = others(beside5, across4)
    ahead0, ahead1 = run(
        [
            dict(
                pieces=pieces,
                uses=[(0, 1), (1, 2)],
                sums={0: image[1], 1: image[2]},
                finish=(0,),
            )
            for pieces, image in ((pieces0, image0), (pieces1, image1))
        ],
        [(3, 0, [(middle5, pair4)]), (1, 1, [pair5])],
    )
    lent0 = (((pair2, pair3), (far_lent, (far_lent, part))), ((beside4, beside5), (far4, far5)))
    lent_weights = [(0, 0, [pair5]), (1, 0, [middle4]), (2, 0, [own2])]
    ((sum4,),) = [
        tuple(got.values()) for got in run([dict(pieces=lent0, uses=[(0, 1)] * 3)], lent_weights)
    ]
    pair6, middle6, tick = wait((pair6, middle6, tick))
    tick = tick * 0.5 + 1.0
    pair6, middle6, beside6, across6, across5, ahead0, ahead1, sum4, far_across4, tick = wait(
        (pair6, middle6, beside6, across6, across5, ahead0, ahead1, sum4, far_across4, tick)
    )

    far_across5, *far6 = [
        lax.ppermute(value, "head", swap) for value in (across5, beside6, across6)
    ]
    done0, done1, lent0 = run(
        [
            dict(pieces=p, uses=[(0, 1)], sums={0: x[1]}, finish=(0,), carry=tuple(zip(h, x[0])))
            for p, h, x in ((pieces0, head0, ahead0), (pieces1, image1[0], ahead1))
        ]
        + [dict(pieces=lent0, uses=[(0, 1)], sums={0: sum4}, finish=(0,))],
        [(3, 0, [(middle6, pair6)])],
    )
    sent = exchange((*done0[0], *done1[0]))
    lent1 = (((across4, across5), (far_across4, far_across5)), ((beside6, across6), far6))
    (lent1,) = run(
        [dict(pieces=lent1, uses=[(0, 1)] * 4, finish=(0,))], [*lent_weights, (3, 0, [middle6])]
    )

    def hand_back(mixed):
        got = []
        for a in range(groups):
            for b in range(seqs):
                steps = [
                    (
                        (g * planes + z) * seqs + s,
                        ((g + a) % groups * planes + (z ^ 1)) * seqs + (s + b) % seqs,
                    )
                    for g in range(groups)
                    for z in (1, 2)
                    for s in range(seqs)
                ]
                sent = mixed[a * seqs + b]
                got.append(lax.ppermute(sent, ("groups", "dp", "seq"), steps))
        return got

    back = hand_back((*lent0[0], *lent1[0]))
    places = [
        (seq - b) % seqs * groups + (group - a) % groups
        for a in range(groups)
        for b in range(seqs)
    ]
    return join(places, inner, tick, sent, back)[None]


def per_device(tokens, ln_gain, qkv_weight):
    groups, planes, seqs, cores = (lax.axis_size(a) for a in ("groups", "dp", "seq", "head"))
    images, rows, width = tokens.shape
    slab, heads, _ = qkv_weight.shape
    if (groups, planes, seqs, cores) == (2, 4, 2, 2) and images == 1 and heads == 3 * groups:
        part = rows // cores
        if rows % (32 * cores) == 0 and slab % part == 0 and 2 * slab == qkv_weight.shape[2] * slab // part:
            return shared(tokens, ln_gain, qkv_weight)
    return plain(tokens, ln_gain, qkv_weight)


def solution(mesh):
    return jax.shard_map(
        per_device,
        mesh=mesh,
        in_specs=(P(("groups", "dp"), "seq", None), P(), P("dp", ("seq", "head"), None)),
        out_specs=P(("groups", "dp"), "seq", "head"),
        check_vma=False,
    )
```

```python
import functools
import math

import jax
import jax.numpy as jnp
from jax import lax
from jax.experimental import pallas as pl
from jax.experimental.pallas import tpu as pltpu
from jax.sharding import PartitionSpec as P


def normalize(array, gain):
    widened = array.astype(jnp.float32)
    centered = widened - jnp.mean(widened, axis=-1, keepdims=True)
    variance = jnp.mean(centered * centered, axis=-1, keepdims=True)
    return (centered * lax.rsqrt(variance + 1e-06) * gain).astype(jnp.bfloat16)


def attend(projected):
    width = projected.shape[2] // 3
    queries = projected[:, :, :width]
    key_rows = projected[:, :, width : 2 * width]
    value_rows = projected[:, :, 2 * width :]
    scores = jnp.einsum("qhd,khd->hqk", queries, key_rows, preferred_element_type=jnp.float32) * (
        1.0 / math.sqrt(width)
    )
    highest = jnp.max(scores, axis=-1, keepdims=True)
    expo = jnp.exp(scores - highest)
    probs = (expo / jnp.sum(expo, axis=-1, keepdims=True)).astype(jnp.bfloat16)
    mixed = jnp.einsum("hqk,khd->qhd", probs, value_rows, preferred_element_type=jnp.float32)
    return mixed.astype(jnp.bfloat16).reshape(projected.shape[0], -1)


def plain(tokens, ln_gain, qkv_weight):
    images = tokens.shape[0]
    width = tokens.shape[2]
    heads_here = qkv_weight.shape[1]
    columns = heads_here * qkv_weight.shape[2]
    source = normalize(tokens, ln_gain)
    half_width = width // lax.axis_size("head")
    core_index = lax.axis_index("head")
    own_half = lax.dynamic_slice_in_dim(source, core_index * half_width, half_width, 2)
    fetched = lax.all_gather(own_half, "seq", axis=1, tiled=True)
    gathered = lax.all_gather(fetched, "head", axis=2, tiled=True)
    full_tokens = gathered.shape[1]
    features = gathered.reshape(images * full_tokens, width)
    piece = lax.all_gather(qkv_weight, "dp", axis=0, tiled=True)
    projected = jnp.dot(
        features, piece.reshape(piece.shape[0], columns), preferred_element_type=jnp.float32
    )
    projected = projected.astype(jnp.bfloat16).reshape(
        images, full_tokens, heads_here, qkv_weight.shape[2]
    )
    mixed = lax.map(attend, projected)
    return lax.all_to_all(mixed, "seq", split_axis=1, concat_axis=2, tiled=True)


def slab_order(plane):
    inner = (plane == 1) | (plane == 2)
    near, far = plane ^ 1, 2 - plane // 2
    return plane, jnp.where(inner, near, far), jnp.where(inner, far, near), 3 - 3 * (plane // 2)


def normalize_kernel(step, other, taken, tokens_ref, gain_ref, weight_ref, *refs):
    refs = list(refs)
    take = lambda n: [refs.pop(0) for _ in range(n)]
    normed_refs, own_refs, (tokens_buf, *normed_bufs) = take(2), take(len(taken)), take(3)
    own_bufs, (in_sems, out_sems, own_sems) = take(len(taken)), take(3)
    part, width = tokens_buf.shape
    lanes = 128
    slab, span = width // 4, width // 2
    core = lax.axis_index("head")
    first = pl.multiple_of((1 - core if other else core) * part, part)
    order = slab_order(lax.axis_index("dp"))
    heads = weight_ref.shape[0] // lax.axis_size("groups")

    def rows_in(i):
        return pltpu.make_async_copy(
            tokens_ref.at[0, pl.ds(pl.multiple_of(first + i * step, step), step)],
            tokens_buf.at[pl.ds(pl.multiple_of(i * step, step), step)],
            in_sems.at[i],
        )

    def rows_out(i):
        rows = pl.ds(pl.multiple_of(i * step, step), step)
        return [
            pltpu.make_async_copy(buf.at[rows], ref.at[rows], out_sems.at[i, cut])
            for cut, (buf, ref) in enumerate(zip(normed_bufs, normed_refs))
        ]

    def own_in(k):
        head = lax.axis_index("groups") * heads + taken[k]
        return pltpu.make_async_copy(weight_ref.at[head], own_bufs[k], own_sems.at[k, 0])

    def own_out(k):
        return pltpu.make_async_copy(own_bufs[k], own_refs[k], own_sems.at[k, 1])

    for i in range(part // step):
        rows_in(i).start()
    for k in range(len(taken)):
        own_in(k).start()

    @pl.loop(0, part // step)
    def _(i):
        rows_in(i).wait()
        rows = pl.ds(pl.multiple_of(i * step, step), step)

        def widened(begin):
            return tokens_buf[rows, pl.ds(begin, lanes)].astype(jnp.float32)

        total = jnp.zeros((step, lanes), jnp.float32)
        for begin in range(0, width, lanes):
            total += widened(begin)
        mean = jnp.sum(total, axis=-1, keepdims=True) / width
        total = jnp.zeros((step, lanes), jnp.float32)
        for begin in range(0, width, lanes):
            centered = widened(begin) - mean
            total += centered * centered
        scale = lax.rsqrt(jnp.sum(total, axis=-1, keepdims=True) / width + 1e-06)
        for k in range(4):
            for begin in range(0, slab, lanes):
                column = pl.multiple_of(order[k] * slab + begin, lanes)
                value = (widened(column) - mean) * scale * gain_ref[:, pl.ds(column, lanes)]
                target = k * slab % span + begin
                normed_bufs[k * slab // span][rows, target : target + lanes] = value.astype(
                    jnp.bfloat16
                )
        for copy in rows_out(i):
            copy.start()

    for k in range(len(taken)):
        own_in(k).wait()
        own_out(k).start()
    for i in range(part // step):
        for copy in rows_out(i):
            copy.wait()
    for k in range(len(taken)):
        own_out(k).wait()


def normalize_part(tokens, ln_gain, weight, part, other, taken=()):
    width = tokens.shape[2]
    piece = weight.shape[1:]
    step = 64 if part % 64 == 0 else 32
    anywhere = pl.BlockSpec(memory_space=pl.ANY)
    half = jax.ShapeDtypeStruct((part, width // 2), jnp.bfloat16)
    got = pl.pallas_call(
        functools.partial(normalize_kernel, step, other, taken),
        out_shape=[half] * 2 + [jax.ShapeDtypeStruct(piece, jnp.bfloat16)] * len(taken),
        in_specs=[anywhere, pl.BlockSpec(memory_space=pltpu.VMEM), anywhere],
        out_specs=[anywhere] * (2 + len(taken)),
        scratch_shapes=[
            pltpu.VMEM((part, width), jnp.bfloat16),
            *[pltpu.VMEM((part, width // 2), jnp.bfloat16)] * 2,
            *[pltpu.VMEM(piece, jnp.bfloat16)] * len(taken),
            pltpu.SemaphoreType.DMA((part // step,)),
            pltpu.SemaphoreType.DMA((part // step, 2)),
            pltpu.SemaphoreType.DMA((max(len(taken), 1), 2)),
        ],
        compiler_params=pltpu.CompilerParams(vmem_limit_bytes=62 << 20),
        cost_estimate=pl.CostEstimate(
            flops=8 * part * width, bytes_accessed=4 * part * width, transcendentals=part
        ),
    )(tokens, ln_gain[None], weight)
    return got[:2], got[2:]


def attend_rows(projected_ref, parts, column):
    width = projected_ref.shape[1] // 3
    key_rows = projected_ref[:, width : 2 * width]
    value_rows = projected_ref[:, 2 * width :]
    value_rows = jnp.concatenate([value_rows, jnp.ones_like(value_rows)], axis=1)
    begin = 0
    for part in parts:
        step = part.shape[0]
        queries = projected_ref[begin : begin + step, :width]
        scores = lax.dot_general(
            queries, key_rows, (((1,), (1,)), ((), ())), preferred_element_type=jnp.float32
        )
        highest = jnp.max(scores, axis=-1, keepdims=True)
        expo = jnp.exp2((scores - highest) * (math.log2(math.e) / math.sqrt(width)))
        mixed = jnp.dot(expo.astype(jnp.bfloat16), value_rows, preferred_element_type=jnp.float32)
        mixed = mixed[:, :width] / mixed[:, width:]
        part[:, column : column + width] = mixed.astype(jnp.bfloat16)
        begin += step


class Jobs:
    def __init__(self, **numbers):
        self.__dict__.update(numbers)

    def jobs(self, image):
        return sorted({j for use in self.uses[image] if use for j in range(*use)})


def job_kernel(plan, role_ref, *refs):
    refs = list(refs)
    take = lambda n: [refs.pop(0) for _ in range(n)]
    images, ns = range(len(plan.uses)), range(len(plan.slots))
    pieces = [[[take(2) for _ in place] for place in image] for image in plan.origins]
    weights = [[take(1) * 2 if alike else take(2) for alike in row] for row in plan.same]
    partials = [{j: take(1)[0] for j in plan.added[i]} for i in images]
    carried = [[take(plan.carried[i]) for _ in range(2)] for i in images]
    outs = [
        {j: take(2) if j in plan.finished[i] else take(1)[0] for j in plan.jobs(i)} for i in images
    ]
    features_ref, weight_ref, total_ref, projected_ref = take(4)
    token_sems, weight_sems, sum_sems, out_sems, carry_sems = take(5)
    core, inner = role_ref[0], role_ref[1]
    slab = pieces[0][0][0][0].shape[1] // 2
    tokens, wide = projected_ref.shape
    part = tokens // 4

    def features(i, n):
        return features_ref.at[pl.ds(i * tokens, tokens), pl.ds(n * slab, slab)]

    def weight(n, j):
        return weight_ref.at[pl.ds(n * slab, slab), pl.ds(j * wide, wide)]

    def total(i, j):
        return total_ref.at[pl.ds(i * tokens, tokens), pl.ds(j * wide, wide)]

    def start_tokens(i, n):
        cut, begin = plan.slots[n] // 2, plan.slots[n] % 2 * slab
        for place in range(2):
            split = len(plan.origins[i][place])
            for owner in range(split):
                row = i * tokens + 2 * place * part
                if split == 2:
                    row += (1 - core if owner else core) * part
                count = 2 * part // split
                from_rows = pl.ds(plan.origins[i][place][owner][cut], count)
                rows = pl.ds(pl.multiple_of(row, 32), count)
                pltpu.make_async_copy(
                    pieces[i][place][owner][cut].at[from_rows, pl.ds(begin, slab)],
                    features_ref.at[rows, pl.ds(n * slab, slab)],
                    token_sems.at[i, n],
                ).start()

    def start_weight(n, j, role):
        source = weights[n][j - plan.first[n]][role]
        if source.shape[0] == slab:
            pltpu.make_async_copy(source, weight(n, j), weight_sems.at[n, j]).start()
            return
        for b in range(source.shape[1] // wide):
            pltpu.make_async_copy(
                source.at[:, pl.ds(b * wide, wide)],
                weight_ref.at[pl.ds(n * slab + b * part, part), pl.ds(j * wide, wide)],
                weight_sems.at[n, j],
            ).start()

    def start_role_weight(n, j):
        if plan.same[n][j - plan.first[n]]:
            start_weight(n, j, 0)
            return

        @pl.when(inner == 1)
        def _():
            start_weight(n, j, 0)

        @pl.when(inner != 1)
        def _():
            start_weight(n, j, 1)

    def partial_copy(i, j):
        return pltpu.make_async_copy(partials[i][j], total(i, j), sum_sems.at[i, j])

    def out_copy(i, j):
        return pltpu.make_async_copy(total(i, j), outs[i][j], out_sems.at[i, j])

    def carry_copies():
        for i in images:
            for place in range(2):
                for k in range(plan.carried[i]):
                    (finished,) = plan.finished[i]
                    target = outs[i][finished][place].at[:, pl.ds(k * wide // 3, wide // 3)]
                    yield pltpu.make_async_copy(
                        carried[i][place][k], target, carry_sems.at[i, place, k]
                    )

    stages = [(i, n) for i in images for n in ns if plan.uses[i][n]]
    held = set()

    def start_stage(i, n):
        start_tokens(i, n)
        for j in range(*plan.uses[i][n]):
            if (n, j) not in held:
                held.add((n, j))
                start_role_weight(n, j)
        if not any((i, n) > (i, m) and plan.uses[i][m] for m in ns):
            for j in plan.added[i]:
                partial_copy(i, j).start()

    ahead = 2
    for stage in stages[:ahead]:
        start_stage(*stage)
    for copy in carry_copies():
        copy.start()
    ready = set()
    for index, (i, n) in enumerate(stages):
        low, high = plan.uses[i][n]
        pltpu.make_async_copy(features(i, n), features(i, n), token_sems.at[i, n]).wait()
        for j in range(low, high):
            if (n, j) not in ready:
                ready.add((n, j))
                pltpu.make_async_copy(weight(n, j), weight(n, j), weight_sems.at[n, j]).wait()
        if index + ahead < len(stages):
            start_stage(*stages[index + ahead])
        term = jnp.dot(
            features(i, n)[...],
            weight_ref[n * slab : (n + 1) * slab, low * wide : high * wide],
            preferred_element_type=jnp.float32,
        )
        for j in range(low, high):
            value = term[:, (j - low) * wide : (j - low + 1) * wide]
            mine = [m for m in ns if plan.uses[i][m] and j in range(*plan.uses[i][m])]
            if n == mine[0] and j in plan.added[i]:
                partial_copy(i, j).wait()
            if n != mine[0] or j in plan.added[i]:
                value += total(i, j)[...]
            if n == mine[-1] and j in plan.finished[i]:
                projected_ref[...] = value.astype(jnp.bfloat16)
                attend_rows(projected_ref, outs[i][j], plan.carried[i] * wide // 3)
                continue
            total(i, j)[...] = value
            if n == mine[-1]:
                out_copy(i, j).start()
    for copy in carry_copies():
        copy.wait()
    for i in images:
        for j in plan.jobs(i):
            if j not in plan.finished[i]:
                out_copy(i, j).wait()


def run_jobs(core, inner, tokens, wide, images, weights):
    images = [
        dict(
            image,
            pieces=[
                [[x if isinstance(x, tuple) else (x, 0) for x in owner] for owner in place]
                for place in image["pieces"]
            ],
            sums=image.get("sums", {}),
            finish=image.get("finish", ()),
            carry=image.get("carry", ((), ())),
        )
        for image in images
    ]
    plan = Jobs(
        origins=[[[[r for _, r in o] for o in p] for p in image["pieces"]] for image in images],
        slots=[slot for slot, _, _ in weights],
        first=[first for _, first, _ in weights],
        same=[[not isinstance(w, tuple) for w in row] for _, _, row in weights],
        uses=[image["uses"] for image in images],
        added=[tuple(image["sums"]) for image in images],
        finished=[image["finish"] for image in images],
        carried=[len(image["carry"][0]) for image in images],
    )
    operands = [x for i in images for place in i["pieces"] for owner in place for x, _ in owner]
    slab = operands[0].shape[1] // 2
    for _, _, row in weights:
        for w in row:
            operands += list(w) if isinstance(w, tuple) else [w]
    operands += [x for image in images for x in image["sums"].values()]
    operands += [x for image in images for place in image["carry"] for x in place]
    anywhere, vmem = pl.BlockSpec(memory_space=pl.ANY), pl.BlockSpec(memory_space=pltpu.VMEM)
    head = wide // 3
    shapes, specs = [], []
    for i in range(len(images)):
        for j in plan.jobs(i):
            if j in plan.finished[i]:
                shape = (tokens // 2, head * (plan.carried[i] + 1))
                shapes += [jax.ShapeDtypeStruct(shape, jnp.bfloat16)] * 2
                specs += [vmem] * 2
            else:
                shapes.append(jax.ShapeDtypeStruct((tokens, wide), jnp.float32))
                specs.append(anywhere)
    jobs = 1 + max(j for i in range(len(images)) for j in plan.jobs(i))
    count, depth, total = len(images), len(weights) * slab, len(images) * tokens
    added = sum(high - low for uses in plan.uses for low, high in filter(None, uses))
    got = pl.pallas_call(
        functools.partial(job_kernel, plan),
        out_shape=shapes,
        in_specs=[pl.BlockSpec(memory_space=pltpu.SMEM)] + [anywhere] * len(operands),
        out_specs=specs,
        scratch_shapes=[
            pltpu.VMEM((total, depth), jnp.bfloat16),
            pltpu.VMEM((depth, jobs * wide), jnp.bfloat16),
            pltpu.VMEM((total, jobs * wide), jnp.float32),
            pltpu.VMEM((tokens, wide), jnp.bfloat16),
            pltpu.SemaphoreType.DMA((count, len(weights))),
            pltpu.SemaphoreType.DMA((len(weights), jobs)),
            pltpu.SemaphoreType.DMA((count, jobs)),
            pltpu.SemaphoreType.DMA((count, jobs)),
            pltpu.SemaphoreType.DMA((count, 2, max(*plan.carried, 1))),
        ],
        compiler_params=pltpu.CompilerParams(vmem_limit_bytes=62 << 20),
        cost_estimate=pl.CostEstimate(
            flops=2 * tokens * slab * wide * added, bytes_accessed=0, transcendentals=0
        ),
    )(jnp.stack([core, inner]).astype(jnp.int32), *operands)
    got = list(got)
    return [
        {
            j: (got.pop(0), got.pop(0)) if j in plan.finished[i] else got.pop(0)
            for j in plan.jobs(i)
        }
        for i in range(count)
    ]


def join_kernel(place_ref, *refs):
    *parts, out_ref, sems = refs
    count = len(parts) // 2
    inner = place_ref[count]
    wide, head = parts[0].shape[1], parts[count].shape[1]

    def copies(i, role):
        begin = pl.multiple_of(place_ref[i] * wide, wide)
        if role:
            yield parts[i], out_ref.at[:, pl.ds(begin, wide)], sems.at[i, 0]
            return
        kept = wide - head
        yield parts[i].at[:, pl.ds(head, kept)], out_ref.at[:, pl.ds(begin, kept)], sems.at[i, 0]
        last = pl.multiple_of(begin + kept, head)
        yield parts[count + i], out_ref.at[:, pl.ds(last, head)], sems.at[i, 1]

    for role in (1, 0):

        @pl.when((inner == 1) == (role == 1))
        def _():
            every = [pltpu.make_async_copy(*c) for i in range(count) for c in copies(i, role)]
            for copy in every:
                copy.start()
            for copy in every:
                copy.wait()


def join(places, inner, parts, back):
    rows, wide = parts[0].shape
    anywhere = pl.BlockSpec(memory_space=pl.ANY)
    return pl.pallas_call(
        join_kernel,
        out_shape=jax.ShapeDtypeStruct((rows, wide * len(parts)), jnp.bfloat16),
        in_specs=[pl.BlockSpec(memory_space=pltpu.SMEM)] + [anywhere] * (2 * len(parts)),
        out_specs=pl.BlockSpec(memory_space=pltpu.VMEM),
        scratch_shapes=[pltpu.SemaphoreType.DMA((len(parts), 2))],
        cost_estimate=pl.CostEstimate(
            flops=0, bytes_accessed=4 * rows * wide * len(parts), transcendentals=0
        ),
    )(jnp.stack([*places, inner]).astype(jnp.int32), *parts, *back)


def shared(tokens, ln_gain, qkv_weight):
    groups, planes, seqs, cores = (lax.axis_size(a) for a in ("groups", "dp", "seq", "head"))
    group, plane, seq, core = (lax.axis_index(a) for a in ("groups", "dp", "seq", "head"))
    _, rows, _ = tokens.shape
    slab, heads, columns = qkv_weight.shape
    heads, part = heads // groups, rows // cores
    inner = (plane == 1) | (plane == 2)
    wait = lax.optimization_barrier

    def fold(piece):
        piece = piece.reshape(-1, part, columns).transpose(1, 0, 2)
        return piece.reshape(part, -1)

    def pick(for_inner, for_ends):
        return jnp.where(inner, for_inner, for_ends)

    def pair(value):
        return lax.ppermute(value, "dp", [(0, 1), (1, 0), (2, 3), (3, 2)])

    def outward(value):
        return lax.ppermute(value, "dp", [(1, 0), (2, 3)])

    def middle(value):
        return lax.ppermute(value, "dp", [(1, 2), (2, 1)])

    swap = [(0, 1), (1, 0)]
    beside = lambda value: lax.ppermute(value, "seq", swap)
    across = lambda value: lax.ppermute(value, "groups", swap)

    def others(*values):
        got = []
        for value in values:
            if got:
                value, got[-1] = wait((value, got[-1]))
            got.append(lax.ppermute(value, "head", swap))
        return got

    run = functools.partial(run_jobs, core, inner, seqs * rows, columns)

    def exchange(mixed):
        got = []
        for a in range(groups):
            for b in range(seqs):
                sent = mixed[a * seqs + b]
                if a or b:
                    steps = [
                        (g * seqs + s, (g + a) % groups * seqs + (s + b) % seqs)
                        for g in range(groups)
                        for s in range(seqs)
                    ]
                    sent = lax.ppermute(sent, ("groups", "seq"), steps)
                got.append(sent)
        return got

    weight = qkv_weight.transpose(1, 0, 2)
    normed, (own0,) = normalize_part(tokens, ln_gain, weight, part, False, (0,))
    normed, own0, later_weight = wait((normed, own0, weight))
    cut0, cut1 = normed
    pair1, middle1 = pair(own0), middle(own0)
    beside1, across1 = beside(cut0), across(cut0)
    own1, own2 = [
        lax.dynamic_index_in_dim(later_weight, group * heads + j, 0, keepdims=False) for j in (1, 2)
    ]
    give = pick(fold(own1), cut0)
    pair1, middle1, beside1, across1, own1, own2, cut0, cut1, tokens, give = wait(
        (pair1, middle1, beside1, across1, own1, own2, cut0, cut1, tokens, give)
    )

    pair2, middle2 = pair(give), middle(pair1)
    beside2, across2 = beside(cut1), across(cut1)
    give = pick(fold(middle1), cut1)
    far_normed, _ = normalize_part(tokens, ln_gain, weight, part, True)
    far1 = others(beside1, across1)
    pair2, middle2, beside2, across2, across1, own1, own2, far_normed, far1, give = wait(
        (pair2, middle2, beside2, across2, across1, own1, own2, far_normed, far1, give)
    )

    pair3, middle3 = pair(give), middle(own1)
    beside3, across3 = beside(across1), across(beside2)
    give = pick(middle2, own1)
    far2 = others(beside2, across2)
    pair3, middle3, beside3, across3, pair1, pair2, own2, far2, give = wait(
        (pair3, middle3, beside3, across3, pair1, pair2, own2, far2, give)
    )

    pair4, middle4 = pair(give), middle(own2)
    beside4, across4 = beside(pair2), across(pair2)
    give = pick(middle3, own2)
    pieces0 = ((normed, far_normed), ((beside1, beside2), (far1[0], far2[0])))
    owns = [own0, (own1, own0), (own2, own1)]
    ((head0, sum20, sum30),) = [
        tuple(got.values())
        for got in run(
            [dict(pieces=pieces0, uses=[(0, 3), (0, 2), (0, 1), (0, 1)], finish=(0,))],
            [(0, 0, owns), (2, 0, [middle1, (middle3, pair1)]), (1, 0, [pair1]), (3, 0, [middle2])],
        )
    ]
    far3 = others(beside3, across3)
    lent = jnp.concatenate([pair2, pair3])
    pair4, middle4, beside4, across4, own2, pair3, lent, head0, sum20, sum30, far3, give = wait(
        (pair4, middle4, beside4, across4, own2, pair3, lent, head0, sum20, sum30, far3, give)
    )

    pair5, middle5 = pair(give), middle(pair4)
    beside5, across5 = beside(pair3), across(pair3)
    pieces1 = (((across1, across2), (far1[1], far2[1])), ((beside3, across3), far3))
    image1, image0 = run(
        [
            dict(pieces=pieces1, uses=[(0, 3), (0, 3), (0, 2), (0, 1)], finish=(0,)),
            dict(pieces=pieces0, uses=[None, (2, 3), (1, 2), None], sums={1: sum20, 2: sum30}),
        ],
        [
            (0, 0, owns),
            (2, 0, [middle1, (middle3, pair1), (middle4, pair2)]),
            (1, 0, [pair1, (pair4, pair3)]),
            (3, 0, [middle2]),
        ],
    )
    far_lent, far4 = others(lent, beside4)
    pair5, middle5, beside5, across5, across4, image0, image1, far_lent, far4 = wait(
        (
            *(pair5, middle5, beside5, across5, across4),
            *(image0, image1, far_lent, far4),
        )
    )

    pair6, middle6 = outward(middle5), middle(pair5)
    beside6, across6 = beside(across4), across(beside5)
    far5, far_across4 = others(beside5, across4)
    ahead0, ahead1 = run(
        [
            dict(
                pieces=pieces,
                uses=[(0, 1), (1, 2)],
                sums={0: image[1], 1: image[2]},
                finish=(0,),
            )
            for pieces, image in ((pieces0, image0), (pieces1, image1))
        ],
        [(3, 0, [(middle5, pair4)]), (1, 1, [pair5])],
    )
    lent0 = (((pair2, pair3), (far_lent, (far_lent, part))), ((beside4, beside5), (far4, far5)))
    lent_weights = [(0, 0, [pair5]), (1, 0, [middle4]), (2, 0, [own2])]
    ((sum4,),) = [
        tuple(got.values()) for got in run([dict(pieces=lent0, uses=[(0, 1)] * 3)], lent_weights)
    ]
    pair6, middle6, beside6, across6, across5, ahead0, ahead1, sum4, far_across4 = wait(
        (pair6, middle6, beside6, across6, across5, ahead0, ahead1, sum4, far_across4)
    )

    far_across5, *far6 = [
        lax.ppermute(value, "head", swap) for value in (across5, beside6, across6)
    ]
    done0, done1, lent0 = run(
        [
            dict(pieces=p, uses=[(0, 1)], sums={0: x[1]}, finish=(0,), carry=tuple(zip(h, x[0])))
            for p, h, x in ((pieces0, head0, ahead0), (pieces1, image1[0], ahead1))
        ]
        + [dict(pieces=lent0, uses=[(0, 1)], sums={0: sum4}, finish=(0,))],
        [(3, 0, [(middle6, pair6)])],
    )
    sent = exchange((*done0[0], *done1[0]))
    lent1 = (((across4, across5), (far_across4, far_across5)), ((beside6, across6), far6))
    (lent1,) = run(
        [dict(pieces=lent1, uses=[(0, 1)] * 4, finish=(0,))], [*lent_weights, (3, 0, [middle6])]
    )

    def hand_back(mixed):
        got = []
        for a in range(groups):
            for b in range(seqs):
                steps = [
                    (
                        (g * planes + z) * seqs + s,
                        ((g + a) % groups * planes + (z ^ 1)) * seqs + (s + b) % seqs,
                    )
                    for g in range(groups)
                    for z in (1, 2)
                    for s in range(seqs)
                ]
                sent = mixed[a * seqs + b]
                got.append(lax.ppermute(sent, ("groups", "dp", "seq"), steps))
        return got

    back = hand_back((*lent0[0], *lent1[0]))
    places = [
        (seq - b) % seqs * groups + (group - a) % groups
        for a in range(groups)
        for b in range(seqs)
    ]
    return join(places, inner, sent, back)[None]


def per_device(tokens, ln_gain, qkv_weight):
    groups, planes, seqs, cores = (lax.axis_size(a) for a in ("groups", "dp", "seq", "head"))
    images, rows, width = tokens.shape
    slab, heads, _ = qkv_weight.shape
    if (groups, planes, seqs, cores) == (2, 4, 2, 2) and images == 1 and heads == 3 * groups:
        part = rows // cores
        if rows % (32 * cores) == 0 and slab % part == 0 and 2 * slab == qkv_weight.shape[2] * slab // part:
            return shared(tokens, ln_gain, qkv_weight)
    return plain(tokens, ln_gain, qkv_weight)


def solution(mesh):
    return jax.shard_map(
        per_device,
        mesh=mesh,
        in_specs=(P(("groups", "dp"), "seq", None), P(), P("dp", ("seq", "head"), None)),
        out_specs=P(("groups", "dp"), "seq", "head"),
        check_vma=False,
    )
```

```python
import functools
import math

import jax
import jax.numpy as jnp
from jax import lax
from jax.experimental import pallas as pl
from jax.experimental.pallas import tpu as pltpu
from jax.sharding import PartitionSpec as P


def normalize(array, gain):
    widened = array.astype(jnp.float32)
    centered = widened - jnp.mean(widened, axis=-1, keepdims=True)
    variance = jnp.mean(centered * centered, axis=-1, keepdims=True)
    return (centered * lax.rsqrt(variance + 1e-06) * gain).astype(jnp.bfloat16)


def attend(projected):
    width = projected.shape[2] // 3
    queries = projected[:, :, :width]
    key_rows = projected[:, :, width : 2 * width]
    value_rows = projected[:, :, 2 * width :]
    scores = jnp.einsum("qhd,khd->hqk", queries, key_rows, preferred_element_type=jnp.float32) * (
        1.0 / math.sqrt(width)
    )
    highest = jnp.max(scores, axis=-1, keepdims=True)
    expo = jnp.exp(scores - highest)
    probs = (expo / jnp.sum(expo, axis=-1, keepdims=True)).astype(jnp.bfloat16)
    mixed = jnp.einsum("hqk,khd->qhd", probs, value_rows, preferred_element_type=jnp.float32)
    return mixed.astype(jnp.bfloat16).reshape(projected.shape[0], -1)


def plain(tokens, ln_gain, qkv_weight):
    images = tokens.shape[0]
    width = tokens.shape[2]
    heads_here = qkv_weight.shape[1]
    columns = heads_here * qkv_weight.shape[2]
    source = normalize(tokens, ln_gain)
    half_width = width // lax.axis_size("head")
    core_index = lax.axis_index("head")
    own_half = lax.dynamic_slice_in_dim(source, core_index * half_width, half_width, 2)
    fetched = lax.all_gather(own_half, "seq", axis=1, tiled=True)
    gathered = lax.all_gather(fetched, "head", axis=2, tiled=True)
    full_tokens = gathered.shape[1]
    features = gathered.reshape(images * full_tokens, width)
    piece = lax.all_gather(qkv_weight, "dp", axis=0, tiled=True)
    projected = jnp.dot(
        features, piece.reshape(piece.shape[0], columns), preferred_element_type=jnp.float32
    )
    projected = projected.astype(jnp.bfloat16).reshape(
        images, full_tokens, heads_here, qkv_weight.shape[2]
    )
    mixed = lax.map(attend, projected)
    return lax.all_to_all(mixed, "seq", split_axis=1, concat_axis=2, tiled=True)


def slab_order(plane):
    inner = (plane == 1) | (plane == 2)
    near, far = plane ^ 1, 2 - plane // 2
    return plane, jnp.where(inner, near, far), jnp.where(inner, far, near), 3 - 3 * (plane // 2)


def normalize_kernel(place_ref, tokens_ref, gain_ref, weight_ref, *refs):
    normed_refs, rest = refs[:2], refs[2:]
    rows, width = tokens_ref.shape[1:]
    lanes = 128
    slab, span = width // 4, width // 2
    step, steps = pl.program_id(0), pl.num_programs(0)
    if rest:
        own_ref, own_buf, own_sems = rest
        own_in = pltpu.make_async_copy(weight_ref.at[place_ref[5]], own_buf, own_sems.at[0])
        own_out = pltpu.make_async_copy(own_buf, own_ref, own_sems.at[1])

        @pl.when(step == 0)
        def _():
            own_in.start()

        @pl.when(step == 1)
        def _():
            own_in.wait()
            own_out.start()

    def widened(begin):
        return tokens_ref[0, :, pl.ds(begin, lanes)].astype(jnp.float32)

    total = jnp.zeros((rows, lanes), jnp.float32)
    for begin in range(0, width, lanes):
        total += widened(begin)
    mean = jnp.sum(total, axis=-1, keepdims=True) / width
    total = jnp.zeros((rows, lanes), jnp.float32)
    for begin in range(0, width, lanes):
        centered = widened(begin) - mean
        total += centered * centered
    scale = lax.rsqrt(jnp.sum(total, axis=-1, keepdims=True) / width + 1e-06)
    for i in range(4):
        source = place_ref[i + 1] * slab
        for begin in range(0, slab, lanes):
            column = pl.multiple_of(source + begin, lanes)
            part = (widened(column) - mean) * scale * gain_ref[:, pl.ds(column, lanes)]
            target = i * slab % span + begin
            normed_refs[i * slab // span][:, target : target + lanes] = part.astype(jnp.bfloat16)

    if rest:

        @pl.when(step == steps - 1)
        def _():
            own_out.wait()


def normalize_part(tokens, ln_gain, weight, part, core, order, head=None):
    width = tokens.shape[2]
    piece = weight.shape[1:]
    step = 64 if part % 64 == 0 else 32
    steps = part // step
    place = [core, *order] + ([] if head is None else [head])
    place = jnp.stack([jnp.asarray(v, jnp.int32) for v in place])
    half = jax.ShapeDtypeStruct((part, width // 2), jnp.bfloat16)
    anywhere = pl.BlockSpec(memory_space=pl.ANY)
    got = pl.pallas_call(
        normalize_kernel,
        out_shape=[half] * 2 + [jax.ShapeDtypeStruct(piece, jnp.bfloat16)] * (head is not None),
        grid_spec=pltpu.PrefetchScalarGridSpec(
            num_scalar_prefetch=1,
            grid=(steps,),
            in_specs=[
                pl.BlockSpec((1, step, width), lambda i, place: (0, place[0] * steps + i, 0)),
                pl.BlockSpec((1, width), lambda i, place: (0, 0)),
                anywhere,
            ],
            out_specs=[pl.BlockSpec((step, width // 2), lambda i, place: (i, 0))] * 2
            + [anywhere] * (head is not None),
            scratch_shapes=[pltpu.VMEM(piece, jnp.bfloat16), pltpu.SemaphoreType.DMA((2,))]
            if head is not None
            else [],
        ),
        compiler_params=pltpu.CompilerParams(vmem_limit_bytes=62 << 20),
        cost_estimate=pl.CostEstimate(
            flops=8 * part * width, bytes_accessed=4 * part * width, transcendentals=part
        ),
    )(place, tokens, ln_gain[None], weight)
    return got[:2], got[2:]


def attend_rows(projected_ref, parts, column):
    width = projected_ref.shape[1] // 3
    key_rows = projected_ref[:, width : 2 * width]
    value_rows = projected_ref[:, 2 * width :]
    value_rows = jnp.concatenate([value_rows, jnp.ones_like(value_rows)], axis=1)
    begin = 0
    for part in parts:
        step = part.shape[0]
        queries = projected_ref[begin : begin + step, :width]
        scores = lax.dot_general(
            queries, key_rows, (((1,), (1,)), ((), ())), preferred_element_type=jnp.float32
        )
        highest = jnp.max(scores, axis=-1, keepdims=True)
        expo = jnp.exp2((scores - highest) * (math.log2(math.e) / math.sqrt(width)))
        mixed = jnp.dot(expo.astype(jnp.bfloat16), value_rows, preferred_element_type=jnp.float32)
        mixed = mixed[:, :width] / mixed[:, width:]
        part[:, column : column + width] = mixed.astype(jnp.bfloat16)
        begin += step


class Jobs:
    def __init__(self, **numbers):
        self.__dict__.update(numbers)

    def jobs(self, image):
        return sorted({j for use in self.uses[image] if use for j in range(*use)})


def job_kernel(plan, role_ref, *refs):
    refs = list(refs)
    take = lambda n: [refs.pop(0) for _ in range(n)]
    images, ns = range(len(plan.uses)), range(len(plan.slots))
    pieces = [[[take(2) for _ in place] for place in image] for image in plan.origins]
    weights = [[take(1) * 2 if alike else take(2) for alike in row] for row in plan.same]
    partials = [{j: take(1)[0] for j in plan.added[i]} for i in images]
    carried = [[take(plan.carried[i]) for _ in range(2)] for i in images]
    outs = [
        {j: take(2) if j in plan.finished[i] else take(1)[0] for j in plan.jobs(i)} for i in images
    ]
    features_ref, weight_ref, total_ref, projected_ref = take(4)
    token_sems, weight_sems, sum_sems, out_sems, carry_sems = take(5)
    core, inner = role_ref[0], role_ref[1]
    slab = pieces[0][0][0][0].shape[1] // 2
    tokens, wide = projected_ref.shape
    part = tokens // 4

    def features(i, n):
        return features_ref.at[pl.ds(i * tokens, tokens), pl.ds(n * slab, slab)]

    def weight(n, j):
        return weight_ref.at[pl.ds(n * slab, slab), pl.ds(j * wide, wide)]

    def total(i, j):
        return total_ref.at[pl.ds(i * tokens, tokens), pl.ds(j * wide, wide)]

    def start_tokens(i, n):
        cut, begin = plan.slots[n] // 2, plan.slots[n] % 2 * slab
        for place in range(2):
            split = len(plan.origins[i][place])
            for owner in range(split):
                row = i * tokens + 2 * place * part
                if split == 2:
                    row += (1 - core if owner else core) * part
                count = 2 * part // split
                from_rows = pl.ds(plan.origins[i][place][owner][cut], count)
                rows = pl.ds(pl.multiple_of(row, 32), count)
                pltpu.make_async_copy(
                    pieces[i][place][owner][cut].at[from_rows, pl.ds(begin, slab)],
                    features_ref.at[rows, pl.ds(n * slab, slab)],
                    token_sems.at[i, n],
                ).start()

    def start_weight(n, j, role):
        source = weights[n][j - plan.first[n]][role]
        if source.shape[0] == slab:
            pltpu.make_async_copy(source, weight(n, j), weight_sems.at[n, j]).start()
            return
        for b in range(source.shape[1] // wide):
            pltpu.make_async_copy(
                source.at[:, pl.ds(b * wide, wide)],
                weight_ref.at[pl.ds(n * slab + b * part, part), pl.ds(j * wide, wide)],
                weight_sems.at[n, j],
            ).start()

    def start_role_weight(n, j):
        if plan.same[n][j - plan.first[n]]:
            start_weight(n, j, 0)
            return

        @pl.when(inner == 1)
        def _():
            start_weight(n, j, 0)

        @pl.when(inner != 1)
        def _():
            start_weight(n, j, 1)

    def partial_copy(i, j):
        return pltpu.make_async_copy(partials[i][j], total(i, j), sum_sems.at[i, j])

    def out_copy(i, j):
        return pltpu.make_async_copy(total(i, j), outs[i][j], out_sems.at[i, j])

    def carry_copies():
        for i in images:
            for place in range(2):
                for k in range(plan.carried[i]):
                    (finished,) = plan.finished[i]
                    target = outs[i][finished][place].at[:, pl.ds(k * wide // 3, wide // 3)]
                    yield pltpu.make_async_copy(
                        carried[i][place][k], target, carry_sems.at[i, place, k]
                    )

    stages = [(i, n) for i in images for n in ns if plan.uses[i][n]]
    held = set()

    def start_stage(i, n):
        start_tokens(i, n)
        for j in range(*plan.uses[i][n]):
            if (n, j) not in held:
                held.add((n, j))
                start_role_weight(n, j)
        if not any((i, n) > (i, m) and plan.uses[i][m] for m in ns):
            for j in plan.added[i]:
                partial_copy(i, j).start()

    ahead = 2
    for stage in stages[:ahead]:
        start_stage(*stage)
    for copy in carry_copies():
        copy.start()
    ready = set()
    for index, (i, n) in enumerate(stages):
        low, high = plan.uses[i][n]
        pltpu.make_async_copy(features(i, n), features(i, n), token_sems.at[i, n]).wait()
        for j in range(low, high):
            if (n, j) not in ready:
                ready.add((n, j))
                pltpu.make_async_copy(weight(n, j), weight(n, j), weight_sems.at[n, j]).wait()
        if index + ahead < len(stages):
            start_stage(*stages[index + ahead])
        term = jnp.dot(
            features(i, n)[...],
            weight_ref[n * slab : (n + 1) * slab, low * wide : high * wide],
            preferred_element_type=jnp.float32,
        )
        for j in range(low, high):
            value = term[:, (j - low) * wide : (j - low + 1) * wide]
            mine = [m for m in ns if plan.uses[i][m] and j in range(*plan.uses[i][m])]
            if n == mine[0] and j in plan.added[i]:
                partial_copy(i, j).wait()
            if n != mine[0] or j in plan.added[i]:
                value += total(i, j)[...]
            if n == mine[-1] and j in plan.finished[i]:
                projected_ref[...] = value.astype(jnp.bfloat16)
                attend_rows(projected_ref, outs[i][j], plan.carried[i] * wide // 3)
                continue
            total(i, j)[...] = value
            if n == mine[-1]:
                out_copy(i, j).start()
    for copy in carry_copies():
        copy.wait()
    for i in images:
        for j in plan.jobs(i):
            if j not in plan.finished[i]:
                out_copy(i, j).wait()


def run_jobs(core, inner, tokens, wide, images, weights):
    images = [
        dict(
            image,
            pieces=[
                [[x if isinstance(x, tuple) else (x, 0) for x in owner] for owner in place]
                for place in image["pieces"]
            ],
            sums=image.get("sums", {}),
            finish=image.get("finish", ()),
            carry=image.get("carry", ((), ())),
        )
        for image in images
    ]
    plan = Jobs(
        origins=[[[[r for _, r in o] for o in p] for p in image["pieces"]] for image in images],
        slots=[slot for slot, _, _ in weights],
        first=[first for _, first, _ in weights],
        same=[[not isinstance(w, tuple) for w in row] for _, _, row in weights],
        uses=[image["uses"] for image in images],
        added=[tuple(image["sums"]) for image in images],
        finished=[image["finish"] for image in images],
        carried=[len(image["carry"][0]) for image in images],
    )
    operands = [x for i in images for place in i["pieces"] for owner in place for x, _ in owner]
    slab = operands[0].shape[1] // 2
    for _, _, row in weights:
        for w in row:
            operands += list(w) if isinstance(w, tuple) else [w]
    operands += [x for image in images for x in image["sums"].values()]
    operands += [x for image in images for place in image["carry"] for x in place]
    anywhere, vmem = pl.BlockSpec(memory_space=pl.ANY), pl.BlockSpec(memory_space=pltpu.VMEM)
    head = wide // 3
    shapes, specs = [], []
    for i in range(len(images)):
        for j in plan.jobs(i):
            if j in plan.finished[i]:
                shape = (tokens // 2, head * (plan.carried[i] + 1))
                shapes += [jax.ShapeDtypeStruct(shape, jnp.bfloat16)] * 2
                specs += [vmem] * 2
            else:
                shapes.append(jax.ShapeDtypeStruct((tokens, wide), jnp.float32))
                specs.append(anywhere)
    jobs = 1 + max(j for i in range(len(images)) for j in plan.jobs(i))
    count, depth, total = len(images), len(weights) * slab, len(images) * tokens
    added = sum(high - low for uses in plan.uses for low, high in filter(None, uses))
    got = pl.pallas_call(
        functools.partial(job_kernel, plan),
        out_shape=shapes,
        in_specs=[pl.BlockSpec(memory_space=pltpu.SMEM)] + [anywhere] * len(operands),
        out_specs=specs,
        scratch_shapes=[
            pltpu.VMEM((total, depth), jnp.bfloat16),
            pltpu.VMEM((depth, jobs * wide), jnp.bfloat16),
            pltpu.VMEM((total, jobs * wide), jnp.float32),
            pltpu.VMEM((tokens, wide), jnp.bfloat16),
            pltpu.SemaphoreType.DMA((count, len(weights))),
            pltpu.SemaphoreType.DMA((len(weights), jobs)),
            pltpu.SemaphoreType.DMA((count, jobs)),
            pltpu.SemaphoreType.DMA((count, jobs)),
            pltpu.SemaphoreType.DMA((count, 2, max(*plan.carried, 1))),
        ],
        compiler_params=pltpu.CompilerParams(vmem_limit_bytes=62 << 20),
        cost_estimate=pl.CostEstimate(
            flops=2 * tokens * slab * wide * added, bytes_accessed=0, transcendentals=0
        ),
    )(jnp.stack([core, inner]).astype(jnp.int32), *operands)
    got = list(got)
    return [
        {
            j: (got.pop(0), got.pop(0)) if j in plan.finished[i] else got.pop(0)
            for j in plan.jobs(i)
        }
        for i in range(count)
    ]


def join_kernel(place_ref, *refs):
    *parts, out_ref, sems = refs
    count = len(parts) // 2
    inner = place_ref[count]
    wide, head = parts[0].shape[1], parts[count].shape[1]

    def copies(i, role):
        begin = pl.multiple_of(place_ref[i] * wide, wide)
        if role:
            yield parts[i], out_ref.at[:, pl.ds(begin, wide)], sems.at[i, 0]
            return
        kept = wide - head
        yield parts[i].at[:, pl.ds(head, kept)], out_ref.at[:, pl.ds(begin, kept)], sems.at[i, 0]
        last = pl.multiple_of(begin + kept, head)
        yield parts[count + i], out_ref.at[:, pl.ds(last, head)], sems.at[i, 1]

    for role in (1, 0):

        @pl.when((inner == 1) == (role == 1))
        def _():
            every = [pltpu.make_async_copy(*c) for i in range(count) for c in copies(i, role)]
            for copy in every:
                copy.start()
            for copy in every:
                copy.wait()


def join(places, inner, parts, back):
    rows, wide = parts[0].shape
    anywhere = pl.BlockSpec(memory_space=pl.ANY)
    return pl.pallas_call(
        join_kernel,
        out_shape=jax.ShapeDtypeStruct((rows, wide * len(parts)), jnp.bfloat16),
        in_specs=[pl.BlockSpec(memory_space=pltpu.SMEM)] + [anywhere] * (2 * len(parts)),
        out_specs=pl.BlockSpec(memory_space=pltpu.VMEM),
        scratch_shapes=[pltpu.SemaphoreType.DMA((len(parts), 2))],
        cost_estimate=pl.CostEstimate(
            flops=0, bytes_accessed=4 * rows * wide * len(parts), transcendentals=0
        ),
    )(jnp.stack([*places, inner]).astype(jnp.int32), *parts, *back)


def shared(tokens, ln_gain, qkv_weight):
    groups, planes, seqs, cores = (lax.axis_size(a) for a in ("groups", "dp", "seq", "head"))
    group, plane, seq, core = (lax.axis_index(a) for a in ("groups", "dp", "seq", "head"))
    _, rows, _ = tokens.shape
    slab, heads, columns = qkv_weight.shape
    heads, part = heads // groups, rows // cores
    inner = (plane == 1) | (plane == 2)
    wait = lax.optimization_barrier

    def fold(piece):
        piece = piece.reshape(-1, part, columns).transpose(1, 0, 2)
        return piece.reshape(part, -1)

    def pick(for_inner, for_ends):
        return jnp.where(inner, for_inner, for_ends)

    def pair(value):
        return lax.ppermute(value, "dp", [(0, 1), (1, 0), (2, 3), (3, 2)])

    def outward(value):
        return lax.ppermute(value, "dp", [(1, 0), (2, 3)])

    def middle(value):
        return lax.ppermute(value, "dp", [(1, 2), (2, 1)])

    swap = [(0, 1), (1, 0)]
    beside = lambda value: lax.ppermute(value, "seq", swap)
    across = lambda value: lax.ppermute(value, "groups", swap)

    def others(*values):
        got = []
        for value in values:
            if got:
                value, got[-1] = wait((value, got[-1]))
            got.append(lax.ppermute(value, "head", swap))
        return got

    run = functools.partial(run_jobs, core, inner, seqs * rows, columns)

    def exchange(mixed):
        got = []
        for a in range(groups):
            for b in range(seqs):
                sent = mixed[a * seqs + b]
                if a or b:
                    steps = [
                        (g * seqs + s, (g + a) % groups * seqs + (s + b) % seqs)
                        for g in range(groups)
                        for s in range(seqs)
                    ]
                    sent = lax.ppermute(sent, ("groups", "seq"), steps)
                got.append(sent)
        return got

    weight = qkv_weight.transpose(1, 0, 2)
    order = slab_order(plane)
    normed, (own0,) = normalize_part(
        tokens, ln_gain, weight, part, core, order, group * heads
    )
    normed, own0, later_weight = wait((normed, own0, weight))
    cut0, cut1 = normed
    pair1, middle1 = pair(own0), middle(own0)
    beside1, across1 = beside(cut0), across(cut0)
    own1, own2 = [
        lax.dynamic_index_in_dim(later_weight, group * heads + j, 0, keepdims=False) for j in (1, 2)
    ]
    give = pick(fold(own1), cut0)
    pair1, middle1, beside1, across1, own1, own2, cut0, cut1, tokens, give = wait(
        (pair1, middle1, beside1, across1, own1, own2, cut0, cut1, tokens, give)
    )

    pair2, middle2 = pair(give), middle(pair1)
    beside2, across2 = beside(cut1), across(cut1)
    give = pick(fold(middle1), cut1)
    far_normed, _ = normalize_part(tokens, ln_gain, weight, part, 1 - core, order)
    far1 = others(beside1, across1)
    pair2, middle2, beside2, across2, across1, own1, own2, far_normed, far1, give = wait(
        (pair2, middle2, beside2, across2, across1, own1, own2, far_normed, far1, give)
    )

    pair3, middle3 = pair(give), middle(own1)
    beside3, across3 = beside(across1), across(beside2)
    give = pick(middle2, own1)
    far2 = others(beside2, across2)
    pair3, middle3, beside3, across3, pair1, pair2, own2, far2, give = wait(
        (pair3, middle3, beside3, across3, pair1, pair2, own2, far2, give)
    )

    pair4, middle4 = pair(give), middle(own2)
    beside4, across4 = beside(pair2), across(pair2)
    give = pick(middle3, own2)
    pieces0 = ((normed, far_normed), ((beside1, beside2), (far1[0], far2[0])))
    owns = [own0, (own1, own0), (own2, own1)]
    ((head0, sum20, sum30),) = [
        tuple(got.values())
        for got in run(
            [dict(pieces=pieces0, uses=[(0, 3), (0, 2), (0, 1), (0, 1)], finish=(0,))],
            [(0, 0, owns), (2, 0, [middle1, (middle3, pair1)]), (1, 0, [pair1]), (3, 0, [middle2])],
        )
    ]
    far3 = others(beside3, across3)
    lent = jnp.concatenate([pair2, pair3])
    pair4, middle4, beside4, across4, own2, pair3, lent, head0, sum20, sum30, far3, give = wait(
        (pair4, middle4, beside4, across4, own2, pair3, lent, head0, sum20, sum30, far3, give)
    )

    pair5, middle5 = pair(give), middle(pair4)
    beside5, across5 = beside(pair3), across(pair3)
    pieces1 = (((across1, across2), (far1[1], far2[1])), ((beside3, across3), far3))
    image1, image0 = run(
        [
            dict(pieces=pieces1, uses=[(0, 3), (0, 3), (0, 2), (0, 1)], finish=(0,)),
            dict(pieces=pieces0, uses=[None, (2, 3), (1, 2), None], sums={1: sum20, 2: sum30}),
        ],
        [
            (0, 0, owns),
            (2, 0, [middle1, (middle3, pair1), (middle4, pair2)]),
            (1, 0, [pair1, (pair4, pair3)]),
            (3, 0, [middle2]),
        ],
    )
    far_lent, far4 = others(lent, beside4)
    pair5, middle5, beside5, across5, across4, image0, image1, far_lent, far4 = wait(
        (
            *(pair5, middle5, beside5, across5, across4),
            *(image0, image1, far_lent, far4),
        )
    )

    pair6, middle6 = outward(middle5), middle(pair5)
    beside6, across6 = beside(across4), across(beside5)
    far5, far_across4 = others(beside5, across4)
    ahead0, ahead1 = run(
        [
            dict(
                pieces=pieces,
                uses=[(0, 1), (1, 2)],
                sums={0: image[1], 1: image[2]},
                finish=(0,),
            )
            for pieces, image in ((pieces0, image0), (pieces1, image1))
        ],
        [(3, 0, [(middle5, pair4)]), (1, 1, [pair5])],
    )
    lent0 = (((pair2, pair3), (far_lent, (far_lent, part))), ((beside4, beside5), (far4, far5)))
    lent_weights = [(0, 0, [pair5]), (1, 0, [middle4]), (2, 0, [own2])]
    ((sum4,),) = [
        tuple(got.values()) for got in run([dict(pieces=lent0, uses=[(0, 1)] * 3)], lent_weights)
    ]
    pair6, middle6, beside6, across6, across5, ahead0, ahead1, sum4, far_across4 = wait(
        (pair6, middle6, beside6, across6, across5, ahead0, ahead1, sum4, far_across4)
    )

    far_across5, *far6 = [
        lax.ppermute(value, "head", swap) for value in (across5, beside6, across6)
    ]
    done0, done1, lent0 = run(
        [
            dict(pieces=p, uses=[(0, 1)], sums={0: x[1]}, finish=(0,), carry=tuple(zip(h, x[0])))
            for p, h, x in ((pieces0, head0, ahead0), (pieces1, image1[0], ahead1))
        ]
        + [dict(pieces=lent0, uses=[(0, 1)], sums={0: sum4}, finish=(0,))],
        [(3, 0, [(middle6, pair6)])],
    )
    lent1 = (((across4, across5), (far_across4, far_across5)), ((beside6, across6), far6))
    (lent1,) = run(
        [dict(pieces=lent1, uses=[(0, 1)] * 4, finish=(0,))], [*lent_weights, (3, 0, [middle6])]
    )

    def hand_back(mixed):
        got = []
        for a in range(groups):
            for b in range(seqs):
                steps = [
                    (
                        (g * planes + z) * seqs + s,
                        ((g + a) % groups * planes + (z ^ 1)) * seqs + (s + b) % seqs,
                    )
                    for g in range(groups)
                    for z in (1, 2)
                    for s in range(seqs)
                ]
                sent = mixed[a * seqs + b]
                got.append(lax.ppermute(sent, ("groups", "dp", "seq"), steps))
        return got

    sent = exchange((*done0[0], *done1[0]))
    back = hand_back((*lent0[0], *lent1[0]))
    places = [
        (seq - b) % seqs * groups + (group - a) % groups
        for a in range(groups)
        for b in range(seqs)
    ]
    return join(places, inner, sent, back)[None]


def per_device(tokens, ln_gain, qkv_weight):
    groups, planes, seqs, cores = (lax.axis_size(a) for a in ("groups", "dp", "seq", "head"))
    images, rows, width = tokens.shape
    slab, heads, _ = qkv_weight.shape
    if (groups, planes, seqs, cores) == (2, 4, 2, 2) and images == 1 and heads == 3 * groups:
        part = rows // cores
        if rows % (32 * cores) == 0 and slab % part == 0 and 2 * slab == qkv_weight.shape[2] * slab // part:
            return shared(tokens, ln_gain, qkv_weight)
    return plain(tokens, ln_gain, qkv_weight)


def solution(mesh):
    return jax.shard_map(
        per_device,
        mesh=mesh,
        in_specs=(P(("groups", "dp"), "seq", None), P(), P("dp", ("seq", "head"), None)),
        out_specs=P(("groups", "dp"), "seq", "head"),
        check_vma=False,
    )
```

```python
import functools
import math

import jax
import jax.numpy as jnp
from jax import lax
from jax.experimental import pallas as pl
from jax.experimental.pallas import tpu as pltpu
from jax.sharding import PartitionSpec as P


def normalize(array, gain):
    widened = array.astype(jnp.float32)
    centered = widened - jnp.mean(widened, axis=-1, keepdims=True)
    variance = jnp.mean(centered * centered, axis=-1, keepdims=True)
    return (centered * lax.rsqrt(variance + 1e-06) * gain).astype(jnp.bfloat16)


def attend(projected):
    width = projected.shape[2] // 3
    queries = projected[:, :, :width]
    key_rows = projected[:, :, width : 2 * width]
    value_rows = projected[:, :, 2 * width :]
    scores = jnp.einsum("qhd,khd->hqk", queries, key_rows, preferred_element_type=jnp.float32) * (
        1.0 / math.sqrt(width)
    )
    highest = jnp.max(scores, axis=-1, keepdims=True)
    expo = jnp.exp(scores - highest)
    probs = (expo / jnp.sum(expo, axis=-1, keepdims=True)).astype(jnp.bfloat16)
    mixed = jnp.einsum("hqk,khd->qhd", probs, value_rows, preferred_element_type=jnp.float32)
    return mixed.astype(jnp.bfloat16).reshape(projected.shape[0], -1)


def plain(tokens, ln_gain, qkv_weight):
    images = tokens.shape[0]
    width = tokens.shape[2]
    heads_here = qkv_weight.shape[1]
    columns = heads_here * qkv_weight.shape[2]
    source = normalize(tokens, ln_gain)
    half_width = width // lax.axis_size("head")
    core_index = lax.axis_index("head")
    own_half = lax.dynamic_slice_in_dim(source, core_index * half_width, half_width, 2)
    fetched = lax.all_gather(own_half, "seq", axis=1, tiled=True)
    gathered = lax.all_gather(fetched, "head", axis=2, tiled=True)
    full_tokens = gathered.shape[1]
    features = gathered.reshape(images * full_tokens, width)
    piece = lax.all_gather(qkv_weight, "dp", axis=0, tiled=True)
    projected = jnp.dot(
        features, piece.reshape(piece.shape[0], columns), preferred_element_type=jnp.float32
    )
    projected = projected.astype(jnp.bfloat16).reshape(
        images, full_tokens, heads_here, qkv_weight.shape[2]
    )
    mixed = lax.map(attend, projected)
    return lax.all_to_all(mixed, "seq", split_axis=1, concat_axis=2, tiled=True)


def slab_order(plane):
    inner = (plane == 1) | (plane == 2)
    near, far = plane ^ 1, 2 - plane // 2
    return plane, jnp.where(inner, near, far), jnp.where(inner, far, near), 3 - 3 * (plane // 2)


def normalize_kernel(place_ref, tokens_ref, gain_ref, weight_ref, *refs):
    normed_refs, rest = refs[:2], refs[2:]
    rows, width = tokens_ref.shape[1:]
    lanes = 128
    slab, span = width // 4, width // 2
    step, steps = pl.program_id(0), pl.num_programs(0)
    if rest:
        own_ref, folded_ref, own_buf, own_sems = rest
        own_in = pltpu.make_async_copy(weight_ref.at[place_ref[5]], own_buf, own_sems.at[0])
        part, columns = folded_ref.shape[0], own_ref.shape[1]
        own_out = [pltpu.make_async_copy(own_buf, own_ref, own_sems.at[1])] + [
            pltpu.make_async_copy(
                own_buf.at[pl.ds(b * part, part)],
                folded_ref.at[:, pl.ds(b * columns, columns)],
                own_sems.at[2 + b],
            )
            for b in range(own_ref.shape[0] // part)
        ]

        @pl.when(step == 0)
        def _():
            own_in.start()

        @pl.when(step == 1)
        def _():
            own_in.wait()
            for copy in own_out:
                copy.start()

    def widened(begin):
        return tokens_ref[0, :, pl.ds(begin, lanes)].astype(jnp.float32)

    total = jnp.zeros((rows, lanes), jnp.float32)
    for begin in range(0, width, lanes):
        total += widened(begin)
    mean = jnp.sum(total, axis=-1, keepdims=True) / width
    total = jnp.zeros((rows, lanes), jnp.float32)
    for begin in range(0, width, lanes):
        centered = widened(begin) - mean
        total += centered * centered
    scale = lax.rsqrt(jnp.sum(total, axis=-1, keepdims=True) / width + 1e-06)
    for i in range(4):
        source = place_ref[i + 1] * slab
        for begin in range(0, slab, lanes):
            column = pl.multiple_of(source + begin, lanes)
            part = (widened(column) - mean) * scale * gain_ref[:, pl.ds(column, lanes)]
            target = i * slab % span + begin
            normed_refs[i * slab // span][:, target : target + lanes] = part.astype(jnp.bfloat16)

    if rest:

        @pl.when(step == steps - 1)
        def _():
            for copy in own_out:
                copy.wait()


def normalize_part(tokens, ln_gain, weight, part, core, order, head=None):
    width = tokens.shape[2]
    piece = weight.shape[1:]
    step = 64 if part % 64 == 0 else 32
    steps = part // step
    place = [core, *order] + ([] if head is None else [head])
    place = jnp.stack([jnp.asarray(v, jnp.int32) for v in place])
    half = jax.ShapeDtypeStruct((part, width // 2), jnp.bfloat16)
    anywhere = pl.BlockSpec(memory_space=pl.ANY)
    with_weight = [] if head is None else [jax.ShapeDtypeStruct(piece, jnp.bfloat16), half]
    got = pl.pallas_call(
        normalize_kernel,
        out_shape=[half] * 2 + with_weight,
        grid_spec=pltpu.PrefetchScalarGridSpec(
            num_scalar_prefetch=1,
            grid=(steps,),
            in_specs=[
                pl.BlockSpec((1, step, width), lambda i, place: (0, place[0] * steps + i, 0)),
                pl.BlockSpec((1, width), lambda i, place: (0, 0)),
                anywhere,
            ],
            out_specs=[pl.BlockSpec((step, width // 2), lambda i, place: (i, 0))] * 2
            + [anywhere] * len(with_weight),
            scratch_shapes=[
                pltpu.VMEM(piece, jnp.bfloat16),
                pltpu.SemaphoreType.DMA((2 + piece[0] // part,)),
            ]
            if head is not None
            else [],
        ),
        compiler_params=pltpu.CompilerParams(vmem_limit_bytes=62 << 20),
        cost_estimate=pl.CostEstimate(
            flops=8 * part * width, bytes_accessed=4 * part * width, transcendentals=part
        ),
    )(place, tokens, ln_gain[None], weight)
    return got[:2], got[2:]


def attend_rows(projected_ref, parts, column):
    width = projected_ref.shape[1] // 3
    key_rows = projected_ref[:, width : 2 * width]
    value_rows = projected_ref[:, 2 * width :]
    value_rows = jnp.concatenate([value_rows, jnp.ones_like(value_rows)], axis=1)
    begin = 0
    for part in parts:
        step = part.shape[0]
        queries = projected_ref[begin : begin + step, :width]
        scores = lax.dot_general(
            queries, key_rows, (((1,), (1,)), ((), ())), preferred_element_type=jnp.float32
        )
        highest = jnp.max(scores, axis=-1, keepdims=True)
        expo = jnp.exp2((scores - highest) * (math.log2(math.e) / math.sqrt(width)))
        mixed = jnp.dot(expo.astype(jnp.bfloat16), value_rows, preferred_element_type=jnp.float32)
        mixed = mixed[:, :width] / mixed[:, width:]
        part[:, column : column + width] = mixed.astype(jnp.bfloat16)
        begin += step


class Jobs:
    def __init__(self, **numbers):
        self.__dict__.update(numbers)

    def jobs(self, image):
        return sorted({j for use in self.uses[image] if use for j in range(*use)})


def job_kernel(plan, role_ref, *refs):
    refs = list(refs)
    take = lambda n: [refs.pop(0) for _ in range(n)]
    images, ns = range(len(plan.uses)), range(len(plan.slots))
    pieces = [[[take(2) for _ in place] for place in image] for image in plan.origins]
    weights = [[take(1) * 2 if alike else take(2) for alike in row] for row in plan.same]
    partials = [{j: take(1)[0] for j in plan.added[i]} for i in images]
    carried = [[take(plan.carried[i]) for _ in range(2)] for i in images]
    outs = [
        {j: take(2) if j in plan.finished[i] else take(1)[0] for j in plan.jobs(i)} for i in images
    ]
    features_ref, weight_ref, total_ref, projected_ref = take(4)
    token_sems, weight_sems, sum_sems, out_sems, carry_sems = take(5)
    core, inner = role_ref[0], role_ref[1]
    slab = pieces[0][0][0][0].shape[1] // 2
    tokens, wide = projected_ref.shape[1:]
    part = tokens // 4

    def features(i, n):
        return features_ref.at[pl.ds(i * tokens, tokens), pl.ds(n * slab, slab)]

    def weight(n, j):
        return weight_ref.at[pl.ds(n * slab, slab), pl.ds(j * wide, wide)]

    def total(i, j):
        return total_ref.at[pl.ds(i * tokens, tokens), pl.ds(j * wide, wide)]

    def start_tokens(i, n):
        cut, begin = plan.slots[n] // 2, plan.slots[n] % 2 * slab
        for place in range(2):
            split = len(plan.origins[i][place])
            for owner in range(split):
                row = i * tokens + 2 * place * part
                if split == 2:
                    row += (1 - core if owner else core) * part
                count = 2 * part // split
                from_rows = pl.ds(plan.origins[i][place][owner][cut], count)
                rows = pl.ds(pl.multiple_of(row, 32), count)
                pltpu.make_async_copy(
                    pieces[i][place][owner][cut].at[from_rows, pl.ds(begin, slab)],
                    features_ref.at[rows, pl.ds(n * slab, slab)],
                    token_sems.at[i, n],
                ).start()

    def start_weight(n, j, role):
        source = weights[n][j - plan.first[n]][role]
        if source.shape[0] == slab:
            pltpu.make_async_copy(source, weight(n, j), weight_sems.at[n, j]).start()
            return
        for b in range(source.shape[1] // wide):
            pltpu.make_async_copy(
                source.at[:, pl.ds(b * wide, wide)],
                weight_ref.at[pl.ds(n * slab + b * part, part), pl.ds(j * wide, wide)],
                weight_sems.at[n, j],
            ).start()

    def start_role_weight(n, j):
        if plan.same[n][j - plan.first[n]]:
            start_weight(n, j, 0)
            return

        @pl.when(inner == 1)
        def _():
            start_weight(n, j, 0)

        @pl.when(inner != 1)
        def _():
            start_weight(n, j, 1)

    def partial_copy(i, j):
        return pltpu.make_async_copy(partials[i][j], total(i, j), sum_sems.at[i, j])

    def out_copy(i, j):
        return pltpu.make_async_copy(total(i, j), outs[i][j], out_sems.at[i, j])

    def carry_copies():
        for i in images:
            for place in range(2):
                for k in range(plan.carried[i]):
                    (finished,) = plan.finished[i]
                    target = outs[i][finished][place].at[:, pl.ds(k * wide // 3, wide // 3)]
                    yield pltpu.make_async_copy(
                        carried[i][place][k], target, carry_sems.at[i, place, k]
                    )

    stages = [(i, n) for i in images for n in ns if plan.uses[i][n]]
    held = set()

    def start_stage(i, n):
        start_tokens(i, n)
        for j in range(*plan.uses[i][n]):
            if (n, j) not in held:
                held.add((n, j))
                start_role_weight(n, j)
        if not any((i, n) > (i, m) and plan.uses[i][m] for m in ns):
            for j in plan.added[i]:
                partial_copy(i, j).start()

    ahead = 2
    for stage in stages[:ahead]:
        start_stage(*stage)
    for copy in carry_copies():
        copy.start()
    ready, waiting = set(), []
    for index, (i, n) in enumerate(stages):
        low, high = plan.uses[i][n]
        pltpu.make_async_copy(features(i, n), features(i, n), token_sems.at[i, n]).wait()
        for j in range(low, high):
            if (n, j) not in ready:
                ready.add((n, j))
                pltpu.make_async_copy(weight(n, j), weight(n, j), weight_sems.at[n, j]).wait()
        if index + ahead < len(stages):
            start_stage(*stages[index + ahead])
        term = jnp.dot(
            features(i, n)[...],
            weight_ref[n * slab : (n + 1) * slab, low * wide : high * wide],
            preferred_element_type=jnp.float32,
        )
        for j in range(low, high):
            value = term[:, (j - low) * wide : (j - low + 1) * wide]
            mine = [m for m in ns if plan.uses[i][m] and j in range(*plan.uses[i][m])]
            if n == mine[0] and j in plan.added[i]:
                partial_copy(i, j).wait()
            if n != mine[0] or j in plan.added[i]:
                value += total(i, j)[...]
            if n == mine[-1] and j in plan.finished[i]:
                projected_ref[i % 2] = value.astype(jnp.bfloat16)
                if waiting:
                    attend_rows(*waiting.pop())
                column = plan.carried[i] * wide // 3
                waiting.append((projected_ref.at[i % 2], outs[i][j], column))
                continue
            total(i, j)[...] = value
            if n == mine[-1]:
                out_copy(i, j).start()
    if waiting:
        attend_rows(*waiting.pop())
    for copy in carry_copies():
        copy.wait()
    for i in images:
        for j in plan.jobs(i):
            if j not in plan.finished[i]:
                out_copy(i, j).wait()


def run_jobs(role, tokens, wide, images, weights):
    images = [
        dict(
            image,
            pieces=[
                [[x if isinstance(x, tuple) else (x, 0) for x in owner] for owner in place]
                for place in image["pieces"]
            ],
            sums=image.get("sums", {}),
            finish=image.get("finish", ()),
            carry=image.get("carry", ((), ())),
        )
        for image in images
    ]
    plan = Jobs(
        origins=[[[[r for _, r in o] for o in p] for p in image["pieces"]] for image in images],
        slots=[slot for slot, _, _ in weights],
        first=[first for _, first, _ in weights],
        same=[[not isinstance(w, tuple) for w in row] for _, _, row in weights],
        uses=[image["uses"] for image in images],
        added=[tuple(image["sums"]) for image in images],
        finished=[image["finish"] for image in images],
        carried=[len(image["carry"][0]) for image in images],
    )
    operands = [x for i in images for place in i["pieces"] for owner in place for x, _ in owner]
    slab = operands[0].shape[1] // 2
    for _, _, row in weights:
        for w in row:
            operands += list(w) if isinstance(w, tuple) else [w]
    operands += [x for image in images for x in image["sums"].values()]
    operands += [x for image in images for place in image["carry"] for x in place]
    anywhere, vmem = pl.BlockSpec(memory_space=pl.ANY), pl.BlockSpec(memory_space=pltpu.VMEM)
    head = wide // 3
    shapes, specs = [], []
    for i in range(len(images)):
        for j in plan.jobs(i):
            if j in plan.finished[i]:
                shape = (tokens // 2, head * (plan.carried[i] + 1))
                shapes += [jax.ShapeDtypeStruct(shape, jnp.bfloat16)] * 2
                specs += [vmem] * 2
            else:
                shapes.append(jax.ShapeDtypeStruct((tokens, wide), jnp.float32))
                specs.append(anywhere)
    jobs = 1 + max(j for i in range(len(images)) for j in plan.jobs(i))
    count, depth, total = len(images), len(weights) * slab, len(images) * tokens
    added = sum(high - low for uses in plan.uses for low, high in filter(None, uses))
    got = pl.pallas_call(
        functools.partial(job_kernel, plan),
        out_shape=shapes,
        in_specs=[pl.BlockSpec(memory_space=pltpu.SMEM)] + [anywhere] * len(operands),
        out_specs=specs,
        scratch_shapes=[
            pltpu.VMEM((total, depth), jnp.bfloat16),
            pltpu.VMEM((depth, jobs * wide), jnp.bfloat16),
            pltpu.VMEM((total, jobs * wide), jnp.float32),
            pltpu.VMEM((2, tokens, wide), jnp.bfloat16),
            pltpu.SemaphoreType.DMA((count, len(weights))),
            pltpu.SemaphoreType.DMA((len(weights), jobs)),
            pltpu.SemaphoreType.DMA((count, jobs)),
            pltpu.SemaphoreType.DMA((count, jobs)),
            pltpu.SemaphoreType.DMA((count, 2, max(*plan.carried, 1))),
        ],
        compiler_params=pltpu.CompilerParams(vmem_limit_bytes=62 << 20),
        cost_estimate=pl.CostEstimate(
            flops=2 * tokens * slab * wide * added, bytes_accessed=0, transcendentals=0
        ),
    )(role, *operands)
    got = list(got)
    return [
        {
            j: (got.pop(0), got.pop(0)) if j in plan.finished[i] else got.pop(0)
            for j in plan.jobs(i)
        }
        for i in range(count)
    ]


def join_kernel(place_ref, *refs):
    *parts, out_ref, sems = refs
    count = len(parts) // 2
    inner = place_ref[count]
    wide, head = parts[0].shape[1], parts[count].shape[1]

    def copies(i, role):
        begin = pl.multiple_of(place_ref[i] * wide, wide)
        if role:
            yield parts[i], out_ref.at[:, pl.ds(begin, wide)], sems.at[i, 0]
            return
        kept = wide - head
        yield parts[i].at[:, pl.ds(head, kept)], out_ref.at[:, pl.ds(begin, kept)], sems.at[i, 0]
        last = pl.multiple_of(begin + kept, head)
        yield parts[count + i], out_ref.at[:, pl.ds(last, head)], sems.at[i, 1]

    for role in (1, 0):

        @pl.when((inner == 1) == (role == 1))
        def _():
            every = [pltpu.make_async_copy(*c) for i in range(count) for c in copies(i, role)]
            for copy in every:
                copy.start()
            for copy in every:
                copy.wait()


def join(places, inner, parts, back):
    rows, wide = parts[0].shape
    anywhere = pl.BlockSpec(memory_space=pl.ANY)
    return pl.pallas_call(
        join_kernel,
        out_shape=jax.ShapeDtypeStruct((rows, wide * len(parts)), jnp.bfloat16),
        in_specs=[pl.BlockSpec(memory_space=pltpu.SMEM)] + [anywhere] * (2 * len(parts)),
        out_specs=pl.BlockSpec(memory_space=pltpu.VMEM),
        scratch_shapes=[pltpu.SemaphoreType.DMA((len(parts), 2))],
        cost_estimate=pl.CostEstimate(
            flops=0, bytes_accessed=4 * rows * wide * len(parts), transcendentals=0
        ),
    )(jnp.stack([*places, inner]).astype(jnp.int32), *parts, *back)


def shared(tokens, ln_gain, qkv_weight):
    groups, planes, seqs, cores = (lax.axis_size(a) for a in ("groups", "dp", "seq", "head"))
    group, plane, seq, core = (lax.axis_index(a) for a in ("groups", "dp", "seq", "head"))
    _, rows, _ = tokens.shape
    slab, heads, columns = qkv_weight.shape
    heads, part = heads // groups, rows // cores
    inner = (plane == 1) | (plane == 2)
    wait = lax.optimization_barrier

    def fold(piece):
        piece = piece.reshape(-1, part, columns).transpose(1, 0, 2)
        return piece.reshape(part, -1)

    def pick(for_inner, for_ends):
        return jnp.where(inner, for_inner, for_ends)

    def pair(value):
        return lax.ppermute(value, "dp", [(0, 1), (1, 0), (2, 3), (3, 2)])

    def outward(value):
        return lax.ppermute(value, "dp", [(1, 0), (2, 3)])

    def middle(value):
        return lax.ppermute(value, "dp", [(1, 2), (2, 1)])

    swap = [(0, 1), (1, 0)]
    beside = lambda value: lax.ppermute(value, "seq", swap)
    across = lambda value: lax.ppermute(value, "groups", swap)

    def others(*values):
        got = []
        for value in values:
            if got:
                value, got[-1] = wait((value, got[-1]))
            got.append(lax.ppermute(value, "head", swap))
        return got


    def exchange(mixed):
        got = []
        for a in range(groups):
            for b in range(seqs):
                sent = mixed[a * seqs + b]
                if a or b:
                    steps = [
                        (g * seqs + s, (g + a) % groups * seqs + (s + b) % seqs)
                        for g in range(groups)
                        for s in range(seqs)
                    ]
                    sent = lax.ppermute(sent, ("groups", "seq"), steps)
                got.append(sent)
        return got

    weight = qkv_weight.transpose(1, 0, 2)
    order = slab_order(plane)
    normed, (own0, folded0) = normalize_part(
        tokens, ln_gain, weight, part, core, order, group * heads
    )
    normed, own0, folded0, later_weight = wait((normed, own0, folded0, weight))
    cut0, cut1 = normed
    pair1, middle1 = pair(own0), middle(folded0)
    beside1, across1 = beside(cut0), across(cut0)
    own1, own2 = [
        lax.dynamic_index_in_dim(later_weight, group * heads + j, 0, keepdims=False) for j in (1, 2)
    ]
    give = pick(fold(own1), cut0)
    role = jnp.stack([core, inner]).astype(jnp.int32)
    beside1, across1, own1, own2, cut1, tokens, give, role = wait(
        (beside1, across1, own1, own2, cut1, tokens, give, role)
    )
    pair1, middle1, give = wait((pair1, middle1, give))
    run = functools.partial(run_jobs, role, seqs * rows, columns)

    pair2, middle2 = pair(give), middle(pair1)
    beside2, across2 = beside(cut1), across(cut1)
    give = pick(middle1, cut1)
    far_normed, _ = normalize_part(tokens, ln_gain, weight, part, 1 - core, order)
    far1 = others(beside1, across1)
    pair2, middle2, beside2, across2, across1, own1, own2, far_normed, far1, give = wait(
        (pair2, middle2, beside2, across2, across1, own1, own2, far_normed, far1, give)
    )

    pair3, middle3 = pair(give), middle(own1)
    beside3, across3 = beside(across1), across(beside2)
    give = pick(middle2, own1)
    far2 = others(beside2, across2)
    pair3, middle3, beside3, across3, pair1, pair2, own2, far2, give = wait(
        (pair3, middle3, beside3, across3, pair1, pair2, own2, far2, give)
    )

    pair4, middle4 = pair(give), middle(own2)
    beside4, across4 = beside(pair2), across(pair2)
    give = pick(middle3, own2)
    pieces0 = ((normed, far_normed), ((beside1, beside2), (far1[0], far2[0])))
    owns = [own0, (own1, own0), (own2, own1)]
    ((head0, sum20, sum30),) = [
        tuple(got.values())
        for got in run(
            [dict(pieces=pieces0, uses=[(0, 3), (0, 2), (0, 1), (0, 1)], finish=(0,))],
            [(0, 0, owns), (2, 0, [middle1, (middle3, pair1)]), (1, 0, [pair1]), (3, 0, [middle2])],
        )
    ]
    far3 = others(beside3, across3)
    lent = jnp.concatenate([pair2, pair3])
    pair4, middle4, beside4, across4, own2, pair3, lent, head0, sum20, sum30, far3, give = wait(
        (pair4, middle4, beside4, across4, own2, pair3, lent, head0, sum20, sum30, far3, give)
    )

    pair5, middle5 = pair(give), middle(pair4)
    beside5, across5 = beside(pair3), across(pair3)
    pieces1 = (((across1, across2), (far1[1], far2[1])), ((beside3, across3), far3))
    image1, image0 = run(
        [
            dict(pieces=pieces1, uses=[(0, 3), (0, 3), (0, 2), (0, 1)], finish=(0,)),
            dict(pieces=pieces0, uses=[None, (2, 3), (1, 2), None], sums={1: sum20, 2: sum30}),
        ],
        [
            (0, 0, owns),
            (2, 0, [middle1, (middle3, pair1), (middle4, pair2)]),
            (1, 0, [pair1, (pair4, pair3)]),
            (3, 0, [middle2]),
        ],
    )
    far_lent, far4 = others(lent, beside4)
    pair5, middle5, beside5, across5, across4, image0, image1, far_lent, far4 = wait(
        (
            *(pair5, middle5, beside5, across5, across4),
            *(image0, image1, far_lent, far4),
        )
    )

    pair6, middle6 = outward(middle5), middle(pair5)
    beside6, across6 = beside(across4), across(beside5)
    far5, far_across4 = others(beside5, across4)
    ahead0, ahead1 = run(
        [
            dict(
                pieces=pieces,
                uses=[(0, 1), (1, 2)],
                sums={0: image[1], 1: image[2]},
                finish=(0,),
            )
            for pieces, image in ((pieces0, image0), (pieces1, image1))
        ],
        [(3, 0, [(middle5, pair4)]), (1, 1, [pair5])],
    )
    lent0 = (((pair2, pair3), (far_lent, (far_lent, part))), ((beside4, beside5), (far4, far5)))
    lent_weights = [(0, 0, [pair5]), (1, 0, [middle4]), (2, 0, [own2])]
    ((sum4,),) = [
        tuple(got.values()) for got in run([dict(pieces=lent0, uses=[(0, 1)] * 3)], lent_weights)
    ]
    pair6, middle6, beside6, across6, across5, ahead0, ahead1, sum4, far_across4 = wait(
        (pair6, middle6, beside6, across6, across5, ahead0, ahead1, sum4, far_across4)
    )

    far_across5, *far6 = [
        lax.ppermute(value, "head", swap) for value in (across5, beside6, across6)
    ]
    done0, done1, lent0 = run(
        [
            dict(pieces=p, uses=[(0, 1)], sums={0: x[1]}, finish=(0,), carry=tuple(zip(h, x[0])))
            for p, h, x in ((pieces0, head0, ahead0), (pieces1, image1[0], ahead1))
        ]
        + [dict(pieces=lent0, uses=[(0, 1)], sums={0: sum4}, finish=(0,))],
        [(3, 0, [(middle6, pair6)])],
    )
    lent1 = (((across4, across5), (far_across4, far_across5)), ((beside6, across6), far6))
    (lent1,) = run(
        [dict(pieces=lent1, uses=[(0, 1)] * 4, finish=(0,))], [*lent_weights, (3, 0, [middle6])]
    )

    def hand_back(mixed):
        got = []
        for a in range(groups):
            for b in range(seqs):
                steps = [
                    (
                        (g * planes + z) * seqs + s,
                        ((g + a) % groups * planes + (z ^ 1)) * seqs + (s + b) % seqs,
                    )
                    for g in range(groups)
                    for z in (1, 2)
                    for s in range(seqs)
                ]
                sent = mixed[a * seqs + b]
                got.append(lax.ppermute(sent, ("groups", "dp", "seq"), steps))
        return got

    sent = exchange((*done0[0], *done1[0]))
    back = hand_back((*lent0[0], *lent1[0]))
    places = [
        (seq - b) % seqs * groups + (group - a) % groups
        for a in range(groups)
        for b in range(seqs)
    ]
    return join(places, inner, sent, back)[None]


def per_device(tokens, ln_gain, qkv_weight):
    groups, planes, seqs, cores = (lax.axis_size(a) for a in ("groups", "dp", "seq", "head"))
    images, rows, width = tokens.shape
    slab, heads, _ = qkv_weight.shape
    if (groups, planes, seqs, cores) == (2, 4, 2, 2) and images == 1 and heads == 3 * groups:
        part = rows // cores
        if rows % (32 * cores) == 0 and slab % part == 0 and 2 * slab == qkv_weight.shape[2] * slab // part:
            return shared(tokens, ln_gain, qkv_weight)
    return plain(tokens, ln_gain, qkv_weight)


def solution(mesh):
    return jax.shard_map(
        per_device,
        mesh=mesh,
        in_specs=(P(("groups", "dp"), "seq", None), P(), P("dp", ("seq", "head"), None)),
        out_specs=P(("groups", "dp"), "seq", "head"),
        check_vma=False,
    )
```

```python
import functools
import math

import jax
import jax.numpy as jnp
from jax import lax
from jax.experimental import pallas as pl
from jax.experimental.pallas import tpu as pltpu
from jax.sharding import PartitionSpec as P


def normalize(array, gain):
    widened = array.astype(jnp.float32)
    centered = widened - jnp.mean(widened, axis=-1, keepdims=True)
    variance = jnp.mean(centered * centered, axis=-1, keepdims=True)
    return (centered * lax.rsqrt(variance + 1e-06) * gain).astype(jnp.bfloat16)


def attend(projected):
    width = projected.shape[2] // 3
    queries = projected[:, :, :width]
    key_rows = projected[:, :, width : 2 * width]
    value_rows = projected[:, :, 2 * width :]
    scores = jnp.einsum("qhd,khd->hqk", queries, key_rows, preferred_element_type=jnp.float32) * (
        1.0 / math.sqrt(width)
    )
    highest = jnp.max(scores, axis=-1, keepdims=True)
    expo = jnp.exp(scores - highest)
    probs = (expo / jnp.sum(expo, axis=-1, keepdims=True)).astype(jnp.bfloat16)
    mixed = jnp.einsum("hqk,khd->qhd", probs, value_rows, preferred_element_type=jnp.float32)
    return mixed.astype(jnp.bfloat16).reshape(projected.shape[0], -1)


def plain(tokens, ln_gain, qkv_weight):
    images = tokens.shape[0]
    width = tokens.shape[2]
    heads_here = qkv_weight.shape[1]
    columns = heads_here * qkv_weight.shape[2]
    source = normalize(tokens, ln_gain)
    half_width = width // lax.axis_size("head")
    core_index = lax.axis_index("head")
    own_half = lax.dynamic_slice_in_dim(source, core_index * half_width, half_width, 2)
    fetched = lax.all_gather(own_half, "seq", axis=1, tiled=True)
    gathered = lax.all_gather(fetched, "head", axis=2, tiled=True)
    full_tokens = gathered.shape[1]
    features = gathered.reshape(images * full_tokens, width)
    piece = lax.all_gather(qkv_weight, "dp", axis=0, tiled=True)
    projected = jnp.dot(
        features, piece.reshape(piece.shape[0], columns), preferred_element_type=jnp.float32
    )
    projected = projected.astype(jnp.bfloat16).reshape(
        images, full_tokens, heads_here, qkv_weight.shape[2]
    )
    mixed = lax.map(attend, projected)
    return lax.all_to_all(mixed, "seq", split_axis=1, concat_axis=2, tiled=True)


def slab_order(plane):
    inner = (plane == 1) | (plane == 2)
    near, far = plane ^ 1, 2 - plane // 2
    return plane, jnp.where(inner, near, far), jnp.where(inner, far, near), 3 - 3 * (plane // 2)


def normalize_kernel(place_ref, tokens_ref, gain_ref, weight_ref, *refs):
    normed_refs, rest = refs[:2], refs[2:]
    rows, width = tokens_ref.shape[1:]
    lanes = 128
    slab, span = width // 4, width // 2
    step, steps = pl.program_id(0), pl.num_programs(0)
    if rest:
        own_ref, own_buf, own_sems = rest
        own_in = pltpu.make_async_copy(weight_ref.at[place_ref[5]], own_buf, own_sems.at[0])
        own_out = pltpu.make_async_copy(own_buf, own_ref, own_sems.at[1])

        @pl.when(step == 0)
        def _():
            own_in.start()

        @pl.when(step == 1)
        def _():
            own_in.wait()
            own_out.start()

    def widened(begin):
        return tokens_ref[0, :, pl.ds(begin, lanes)].astype(jnp.float32)

    total = jnp.zeros((rows, lanes), jnp.float32)
    for begin in range(0, width, lanes):
        total += widened(begin)
    mean = jnp.sum(total, axis=-1, keepdims=True) / width
    total = jnp.zeros((rows, lanes), jnp.float32)
    for begin in range(0, width, lanes):
        centered = widened(begin) - mean
        total += centered * centered
    scale = lax.rsqrt(jnp.sum(total, axis=-1, keepdims=True) / width + 1e-06)
    for i in range(4):
        source = place_ref[i + 1] * slab
        for begin in range(0, slab, lanes):
            column = pl.multiple_of(source + begin, lanes)
            part = (widened(column) - mean) * scale * gain_ref[:, pl.ds(column, lanes)]
            target = i * slab % span + begin
            normed_refs[i * slab // span][:, target : target + lanes] = part.astype(jnp.bfloat16)

    if rest:

        @pl.when(step == steps - 1)
        def _():
            own_out.wait()


def normalize_part(tokens, ln_gain, weight, part, core, order, head=None):
    width = tokens.shape[2]
    piece = weight.shape[1:]
    step = 64 if part % 64 == 0 else 32
    steps = part // step
    place = [core, *order] + ([] if head is None else [head])
    place = jnp.stack([jnp.asarray(v, jnp.int32) for v in place])
    half = jax.ShapeDtypeStruct((part, width // 2), jnp.bfloat16)
    anywhere = pl.BlockSpec(memory_space=pl.ANY)
    got = pl.pallas_call(
        normalize_kernel,
        out_shape=[half] * 2 + [jax.ShapeDtypeStruct(piece, jnp.bfloat16)] * (head is not None),
        grid_spec=pltpu.PrefetchScalarGridSpec(
            num_scalar_prefetch=1,
            grid=(steps,),
            in_specs=[
                pl.BlockSpec((1, step, width), lambda i, place: (0, place[0] * steps + i, 0)),
                pl.BlockSpec((1, width), lambda i, place: (0, 0)),
                anywhere,
            ],
            out_specs=[pl.BlockSpec((step, width // 2), lambda i, place: (i, 0))] * 2
            + [anywhere] * (head is not None),
            scratch_shapes=[pltpu.VMEM(piece, jnp.bfloat16), pltpu.SemaphoreType.DMA((2,))]
            if head is not None
            else [],
        ),
        compiler_params=pltpu.CompilerParams(vmem_limit_bytes=62 << 20),
        cost_estimate=pl.CostEstimate(
            flops=8 * part * width, bytes_accessed=4 * part * width, transcendentals=part
        ),
    )(place, tokens, ln_gain[None], weight)
    return got[:2], got[2:]


def attend_rows(projected_ref, parts, column):
    width = projected_ref.shape[1] // 3
    key_rows = projected_ref[:, width : 2 * width]
    value_rows = projected_ref[:, 2 * width :]
    value_rows = jnp.concatenate([value_rows, jnp.ones_like(value_rows)], axis=1)
    begin = 0
    for part in parts:
        step = part.shape[0]
        queries = projected_ref[begin : begin + step, :width]
        scores = lax.dot_general(
            queries, key_rows, (((1,), (1,)), ((), ())), preferred_element_type=jnp.float32
        )
        highest = jnp.max(scores, axis=-1, keepdims=True)
        expo = jnp.exp2((scores - highest) * (math.log2(math.e) / math.sqrt(width)))
        mixed = jnp.dot(expo.astype(jnp.bfloat16), value_rows, preferred_element_type=jnp.float32)
        mixed = mixed[:, :width] / mixed[:, width:]
        part[:, column : column + width] = mixed.astype(jnp.bfloat16)
        begin += step


class Jobs:
    def __init__(self, **numbers):
        self.__dict__.update(numbers)

    def jobs(self, image):
        return sorted({j for use in self.uses[image] if use for j in range(*use)})


def job_kernel(plan, role_ref, *refs):
    refs = list(refs)
    take = lambda n: [refs.pop(0) for _ in range(n)]
    images, ns = range(len(plan.uses)), range(len(plan.slots))
    pieces = [[[take(2) for _ in place] for place in image] for image in plan.origins]
    weights = [[take(1) * 2 if alike else take(2) for alike in row] for row in plan.same]
    partials = [{j: take(1)[0] for j in plan.added[i]} for i in images]
    carried = [[take(plan.carried[i]) for _ in range(2)] for i in images]
    outs = [
        {j: take(2) if j in plan.finished[i] else take(1)[0] for j in plan.jobs(i)} for i in images
    ]
    features_ref, weight_ref, total_ref, projected_ref = take(4)
    token_sems, weight_sems, sum_sems, out_sems, carry_sems = take(5)
    core, inner = role_ref[0], role_ref[1]
    slab = pieces[0][0][0][0].shape[1] // 2
    tokens, wide = projected_ref.shape[1:]
    part = tokens // 4

    def features(i, n):
        return features_ref.at[pl.ds(i * tokens, tokens), pl.ds(n * slab, slab)]

    def weight(n, j):
        return weight_ref.at[pl.ds(n * slab, slab), pl.ds(j * wide, wide)]

    def total(i, j):
        return total_ref.at[pl.ds(i * tokens, tokens), pl.ds(j * wide, wide)]

    def start_tokens(i, n):
        cut, begin = plan.slots[n] // 2, plan.slots[n] % 2 * slab
        for place in range(2):
            split = len(plan.origins[i][place])
            for owner in range(split):
                row = i * tokens + 2 * place * part
                if split == 2:
                    row += (1 - core if owner else core) * part
                count = 2 * part // split
                from_rows = pl.ds(plan.origins[i][place][owner][cut], count)
                rows = pl.ds(pl.multiple_of(row, 32), count)
                pltpu.make_async_copy(
                    pieces[i][place][owner][cut].at[from_rows, pl.ds(begin, slab)],
                    features_ref.at[rows, pl.ds(n * slab, slab)],
                    token_sems.at[i, n],
                ).start()

    def start_weight(n, j, role):
        source = weights[n][j - plan.first[n]][role]
        if source.shape[0] == slab:
            pltpu.make_async_copy(source, weight(n, j), weight_sems.at[n, j]).start()
            return
        for b in range(source.shape[1] // wide):
            pltpu.make_async_copy(
                source.at[:, pl.ds(b * wide, wide)],
                weight_ref.at[pl.ds(n * slab + b * part, part), pl.ds(j * wide, wide)],
                weight_sems.at[n, j],
            ).start()

    def start_role_weight(n, j):
        if plan.same[n][j - plan.first[n]]:
            start_weight(n, j, 0)
            return

        @pl.when(inner == 1)
        def _():
            start_weight(n, j, 0)

        @pl.when(inner != 1)
        def _():
            start_weight(n, j, 1)

    def partial_copy(i, j):
        return pltpu.make_async_copy(partials[i][j], total(i, j), sum_sems.at[i, j])

    def out_copy(i, j):
        return pltpu.make_async_copy(total(i, j), outs[i][j], out_sems.at[i, j])

    def carry_copies():
        for i in images:
            for place in range(2):
                for k in range(plan.carried[i]):
                    (finished,) = plan.finished[i]
                    target = outs[i][finished][place].at[:, pl.ds(k * wide // 3, wide // 3)]
                    yield pltpu.make_async_copy(
                        carried[i][place][k], target, carry_sems.at[i, place, k]
                    )

    stages = [(i, n) for i in images for n in ns if plan.uses[i][n]]
    held = set()

    def start_stage(i, n):
        start_tokens(i, n)
        for j in range(*plan.uses[i][n]):
            if (n, j) not in held:
                held.add((n, j))
                start_role_weight(n, j)
        if not any((i, n) > (i, m) and plan.uses[i][m] for m in ns):
            for j in plan.added[i]:
                partial_copy(i, j).start()

    ahead = 2
    for stage in stages[:ahead]:
        start_stage(*stage)
    for copy in carry_copies():
        copy.start()
    ready, waiting = set(), []
    for index, (i, n) in enumerate(stages):
        low, high = plan.uses[i][n]
        pltpu.make_async_copy(features(i, n), features(i, n), token_sems.at[i, n]).wait()
        for j in range(low, high):
            if (n, j) not in ready:
                ready.add((n, j))
                pltpu.make_async_copy(weight(n, j), weight(n, j), weight_sems.at[n, j]).wait()
        if index + ahead < len(stages):
            start_stage(*stages[index + ahead])
        term = jnp.dot(
            features(i, n)[...],
            weight_ref[n * slab : (n + 1) * slab, low * wide : high * wide],
            preferred_element_type=jnp.float32,
        )
        for j in range(low, high):
            value = term[:, (j - low) * wide : (j - low + 1) * wide]
            mine = [m for m in ns if plan.uses[i][m] and j in range(*plan.uses[i][m])]
            if n == mine[0] and j in plan.added[i]:
                partial_copy(i, j).wait()
            if n != mine[0] or j in plan.added[i]:
                value += total(i, j)[...]
            if n == mine[-1] and j in plan.finished[i]:
                projected_ref[i % 2] = value.astype(jnp.bfloat16)
                if waiting:
                    attend_rows(*waiting.pop())
                column = plan.carried[i] * wide // 3
                waiting.append((projected_ref.at[i % 2], outs[i][j], column))
                continue
            total(i, j)[...] = value
            if n == mine[-1]:
                out_copy(i, j).start()
    if waiting:
        attend_rows(*waiting.pop())
    for copy in carry_copies():
        copy.wait()
    for i in images:
        for j in plan.jobs(i):
            if j not in plan.finished[i]:
                out_copy(i, j).wait()


def run_jobs(role, tokens, wide, images, weights):
    images = [
        dict(
            image,
            pieces=[
                [[x if isinstance(x, tuple) else (x, 0) for x in owner] for owner in place]
                for place in image["pieces"]
            ],
            sums=image.get("sums", {}),
            finish=image.get("finish", ()),
            carry=image.get("carry", ((), ())),
        )
        for image in images
    ]
    plan = Jobs(
        origins=[[[[r for _, r in o] for o in p] for p in image["pieces"]] for image in images],
        slots=[slot for slot, _, _ in weights],
        first=[first for _, first, _ in weights],
        same=[[not isinstance(w, tuple) for w in row] for _, _, row in weights],
        uses=[image["uses"] for image in images],
        added=[tuple(image["sums"]) for image in images],
        finished=[image["finish"] for image in images],
        carried=[len(image["carry"][0]) for image in images],
    )
    operands = [x for i in images for place in i["pieces"] for owner in place for x, _ in owner]
    slab = operands[0].shape[1] // 2
    for _, _, row in weights:
        for w in row:
            operands += list(w) if isinstance(w, tuple) else [w]
    operands += [x for image in images for x in image["sums"].values()]
    operands += [x for image in images for place in image["carry"] for x in place]
    anywhere, vmem = pl.BlockSpec(memory_space=pl.ANY), pl.BlockSpec(memory_space=pltpu.VMEM)
    head = wide // 3
    shapes, specs = [], []
    for i in range(len(images)):
        for j in plan.jobs(i):
            if j in plan.finished[i]:
                shape = (tokens // 2, head * (plan.carried[i] + 1))
                shapes += [jax.ShapeDtypeStruct(shape, jnp.bfloat16)] * 2
                specs += [vmem] * 2
            else:
                shapes.append(jax.ShapeDtypeStruct((tokens, wide), jnp.float32))
                specs.append(anywhere)
    jobs = 1 + max(j for i in range(len(images)) for j in plan.jobs(i))
    count, depth, total = len(images), len(weights) * slab, len(images) * tokens
    added = sum(high - low for uses in plan.uses for low, high in filter(None, uses))
    got = pl.pallas_call(
        functools.partial(job_kernel, plan),
        out_shape=shapes,
        in_specs=[pl.BlockSpec(memory_space=pltpu.SMEM)] + [anywhere] * len(operands),
        out_specs=specs,
        scratch_shapes=[
            pltpu.VMEM((total, depth), jnp.bfloat16),
            pltpu.VMEM((depth, jobs * wide), jnp.bfloat16),
            pltpu.VMEM((total, jobs * wide), jnp.float32),
            pltpu.VMEM((2, tokens, wide), jnp.bfloat16),
            pltpu.SemaphoreType.DMA((count, len(weights))),
            pltpu.SemaphoreType.DMA((len(weights), jobs)),
            pltpu.SemaphoreType.DMA((count, jobs)),
            pltpu.SemaphoreType.DMA((count, jobs)),
            pltpu.SemaphoreType.DMA((count, 2, max(*plan.carried, 1))),
        ],
        compiler_params=pltpu.CompilerParams(vmem_limit_bytes=62 << 20),
        cost_estimate=pl.CostEstimate(
            flops=2 * tokens * slab * wide * added, bytes_accessed=0, transcendentals=0
        ),
    )(role, *operands)
    got = list(got)
    return [
        {
            j: (got.pop(0), got.pop(0)) if j in plan.finished[i] else got.pop(0)
            for j in plan.jobs(i)
        }
        for i in range(count)
    ]


def join_kernel(place_ref, *refs):
    *parts, out_ref, sems = refs
    count = len(parts) // 2
    inner = place_ref[count]
    wide, head = parts[0].shape[1], parts[count].shape[1]

    def copies(i, role):
        begin = pl.multiple_of(place_ref[i] * wide, wide)
        if role:
            yield parts[i], out_ref.at[:, pl.ds(begin, wide)], sems.at[i, 0]
            return
        kept = wide - head
        yield parts[i].at[:, pl.ds(head, kept)], out_ref.at[:, pl.ds(begin, kept)], sems.at[i, 0]
        last = pl.multiple_of(begin + kept, head)
        yield parts[count + i], out_ref.at[:, pl.ds(last, head)], sems.at[i, 1]

    for role in (1, 0):

        @pl.when((inner == 1) == (role == 1))
        def _():
            every = [pltpu.make_async_copy(*c) for i in range(count) for c in copies(i, role)]
            for copy in every:
                copy.start()
            for copy in every:
                copy.wait()


def join(places, inner, parts, back):
    rows, wide = parts[0].shape
    anywhere = pl.BlockSpec(memory_space=pl.ANY)
    return pl.pallas_call(
        join_kernel,
        out_shape=jax.ShapeDtypeStruct((rows, wide * len(parts)), jnp.bfloat16),
        in_specs=[pl.BlockSpec(memory_space=pltpu.SMEM)] + [anywhere] * (2 * len(parts)),
        out_specs=pl.BlockSpec(memory_space=pltpu.VMEM),
        scratch_shapes=[pltpu.SemaphoreType.DMA((len(parts), 2))],
        cost_estimate=pl.CostEstimate(
            flops=0, bytes_accessed=4 * rows * wide * len(parts), transcendentals=0
        ),
    )(jnp.stack([*places, inner]).astype(jnp.int32), *parts, *back)


def shared(tokens, ln_gain, qkv_weight):
    groups, planes, seqs, cores = (lax.axis_size(a) for a in ("groups", "dp", "seq", "head"))
    group, plane, seq, core = (lax.axis_index(a) for a in ("groups", "dp", "seq", "head"))
    _, rows, _ = tokens.shape
    slab, heads, columns = qkv_weight.shape
    heads, part = heads // groups, rows // cores
    inner = (plane == 1) | (plane == 2)
    wait = lax.optimization_barrier

    def fold(piece):
        piece = piece.reshape(-1, part, columns).transpose(1, 0, 2)
        return piece.reshape(part, -1)

    def pick(for_inner, for_ends):
        return jnp.where(inner, for_inner, for_ends)

    def pair(value):
        return lax.ppermute(value, "dp", [(0, 1), (1, 0), (2, 3), (3, 2)])

    def outward(value):
        return lax.ppermute(value, "dp", [(1, 0), (2, 3)])

    def middle(value):
        return lax.ppermute(value, "dp", [(1, 2), (2, 1)])

    swap = [(0, 1), (1, 0)]
    beside = lambda value: lax.ppermute(value, "seq", swap)
    across = lambda value: lax.ppermute(value, "groups", swap)

    def others(*values):
        got = []
        for value in values:
            if got:
                value, got[-1] = wait((value, got[-1]))
            got.append(lax.ppermute(value, "head", swap))
        return got


    def exchange(mixed):
        got = []
        for a in range(groups):
            for b in range(seqs):
                sent = mixed[a * seqs + b]
                if a or b:
                    steps = [
                        (g * seqs + s, (g + a) % groups * seqs + (s + b) % seqs)
                        for g in range(groups)
                        for s in range(seqs)
                    ]
                    sent = lax.ppermute(sent, ("groups", "seq"), steps)
                got.append(sent)
        return got

    weight = qkv_weight.transpose(1, 0, 2)
    order = slab_order(plane)
    normed, (own0,) = normalize_part(
        tokens, ln_gain, weight, part, core, order, group * heads
    )
    normed, own0, later_weight = wait((normed, own0, weight))
    cut0, cut1 = normed
    pair1, middle1 = pair(own0), middle(own0)
    beside1, across1 = beside(cut0), across(cut0)
    own1, own2 = [
        lax.dynamic_index_in_dim(later_weight, group * heads + j, 0, keepdims=False) for j in (1, 2)
    ]
    give = pick(fold(own1), cut0)
    role = jnp.stack([core, inner]).astype(jnp.int32)
    beside1, across1, own1, own2, cut1, tokens, give, role = wait(
        (beside1, across1, own1, own2, cut1, tokens, give, role)
    )
    pair1, middle1, give = wait((pair1, middle1, give))
    run = functools.partial(run_jobs, role, seqs * rows, columns)

    pair2, middle2 = pair(give), middle(pair1)
    beside2, across2 = beside(cut1), across(cut1)
    give = pick(fold(middle1), cut1)
    far_normed, _ = normalize_part(tokens, ln_gain, weight, part, 1 - core, order)
    far1 = others(beside1, across1)
    pair2, middle2, beside2, across2, across1, own1, own2, far_normed, far1, give = wait(
        (pair2, middle2, beside2, across2, across1, own1, own2, far_normed, far1, give)
    )

    pair3, middle3 = pair(give), middle(own1)
    beside3, across3 = beside(across1), across(beside2)
    give = pick(middle2, own1)
    far2 = others(beside2, across2)
    pair3, middle3, beside3, across3, pair1, pair2, own2, far2, give = wait(
        (pair3, middle3, beside3, across3, pair1, pair2, own2, far2, give)
    )

    pair4, middle4 = pair(give), middle(own2)
    beside4, across4 = beside(pair2), across(pair2)
    give = pick(middle3, own2)
    pieces0 = ((normed, far_normed), ((beside1, beside2), (far1[0], far2[0])))
    owns = [own0, (own1, own0), (own2, own1)]
    ((head0, sum20, sum30),) = [
        tuple(got.values())
        for got in run(
            [dict(pieces=pieces0, uses=[(0, 3), (0, 2), (0, 1), (0, 1)], finish=(0,))],
            [(0, 0, owns), (2, 0, [middle1, (middle3, pair1)]), (1, 0, [pair1]), (3, 0, [middle2])],
        )
    ]
    far3 = others(beside3, across3)
    lent = jnp.concatenate([pair2, pair3])
    pair4, middle4, beside4, across4, own2, pair3, lent, head0, sum20, sum30, far3, give = wait(
        (pair4, middle4, beside4, across4, own2, pair3, lent, head0, sum20, sum30, far3, give)
    )

    pair5, middle5 = pair(give), middle(pair4)
    beside5, across5 = beside(pair3), across(pair3)
    pieces1 = (((across1, across2), (far1[1], far2[1])), ((beside3, across3), far3))
    image1, image0 = run(
        [
            dict(pieces=pieces1, uses=[(0, 3), (0, 3), (0, 2), (0, 1)], finish=(0,)),
            dict(pieces=pieces0, uses=[None, (2, 3), (1, 2), None], sums={1: sum20, 2: sum30}),
        ],
        [
            (0, 0, owns),
            (2, 0, [middle1, (middle3, pair1), (middle4, pair2)]),
            (1, 0, [pair1, (pair4, pair3)]),
            (3, 0, [middle2]),
        ],
    )
    far_lent, far4 = others(lent, beside4)
    pair5, middle5, beside5, across5, across4, image0, image1, far_lent, far4 = wait(
        (
            *(pair5, middle5, beside5, across5, across4),
            *(image0, image1, far_lent, far4),
        )
    )

    pair6, middle6 = outward(middle5), middle(pair5)
    beside6, across6 = beside(across4), across(beside5)
    far5, far_across4 = others(beside5, across4)
    ahead0, ahead1 = run(
        [
            dict(
                pieces=pieces,
                uses=[(0, 1), (1, 2)],
                sums={0: image[1], 1: image[2]},
                finish=(0,),
            )
            for pieces, image in ((pieces0, image0), (pieces1, image1))
        ],
        [(3, 0, [(middle5, pair4)]), (1, 1, [pair5])],
    )
    lent0 = (((pair2, pair3), (far_lent, (far_lent, part))), ((beside4, beside5), (far4, far5)))
    lent_weights = [(0, 0, [pair5]), (1, 0, [middle4]), (2, 0, [own2])]
    ((sum4,),) = [
        tuple(got.values()) for got in run([dict(pieces=lent0, uses=[(0, 1)] * 3)], lent_weights)
    ]
    pair6, middle6, beside6, across6, across5, ahead0, ahead1, sum4, far_across4 = wait(
        (pair6, middle6, beside6, across6, across5, ahead0, ahead1, sum4, far_across4)
    )

    far_across5, *far6 = [
        lax.ppermute(value, "head", swap) for value in (across5, beside6, across6)
    ]
    done0, done1, lent0 = run(
        [
            dict(pieces=p, uses=[(0, 1)], sums={0: x[1]}, finish=(0,), carry=tuple(zip(h, x[0])))
            for p, h, x in ((pieces0, head0, ahead0), (pieces1, image1[0], ahead1))
        ]
        + [dict(pieces=lent0, uses=[(0, 1)], sums={0: sum4}, finish=(0,))],
        [(3, 0, [(middle6, pair6)])],
    )
    lent1 = (((across4, across5), (far_across4, far_across5)), ((beside6, across6), far6))
    (lent1,) = run(
        [dict(pieces=lent1, uses=[(0, 1)] * 4, finish=(0,))], [*lent_weights, (3, 0, [middle6])]
    )

    def hand_back(mixed):
        got = []
        for a in range(groups):
            for b in range(seqs):
                steps = [
                    (
                        (g * planes + z) * seqs + s,
                        ((g + a) % groups * planes + (z ^ 1)) * seqs + (s + b) % seqs,
                    )
                    for g in range(groups)
                    for z in (1, 2)
                    for s in range(seqs)
                ]
                sent = mixed[a * seqs + b]
                got.append(lax.ppermute(sent, ("groups", "dp", "seq"), steps))
        return got

    sent = exchange((*done0[0], *done1[0]))
    back = hand_back((*lent0[0], *lent1[0]))
    places = [
        (seq - b) % seqs * groups + (group - a) % groups
        for a in range(groups)
        for b in range(seqs)
    ]
    return join(places, inner, sent, back)[None]


def per_device(tokens, ln_gain, qkv_weight):
    groups, planes, seqs, cores = (lax.axis_size(a) for a in ("groups", "dp", "seq", "head"))
    images, rows, width = tokens.shape
    slab, heads, _ = qkv_weight.shape
    if (groups, planes, seqs, cores) == (2, 4, 2, 2) and images == 1 and heads == 3 * groups:
        part = rows // cores
        if rows % (32 * cores) == 0 and slab % part == 0 and 2 * slab == qkv_weight.shape[2] * slab // part:
            return shared(tokens, ln_gain, qkv_weight)
    return plain(tokens, ln_gain, qkv_weight)


def solution(mesh):
    return jax.shard_map(
        per_device,
        mesh=mesh,
        in_specs=(P(("groups", "dp"), "seq", None), P(), P("dp", ("seq", "head"), None)),
        out_specs=P(("groups", "dp"), "seq", "head"),
        check_vma=False,
    )
```

```python
import functools
import math

import jax
import jax.numpy as jnp
from jax import lax
from jax.experimental import pallas as pl
from jax.experimental.pallas import tpu as pltpu
from jax.sharding import PartitionSpec as P


def normalize(array, gain):
    widened = array.astype(jnp.float32)
    centered = widened - jnp.mean(widened, axis=-1, keepdims=True)
    variance = jnp.mean(centered * centered, axis=-1, keepdims=True)
    return (centered * lax.rsqrt(variance + 1e-06) * gain).astype(jnp.bfloat16)


def attend(projected):
    width = projected.shape[2] // 3
    queries = projected[:, :, :width]
    key_rows = projected[:, :, width : 2 * width]
    value_rows = projected[:, :, 2 * width :]
    scores = jnp.einsum("qhd,khd->hqk", queries, key_rows, preferred_element_type=jnp.float32) * (
        1.0 / math.sqrt(width)
    )
    highest = jnp.max(scores, axis=-1, keepdims=True)
    expo = jnp.exp(scores - highest)
    probs = (expo / jnp.sum(expo, axis=-1, keepdims=True)).astype(jnp.bfloat16)
    mixed = jnp.einsum("hqk,khd->qhd", probs, value_rows, preferred_element_type=jnp.float32)
    return mixed.astype(jnp.bfloat16).reshape(projected.shape[0], -1)


def plain(tokens, ln_gain, qkv_weight):
    images = tokens.shape[0]
    width = tokens.shape[2]
    heads_here = qkv_weight.shape[1]
    columns = heads_here * qkv_weight.shape[2]
    source = normalize(tokens, ln_gain)
    half_width = width // lax.axis_size("head")
    core_index = lax.axis_index("head")
    own_half = lax.dynamic_slice_in_dim(source, core_index * half_width, half_width, 2)
    fetched = lax.all_gather(own_half, "seq", axis=1, tiled=True)
    gathered = lax.all_gather(fetched, "head", axis=2, tiled=True)
    full_tokens = gathered.shape[1]
    features = gathered.reshape(images * full_tokens, width)
    piece = lax.all_gather(qkv_weight, "dp", axis=0, tiled=True)
    projected = jnp.dot(
        features, piece.reshape(piece.shape[0], columns), preferred_element_type=jnp.float32
    )
    projected = projected.astype(jnp.bfloat16).reshape(
        images, full_tokens, heads_here, qkv_weight.shape[2]
    )
    mixed = lax.map(attend, projected)
    return lax.all_to_all(mixed, "seq", split_axis=1, concat_axis=2, tiled=True)


def slab_order(plane):
    inner = (plane == 1) | (plane == 2)
    near, far = plane ^ 1, 2 - plane // 2
    return plane, jnp.where(inner, near, far), jnp.where(inner, far, near), 3 - 3 * (plane // 2)


def normalize_kernel(place_ref, tokens_ref, gain_ref, weight_ref, *refs):
    normed_refs, rest = refs[:2], refs[2:]
    rows, width = tokens_ref.shape[1:]
    lanes = 128
    slab, span = width // 4, width // 2
    step, steps = pl.program_id(0), pl.num_programs(0)
    if rest:
        own_ref, own_buf, own_sems = rest
        own_in = pltpu.make_async_copy(weight_ref.at[place_ref[5]], own_buf, own_sems.at[0])
        own_out = pltpu.make_async_copy(own_buf, own_ref, own_sems.at[1])

        @pl.when(step == 0)
        def _():
            own_in.start()

        @pl.when(step == 1)
        def _():
            own_in.wait()
            own_out.start()

    def widened(begin):
        return tokens_ref[0, :, pl.ds(begin, lanes)].astype(jnp.float32)

    total = jnp.zeros((rows, lanes), jnp.float32)
    for begin in range(0, width, lanes):
        total += widened(begin)
    mean = jnp.sum(total, axis=-1, keepdims=True) / width
    total = jnp.zeros((rows, lanes), jnp.float32)
    for begin in range(0, width, lanes):
        centered = widened(begin) - mean
        total += centered * centered
    scale = lax.rsqrt(jnp.sum(total, axis=-1, keepdims=True) / width + 1e-06)
    for i in range(4):
        source = place_ref[i + 1] * slab
        for begin in range(0, slab, lanes):
            column = pl.multiple_of(source + begin, lanes)
            part = (widened(column) - mean) * scale * gain_ref[:, pl.ds(column, lanes)]
            target = i * slab % span + begin
            normed_refs[i * slab // span][:, target : target + lanes] = part.astype(jnp.bfloat16)

    if rest:

        @pl.when(step == steps - 1)
        def _():
            own_out.wait()


def normalize_part(tokens, ln_gain, weight, part, core, order, head=None):
    width = tokens.shape[2]
    piece = weight.shape[1:]
    step = 64 if part % 64 == 0 else 32
    steps = part // step
    place = [core, *order] + ([] if head is None else [head])
    place = jnp.stack([jnp.asarray(v, jnp.int32) for v in place])
    half = jax.ShapeDtypeStruct((part, width // 2), jnp.bfloat16)
    anywhere = pl.BlockSpec(memory_space=pl.ANY)
    got = pl.pallas_call(
        normalize_kernel,
        out_shape=[half] * 2 + [jax.ShapeDtypeStruct(piece, jnp.bfloat16)] * (head is not None),
        grid_spec=pltpu.PrefetchScalarGridSpec(
            num_scalar_prefetch=1,
            grid=(steps,),
            in_specs=[
                pl.BlockSpec((1, step, width), lambda i, place: (0, place[0] * steps + i, 0)),
                pl.BlockSpec((1, width), lambda i, place: (0, 0)),
                anywhere,
            ],
            out_specs=[pl.BlockSpec((step, width // 2), lambda i, place: (i, 0))] * 2
            + [anywhere] * (head is not None),
            scratch_shapes=[pltpu.VMEM(piece, jnp.bfloat16), pltpu.SemaphoreType.DMA((2,))]
            if head is not None
            else [],
        ),
        compiler_params=pltpu.CompilerParams(vmem_limit_bytes=62 << 20),
        cost_estimate=pl.CostEstimate(
            flops=8 * part * width, bytes_accessed=4 * part * width, transcendentals=part
        ),
    )(place, tokens, ln_gain[None], weight)
    return got[:2], got[2:]


def attend_rows(projected_ref, parts, column):
    width = projected_ref.shape[1] // 3
    key_rows = projected_ref[:, width : 2 * width]
    value_rows = projected_ref[:, 2 * width :]
    value_rows = jnp.concatenate([value_rows, jnp.ones_like(value_rows)], axis=1)
    begin = 0
    for part in parts:
        step = part.shape[0]
        queries = projected_ref[begin : begin + step, :width]
        scores = lax.dot_general(
            queries, key_rows, (((1,), (1,)), ((), ())), preferred_element_type=jnp.float32
        )
        highest = jnp.max(scores, axis=-1, keepdims=True)
        expo = jnp.exp2((scores - highest) * (math.log2(math.e) / math.sqrt(width)))
        mixed = jnp.dot(expo.astype(jnp.bfloat16), value_rows, preferred_element_type=jnp.float32)
        mixed = mixed[:, :width] / mixed[:, width:]
        part[:, column : column + width] = mixed.astype(jnp.bfloat16)
        begin += step


class Jobs:
    def __init__(self, **numbers):
        self.__dict__.update(numbers)

    def jobs(self, image):
        return sorted({j for use in self.uses[image] if use for j in range(*use)})


def job_kernel(plan, role_ref, *refs):
    refs = list(refs)
    take = lambda n: [refs.pop(0) for _ in range(n)]
    images, ns = range(len(plan.uses)), range(len(plan.slots))
    pieces = [[[take(2) for _ in place] for place in image] for image in plan.origins]
    weights = [[take(1) * 2 if alike else take(2) for alike in row] for row in plan.same]
    partials = [{j: take(1)[0] for j in plan.added[i]} for i in images]
    carried = [[take(plan.carried[i]) for _ in range(2)] for i in images]
    outs = [
        {j: take(2) if j in plan.finished[i] else take(1)[0] for j in plan.jobs(i)} for i in images
    ]
    features_ref, weight_ref, total_ref, projected_ref = take(4)
    token_sems, weight_sems, sum_sems, out_sems, carry_sems = take(5)
    core, inner = role_ref[0], role_ref[1]
    slab = pieces[0][0][0][0].shape[1] // 2
    tokens, wide = projected_ref.shape[1:]
    part = tokens // 4

    def features(i, n):
        return features_ref.at[pl.ds(i * tokens, tokens), pl.ds(n * slab, slab)]

    def weight(n, j):
        return weight_ref.at[pl.ds(n * slab, slab), pl.ds(j * wide, wide)]

    def total(i, j):
        return total_ref.at[pl.ds(i * tokens, tokens), pl.ds(j * wide, wide)]

    def start_tokens(i, n):
        cut, begin = plan.slots[n] // 2, plan.slots[n] % 2 * slab
        for place in range(2):
            split = len(plan.origins[i][place])
            for owner in range(split):
                row = i * tokens + 2 * place * part
                if split == 2:
                    row += (1 - core if owner else core) * part
                count = 2 * part // split
                from_rows = pl.ds(plan.origins[i][place][owner][cut], count)
                rows = pl.ds(pl.multiple_of(row, 32), count)
                pltpu.make_async_copy(
                    pieces[i][place][owner][cut].at[from_rows, pl.ds(begin, slab)],
                    features_ref.at[rows, pl.ds(n * slab, slab)],
                    token_sems.at[i, n],
                ).start()

    def start_weight(n, j, role):
        source = weights[n][j - plan.first[n]][role]
        if source.shape[0] == slab:
            pltpu.make_async_copy(source, weight(n, j), weight_sems.at[n, j]).start()
            return
        for b in range(source.shape[1] // wide):
            pltpu.make_async_copy(
                source.at[:, pl.ds(b * wide, wide)],
                weight_ref.at[pl.ds(n * slab + b * part, part), pl.ds(j * wide, wide)],
                weight_sems.at[n, j],
            ).start()

    def start_role_weight(n, j):
        if plan.same[n][j - plan.first[n]]:
            start_weight(n, j, 0)
            return

        @pl.when(inner == 1)
        def _():
            start_weight(n, j, 0)

        @pl.when(inner != 1)
        def _():
            start_weight(n, j, 1)

    def partial_copy(i, j):
        return pltpu.make_async_copy(partials[i][j], total(i, j), sum_sems.at[i, j])

    def out_copy(i, j):
        return pltpu.make_async_copy(total(i, j), outs[i][j], out_sems.at[i, j])

    def carry_copies():
        for i in images:
            for place in range(2):
                for k in range(plan.carried[i]):
                    (finished,) = plan.finished[i]
                    target = outs[i][finished][place].at[:, pl.ds(k * wide // 3, wide // 3)]
                    yield pltpu.make_async_copy(
                        carried[i][place][k], target, carry_sems.at[i, place, k]
                    )

    stages = [(i, n) for i in images for n in ns if plan.uses[i][n]]
    held = set()

    def start_stage(i, n):
        start_tokens(i, n)
        for j in range(*plan.uses[i][n]):
            if (n, j) not in held:
                held.add((n, j))
                start_role_weight(n, j)
        if not any((i, n) > (i, m) and plan.uses[i][m] for m in ns):
            for j in plan.added[i]:
                partial_copy(i, j).start()

    ahead = 2
    for stage in stages[:ahead]:
        start_stage(*stage)
    for copy in carry_copies():
        copy.start()
    ready, waiting, step = set(), [], 384
    for index, (i, n) in enumerate(stages):
        low, high = plan.uses[i][n]
        pltpu.make_async_copy(features(i, n), features(i, n), token_sems.at[i, n]).wait()
        for j in range(low, high):
            if (n, j) not in ready:
                ready.add((n, j))
                pltpu.make_async_copy(weight(n, j), weight(n, j), weight_sems.at[n, j]).wait()
        if index + ahead < len(stages):
            start_stage(*stages[index + ahead])
        mine = {
            j: [m for m in ns if plan.uses[i][m] and j in range(*plan.uses[i][m])]
            for j in range(low, high)
        }
        for j in range(low, high):
            if n == mine[j][0] and j in plan.added[i]:
                partial_copy(i, j).wait()

        @pl.loop(0, tokens // step)
        def _(r):
            local = pl.ds(pl.multiple_of(r * step, step), step)
            rows = pl.ds(pl.multiple_of(i * tokens + r * step, step), step)
            term = jnp.dot(
                features_ref[rows, n * slab : (n + 1) * slab],
                weight_ref[n * slab : (n + 1) * slab, low * wide : high * wide],
                preferred_element_type=jnp.float32,
            )
            for j in range(low, high):
                value = term[:, (j - low) * wide : (j - low + 1) * wide]
                if n != mine[j][0] or j in plan.added[i]:
                    value += total_ref[rows, j * wide : (j + 1) * wide]
                if n == mine[j][-1] and j in plan.finished[i]:
                    projected_ref[i % 2, local, :] = value.astype(jnp.bfloat16)
                else:
                    total_ref[rows, j * wide : (j + 1) * wide] = value

        for j in range(low, high):
            if n != mine[j][-1]:
                continue
            if j in plan.finished[i]:
                if waiting:
                    attend_rows(*waiting.pop())
                column = plan.carried[i] * wide // 3
                waiting.append((projected_ref.at[i % 2], outs[i][j], column))
            else:
                out_copy(i, j).start()
    if waiting:
        attend_rows(*waiting.pop())
    for copy in carry_copies():
        copy.wait()
    for i in images:
        for j in plan.jobs(i):
            if j not in plan.finished[i]:
                out_copy(i, j).wait()


def run_jobs(role, tokens, wide, images, weights):
    images = [
        dict(
            image,
            pieces=[
                [[x if isinstance(x, tuple) else (x, 0) for x in owner] for owner in place]
                for place in image["pieces"]
            ],
            sums=image.get("sums", {}),
            finish=image.get("finish", ()),
            carry=image.get("carry", ((), ())),
        )
        for image in images
    ]
    plan = Jobs(
        origins=[[[[r for _, r in o] for o in p] for p in image["pieces"]] for image in images],
        slots=[slot for slot, _, _ in weights],
        first=[first for _, first, _ in weights],
        same=[[not isinstance(w, tuple) for w in row] for _, _, row in weights],
        uses=[image["uses"] for image in images],
        added=[tuple(image["sums"]) for image in images],
        finished=[image["finish"] for image in images],
        carried=[len(image["carry"][0]) for image in images],
    )
    operands = [x for i in images for place in i["pieces"] for owner in place for x, _ in owner]
    slab = operands[0].shape[1] // 2
    for _, _, row in weights:
        for w in row:
            operands += list(w) if isinstance(w, tuple) else [w]
    operands += [x for image in images for x in image["sums"].values()]
    operands += [x for image in images for place in image["carry"] for x in place]
    anywhere, vmem = pl.BlockSpec(memory_space=pl.ANY), pl.BlockSpec(memory_space=pltpu.VMEM)
    head = wide // 3
    shapes, specs = [], []
    for i in range(len(images)):
        for j in plan.jobs(i):
            if j in plan.finished[i]:
                shape = (tokens // 2, head * (plan.carried[i] + 1))
                shapes += [jax.ShapeDtypeStruct(shape, jnp.bfloat16)] * 2
                specs += [vmem] * 2
            else:
                shapes.append(jax.ShapeDtypeStruct((tokens, wide), jnp.float32))
                specs.append(anywhere)
    jobs = 1 + max(j for i in range(len(images)) for j in plan.jobs(i))
    count, depth, total = len(images), len(weights) * slab, len(images) * tokens
    added = sum(high - low for uses in plan.uses for low, high in filter(None, uses))
    got = pl.pallas_call(
        functools.partial(job_kernel, plan),
        out_shape=shapes,
        in_specs=[pl.BlockSpec(memory_space=pltpu.SMEM)] + [anywhere] * len(operands),
        out_specs=specs,
        scratch_shapes=[
            pltpu.VMEM((total, depth), jnp.bfloat16),
            pltpu.VMEM((depth, jobs * wide), jnp.bfloat16),
            pltpu.VMEM((total, jobs * wide), jnp.float32),
            pltpu.VMEM((2, tokens, wide), jnp.bfloat16),
            pltpu.SemaphoreType.DMA((count, len(weights))),
            pltpu.SemaphoreType.DMA((len(weights), jobs)),
            pltpu.SemaphoreType.DMA((count, jobs)),
            pltpu.SemaphoreType.DMA((count, jobs)),
            pltpu.SemaphoreType.DMA((count, 2, max(*plan.carried, 1))),
        ],
        compiler_params=pltpu.CompilerParams(vmem_limit_bytes=62 << 20),
        cost_estimate=pl.CostEstimate(
            flops=2 * tokens * slab * wide * added, bytes_accessed=0, transcendentals=0
        ),
    )(role, *operands)
    got = list(got)
    return [
        {
            j: (got.pop(0), got.pop(0)) if j in plan.finished[i] else got.pop(0)
            for j in plan.jobs(i)
        }
        for i in range(count)
    ]


def join_kernel(place_ref, *refs):
    *parts, out_ref, sems = refs
    count = len(parts) // 2
    inner = place_ref[count]
    wide, head = parts[0].shape[1], parts[count].shape[1]

    def copies(i, role):
        begin = pl.multiple_of(place_ref[i] * wide, wide)
        if role:
            yield parts[i], out_ref.at[:, pl.ds(begin, wide)], sems.at[i, 0]
            return
        kept = wide - head
        yield parts[i].at[:, pl.ds(head, kept)], out_ref.at[:, pl.ds(begin, kept)], sems.at[i, 0]
        last = pl.multiple_of(begin + kept, head)
        yield parts[count + i], out_ref.at[:, pl.ds(last, head)], sems.at[i, 1]

    for role in (1, 0):

        @pl.when((inner == 1) == (role == 1))
        def _():
            every = [pltpu.make_async_copy(*c) for i in range(count) for c in copies(i, role)]
            for copy in every:
                copy.start()
            for copy in every:
                copy.wait()


def join(places, inner, parts, back):
    rows, wide = parts[0].shape
    anywhere = pl.BlockSpec(memory_space=pl.ANY)
    return pl.pallas_call(
        join_kernel,
        out_shape=jax.ShapeDtypeStruct((rows, wide * len(parts)), jnp.bfloat16),
        in_specs=[pl.BlockSpec(memory_space=pltpu.SMEM)] + [anywhere] * (2 * len(parts)),
        out_specs=pl.BlockSpec(memory_space=pltpu.VMEM),
        scratch_shapes=[pltpu.SemaphoreType.DMA((len(parts), 2))],
        cost_estimate=pl.CostEstimate(
            flops=0, bytes_accessed=4 * rows * wide * len(parts), transcendentals=0
        ),
    )(jnp.stack([*places, inner]).astype(jnp.int32), *parts, *back)


def shared(tokens, ln_gain, qkv_weight):
    groups, planes, seqs, cores = (lax.axis_size(a) for a in ("groups", "dp", "seq", "head"))
    group, plane, seq, core = (lax.axis_index(a) for a in ("groups", "dp", "seq", "head"))
    _, rows, _ = tokens.shape
    slab, heads, columns = qkv_weight.shape
    heads, part = heads // groups, rows // cores
    inner = (plane == 1) | (plane == 2)
    wait = lax.optimization_barrier

    def fold(piece):
        piece = piece.reshape(-1, part, columns).transpose(1, 0, 2)
        return piece.reshape(part, -1)

    def pick(for_inner, for_ends):
        return jnp.where(inner, for_inner, for_ends)

    def pair(value):
        return lax.ppermute(value, "dp", [(0, 1), (1, 0), (2, 3), (3, 2)])

    def outward(value):
        return lax.ppermute(value, "dp", [(1, 0), (2, 3)])

    def middle(value):
        return lax.ppermute(value, "dp", [(1, 2), (2, 1)])

    swap = [(0, 1), (1, 0)]
    beside = lambda value: lax.ppermute(value, "seq", swap)
    across = lambda value: lax.ppermute(value, "groups", swap)

    def others(*values):
        got = []
        for value in values:
            if got:
                value, got[-1] = wait((value, got[-1]))
            got.append(lax.ppermute(value, "head", swap))
        return got


    def exchange(mixed):
        got = []
        for a in range(groups):
            for b in range(seqs):
                sent = mixed[a * seqs + b]
                if a or b:
                    steps = [
                        (g * seqs + s, (g + a) % groups * seqs + (s + b) % seqs)
                        for g in range(groups)
                        for s in range(seqs)
                    ]
                    sent = lax.ppermute(sent, ("groups", "seq"), steps)
                got.append(sent)
        return got

    weight = qkv_weight.transpose(1, 0, 2)
    order = slab_order(plane)
    normed, (own0,) = normalize_part(
        tokens, ln_gain, weight, part, core, order, group * heads
    )
    normed, own0, later_weight = wait((normed, own0, weight))
    cut0, cut1 = normed
    pair1, middle1 = pair(own0), middle(own0)
    beside1, across1 = beside(cut0), across(cut0)
    own1, own2 = [
        lax.dynamic_index_in_dim(later_weight, group * heads + j, 0, keepdims=False) for j in (1, 2)
    ]
    give = pick(fold(own1), cut0)
    role = jnp.stack([core, inner]).astype(jnp.int32)
    beside1, across1, own1, own2, cut1, tokens, give, role = wait(
        (beside1, across1, own1, own2, cut1, tokens, give, role)
    )
    pair1, middle1, give = wait((pair1, middle1, give))
    run = functools.partial(run_jobs, role, seqs * rows, columns)

    pair2, middle2 = pair(give), middle(pair1)
    beside2, across2 = beside(cut1), across(cut1)
    give = pick(fold(middle1), cut1)
    far_normed, _ = normalize_part(tokens, ln_gain, weight, part, 1 - core, order)
    far1 = others(beside1, across1)
    pair2, middle2, beside2, across2, across1, own1, own2, far_normed, far1, give = wait(
        (pair2, middle2, beside2, across2, across1, own1, own2, far_normed, far1, give)
    )

    pair3, middle3 = pair(give), middle(own1)
    beside3, across3 = beside(across1), across(beside2)
    give = pick(middle2, own1)
    far2 = others(beside2, across2)
    pair3, middle3, beside3, across3, pair1, pair2, own2, far2, give = wait(
        (pair3, middle3, beside3, across3, pair1, pair2, own2, far2, give)
    )

    pair4, middle4 = pair(give), middle(own2)
    beside4, across4 = beside(pair2), across(pair2)
    give = pick(middle3, own2)
    pieces0 = ((normed, far_normed), ((beside1, beside2), (far1[0], far2[0])))
    owns = [own0, (own1, own0), (own2, own1)]
    ((head0, sum20, sum30),) = [
        tuple(got.values())
        for got in run(
            [dict(pieces=pieces0, uses=[(0, 3), (0, 2), (0, 1), (0, 1)], finish=(0,))],
            [(0, 0, owns), (2, 0, [middle1, (middle3, pair1)]), (1, 0, [pair1]), (3, 0, [middle2])],
        )
    ]
    far3 = others(beside3, across3)
    lent = jnp.concatenate([pair2, pair3])
    pair4, middle4, beside4, across4, own2, pair3, lent, head0, sum20, sum30, far3, give = wait(
        (pair4, middle4, beside4, across4, own2, pair3, lent, head0, sum20, sum30, far3, give)
    )

    pair5, middle5 = pair(give), middle(pair4)
    beside5, across5 = beside(pair3), across(pair3)
    pieces1 = (((across1, across2), (far1[1], far2[1])), ((beside3, across3), far3))
    image1, image0 = run(
        [
            dict(pieces=pieces1, uses=[(0, 3), (0, 3), (0, 2), (0, 1)], finish=(0,)),
            dict(pieces=pieces0, uses=[None, (2, 3), (1, 2), None], sums={1: sum20, 2: sum30}),
        ],
        [
            (0, 0, owns),
            (2, 0, [middle1, (middle3, pair1), (middle4, pair2)]),
            (1, 0, [pair1, (pair4, pair3)]),
            (3, 0, [middle2]),
        ],
    )
    far_lent, far4 = others(lent, beside4)
    pair5, middle5, beside5, across5, across4, image0, image1, far_lent, far4 = wait(
        (
            *(pair5, middle5, beside5, across5, across4),
            *(image0, image1, far_lent, far4),
        )
    )

    pair6, middle6 = outward(middle5), middle(pair5)
    beside6, across6 = beside(across4), across(beside5)
    far5, far_across4 = others(beside5, across4)
    ahead0, ahead1 = run(
        [
            dict(
                pieces=pieces,
                uses=[(0, 1), (1, 2)],
                sums={0: image[1], 1: image[2]},
                finish=(0,),
            )
            for pieces, image in ((pieces0, image0), (pieces1, image1))
        ],
        [(3, 0, [(middle5, pair4)]), (1, 1, [pair5])],
    )
    lent0 = (((pair2, pair3), (far_lent, (far_lent, part))), ((beside4, beside5), (far4, far5)))
    lent_weights = [(0, 0, [pair5]), (1, 0, [middle4]), (2, 0, [own2])]
    ((sum4,),) = [
        tuple(got.values()) for got in run([dict(pieces=lent0, uses=[(0, 1)] * 3)], lent_weights)
    ]
    pair6, middle6, beside6, across6, across5, ahead0, ahead1, sum4, far_across4 = wait(
        (pair6, middle6, beside6, across6, across5, ahead0, ahead1, sum4, far_across4)
    )

    far_across5, *far6 = [
        lax.ppermute(value, "head", swap) for value in (across5, beside6, across6)
    ]
    done0, done1, lent0 = run(
        [
            dict(pieces=p, uses=[(0, 1)], sums={0: x[1]}, finish=(0,), carry=tuple(zip(h, x[0])))
            for p, h, x in ((pieces0, head0, ahead0), (pieces1, image1[0], ahead1))
        ]
        + [dict(pieces=lent0, uses=[(0, 1)], sums={0: sum4}, finish=(0,))],
        [(3, 0, [(middle6, pair6)])],
    )
    lent1 = (((across4, across5), (far_across4, far_across5)), ((beside6, across6), far6))
    (lent1,) = run(
        [dict(pieces=lent1, uses=[(0, 1)] * 4, finish=(0,))], [*lent_weights, (3, 0, [middle6])]
    )

    def hand_back(mixed):
        got = []
        for a in range(groups):
            for b in range(seqs):
                steps = [
                    (
                        (g * planes + z) * seqs + s,
                        ((g + a) % groups * planes + (z ^ 1)) * seqs + (s + b) % seqs,
                    )
                    for g in range(groups)
                    for z in (1, 2)
                    for s in range(seqs)
                ]
                sent = mixed[a * seqs + b]
                got.append(lax.ppermute(sent, ("groups", "dp", "seq"), steps))
        return got

    sent = exchange((*done0[0], *done1[0]))
    back = hand_back((*lent0[0], *lent1[0]))
    places = [
        (seq - b) % seqs * groups + (group - a) % groups
        for a in range(groups)
        for b in range(seqs)
    ]
    return join(places, inner, sent, back)[None]


def per_device(tokens, ln_gain, qkv_weight):
    groups, planes, seqs, cores = (lax.axis_size(a) for a in ("groups", "dp", "seq", "head"))
    images, rows, width = tokens.shape
    slab, heads, _ = qkv_weight.shape
    if (groups, planes, seqs, cores) == (2, 4, 2, 2) and images == 1 and heads == 3 * groups:
        part = rows // cores
        if rows % (32 * cores) == 0 and slab % part == 0 and 2 * slab == qkv_weight.shape[2] * slab // part:
            return shared(tokens, ln_gain, qkv_weight)
    return plain(tokens, ln_gain, qkv_weight)


def solution(mesh):
    return jax.shard_map(
        per_device,
        mesh=mesh,
        in_specs=(P(("groups", "dp"), "seq", None), P(), P("dp", ("seq", "head"), None)),
        out_specs=P(("groups", "dp"), "seq", "head"),
        check_vma=False,
    )
```

```python
import functools
import math

import jax
import jax.numpy as jnp
from jax import lax
from jax.experimental import pallas as pl
from jax.experimental.pallas import tpu as pltpu
from jax.sharding import PartitionSpec as P


def normalize(array, gain):
    widened = array.astype(jnp.float32)
    centered = widened - jnp.mean(widened, axis=-1, keepdims=True)
    variance = jnp.mean(centered * centered, axis=-1, keepdims=True)
    return (centered * lax.rsqrt(variance + 1e-06) * gain).astype(jnp.bfloat16)


def attend(projected):
    width = projected.shape[2] // 3
    queries = projected[:, :, :width]
    key_rows = projected[:, :, width : 2 * width]
    value_rows = projected[:, :, 2 * width :]
    scores = jnp.einsum("qhd,khd->hqk", queries, key_rows, preferred_element_type=jnp.float32) * (
        1.0 / math.sqrt(width)
    )
    highest = jnp.max(scores, axis=-1, keepdims=True)
    expo = jnp.exp(scores - highest)
    probs = (expo / jnp.sum(expo, axis=-1, keepdims=True)).astype(jnp.bfloat16)
    mixed = jnp.einsum("hqk,khd->qhd", probs, value_rows, preferred_element_type=jnp.float32)
    return mixed.astype(jnp.bfloat16).reshape(projected.shape[0], -1)


def plain(tokens, ln_gain, qkv_weight):
    images = tokens.shape[0]
    width = tokens.shape[2]
    heads_here = qkv_weight.shape[1]
    columns = heads_here * qkv_weight.shape[2]
    source = normalize(tokens, ln_gain)
    half_width = width // lax.axis_size("head")
    core_index = lax.axis_index("head")
    own_half = lax.dynamic_slice_in_dim(source, core_index * half_width, half_width, 2)
    fetched = lax.all_gather(own_half, "seq", axis=1, tiled=True)
    gathered = lax.all_gather(fetched, "head", axis=2, tiled=True)
    full_tokens = gathered.shape[1]
    features = gathered.reshape(images * full_tokens, width)
    piece = lax.all_gather(qkv_weight, "dp", axis=0, tiled=True)
    projected = jnp.dot(
        features, piece.reshape(piece.shape[0], columns), preferred_element_type=jnp.float32
    )
    projected = projected.astype(jnp.bfloat16).reshape(
        images, full_tokens, heads_here, qkv_weight.shape[2]
    )
    mixed = lax.map(attend, projected)
    return lax.all_to_all(mixed, "seq", split_axis=1, concat_axis=2, tiled=True)


def slab_order(plane):
    inner = (plane == 1) | (plane == 2)
    near, far = plane ^ 1, 2 - plane // 2
    return plane, jnp.where(inner, near, far), jnp.where(inner, far, near), 3 - 3 * (plane // 2)


def normalize_kernel(place_ref, tokens_ref, gain_ref, weight_ref, *refs):
    normed_refs, rest = refs[:2], refs[2:]
    rows, width = tokens_ref.shape[1:]
    lanes = 128
    slab = width // 4
    step, steps = pl.program_id(0), pl.num_programs(0)
    if rest:
        own_ref, own_buf, own_sems = rest
        own_in = pltpu.make_async_copy(weight_ref.at[place_ref[5]], own_buf, own_sems.at[0])
        own_out = pltpu.make_async_copy(own_buf, own_ref, own_sems.at[1])

        @pl.when(step == 0)
        def _():
            own_in.start()

        @pl.when(step == 1)
        def _():
            own_in.wait()
            own_out.start()

    def widened(begin):
        return tokens_ref[0, :, pl.ds(begin, lanes)].astype(jnp.float32)

    def sums(block, total):
        for begin in range(0, slab, lanes):
            total += widened(pl.multiple_of(block * slab + begin, lanes))
        return total

    zero = jnp.zeros((rows, lanes), jnp.float32)
    mean = jnp.sum(lax.fori_loop(0, 4, sums, zero), axis=-1, keepdims=True) / width

    def squares(block, total):
        for begin in range(0, slab, lanes):
            centered = widened(pl.multiple_of(block * slab + begin, lanes)) - mean
            total += centered * centered
        return total

    total = lax.fori_loop(0, 4, squares, zero)
    scale = lax.rsqrt(jnp.sum(total, axis=-1, keepdims=True) / width + 1e-06)
    for cut, normed_ref in enumerate(normed_refs):

        @pl.loop(0, 2)
        def _(half):
            for begin in range(0, slab, lanes):
                column = pl.multiple_of(place_ref[1 + 2 * cut + half] * slab + begin, lanes)
                part = (widened(column) - mean) * scale * gain_ref[:, pl.ds(column, lanes)]
                target = pl.multiple_of(half * slab + begin, lanes)
                normed_ref[:, pl.ds(target, lanes)] = part.astype(jnp.bfloat16)

    if rest:

        @pl.when(step == steps - 1)
        def _():
            own_out.wait()


def normalize_part(tokens, ln_gain, weight, part, core, order, head=None):
    width = tokens.shape[2]
    piece = weight.shape[1:]
    step = 64 if part % 64 == 0 else 32
    steps = part // step
    place = [core, *order] + ([] if head is None else [head])
    place = jnp.stack([jnp.asarray(v, jnp.int32) for v in place])
    half = jax.ShapeDtypeStruct((part, width // 2), jnp.bfloat16)
    anywhere = pl.BlockSpec(memory_space=pl.ANY)
    got = pl.pallas_call(
        normalize_kernel,
        out_shape=[half] * 2 + [jax.ShapeDtypeStruct(piece, jnp.bfloat16)] * (head is not None),
        grid_spec=pltpu.PrefetchScalarGridSpec(
            num_scalar_prefetch=1,
            grid=(steps,),
            in_specs=[
                pl.BlockSpec((1, step, width), lambda i, place: (0, place[0] * steps + i, 0)),
                pl.BlockSpec((1, width), lambda i, place: (0, 0)),
                anywhere,
            ],
            out_specs=[pl.BlockSpec((step, width // 2), lambda i, place: (i, 0))] * 2
            + [anywhere] * (head is not None),
            scratch_shapes=[pltpu.VMEM(piece, jnp.bfloat16), pltpu.SemaphoreType.DMA((2,))]
            if head is not None
            else [],
        ),
        compiler_params=pltpu.CompilerParams(vmem_limit_bytes=62 << 20),
        cost_estimate=pl.CostEstimate(
            flops=8 * part * width, bytes_accessed=4 * part * width, transcendentals=part
        ),
    )(place, tokens, ln_gain[None], weight)
    return got[:2], got[2:]


def attend_rows(projected_ref, parts, column):
    width = projected_ref.shape[1] // 3
    key_rows = projected_ref[:, width : 2 * width]
    value_rows = projected_ref[:, 2 * width :]
    value_rows = jnp.concatenate([value_rows, jnp.ones_like(value_rows)], axis=1)
    begin = 0
    for part in parts:
        step = part.shape[0]
        queries = projected_ref[begin : begin + step, :width]
        scores = lax.dot_general(
            queries, key_rows, (((1,), (1,)), ((), ())), preferred_element_type=jnp.float32
        )
        highest = jnp.max(scores, axis=-1, keepdims=True)
        expo = jnp.exp2((scores - highest) * (math.log2(math.e) / math.sqrt(width)))
        mixed = jnp.dot(expo.astype(jnp.bfloat16), value_rows, preferred_element_type=jnp.float32)
        mixed = mixed[:, :width] / mixed[:, width:]
        part[:, column : column + width] = mixed.astype(jnp.bfloat16)
        begin += step


class Jobs:
    def __init__(self, **numbers):
        self.__dict__.update(numbers)

    def jobs(self, image):
        return sorted({j for use in self.uses[image] if use for j in range(*use)})


def job_kernel(plan, role_ref, *refs):
    refs = list(refs)
    take = lambda n: [refs.pop(0) for _ in range(n)]
    images, ns = range(len(plan.uses)), range(len(plan.slots))
    pieces = [[[take(2) for _ in place] for place in image] for image in plan.origins]
    weights = [[take(1) * 2 if alike else take(2) for alike in row] for row in plan.same]
    partials = [{j: take(1)[0] for j in plan.added[i]} for i in images]
    carried = [[take(plan.carried[i]) for _ in range(2)] for i in images]
    outs = [
        {j: take(2) if j in plan.finished[i] else take(1)[0] for j in plan.jobs(i)} for i in images
    ]
    features_ref, weight_ref, total_ref, projected_ref = take(4)
    token_sems, weight_sems, sum_sems, out_sems, carry_sems = take(5)
    core, inner = role_ref[0], role_ref[1]
    slab = pieces[0][0][0][0].shape[1] // 2
    tokens, wide = projected_ref.shape[1:]
    part = tokens // 4

    def features(i, n):
        return features_ref.at[pl.ds(i * tokens, tokens), pl.ds(n * slab, slab)]

    def weight(n, j):
        return weight_ref.at[pl.ds(n * slab, slab), pl.ds(j * wide, wide)]

    def total(i, j):
        return total_ref.at[pl.ds(i * tokens, tokens), pl.ds(j * wide, wide)]

    def start_tokens(i, n):
        cut, begin = plan.slots[n] // 2, plan.slots[n] % 2 * slab
        for place in range(2):
            split = len(plan.origins[i][place])
            for owner in range(split):
                row = i * tokens + 2 * place * part
                if split == 2:
                    row += (1 - core if owner else core) * part
                count = 2 * part // split
                from_rows = pl.ds(plan.origins[i][place][owner][cut], count)
                rows = pl.ds(pl.multiple_of(row, 32), count)
                pltpu.make_async_copy(
                    pieces[i][place][owner][cut].at[from_rows, pl.ds(begin, slab)],
                    features_ref.at[rows, pl.ds(n * slab, slab)],
                    token_sems.at[i, n],
                ).start()

    def start_weight(n, j, role):
        source = weights[n][j - plan.first[n]][role]
        if source.shape[0] == slab:
            pltpu.make_async_copy(source, weight(n, j), weight_sems.at[n, j]).start()
            return
        for b in range(source.shape[1] // wide):
            pltpu.make_async_copy(
                source.at[:, pl.ds(b * wide, wide)],
                weight_ref.at[pl.ds(n * slab + b * part, part), pl.ds(j * wide, wide)],
                weight_sems.at[n, j],
            ).start()

    def start_role_weight(n, j):
        if plan.same[n][j - plan.first[n]]:
            start_weight(n, j, 0)
            return

        @pl.when(inner == 1)
        def _():
            start_weight(n, j, 0)

        @pl.when(inner != 1)
        def _():
            start_weight(n, j, 1)

    def partial_copy(i, j):
        return pltpu.make_async_copy(partials[i][j], total(i, j), sum_sems.at[i, j])

    def out_copy(i, j):
        return pltpu.make_async_copy(total(i, j), outs[i][j], out_sems.at[i, j])

    def carry_copies():
        for i in images:
            for place in range(2):
                for k in range(plan.carried[i]):
                    (finished,) = plan.finished[i]
                    target = outs[i][finished][place].at[:, pl.ds(k * wide // 3, wide // 3)]
                    yield pltpu.make_async_copy(
                        carried[i][place][k], target, carry_sems.at[i, place, k]
                    )

    stages = [(i, n) for i in images for n in ns if plan.uses[i][n]]
    held = set()

    def start_stage(i, n):
        start_tokens(i, n)
        for j in range(*plan.uses[i][n]):
            if (n, j) not in held:
                held.add((n, j))
                start_role_weight(n, j)
        if not any((i, n) > (i, m) and plan.uses[i][m] for m in ns):
            for j in plan.added[i]:
                partial_copy(i, j).start()

    ahead = 2
    for stage in stages[:ahead]:
        start_stage(*stage)
    for copy in carry_copies():
        copy.start()
    ready, waiting, step = set(), [], plan.step
    for index, (i, n) in enumerate(stages):
        low, high = plan.uses[i][n]
        pltpu.make_async_copy(features(i, n), features(i, n), token_sems.at[i, n]).wait()
        for j in range(low, high):
            if (n, j) not in ready:
                ready.add((n, j))
                pltpu.make_async_copy(weight(n, j), weight(n, j), weight_sems.at[n, j]).wait()
        if index + ahead < len(stages):
            start_stage(*stages[index + ahead])
        mine = {
            j: [m for m in ns if plan.uses[i][m] and j in range(*plan.uses[i][m])]
            for j in range(low, high)
        }
        for j in range(low, high):
            if n == mine[j][0] and j in plan.added[i]:
                partial_copy(i, j).wait()

        def project(r):
            local = pl.ds(pl.multiple_of(r * step, step), step)
            rows = pl.ds(pl.multiple_of(i * tokens + r * step, step), step)
            term = jnp.dot(
                features_ref[rows, n * slab : (n + 1) * slab],
                weight_ref[n * slab : (n + 1) * slab, low * wide : high * wide],
                preferred_element_type=jnp.float32,
            )
            for j in range(low, high):
                value = term[:, (j - low) * wide : (j - low + 1) * wide]
                if n != mine[j][0] or j in plan.added[i]:
                    value += total_ref[rows, j * wide : (j + 1) * wide]
                if n == mine[j][-1] and j in plan.finished[i]:
                    projected_ref[i % 2, local, :] = value.astype(jnp.bfloat16)
                else:
                    total_ref[rows, j * wide : (j + 1) * wide] = value

        if step == tokens:
            project(0)
        else:
            pl.loop(0, tokens // step)(project)

        for j in range(low, high):
            if n != mine[j][-1]:
                continue
            if j in plan.finished[i]:
                if waiting:
                    attend_rows(*waiting.pop())
                column = plan.carried[i] * wide // 3
                waiting.append((projected_ref.at[i % 2], outs[i][j], column))
            else:
                out_copy(i, j).start()
    if waiting:
        attend_rows(*waiting.pop())
    for copy in carry_copies():
        copy.wait()
    for i in images:
        for j in plan.jobs(i):
            if j not in plan.finished[i]:
                out_copy(i, j).wait()


def run_jobs(role, tokens, wide, images, weights, step=384):
    images = [
        dict(
            image,
            pieces=[
                [[x if isinstance(x, tuple) else (x, 0) for x in owner] for owner in place]
                for place in image["pieces"]
            ],
            sums=image.get("sums", {}),
            finish=image.get("finish", ()),
            carry=image.get("carry", ((), ())),
        )
        for image in images
    ]
    plan = Jobs(
        origins=[[[[r for _, r in o] for o in p] for p in image["pieces"]] for image in images],
        slots=[slot for slot, _, _ in weights],
        first=[first for _, first, _ in weights],
        same=[[not isinstance(w, tuple) for w in row] for _, _, row in weights],
        uses=[image["uses"] for image in images],
        added=[tuple(image["sums"]) for image in images],
        finished=[image["finish"] for image in images],
        carried=[len(image["carry"][0]) for image in images],
        step=step,
    )
    operands = [x for i in images for place in i["pieces"] for owner in place for x, _ in owner]
    slab = operands[0].shape[1] // 2
    for _, _, row in weights:
        for w in row:
            operands += list(w) if isinstance(w, tuple) else [w]
    operands += [x for image in images for x in image["sums"].values()]
    operands += [x for image in images for place in image["carry"] for x in place]
    anywhere, vmem = pl.BlockSpec(memory_space=pl.ANY), pl.BlockSpec(memory_space=pltpu.VMEM)
    head = wide // 3
    shapes, specs = [], []
    for i in range(len(images)):
        for j in plan.jobs(i):
            if j in plan.finished[i]:
                shape = (tokens // 2, head * (plan.carried[i] + 1))
                shapes += [jax.ShapeDtypeStruct(shape, jnp.bfloat16)] * 2
                specs += [vmem] * 2
            else:
                shapes.append(jax.ShapeDtypeStruct((tokens, wide), jnp.float32))
                specs.append(anywhere)
    jobs = 1 + max(j for i in range(len(images)) for j in plan.jobs(i))
    count, depth, total = len(images), len(weights) * slab, len(images) * tokens
    added = sum(high - low for uses in plan.uses for low, high in filter(None, uses))
    got = pl.pallas_call(
        functools.partial(job_kernel, plan),
        out_shape=shapes,
        in_specs=[pl.BlockSpec(memory_space=pltpu.SMEM)] + [anywhere] * len(operands),
        out_specs=specs,
        scratch_shapes=[
            pltpu.VMEM((total, depth), jnp.bfloat16),
            pltpu.VMEM((depth, jobs * wide), jnp.bfloat16),
            pltpu.VMEM((total, jobs * wide), jnp.float32),
            pltpu.VMEM((2, tokens, wide), jnp.bfloat16),
            pltpu.SemaphoreType.DMA((count, len(weights))),
            pltpu.SemaphoreType.DMA((len(weights), jobs)),
            pltpu.SemaphoreType.DMA((count, jobs)),
            pltpu.SemaphoreType.DMA((count, jobs)),
            pltpu.SemaphoreType.DMA((count, 2, max(*plan.carried, 1))),
        ],
        compiler_params=pltpu.CompilerParams(vmem_limit_bytes=62 << 20),
        cost_estimate=pl.CostEstimate(
            flops=2 * tokens * slab * wide * added, bytes_accessed=0, transcendentals=0
        ),
    )(role, *operands)
    got = list(got)
    return [
        {
            j: (got.pop(0), got.pop(0)) if j in plan.finished[i] else got.pop(0)
            for j in plan.jobs(i)
        }
        for i in range(count)
    ]


def join_kernel(place_ref, *refs):
    *parts, out_ref, sems = refs
    count = len(parts) // 2
    inner = place_ref[count]
    wide, head = parts[0].shape[1], parts[count].shape[1]

    def copies(i, role):
        begin = pl.multiple_of(place_ref[i] * wide, wide)
        if role:
            yield parts[i], out_ref.at[:, pl.ds(begin, wide)], sems.at[i, 0]
            return
        kept = wide - head
        yield parts[i].at[:, pl.ds(head, kept)], out_ref.at[:, pl.ds(begin, kept)], sems.at[i, 0]
        last = pl.multiple_of(begin + kept, head)
        yield parts[count + i], out_ref.at[:, pl.ds(last, head)], sems.at[i, 1]

    for role in (1, 0):

        @pl.when((inner == 1) == (role == 1))
        def _():
            every = [pltpu.make_async_copy(*c) for i in range(count) for c in copies(i, role)]
            for copy in every:
                copy.start()
            for copy in every:
                copy.wait()


def join(places, inner, parts, back):
    rows, wide = parts[0].shape
    anywhere = pl.BlockSpec(memory_space=pl.ANY)
    return pl.pallas_call(
        join_kernel,
        out_shape=jax.ShapeDtypeStruct((rows, wide * len(parts)), jnp.bfloat16),
        in_specs=[pl.BlockSpec(memory_space=pltpu.SMEM)] + [anywhere] * (2 * len(parts)),
        out_specs=pl.BlockSpec(memory_space=pltpu.VMEM),
        scratch_shapes=[pltpu.SemaphoreType.DMA((len(parts), 2))],
        cost_estimate=pl.CostEstimate(
            flops=0, bytes_accessed=4 * rows * wide * len(parts), transcendentals=0
        ),
    )(jnp.stack([*places, inner]).astype(jnp.int32), *parts, *back)


def shared(tokens, ln_gain, qkv_weight):
    groups, planes, seqs, cores = (lax.axis_size(a) for a in ("groups", "dp", "seq", "head"))
    group, plane, seq, core = (lax.axis_index(a) for a in ("groups", "dp", "seq", "head"))
    _, rows, _ = tokens.shape
    slab, heads, columns = qkv_weight.shape
    heads, part = heads // groups, rows // cores
    inner = (plane == 1) | (plane == 2)
    wait = lax.optimization_barrier

    def fold(piece):
        piece = piece.reshape(-1, part, columns).transpose(1, 0, 2)
        return piece.reshape(part, -1)

    def pick(for_inner, for_ends):
        return jnp.where(inner, for_inner, for_ends)

    def pair(value):
        return lax.ppermute(value, "dp", [(0, 1), (1, 0), (2, 3), (3, 2)])

    def outward(value):
        return lax.ppermute(value, "dp", [(1, 0), (2, 3)])

    def middle(value):
        return lax.ppermute(value, "dp", [(1, 2), (2, 1)])

    swap = [(0, 1), (1, 0)]
    beside = lambda value: lax.ppermute(value, "seq", swap)
    across = lambda value: lax.ppermute(value, "groups", swap)

    def others(*values):
        got = []
        for value in values:
            if got:
                value, got[-1] = wait((value, got[-1]))
            got.append(lax.ppermute(value, "head", swap))
        return got


    def exchange(mixed):
        got = []
        for a in range(groups):
            for b in range(seqs):
                sent = mixed[a * seqs + b]
                if a or b:
                    steps = [
                        (g * seqs + s, (g + a) % groups * seqs + (s + b) % seqs)
                        for g in range(groups)
                        for s in range(seqs)
                    ]
                    sent = lax.ppermute(sent, ("groups", "seq"), steps)
                got.append(sent)
        return got

    weight = qkv_weight.transpose(1, 0, 2)
    order = slab_order(plane)
    normed, (own0,) = normalize_part(
        tokens, ln_gain, weight, part, core, order, group * heads
    )
    normed, own0, later_weight = wait((normed, own0, weight))
    cut0, cut1 = normed
    pair1, middle1 = pair(own0), middle(own0)
    beside1, across1 = beside(cut0), across(cut0)
    own1, own2 = [
        lax.dynamic_index_in_dim(later_weight, group * heads + j, 0, keepdims=False) for j in (1, 2)
    ]
    give = pick(fold(own1), cut0)
    role = jnp.stack([core, inner]).astype(jnp.int32)
    beside1, across1, own1, own2, cut1, tokens, give, role = wait(
        (beside1, across1, own1, own2, cut1, tokens, give, role)
    )
    pair1, middle1, give = wait((pair1, middle1, give))
    run = functools.partial(run_jobs, role, seqs * rows, columns)

    pair2, middle2 = pair(give), middle(pair1)
    beside2, across2 = beside(cut1), across(cut1)
    give = pick(fold(middle1), cut1)
    far_normed, _ = normalize_part(tokens, ln_gain, weight, part, 1 - core, order)
    far1 = others(beside1, across1)
    pair2, middle2, beside2, across2, across1, own1, own2, far_normed, far1, give = wait(
        (pair2, middle2, beside2, across2, across1, own1, own2, far_normed, far1, give)
    )

    pair3, middle3 = pair(give), middle(own1)
    beside3, across3 = beside(across1), across(beside2)
    give = pick(middle2, own1)
    far2 = others(beside2, across2)
    pair3, middle3, beside3, across3, pair1, pair2, own2, far2, give = wait(
        (pair3, middle3, beside3, across3, pair1, pair2, own2, far2, give)
    )

    pair4, middle4 = pair(give), middle(own2)
    beside4, across4 = beside(pair2), across(pair2)
    give = pick(middle3, own2)
    pieces0 = ((normed, far_normed), ((beside1, beside2), (far1[0], far2[0])))
    owns = [own0, (own1, own0), (own2, own1)]
    ((head0, sum20, sum30),) = [
        tuple(got.values())
        for got in run(
            [dict(pieces=pieces0, uses=[(0, 3), (0, 2), (0, 1), (0, 1)], finish=(0,))],
            [(0, 0, owns), (2, 0, [middle1, (middle3, pair1)]), (1, 0, [pair1]), (3, 0, [middle2])],
        )
    ]
    far3 = others(beside3, across3)
    lent = jnp.concatenate([pair2, pair3])
    pair4, middle4, beside4, across4, own2, pair3, lent, head0, sum20, sum30, far3, give = wait(
        (pair4, middle4, beside4, across4, own2, pair3, lent, head0, sum20, sum30, far3, give)
    )

    pair5, middle5 = pair(give), middle(pair4)
    beside5, across5 = beside(pair3), across(pair3)
    pieces1 = (((across1, across2), (far1[1], far2[1])), ((beside3, across3), far3))
    image1, image0 = run(
        [
            dict(pieces=pieces1, uses=[(0, 3), (0, 3), (0, 2), (0, 1)], finish=(0,)),
            dict(pieces=pieces0, uses=[None, (2, 3), (1, 2), None], sums={1: sum20, 2: sum30}),
        ],
        [
            (0, 0, owns),
            (2, 0, [middle1, (middle3, pair1), (middle4, pair2)]),
            (1, 0, [pair1, (pair4, pair3)]),
            (3, 0, [middle2]),
        ],
    )
    far_lent, far4 = others(lent, beside4)
    pair5, middle5, beside5, across5, across4, image0, image1, far_lent, far4 = wait(
        (
            *(pair5, middle5, beside5, across5, across4),
            *(image0, image1, far_lent, far4),
        )
    )

    pair6, middle6 = outward(middle5), middle(pair5)
    beside6, across6 = beside(across4), across(beside5)
    far5, far_across4 = others(beside5, across4)
    ahead0, ahead1 = run(
        [
            dict(
                pieces=pieces,
                uses=[(0, 1), (1, 2)],
                sums={0: image[1], 1: image[2]},
                finish=(0,),
            )
            for pieces, image in ((pieces0, image0), (pieces1, image1))
        ],
        [(3, 0, [(middle5, pair4)]), (1, 1, [pair5])],
    )
    lent0 = (((pair2, pair3), (far_lent, (far_lent, part))), ((beside4, beside5), (far4, far5)))
    lent_weights = [(0, 0, [pair5]), (1, 0, [middle4]), (2, 0, [own2])]
    ((sum4,),) = [
        tuple(got.values()) for got in run([dict(pieces=lent0, uses=[(0, 1)] * 3)], lent_weights)
    ]
    pair6, middle6, beside6, across6, across5, ahead0, ahead1, sum4, far_across4 = wait(
        (pair6, middle6, beside6, across6, across5, ahead0, ahead1, sum4, far_across4)
    )

    far_across5, *far6 = [
        lax.ppermute(value, "head", swap) for value in (across5, beside6, across6)
    ]
    done0, done1, lent0 = run(
        [
            dict(pieces=p, uses=[(0, 1)], sums={0: x[1]}, finish=(0,), carry=tuple(zip(h, x[0])))
            for p, h, x in ((pieces0, head0, ahead0), (pieces1, image1[0], ahead1))
        ]
        + [dict(pieces=lent0, uses=[(0, 1)], sums={0: sum4}, finish=(0,))],
        [(3, 0, [(middle6, pair6)])],
    )
    lent1 = (((across4, across5), (far_across4, far_across5)), ((beside6, across6), far6))
    (lent1,) = run(
        [dict(pieces=lent1, uses=[(0, 1)] * 4, finish=(0,))],
        [*lent_weights, (3, 0, [middle6])],
        step=seqs * rows,
    )

    def hand_back(mixed):
        got = []
        for a in range(groups):
            for b in range(seqs):
                steps = [
                    (
                        (g * planes + z) * seqs + s,
                        ((g + a) % groups * planes + (z ^ 1)) * seqs + (s + b) % seqs,
                    )
                    for g in range(groups)
                    for z in (1, 2)
                    for s in range(seqs)
                ]
                sent = mixed[a * seqs + b]
                got.append(lax.ppermute(sent, ("groups", "dp", "seq"), steps))
        return got

    sent = exchange((*done0[0], *done1[0]))
    back = hand_back((*lent0[0], *lent1[0]))
    places = [
        (seq - b) % seqs * groups + (group - a) % groups
        for a in range(groups)
        for b in range(seqs)
    ]
    return join(places, inner, sent, back)[None]


def per_device(tokens, ln_gain, qkv_weight):
    groups, planes, seqs, cores = (lax.axis_size(a) for a in ("groups", "dp", "seq", "head"))
    images, rows, width = tokens.shape
    slab, heads, _ = qkv_weight.shape
    if (groups, planes, seqs, cores) == (2, 4, 2, 2) and images == 1 and heads == 3 * groups:
        part = rows // cores
        if rows % (32 * cores) == 0 and slab % part == 0 and 2 * slab == qkv_weight.shape[2] * slab // part:
            return shared(tokens, ln_gain, qkv_weight)
    return plain(tokens, ln_gain, qkv_weight)


def solution(mesh):
    return jax.shard_map(
        per_device,
        mesh=mesh,
        in_specs=(P(("groups", "dp"), "seq", None), P(), P("dp", ("seq", "head"), None)),
        out_specs=P(("groups", "dp"), "seq", "head"),
        check_vma=False,
    )
```

```python
import functools
import math

import jax
import jax.numpy as jnp
from jax import lax
from jax.experimental import pallas as pl
from jax.experimental.pallas import tpu as pltpu
from jax.sharding import PartitionSpec as P


def normalize(array, gain):
    widened = array.astype(jnp.float32)
    centered = widened - jnp.mean(widened, axis=-1, keepdims=True)
    variance = jnp.mean(centered * centered, axis=-1, keepdims=True)
    return (centered * lax.rsqrt(variance + 1e-06) * gain).astype(jnp.bfloat16)


def attend(projected):
    width = projected.shape[2] // 3
    queries = projected[:, :, :width]
    key_rows = projected[:, :, width : 2 * width]
    value_rows = projected[:, :, 2 * width :]
    scores = jnp.einsum("qhd,khd->hqk", queries, key_rows, preferred_element_type=jnp.float32) * (
        1.0 / math.sqrt(width)
    )
    highest = jnp.max(scores, axis=-1, keepdims=True)
    expo = jnp.exp(scores - highest)
    probs = (expo / jnp.sum(expo, axis=-1, keepdims=True)).astype(jnp.bfloat16)
    mixed = jnp.einsum("hqk,khd->qhd", probs, value_rows, preferred_element_type=jnp.float32)
    return mixed.astype(jnp.bfloat16).reshape(projected.shape[0], -1)


def plain(tokens, ln_gain, qkv_weight):
    images = tokens.shape[0]
    width = tokens.shape[2]
    heads_here = qkv_weight.shape[1]
    columns = heads_here * qkv_weight.shape[2]
    source = normalize(tokens, ln_gain)
    half_width = width // lax.axis_size("head")
    core_index = lax.axis_index("head")
    own_half = lax.dynamic_slice_in_dim(source, core_index * half_width, half_width, 2)
    fetched = lax.all_gather(own_half, "seq", axis=1, tiled=True)
    gathered = lax.all_gather(fetched, "head", axis=2, tiled=True)
    full_tokens = gathered.shape[1]
    features = gathered.reshape(images * full_tokens, width)
    piece = lax.all_gather(qkv_weight, "dp", axis=0, tiled=True)
    projected = jnp.dot(
        features, piece.reshape(piece.shape[0], columns), preferred_element_type=jnp.float32
    )
    projected = projected.astype(jnp.bfloat16).reshape(
        images, full_tokens, heads_here, qkv_weight.shape[2]
    )
    mixed = lax.map(attend, projected)
    return lax.all_to_all(mixed, "seq", split_axis=1, concat_axis=2, tiled=True)


def slab_order(plane):
    inner = (plane == 1) | (plane == 2)
    near, far = plane ^ 1, 2 - plane // 2
    return plane, jnp.where(inner, near, far), jnp.where(inner, far, near), 3 - 3 * (plane // 2)


def normalize_kernel(place_ref, tokens_ref, gain_ref, weight_ref, *refs):
    normed_refs, rest = refs[:2], refs[2:]
    rows, width = tokens_ref.shape[1:]
    lanes = 128
    slab, span = width // 4, width // 2
    step, steps = pl.program_id(0), pl.num_programs(0)
    if rest:
        own_ref, own_buf, own_sems = rest
        own_in = pltpu.make_async_copy(weight_ref.at[place_ref[5]], own_buf, own_sems.at[0])
        own_out = pltpu.make_async_copy(own_buf, own_ref, own_sems.at[1])

        @pl.when(step == 0)
        def _():
            own_in.start()

        @pl.when(step == 1)
        def _():
            own_in.wait()
            own_out.start()

    def widened(begin):
        return tokens_ref[0, :, pl.ds(begin, lanes)].astype(jnp.float32)

    total = jnp.zeros((rows, lanes), jnp.float32)
    for begin in range(0, width, lanes):
        total += widened(begin)
    mean = jnp.sum(total, axis=-1, keepdims=True) / width
    total = jnp.zeros((rows, lanes), jnp.float32)
    for begin in range(0, width, lanes):
        centered = widened(begin) - mean
        total += centered * centered
    scale = lax.rsqrt(jnp.sum(total, axis=-1, keepdims=True) / width + 1e-06)
    for i in range(4):
        source = place_ref[i + 1] * slab
        for begin in range(0, slab, lanes):
            column = pl.multiple_of(source + begin, lanes)
            part = (widened(column) - mean) * scale * gain_ref[:, pl.ds(column, lanes)]
            target = i * slab % span + begin
            normed_refs[i * slab // span][:, target : target + lanes] = part.astype(jnp.bfloat16)

    if rest:

        @pl.when(step == steps - 1)
        def _():
            own_out.wait()


def normalize_part(tokens, ln_gain, weight, part, core, order, head=None):
    width = tokens.shape[2]
    piece = weight.shape[1:]
    step = 64 if part % 64 == 0 else 32
    steps = part // step
    place = [core, *order] + ([] if head is None else [head])
    place = jnp.stack([jnp.asarray(v, jnp.int32) for v in place])
    half = jax.ShapeDtypeStruct((part, width // 2), jnp.bfloat16)
    anywhere = pl.BlockSpec(memory_space=pl.ANY)
    got = pl.pallas_call(
        normalize_kernel,
        out_shape=[half] * 2 + [jax.ShapeDtypeStruct(piece, jnp.bfloat16)] * (head is not None),
        grid_spec=pltpu.PrefetchScalarGridSpec(
            num_scalar_prefetch=1,
            grid=(steps,),
            in_specs=[
                pl.BlockSpec((1, step, width), lambda i, place: (0, place[0] * steps + i, 0)),
                pl.BlockSpec((1, width), lambda i, place: (0, 0)),
                anywhere,
            ],
            out_specs=[pl.BlockSpec((step, width // 2), lambda i, place: (i, 0))] * 2
            + [anywhere] * (head is not None),
            scratch_shapes=[pltpu.VMEM(piece, jnp.bfloat16), pltpu.SemaphoreType.DMA((2,))]
            if head is not None
            else [],
        ),
        compiler_params=pltpu.CompilerParams(vmem_limit_bytes=62 << 20),
        cost_estimate=pl.CostEstimate(
            flops=8 * part * width, bytes_accessed=4 * part * width, transcendentals=part
        ),
    )(place, tokens, ln_gain[None], weight)
    return got[:2], got[2:]


def attend_rows(projected_ref, parts, column):
    width = projected_ref.shape[1] // 3
    key_rows = projected_ref[:, width : 2 * width]
    value_rows = projected_ref[:, 2 * width :]
    value_rows = jnp.concatenate([value_rows, jnp.ones_like(value_rows)], axis=1)
    begin = 0
    for part in parts:
        step = part.shape[0]
        queries = projected_ref[begin : begin + step, :width]
        scores = lax.dot_general(
            queries, key_rows, (((1,), (1,)), ((), ())), preferred_element_type=jnp.float32
        )
        highest = jnp.max(scores, axis=-1, keepdims=True)
        expo = jnp.exp2((scores - highest) * (math.log2(math.e) / math.sqrt(width)))
        mixed = jnp.dot(expo.astype(jnp.bfloat16), value_rows, preferred_element_type=jnp.float32)
        mixed = mixed[:, :width] / mixed[:, width:]
        part[:, column : column + width] = mixed.astype(jnp.bfloat16)
        begin += step


class Jobs:
    def __init__(self, **numbers):
        self.__dict__.update(numbers)

    def jobs(self, image):
        return sorted({j for use in self.uses[image] if use for j in range(*use)})


def job_kernel(plan, role_ref, *refs):
    refs = list(refs)
    take = lambda n: [refs.pop(0) for _ in range(n)]
    images, ns = range(len(plan.uses)), range(len(plan.slots))
    pieces = [[[take(2) for _ in place] for place in image] for image in plan.origins]
    weights = [[take(1) * 2 if alike else take(2) for alike in row] for row in plan.same]
    partials = [{j: take(1)[0] for j in plan.added[i]} for i in images]
    carried = [[take(plan.carried[i]) for _ in range(2)] for i in images]
    outs = [
        {j: take(2) if j in plan.finished[i] else take(1)[0] for j in plan.jobs(i)} for i in images
    ]
    features_ref, weight_ref, total_ref, projected_ref = take(4)
    token_sems, weight_sems, sum_sems, out_sems, carry_sems = take(5)
    core, inner = role_ref[0], role_ref[1]
    slab = pieces[0][0][0][0].shape[1] // 2
    tokens, wide = projected_ref.shape[1:]
    part = tokens // 4

    def features(i, n):
        return features_ref.at[pl.ds(i * tokens, tokens), pl.ds(n * slab, slab)]

    def weight(n, j):
        return weight_ref.at[pl.ds(n * slab, slab), pl.ds(j * wide, wide)]

    def total(i, j):
        return total_ref.at[pl.ds(i * tokens, tokens), pl.ds(j * wide, wide)]

    def start_tokens(i, n):
        cut, begin = plan.slots[n] // 2, plan.slots[n] % 2 * slab
        for place in range(2):
            split = len(plan.origins[i][place])
            for owner in range(split):
                row = i * tokens + 2 * place * part
                if split == 2:
                    row += (1 - core if owner else core) * part
                count = 2 * part // split
                from_rows = pl.ds(plan.origins[i][place][owner][cut], count)
                rows = pl.ds(pl.multiple_of(row, 32), count)
                pltpu.make_async_copy(
                    pieces[i][place][owner][cut].at[from_rows, pl.ds(begin, slab)],
                    features_ref.at[rows, pl.ds(n * slab, slab)],
                    token_sems.at[i, n],
                ).start()

    def start_weight(n, j, role):
        source = weights[n][j - plan.first[n]][role]
        if source.shape[0] == slab:
            pltpu.make_async_copy(source, weight(n, j), weight_sems.at[n, j]).start()
            return
        for b in range(source.shape[1] // wide):
            pltpu.make_async_copy(
                source.at[:, pl.ds(b * wide, wide)],
                weight_ref.at[pl.ds(n * slab + b * part, part), pl.ds(j * wide, wide)],
                weight_sems.at[n, j],
            ).start()

    def start_role_weight(n, j):
        if plan.same[n][j - plan.first[n]]:
            start_weight(n, j, 0)
            return

        @pl.when(inner == 1)
        def _():
            start_weight(n, j, 0)

        @pl.when(inner != 1)
        def _():
            start_weight(n, j, 1)

    def partial_copy(i, j):
        return pltpu.make_async_copy(partials[i][j], total(i, j), sum_sems.at[i, j])

    def out_copy(i, j):
        return pltpu.make_async_copy(total(i, j), outs[i][j], out_sems.at[i, j])

    def carry_copies():
        for i in images:
            for place in range(2):
                for k in range(plan.carried[i]):
                    (finished,) = plan.finished[i]
                    target = outs[i][finished][place].at[:, pl.ds(k * wide // 3, wide // 3)]
                    yield pltpu.make_async_copy(
                        carried[i][place][k], target, carry_sems.at[i, place, k]
                    )

    stages = [(i, n) for i in images for n in ns if plan.uses[i][n]]
    held = set()

    def start_stage(i, n):
        start_tokens(i, n)
        for j in range(*plan.uses[i][n]):
            if (n, j) not in held:
                held.add((n, j))
                start_role_weight(n, j)
        if not any((i, n) > (i, m) and plan.uses[i][m] for m in ns):
            for j in plan.added[i]:
                partial_copy(i, j).start()

    ahead = 2
    for stage in stages[:ahead]:
        start_stage(*stage)
    for copy in carry_copies():
        copy.start()
    ready, waiting, step = set(), [], plan.step
    for index, (i, n) in enumerate(stages):
        low, high = plan.uses[i][n]
        pltpu.make_async_copy(features(i, n), features(i, n), token_sems.at[i, n]).wait()
        for j in range(low, high):
            if (n, j) not in ready:
                ready.add((n, j))
                pltpu.make_async_copy(weight(n, j), weight(n, j), weight_sems.at[n, j]).wait()
        if index + ahead < len(stages):
            start_stage(*stages[index + ahead])
        mine = {
            j: [m for m in ns if plan.uses[i][m] and j in range(*plan.uses[i][m])]
            for j in range(low, high)
        }
        for j in range(low, high):
            if n == mine[j][0] and j in plan.added[i]:
                partial_copy(i, j).wait()

        def project(r):
            local = pl.ds(pl.multiple_of(r * step, step), step)
            rows = pl.ds(pl.multiple_of(i * tokens + r * step, step), step)
            term = jnp.dot(
                features_ref[rows, n * slab : (n + 1) * slab],
                weight_ref[n * slab : (n + 1) * slab, low * wide : high * wide],
                preferred_element_type=jnp.float32,
            )
            for j in range(low, high):
                value = term[:, (j - low) * wide : (j - low + 1) * wide]
                if n != mine[j][0] or j in plan.added[i]:
                    value += total_ref[rows, j * wide : (j + 1) * wide]
                if n == mine[j][-1] and j in plan.finished[i]:
                    projected_ref[i % 2, local, :] = value.astype(jnp.bfloat16)
                else:
                    total_ref[rows, j * wide : (j + 1) * wide] = value

        if step == tokens:
            project(0)
        else:
            pl.loop(0, tokens // step)(project)

        for j in range(low, high):
            if n != mine[j][-1]:
                continue
            if j in plan.finished[i]:
                if waiting:
                    attend_rows(*waiting.pop())
                column = plan.carried[i] * wide // 3
                waiting.append((projected_ref.at[i % 2], outs[i][j], column))
            else:
                out_copy(i, j).start()
    if waiting:
        attend_rows(*waiting.pop())
    for copy in carry_copies():
        copy.wait()
    for i in images:
        for j in plan.jobs(i):
            if j not in plan.finished[i]:
                out_copy(i, j).wait()


def run_jobs(role, tokens, wide, images, weights, step=384):
    images = [
        dict(
            image,
            pieces=[
                [[x if isinstance(x, tuple) else (x, 0) for x in owner] for owner in place]
                for place in image["pieces"]
            ],
            sums=image.get("sums", {}),
            finish=image.get("finish", ()),
            carry=image.get("carry", ((), ())),
        )
        for image in images
    ]
    plan = Jobs(
        origins=[[[[r for _, r in o] for o in p] for p in image["pieces"]] for image in images],
        slots=[slot for slot, _, _ in weights],
        first=[first for _, first, _ in weights],
        same=[[not isinstance(w, tuple) for w in row] for _, _, row in weights],
        uses=[image["uses"] for image in images],
        added=[tuple(image["sums"]) for image in images],
        finished=[image["finish"] for image in images],
        carried=[len(image["carry"][0]) for image in images],
        step=step,
    )
    operands = [x for i in images for place in i["pieces"] for owner in place for x, _ in owner]
    slab = operands[0].shape[1] // 2
    for _, _, row in weights:
        for w in row:
            operands += list(w) if isinstance(w, tuple) else [w]
    operands += [x for image in images for x in image["sums"].values()]
    operands += [x for image in images for place in image["carry"] for x in place]
    anywhere, vmem = pl.BlockSpec(memory_space=pl.ANY), pl.BlockSpec(memory_space=pltpu.VMEM)
    head = wide // 3
    shapes, specs = [], []
    for i in range(len(images)):
        for j in plan.jobs(i):
            if j in plan.finished[i]:
                shape = (tokens // 2, head * (plan.carried[i] + 1))
                shapes += [jax.ShapeDtypeStruct(shape, jnp.bfloat16)] * 2
                specs += [vmem] * 2
            else:
                shapes.append(jax.ShapeDtypeStruct((tokens, wide), jnp.float32))
                specs.append(anywhere)
    jobs = 1 + max(j for i in range(len(images)) for j in plan.jobs(i))
    count, depth, total = len(images), len(weights) * slab, len(images) * tokens
    added = sum(high - low for uses in plan.uses for low, high in filter(None, uses))
    got = pl.pallas_call(
        functools.partial(job_kernel, plan),
        out_shape=shapes,
        in_specs=[pl.BlockSpec(memory_space=pltpu.SMEM)] + [anywhere] * len(operands),
        out_specs=specs,
        scratch_shapes=[
            pltpu.VMEM((total, depth), jnp.bfloat16),
            pltpu.VMEM((depth, jobs * wide), jnp.bfloat16),
            pltpu.VMEM((total, jobs * wide), jnp.float32),
            pltpu.VMEM((2, tokens, wide), jnp.bfloat16),
            pltpu.SemaphoreType.DMA((count, len(weights))),
            pltpu.SemaphoreType.DMA((len(weights), jobs)),
            pltpu.SemaphoreType.DMA((count, jobs)),
            pltpu.SemaphoreType.DMA((count, jobs)),
            pltpu.SemaphoreType.DMA((count, 2, max(*plan.carried, 1))),
        ],
        compiler_params=pltpu.CompilerParams(vmem_limit_bytes=62 << 20),
        cost_estimate=pl.CostEstimate(
            flops=2 * tokens * slab * wide * added, bytes_accessed=0, transcendentals=0
        ),
    )(role, *operands)
    got = list(got)
    return [
        {
            j: (got.pop(0), got.pop(0)) if j in plan.finished[i] else got.pop(0)
            for j in plan.jobs(i)
        }
        for i in range(count)
    ]


def join_kernel(place_ref, *refs):
    *parts, out_ref, buf, sems = refs
    count = len(parts) // 2
    inner = place_ref[count]
    wide, head = parts[0].shape[1], parts[count].shape[1]
    kept = wide - head

    def arrive(i):
        return pltpu.make_async_copy(parts[i], buf.at[i], sems.at[i, 0])

    def leave(i, role):
        begin = pl.multiple_of(place_ref[i] * wide, wide)
        if role:
            target = out_ref.at[:, pl.ds(begin, wide)]
            return [pltpu.make_async_copy(buf.at[i], target, sems.at[i, 1])]
        first, last = pl.ds(begin, kept), pl.ds(pl.multiple_of(begin + kept, head), head)
        return [
            pltpu.make_async_copy(
                buf.at[i, :, pl.ds(head, kept)], out_ref.at[:, first], sems.at[i, 1]
            ),
            pltpu.make_async_copy(parts[count + i], out_ref.at[:, last], sems.at[i, 2]),
        ]

    for i in range(count):
        arrive(i).start()
    for i in range(count):
        arrive(i).wait()
        for role in (1, 0):

            @pl.when((inner == 1) == (role == 1))
            def _():
                for copy in leave(i, role):
                    copy.start()

    for role in (1, 0):

        @pl.when((inner == 1) == (role == 1))
        def _():
            for i in range(count):
                for copy in leave(i, role):
                    copy.wait()


def join(places, inner, parts, back):
    rows, wide = parts[0].shape
    anywhere, vmem = pl.BlockSpec(memory_space=pl.ANY), pl.BlockSpec(memory_space=pltpu.VMEM)
    return pl.pallas_call(
        join_kernel,
        out_shape=jax.ShapeDtypeStruct((rows, wide * len(parts)), jnp.bfloat16),
        in_specs=[pl.BlockSpec(memory_space=pltpu.SMEM)]
        + [anywhere] * len(parts)
        + [vmem] * len(back),
        out_specs=anywhere,
        scratch_shapes=[
            pltpu.VMEM((len(parts), *parts[0].shape), jnp.bfloat16),
            pltpu.SemaphoreType.DMA((len(parts), 3)),
        ],
        cost_estimate=pl.CostEstimate(
            flops=0, bytes_accessed=4 * rows * wide * len(parts), transcendentals=0
        ),
    )(jnp.stack([*places, inner]).astype(jnp.int32), *parts, *back)


def shared(tokens, ln_gain, qkv_weight):
    groups, planes, seqs, cores = (lax.axis_size(a) for a in ("groups", "dp", "seq", "head"))
    group, plane, seq, core = (lax.axis_index(a) for a in ("groups", "dp", "seq", "head"))
    _, rows, _ = tokens.shape
    slab, heads, columns = qkv_weight.shape
    heads, part = heads // groups, rows // cores
    inner = (plane == 1) | (plane == 2)
    wait = lax.optimization_barrier

    def fold(piece):
        piece = piece.reshape(-1, part, columns).transpose(1, 0, 2)
        return piece.reshape(part, -1)

    def pick(for_inner, for_ends):
        return jnp.where(inner, for_inner, for_ends)

    def pair(value):
        return lax.ppermute(value, "dp", [(0, 1), (1, 0), (2, 3), (3, 2)])

    def outward(value):
        return lax.ppermute(value, "dp", [(1, 0), (2, 3)])

    def middle(value):
        return lax.ppermute(value, "dp", [(1, 2), (2, 1)])

    swap = [(0, 1), (1, 0)]
    beside = lambda value: lax.ppermute(value, "seq", swap)
    across = lambda value: lax.ppermute(value, "groups", swap)

    def others(*values):
        got = []
        for value in values:
            if got:
                value, got[-1] = wait((value, got[-1]))
            got.append(lax.ppermute(value, "head", swap))
        return got


    def exchange(mixed):
        got = []
        for a in range(groups):
            for b in range(seqs):
                sent = mixed[a * seqs + b]
                if a or b:
                    steps = [
                        (g * seqs + s, (g + a) % groups * seqs + (s + b) % seqs)
                        for g in range(groups)
                        for s in range(seqs)
                    ]
                    sent = lax.ppermute(sent, ("groups", "seq"), steps)
                got.append(sent)
        return got

    weight = qkv_weight.transpose(1, 0, 2)
    order = slab_order(plane)
    normed, (own0,) = normalize_part(
        tokens, ln_gain, weight, part, core, order, group * heads
    )
    normed, own0, later_weight = wait((normed, own0, weight))
    cut0, cut1 = normed
    pair1, middle1 = pair(own0), middle(own0)
    beside1, across1 = beside(cut0), across(cut0)
    own1, own2 = [
        lax.dynamic_index_in_dim(later_weight, group * heads + j, 0, keepdims=False) for j in (1, 2)
    ]
    give = pick(fold(own1), cut0)
    role = jnp.stack([core, inner]).astype(jnp.int32)
    beside1, across1, own1, own2, cut1, tokens, give, role = wait(
        (beside1, across1, own1, own2, cut1, tokens, give, role)
    )
    pair1, middle1, give = wait((pair1, middle1, give))
    run = functools.partial(run_jobs, role, seqs * rows, columns)

    pair2, middle2 = pair(give), middle(pair1)
    beside2, across2 = beside(cut1), across(cut1)
    give = pick(fold(middle1), cut1)
    far_normed, _ = normalize_part(tokens, ln_gain, weight, part, 1 - core, order)
    far1 = others(beside1, across1)
    pair2, middle2, beside2, across2, across1, own1, own2, far_normed, far1, give = wait(
        (pair2, middle2, beside2, across2, across1, own1, own2, far_normed, far1, give)
    )

    pair3, middle3 = pair(give), middle(own1)
    beside3, across3 = beside(across1), across(beside2)
    give = pick(middle2, own1)
    far2 = others(across2, beside2)[::-1]
    pair3, middle3, beside3, across3, pair1, pair2, own2, far2, give = wait(
        (pair3, middle3, beside3, across3, pair1, pair2, own2, far2, give)
    )

    pair4, middle4 = pair(give), middle(own2)
    beside4, across4 = beside(pair2), across(pair2)
    give = pick(middle3, own2)
    pieces0 = ((normed, far_normed), ((beside1, beside2), (far1[0], far2[0])))
    owns = [own0, (own1, own0), (own2, own1)]
    ((head0, sum20, sum30),) = [
        tuple(got.values())
        for got in run(
            [dict(pieces=pieces0, uses=[(0, 3), (0, 2), (0, 1), (0, 1)], finish=(0,))],
            [(0, 0, owns), (2, 0, [middle1, (middle3, pair1)]), (1, 0, [pair1]), (3, 0, [middle2])],
        )
    ]
    far3 = others(beside3, across3)
    lent = jnp.concatenate([pair2, pair3])
    pair4, middle4, beside4, across4, own2, pair3, lent, head0, sum20, sum30, far3, give = wait(
        (pair4, middle4, beside4, across4, own2, pair3, lent, head0, sum20, sum30, far3, give)
    )

    pair5, middle5 = pair(give), middle(pair4)
    beside5, across5 = beside(pair3), across(pair3)
    pieces1 = (((across1, across2), (far1[1], far2[1])), ((beside3, across3), far3))
    image1, image0 = run(
        [
            dict(pieces=pieces1, uses=[(0, 3), (0, 3), (0, 2), (0, 1)], finish=(0,)),
            dict(pieces=pieces0, uses=[None, (2, 3), (1, 2), None], sums={1: sum20, 2: sum30}),
        ],
        [
            (0, 0, owns),
            (2, 0, [middle1, (middle3, pair1), (middle4, pair2)]),
            (1, 0, [pair1, (pair4, pair3)]),
            (3, 0, [middle2]),
        ],
    )
    far_lent, far4 = others(lent, beside4)
    pair5, middle5, beside5, across5, across4, image0, image1, far_lent, far4 = wait(
        (
            *(pair5, middle5, beside5, across5, across4),
            *(image0, image1, far_lent, far4),
        )
    )

    pair6, middle6 = outward(middle5), middle(pair5)
    beside6, across6 = beside(across4), across(beside5)
    far_across4, far5 = others(across4, beside5)
    ahead0, ahead1 = run(
        [
            dict(
                pieces=pieces,
                uses=[(0, 1), (1, 2)],
                sums={0: image[1], 1: image[2]},
                finish=(0,),
            )
            for pieces, image in ((pieces0, image0), (pieces1, image1))
        ],
        [(3, 0, [(middle5, pair4)]), (1, 1, [pair5])],
    )
    lent0 = (((pair2, pair3), (far_lent, (far_lent, part))), ((beside4, beside5), (far4, far5)))
    lent_weights = [(0, 0, [pair5]), (1, 0, [middle4]), (2, 0, [own2])]
    ((sum4,),) = [
        tuple(got.values()) for got in run([dict(pieces=lent0, uses=[(0, 1)] * 3)], lent_weights)
    ]
    pair6, middle6, beside6, across6, across5, ahead0, ahead1, sum4, far_across4 = wait(
        (pair6, middle6, beside6, across6, across5, ahead0, ahead1, sum4, far_across4)
    )

    far_across5, *far6 = [
        lax.ppermute(value, "head", swap) for value in (across5, beside6, across6)
    ]
    done0, done1, lent0 = run(
        [
            dict(pieces=p, uses=[(0, 1)], sums={0: x[1]}, finish=(0,), carry=tuple(zip(h, x[0])))
            for p, h, x in ((pieces0, head0, ahead0), (pieces1, image1[0], ahead1))
        ]
        + [dict(pieces=lent0, uses=[(0, 1)], sums={0: sum4}, finish=(0,))],
        [(3, 0, [(middle6, pair6)])],
    )
    lent1 = (((across4, across5), (far_across4, far_across5)), ((beside6, across6), far6))
    (lent1,) = run(
        [dict(pieces=lent1, uses=[(0, 1)] * 4, finish=(0,))],
        [*lent_weights, (3, 0, [middle6])],
        step=seqs * rows,
    )

    def hand_back(mixed):
        got = []
        for a in range(groups):
            for b in range(seqs):
                steps = [
                    (
                        (g * planes + z) * seqs + s,
                        ((g + a) % groups * planes + (z ^ 1)) * seqs + (s + b) % seqs,
                    )
                    for g in range(groups)
                    for z in (1, 2)
                    for s in range(seqs)
                ]
                sent = mixed[a * seqs + b]
                got.append(lax.ppermute(sent, ("groups", "dp", "seq"), steps))
        return got

    sent = exchange((*done0[0], *done1[0]))
    back = hand_back((*lent0[0], *lent1[0]))
    places = [
        (seq - b) % seqs * groups + (group - a) % groups
        for a in range(groups)
        for b in range(seqs)
    ]
    return join(places, inner, sent, back)[None]


def per_device(tokens, ln_gain, qkv_weight):
    groups, planes, seqs, cores = (lax.axis_size(a) for a in ("groups", "dp", "seq", "head"))
    images, rows, width = tokens.shape
    slab, heads, _ = qkv_weight.shape
    if (groups, planes, seqs, cores) == (2, 4, 2, 2) and images == 1 and heads == 3 * groups:
        part = rows // cores
        if rows % (32 * cores) == 0 and slab % part == 0 and 2 * slab == qkv_weight.shape[2] * slab // part:
            return shared(tokens, ln_gain, qkv_weight)
    return plain(tokens, ln_gain, qkv_weight)


def solution(mesh):
    return jax.shard_map(
        per_device,
        mesh=mesh,
        in_specs=(P(("groups", "dp"), "seq", None), P(), P("dp", ("seq", "head"), None)),
        out_specs=P(("groups", "dp"), "seq", "head"),
        check_vma=False,
    )
```

```python
import functools
import math

import jax
import jax.numpy as jnp
from jax import lax
from jax.experimental import pallas as pl
from jax.experimental.pallas import tpu as pltpu
from jax.sharding import PartitionSpec as P


def normalize(array, gain):
    widened = array.astype(jnp.float32)
    centered = widened - jnp.mean(widened, axis=-1, keepdims=True)
    variance = jnp.mean(centered * centered, axis=-1, keepdims=True)
    return (centered * lax.rsqrt(variance + 1e-06) * gain).astype(jnp.bfloat16)


def attend(projected):
    width = projected.shape[2] // 3
    queries = projected[:, :, :width]
    key_rows = projected[:, :, width : 2 * width]
    value_rows = projected[:, :, 2 * width :]
    scores = jnp.einsum("qhd,khd->hqk", queries, key_rows, preferred_element_type=jnp.float32) * (
        1.0 / math.sqrt(width)
    )
    highest = jnp.max(scores, axis=-1, keepdims=True)
    expo = jnp.exp(scores - highest)
    probs = (expo / jnp.sum(expo, axis=-1, keepdims=True)).astype(jnp.bfloat16)
    mixed = jnp.einsum("hqk,khd->qhd", probs, value_rows, preferred_element_type=jnp.float32)
    return mixed.astype(jnp.bfloat16).reshape(projected.shape[0], -1)


def plain(tokens, ln_gain, qkv_weight):
    images = tokens.shape[0]
    width = tokens.shape[2]
    heads_here = qkv_weight.shape[1]
    columns = heads_here * qkv_weight.shape[2]
    source = normalize(tokens, ln_gain)
    half_width = width // lax.axis_size("head")
    core_index = lax.axis_index("head")
    own_half = lax.dynamic_slice_in_dim(source, core_index * half_width, half_width, 2)
    fetched = lax.all_gather(own_half, "seq", axis=1, tiled=True)
    gathered = lax.all_gather(fetched, "head", axis=2, tiled=True)
    full_tokens = gathered.shape[1]
    features = gathered.reshape(images * full_tokens, width)
    piece = lax.all_gather(qkv_weight, "dp", axis=0, tiled=True)
    projected = jnp.dot(
        features, piece.reshape(piece.shape[0], columns), preferred_element_type=jnp.float32
    )
    projected = projected.astype(jnp.bfloat16).reshape(
        images, full_tokens, heads_here, qkv_weight.shape[2]
    )
    mixed = lax.map(attend, projected)
    return lax.all_to_all(mixed, "seq", split_axis=1, concat_axis=2, tiled=True)


def slab_order(plane):
    inner = (plane == 1) | (plane == 2)
    near, far = plane ^ 1, 2 - plane // 2
    return plane, jnp.where(inner, near, far), jnp.where(inner, far, near), 3 - 3 * (plane // 2)


def normalize_kernel(step, other, taken, tokens_ref, gain_ref, weight_ref, *refs):
    refs = list(refs)
    take = lambda n: [refs.pop(0) for _ in range(n)]
    normed_refs, own_refs, (tokens_buf, *normed_bufs) = take(2), take(len(taken)), take(3)
    own_bufs, (in_sems, out_sems, own_sems) = take(len(taken)), take(3)
    part, width = tokens_buf.shape
    lanes = 128
    slab, span = width // 4, width // 2
    core = lax.axis_index("head")
    first = pl.multiple_of((1 - core if other else core) * part, part)
    order = slab_order(lax.axis_index("dp"))
    heads = weight_ref.shape[0] // lax.axis_size("groups")

    def rows_in(i):
        return pltpu.make_async_copy(
            tokens_ref.at[0, pl.ds(pl.multiple_of(first + i * step, step), step)],
            tokens_buf.at[pl.ds(pl.multiple_of(i * step, step), step)],
            in_sems.at[i],
        )

    def rows_out(i):
        rows = pl.ds(pl.multiple_of(i * step, step), step)
        return [
            pltpu.make_async_copy(buf.at[rows], ref.at[rows], out_sems.at[i, cut])
            for cut, (buf, ref) in enumerate(zip(normed_bufs, normed_refs))
        ]

    def own_in(k):
        head = lax.axis_index("groups") * heads + taken[k]
        return pltpu.make_async_copy(weight_ref.at[head], own_bufs[k], own_sems.at[k, 0])

    def own_out(k):
        return pltpu.make_async_copy(own_bufs[k], own_refs[k], own_sems.at[k, 1])

    for i in range(part // step):
        rows_in(i).start()
    for k in range(len(taken)):
        own_in(k).start()

    @pl.loop(0, part // step)
    def _(i):
        rows_in(i).wait()
        rows = pl.ds(pl.multiple_of(i * step, step), step)

        def widened(begin):
            return tokens_buf[rows, pl.ds(begin, lanes)].astype(jnp.float32)

        total = jnp.zeros((step, lanes), jnp.float32)
        for begin in range(0, width, lanes):
            total += widened(begin)
        mean = jnp.sum(total, axis=-1, keepdims=True) / width
        total = jnp.zeros((step, lanes), jnp.float32)
        for begin in range(0, width, lanes):
            centered = widened(begin) - mean
            total += centered * centered
        scale = lax.rsqrt(jnp.sum(total, axis=-1, keepdims=True) / width + 1e-06)
        for k in range(4):
            for begin in range(0, slab, lanes):
                column = pl.multiple_of(order[k] * slab + begin, lanes)
                value = (widened(column) - mean) * scale * gain_ref[:, pl.ds(column, lanes)]
                target = k * slab % span + begin
                normed_bufs[k * slab // span][rows, target : target + lanes] = value.astype(
                    jnp.bfloat16
                )
        for copy in rows_out(i):
            copy.start()

    for k in range(len(taken)):
        own_in(k).wait()
        own_out(k).start()
    for i in range(part // step):
        for copy in rows_out(i):
            copy.wait()
    for k in range(len(taken)):
        own_out(k).wait()


def normalize_part(tokens, ln_gain, weight, part, other, taken=()):
    width = tokens.shape[2]
    piece = weight.shape[1:]
    step = 64 if part % 64 == 0 else 32
    anywhere = pl.BlockSpec(memory_space=pl.ANY)
    half = jax.ShapeDtypeStruct((part, width // 2), jnp.bfloat16)
    got = pl.pallas_call(
        functools.partial(normalize_kernel, step, other, taken),
        out_shape=[half] * 2 + [jax.ShapeDtypeStruct(piece, jnp.bfloat16)] * len(taken),
        in_specs=[anywhere, pl.BlockSpec(memory_space=pltpu.VMEM), anywhere],
        out_specs=[anywhere] * (2 + len(taken)),
        scratch_shapes=[
            pltpu.VMEM((part, width), jnp.bfloat16),
            *[pltpu.VMEM((part, width // 2), jnp.bfloat16)] * 2,
            *[pltpu.VMEM(piece, jnp.bfloat16)] * len(taken),
            pltpu.SemaphoreType.DMA((part // step,)),
            pltpu.SemaphoreType.DMA((part // step, 2)),
            pltpu.SemaphoreType.DMA((max(len(taken), 1), 2)),
        ],
        compiler_params=pltpu.CompilerParams(vmem_limit_bytes=62 << 20),
        cost_estimate=pl.CostEstimate(
            flops=8 * part * width, bytes_accessed=4 * part * width, transcendentals=part
        ),
    )(tokens, ln_gain[None], weight)
    return got[:2], got[2:]


def attend_rows(projected_ref, parts, column):
    width = projected_ref.shape[1] // 3
    key_rows = projected_ref[:, width : 2 * width]
    value_rows = projected_ref[:, 2 * width :]
    value_rows = jnp.concatenate([value_rows, jnp.ones_like(value_rows)], axis=1)
    begin = 0
    for part in parts:
        step = part.shape[0]
        queries = projected_ref[begin : begin + step, :width]
        scores = lax.dot_general(
            queries, key_rows, (((1,), (1,)), ((), ())), preferred_element_type=jnp.float32
        )
        highest = jnp.max(scores, axis=-1, keepdims=True)
        expo = jnp.exp2((scores - highest) * (math.log2(math.e) / math.sqrt(width)))
        mixed = jnp.dot(expo.astype(jnp.bfloat16), value_rows, preferred_element_type=jnp.float32)
        mixed = mixed[:, :width] / mixed[:, width:]
        part[:, column : column + width] = mixed.astype(jnp.bfloat16)
        begin += step


class Jobs:
    def __init__(self, **numbers):
        self.__dict__.update(numbers)

    def jobs(self, image):
        return sorted({j for use in self.uses[image] if use for j in range(*use)})


def job_kernel(plan, role_ref, *refs):
    refs = list(refs)
    take = lambda n: [refs.pop(0) for _ in range(n)]
    images, ns = range(len(plan.uses)), range(len(plan.slots))
    pieces = [[[take(2) for _ in place] for place in image] for image in plan.origins]
    weights = [[take(1) * 2 if alike else take(2) for alike in row] for row in plan.same]
    partials = [{j: take(1)[0] for j in plan.added[i]} for i in images]
    carried = [[take(plan.carried[i]) for _ in range(2)] for i in images]
    outs = [
        {j: take(2) if j in plan.finished[i] else take(1)[0] for j in plan.jobs(i)} for i in images
    ]
    features_ref, weight_ref, total_ref, projected_ref = take(4)
    token_sems, weight_sems, sum_sems, out_sems, carry_sems = take(5)
    core, inner = role_ref[0], role_ref[1]
    slab = pieces[0][0][0][0].shape[1] // 2
    tokens, wide = projected_ref.shape[1:]
    part = tokens // 4

    def features(i, n):
        return features_ref.at[pl.ds(i * tokens, tokens), pl.ds(n * slab, slab)]

    def weight(n, j):
        return weight_ref.at[pl.ds(n * slab, slab), pl.ds(j * wide, wide)]

    def total(i, j):
        return total_ref.at[pl.ds(i * tokens, tokens), pl.ds(j * wide, wide)]

    def start_tokens(i, n):
        cut, begin = plan.slots[n] // 2, plan.slots[n] % 2 * slab
        for place in range(2):
            split = len(plan.origins[i][place])
            for owner in range(split):
                row = i * tokens + 2 * place * part
                if split == 2:
                    row += (1 - core if owner else core) * part
                count = 2 * part // split
                from_rows = pl.ds(plan.origins[i][place][owner][cut], count)
                rows = pl.ds(pl.multiple_of(row, 32), count)
                pltpu.make_async_copy(
                    pieces[i][place][owner][cut].at[from_rows, pl.ds(begin, slab)],
                    features_ref.at[rows, pl.ds(n * slab, slab)],
                    token_sems.at[i, n],
                ).start()

    def start_weight(n, j, role):
        source = weights[n][j - plan.first[n]][role]
        if source.shape[0] == slab:
            pltpu.make_async_copy(source, weight(n, j), weight_sems.at[n, j]).start()
            return
        for b in range(source.shape[1] // wide):
            pltpu.make_async_copy(
                source.at[:, pl.ds(b * wide, wide)],
                weight_ref.at[pl.ds(n * slab + b * part, part), pl.ds(j * wide, wide)],
                weight_sems.at[n, j],
            ).start()

    def start_role_weight(n, j):
        if plan.same[n][j - plan.first[n]]:
            start_weight(n, j, 0)
            return

        @pl.when(inner == 1)
        def _():
            start_weight(n, j, 0)

        @pl.when(inner != 1)
        def _():
            start_weight(n, j, 1)

    def partial_copy(i, j):
        return pltpu.make_async_copy(partials[i][j], total(i, j), sum_sems.at[i, j])

    def out_copy(i, j):
        return pltpu.make_async_copy(total(i, j), outs[i][j], out_sems.at[i, j])

    def carry_copies():
        for i in images:
            for place in range(2):
                for k in range(plan.carried[i]):
                    (finished,) = plan.finished[i]
                    target = outs[i][finished][place].at[:, pl.ds(k * wide // 3, wide // 3)]
                    yield pltpu.make_async_copy(
                        carried[i][place][k], target, carry_sems.at[i, place, k]
                    )

    stages = [(i, n) for i in images for n in ns if plan.uses[i][n]]
    held = set()

    def start_stage(i, n):
        start_tokens(i, n)
        for j in range(*plan.uses[i][n]):
            if (n, j) not in held:
                held.add((n, j))
                start_role_weight(n, j)
        if not any((i, n) > (i, m) and plan.uses[i][m] for m in ns):
            for j in plan.added[i]:
                partial_copy(i, j).start()

    ahead = 2
    for stage in stages[:ahead]:
        start_stage(*stage)
    for copy in carry_copies():
        copy.start()
    ready, waiting, step = set(), [], plan.step
    for index, (i, n) in enumerate(stages):
        low, high = plan.uses[i][n]
        pltpu.make_async_copy(features(i, n), features(i, n), token_sems.at[i, n]).wait()
        for j in range(low, high):
            if (n, j) not in ready:
                ready.add((n, j))
                pltpu.make_async_copy(weight(n, j), weight(n, j), weight_sems.at[n, j]).wait()
        if index + ahead < len(stages):
            start_stage(*stages[index + ahead])
        mine = {
            j: [m for m in ns if plan.uses[i][m] and j in range(*plan.uses[i][m])]
            for j in range(low, high)
        }
        for j in range(low, high):
            if n == mine[j][0] and j in plan.added[i]:
                partial_copy(i, j).wait()

        def project(r):
            local = pl.ds(pl.multiple_of(r * step, step), step)
            rows = pl.ds(pl.multiple_of(i * tokens + r * step, step), step)
            term = jnp.dot(
                features_ref[rows, n * slab : (n + 1) * slab],
                weight_ref[n * slab : (n + 1) * slab, low * wide : high * wide],
                preferred_element_type=jnp.float32,
            )
            for j in range(low, high):
                value = term[:, (j - low) * wide : (j - low + 1) * wide]
                if n != mine[j][0] or j in plan.added[i]:
                    value += total_ref[rows, j * wide : (j + 1) * wide]
                if n == mine[j][-1] and j in plan.finished[i]:
                    projected_ref[i % 2, local, :] = value.astype(jnp.bfloat16)
                else:
                    total_ref[rows, j * wide : (j + 1) * wide] = value

        if step == tokens:
            project(0)
        else:
            pl.loop(0, tokens // step)(project)

        for j in range(low, high):
            if n != mine[j][-1]:
                continue
            if j in plan.finished[i]:
                if waiting:
                    attend_rows(*waiting.pop())
                column = plan.carried[i] * wide // 3
                waiting.append((projected_ref.at[i % 2], outs[i][j], column))
            else:
                out_copy(i, j).start()
    if waiting:
        attend_rows(*waiting.pop())
    for copy in carry_copies():
        copy.wait()
    for i in images:
        for j in plan.jobs(i):
            if j not in plan.finished[i]:
                out_copy(i, j).wait()


def run_jobs(role, tokens, wide, images, weights, step=384):
    images = [
        dict(
            image,
            pieces=[
                [[x if isinstance(x, tuple) else (x, 0) for x in owner] for owner in place]
                for place in image["pieces"]
            ],
            sums=image.get("sums", {}),
            finish=image.get("finish", ()),
            carry=image.get("carry", ((), ())),
        )
        for image in images
    ]
    plan = Jobs(
        origins=[[[[r for _, r in o] for o in p] for p in image["pieces"]] for image in images],
        slots=[slot for slot, _, _ in weights],
        first=[first for _, first, _ in weights],
        same=[[not isinstance(w, tuple) for w in row] for _, _, row in weights],
        uses=[image["uses"] for image in images],
        added=[tuple(image["sums"]) for image in images],
        finished=[image["finish"] for image in images],
        carried=[len(image["carry"][0]) for image in images],
        step=step,
    )
    operands = [x for i in images for place in i["pieces"] for owner in place for x, _ in owner]
    slab = operands[0].shape[1] // 2
    for _, _, row in weights:
        for w in row:
            operands += list(w) if isinstance(w, tuple) else [w]
    operands += [x for image in images for x in image["sums"].values()]
    operands += [x for image in images for place in image["carry"] for x in place]
    anywhere, vmem = pl.BlockSpec(memory_space=pl.ANY), pl.BlockSpec(memory_space=pltpu.VMEM)
    head = wide // 3
    shapes, specs = [], []
    for i in range(len(images)):
        for j in plan.jobs(i):
            if j in plan.finished[i]:
                shape = (tokens // 2, head * (plan.carried[i] + 1))
                shapes += [jax.ShapeDtypeStruct(shape, jnp.bfloat16)] * 2
                specs += [vmem] * 2
            else:
                shapes.append(jax.ShapeDtypeStruct((tokens, wide), jnp.float32))
                specs.append(anywhere)
    jobs = 1 + max(j for i in range(len(images)) for j in plan.jobs(i))
    count, depth, total = len(images), len(weights) * slab, len(images) * tokens
    added = sum(high - low for uses in plan.uses for low, high in filter(None, uses))
    got = pl.pallas_call(
        functools.partial(job_kernel, plan),
        out_shape=shapes,
        in_specs=[pl.BlockSpec(memory_space=pltpu.SMEM)] + [anywhere] * len(operands),
        out_specs=specs,
        scratch_shapes=[
            pltpu.VMEM((total, depth), jnp.bfloat16),
            pltpu.VMEM((depth, jobs * wide), jnp.bfloat16),
            pltpu.VMEM((total, jobs * wide), jnp.float32),
            pltpu.VMEM((2, tokens, wide), jnp.bfloat16),
            pltpu.SemaphoreType.DMA((count, len(weights))),
            pltpu.SemaphoreType.DMA((len(weights), jobs)),
            pltpu.SemaphoreType.DMA((count, jobs)),
            pltpu.SemaphoreType.DMA((count, jobs)),
            pltpu.SemaphoreType.DMA((count, 2, max(*plan.carried, 1))),
        ],
        compiler_params=pltpu.CompilerParams(vmem_limit_bytes=62 << 20),
        cost_estimate=pl.CostEstimate(
            flops=2 * tokens * slab * wide * added, bytes_accessed=0, transcendentals=0
        ),
    )(role, *operands)
    got = list(got)
    return [
        {
            j: (got.pop(0), got.pop(0)) if j in plan.finished[i] else got.pop(0)
            for j in plan.jobs(i)
        }
        for i in range(count)
    ]


def join_kernel(place_ref, *refs):
    *parts, out_ref, sems = refs
    count = len(parts) // 2
    inner = place_ref[count]
    wide, head = parts[0].shape[1], parts[count].shape[1]

    def copies(i, role):
        begin = pl.multiple_of(place_ref[i] * wide, wide)
        if role:
            yield parts[i], out_ref.at[:, pl.ds(begin, wide)], sems.at[i, 0]
            return
        kept = wide - head
        yield parts[i].at[:, pl.ds(head, kept)], out_ref.at[:, pl.ds(begin, kept)], sems.at[i, 0]
        last = pl.multiple_of(begin + kept, head)
        yield parts[count + i], out_ref.at[:, pl.ds(last, head)], sems.at[i, 1]

    for role in (1, 0):

        @pl.when((inner == 1) == (role == 1))
        def _():
            every = [pltpu.make_async_copy(*c) for i in range(count) for c in copies(i, role)]
            for copy in every:
                copy.start()
            for copy in every:
                copy.wait()


def join(places, inner, parts, back):
    rows, wide = parts[0].shape
    anywhere = pl.BlockSpec(memory_space=pl.ANY)
    return pl.pallas_call(
        join_kernel,
        out_shape=jax.ShapeDtypeStruct((rows, wide * len(parts)), jnp.bfloat16),
        in_specs=[pl.BlockSpec(memory_space=pltpu.SMEM)] + [anywhere] * (2 * len(parts)),
        out_specs=pl.BlockSpec(memory_space=pltpu.VMEM),
        scratch_shapes=[pltpu.SemaphoreType.DMA((len(parts), 2))],
        cost_estimate=pl.CostEstimate(
            flops=0, bytes_accessed=4 * rows * wide * len(parts), transcendentals=0
        ),
    )(jnp.stack([*places, inner]).astype(jnp.int32), *parts, *back)


def shared(tokens, ln_gain, qkv_weight):
    groups, planes, seqs, cores = (lax.axis_size(a) for a in ("groups", "dp", "seq", "head"))
    group, plane, seq, core = (lax.axis_index(a) for a in ("groups", "dp", "seq", "head"))
    _, rows, _ = tokens.shape
    slab, heads, columns = qkv_weight.shape
    heads, part = heads // groups, rows // cores
    inner = (plane == 1) | (plane == 2)
    wait = lax.optimization_barrier

    def fold(piece):
        piece = piece.reshape(-1, part, columns).transpose(1, 0, 2)
        return piece.reshape(part, -1)

    def pick(for_inner, for_ends):
        return jnp.where(inner, for_inner, for_ends)

    def pair(value):
        return lax.ppermute(value, "dp", [(0, 1), (1, 0), (2, 3), (3, 2)])

    def outward(value):
        return lax.ppermute(value, "dp", [(1, 0), (2, 3)])

    def middle(value):
        return lax.ppermute(value, "dp", [(1, 2), (2, 1)])

    swap = [(0, 1), (1, 0)]
    beside = lambda value: lax.ppermute(value, "seq", swap)
    across = lambda value: lax.ppermute(value, "groups", swap)

    def others(*values):
        got = []
        for value in values:
            if got:
                value, got[-1] = wait((value, got[-1]))
            got.append(lax.ppermute(value, "head", swap))
        return got


    def exchange(mixed):
        got = []
        for a in range(groups):
            for b in range(seqs):
                sent = mixed[a * seqs + b]
                if a or b:
                    steps = [
                        (g * seqs + s, (g + a) % groups * seqs + (s + b) % seqs)
                        for g in range(groups)
                        for s in range(seqs)
                    ]
                    sent = lax.ppermute(sent, ("groups", "seq"), steps)
                got.append(sent)
        return got

    weight = qkv_weight.transpose(1, 0, 2)
    normed, (own0,) = normalize_part(tokens, ln_gain, weight, part, False, (0,))
    normed, own0, later_weight = wait((normed, own0, weight))
    cut0, cut1 = normed
    pair1, middle1 = pair(own0), middle(own0)
    beside1, across1 = beside(cut0), across(cut0)
    own1, own2 = [
        lax.dynamic_index_in_dim(later_weight, group * heads + j, 0, keepdims=False) for j in (1, 2)
    ]
    give = pick(fold(own1), cut0)
    role = jnp.stack([core, inner]).astype(jnp.int32)
    beside1, across1, own1, own2, cut1, tokens, give, role = wait(
        (beside1, across1, own1, own2, cut1, tokens, give, role)
    )
    pair1, middle1, give = wait((pair1, middle1, give))
    run = functools.partial(run_jobs, role, seqs * rows, columns)

    pair2, middle2 = pair(give), middle(pair1)
    beside2, across2 = beside(cut1), across(cut1)
    give = pick(fold(middle1), cut1)
    far_normed, _ = normalize_part(tokens, ln_gain, weight, part, True)
    far1 = others(beside1, across1)
    pair2, middle2, beside2, across2, across1, own1, own2, far_normed, far1, give = wait(
        (pair2, middle2, beside2, across2, across1, own1, own2, far_normed, far1, give)
    )

    pair3, middle3 = pair(give), middle(own1)
    beside3, across3 = beside(across1), across(beside2)
    give = pick(middle2, own1)
    far2 = others(across2, beside2)[::-1]
    pair3, middle3, beside3, across3, pair1, pair2, own2, far2, give = wait(
        (pair3, middle3, beside3, across3, pair1, pair2, own2, far2, give)
    )

    pair4, middle4 = pair(give), middle(own2)
    beside4, across4 = beside(pair2), across(pair2)
    give = pick(middle3, own2)
    pieces0 = ((normed, far_normed), ((beside1, beside2), (far1[0], far2[0])))
    owns = [own0, (own1, own0), (own2, own1)]
    ((head0, sum20, sum30),) = [
        tuple(got.values())
        for got in run(
            [dict(pieces=pieces0, uses=[(0, 3), (0, 2), (0, 1), (0, 1)], finish=(0,))],
            [(0, 0, owns), (2, 0, [middle1, (middle3, pair1)]), (1, 0, [pair1]), (3, 0, [middle2])],
        )
    ]
    far3 = others(beside3, across3)
    lent = jnp.concatenate([pair2, pair3])
    pair4, middle4, beside4, across4, own2, pair3, lent, head0, sum20, sum30, far3, give = wait(
        (pair4, middle4, beside4, across4, own2, pair3, lent, head0, sum20, sum30, far3, give)
    )

    pair5, middle5 = pair(give), middle(pair4)
    beside5, across5 = beside(pair3), across(pair3)
    pieces1 = (((across1, across2), (far1[1], far2[1])), ((beside3, across3), far3))
    image1, image0 = run(
        [
            dict(pieces=pieces1, uses=[(0, 3), (0, 3), (0, 2), (0, 1)], finish=(0,)),
            dict(pieces=pieces0, uses=[None, (2, 3), (1, 2), None], sums={1: sum20, 2: sum30}),
        ],
        [
            (0, 0, owns),
            (2, 0, [middle1, (middle3, pair1), (middle4, pair2)]),
            (1, 0, [pair1, (pair4, pair3)]),
            (3, 0, [middle2]),
        ],
    )
    far_lent, far4 = others(lent, beside4)
    pair5, middle5, beside5, across5, across4, image0, image1, far_lent, far4 = wait(
        (
            *(pair5, middle5, beside5, across5, across4),
            *(image0, image1, far_lent, far4),
        )
    )

    pair6, middle6 = outward(middle5), middle(pair5)
    beside6, across6 = beside(across4), across(beside5)
    far5, far_across4 = others(beside5, across4)
    ahead0, ahead1 = run(
        [
            dict(
                pieces=pieces,
                uses=[(0, 1), (1, 2)],
                sums={0: image[1], 1: image[2]},
                finish=(0,),
            )
            for pieces, image in ((pieces0, image0), (pieces1, image1))
        ],
        [(3, 0, [(middle5, pair4)]), (1, 1, [pair5])],
    )
    lent0 = (((pair2, pair3), (far_lent, (far_lent, part))), ((beside4, beside5), (far4, far5)))
    lent_weights = [(0, 0, [pair5]), (1, 0, [middle4]), (2, 0, [own2])]
    ((sum4,),) = [
        tuple(got.values()) for got in run([dict(pieces=lent0, uses=[(0, 1)] * 3)], lent_weights)
    ]
    pair6, middle6, beside6, across6, across5, ahead0, ahead1, sum4, far_across4 = wait(
        (pair6, middle6, beside6, across6, across5, ahead0, ahead1, sum4, far_across4)
    )

    far_across5, *far6 = [
        lax.ppermute(value, "head", swap) for value in (across5, beside6, across6)
    ]
    done0, done1, lent0 = run(
        [
            dict(pieces=p, uses=[(0, 1)], sums={0: x[1]}, finish=(0,), carry=tuple(zip(h, x[0])))
            for p, h, x in ((pieces0, head0, ahead0), (pieces1, image1[0], ahead1))
        ]
        + [dict(pieces=lent0, uses=[(0, 1)], sums={0: sum4}, finish=(0,))],
        [(3, 0, [(middle6, pair6)])],
    )
    lent1 = (((across4, across5), (far_across4, far_across5)), ((beside6, across6), far6))
    (lent1,) = run(
        [dict(pieces=lent1, uses=[(0, 1)] * 4, finish=(0,))],
        [*lent_weights, (3, 0, [middle6])],
        step=seqs * rows,
    )

    def hand_back(mixed):
        got = []
        for a in range(groups):
            for b in range(seqs):
                steps = [
                    (
                        (g * planes + z) * seqs + s,
                        ((g + a) % groups * planes + (z ^ 1)) * seqs + (s + b) % seqs,
                    )
                    for g in range(groups)
                    for z in (1, 2)
                    for s in range(seqs)
                ]
                sent = mixed[a * seqs + b]
                got.append(lax.ppermute(sent, ("groups", "dp", "seq"), steps))
        return got

    sent = exchange((*done0[0], *done1[0]))
    back = hand_back((*lent0[0], *lent1[0]))
    places = [
        (seq - b) % seqs * groups + (group - a) % groups
        for a in range(groups)
        for b in range(seqs)
    ]
    return join(places, inner, sent, back)[None]


def per_device(tokens, ln_gain, qkv_weight):
    groups, planes, seqs, cores = (lax.axis_size(a) for a in ("groups", "dp", "seq", "head"))
    images, rows, width = tokens.shape
    slab, heads, _ = qkv_weight.shape
    if (groups, planes, seqs, cores) == (2, 4, 2, 2) and images == 1 and heads == 3 * groups:
        part = rows // cores
        if rows % (32 * cores) == 0 and slab % part == 0 and 2 * slab == qkv_weight.shape[2] * slab // part:
            return shared(tokens, ln_gain, qkv_weight)
    return plain(tokens, ln_gain, qkv_weight)


def solution(mesh):
    return jax.shard_map(
        per_device,
        mesh=mesh,
        in_specs=(P(("groups", "dp"), "seq", None), P(), P("dp", ("seq", "head"), None)),
        out_specs=P(("groups", "dp"), "seq", "head"),
        check_vma=False,
    )
```

```python
import functools
import math

import jax
import jax.numpy as jnp
from jax import lax
from jax.experimental import pallas as pl
from jax.experimental.pallas import tpu as pltpu
from jax.sharding import PartitionSpec as P


def normalize(array, gain):
    widened = array.astype(jnp.float32)
    centered = widened - jnp.mean(widened, axis=-1, keepdims=True)
    variance = jnp.mean(centered * centered, axis=-1, keepdims=True)
    return (centered * lax.rsqrt(variance + 1e-06) * gain).astype(jnp.bfloat16)


def attend(projected):
    width = projected.shape[2] // 3
    queries = projected[:, :, :width]
    key_rows = projected[:, :, width : 2 * width]
    value_rows = projected[:, :, 2 * width :]
    scores = jnp.einsum("qhd,khd->hqk", queries, key_rows, preferred_element_type=jnp.float32) * (
        1.0 / math.sqrt(width)
    )
    highest = jnp.max(scores, axis=-1, keepdims=True)
    expo = jnp.exp(scores - highest)
    probs = (expo / jnp.sum(expo, axis=-1, keepdims=True)).astype(jnp.bfloat16)
    mixed = jnp.einsum("hqk,khd->qhd", probs, value_rows, preferred_element_type=jnp.float32)
    return mixed.astype(jnp.bfloat16).reshape(projected.shape[0], -1)


def plain(tokens, ln_gain, qkv_weight):
    images = tokens.shape[0]
    width = tokens.shape[2]
    heads_here = qkv_weight.shape[1]
    columns = heads_here * qkv_weight.shape[2]
    source = normalize(tokens, ln_gain)
    half_width = width // lax.axis_size("head")
    core_index = lax.axis_index("head")
    own_half = lax.dynamic_slice_in_dim(source, core_index * half_width, half_width, 2)
    fetched = lax.all_gather(own_half, "seq", axis=1, tiled=True)
    gathered = lax.all_gather(fetched, "head", axis=2, tiled=True)
    full_tokens = gathered.shape[1]
    features = gathered.reshape(images * full_tokens, width)
    piece = lax.all_gather(qkv_weight, "dp", axis=0, tiled=True)
    projected = jnp.dot(
        features, piece.reshape(piece.shape[0], columns), preferred_element_type=jnp.float32
    )
    projected = projected.astype(jnp.bfloat16).reshape(
        images, full_tokens, heads_here, qkv_weight.shape[2]
    )
    mixed = lax.map(attend, projected)
    return lax.all_to_all(mixed, "seq", split_axis=1, concat_axis=2, tiled=True)


def slab_order(plane):
    inner = (plane == 1) | (plane == 2)
    near, far = plane ^ 1, 2 - plane // 2
    return plane, jnp.where(inner, near, far), jnp.where(inner, far, near), 3 - 3 * (plane // 2)


def normalize_kernel(step, other, taken, tokens_ref, gain_ref, weight_ref, *refs):
    refs = list(refs)
    take = lambda n: [refs.pop(0) for _ in range(n)]
    normed_refs, own_refs, (tokens_buf, *normed_bufs) = take(2), take(len(taken)), take(3)
    own_bufs, (in_sems, out_sems, own_sems) = take(len(taken)), take(3)
    part, width = tokens_buf.shape
    lanes = 128
    slab, span = width // 4, width // 2
    core = lax.axis_index("head")
    first = pl.multiple_of((1 - core if other else core) * part, part)
    order = slab_order(lax.axis_index("dp"))
    heads = weight_ref.shape[0] // lax.axis_size("groups")

    def rows_in(i):
        return pltpu.make_async_copy(
            tokens_ref.at[0, pl.ds(pl.multiple_of(first + i * step, step), step)],
            tokens_buf.at[pl.ds(pl.multiple_of(i * step, step), step)],
            in_sems.at[i],
        )

    def rows_out(i):
        rows = pl.ds(pl.multiple_of(i * step, step), step)
        return [
            pltpu.make_async_copy(buf.at[rows], ref.at[rows], out_sems.at[i, cut])
            for cut, (buf, ref) in enumerate(zip(normed_bufs, normed_refs))
        ]

    def own_in(k):
        head = lax.axis_index("groups") * heads + taken[k]
        return pltpu.make_async_copy(weight_ref.at[head], own_bufs[k], own_sems.at[k, 0])

    def own_out(k):
        return pltpu.make_async_copy(own_bufs[k], own_refs[k], own_sems.at[k, 1])

    for i in range(part // step):
        rows_in(i).start()
    for k in range(len(taken)):
        own_in(k).start()

    @pl.loop(0, part // step)
    def _(i):
        rows_in(i).wait()
        rows = pl.ds(pl.multiple_of(i * step, step), step)

        def widened(begin):
            return tokens_buf[rows, pl.ds(begin, lanes)].astype(jnp.float32)

        total = jnp.zeros((step, lanes), jnp.float32)
        for begin in range(0, width, lanes):
            total += widened(begin)
        mean = jnp.sum(total, axis=-1, keepdims=True) / width
        total = jnp.zeros((step, lanes), jnp.float32)
        for begin in range(0, width, lanes):
            centered = widened(begin) - mean
            total += centered * centered
        scale = lax.rsqrt(jnp.sum(total, axis=-1, keepdims=True) / width + 1e-06)
        for k in range(4):
            for begin in range(0, slab, lanes):
                column = pl.multiple_of(order[k] * slab + begin, lanes)
                value = (widened(column) - mean) * scale * gain_ref[:, pl.ds(column, lanes)]
                target = k * slab % span + begin
                normed_bufs[k * slab // span][rows, target : target + lanes] = value.astype(
                    jnp.bfloat16
                )
        for copy in rows_out(i):
            copy.start()

    for k in range(len(taken)):
        own_in(k).wait()
        own_out(k).start()
    for i in range(part // step):
        for copy in rows_out(i):
            copy.wait()
    for k in range(len(taken)):
        own_out(k).wait()


def normalize_part(tokens, ln_gain, weight, part, other, taken=()):
    width = tokens.shape[2]
    piece = weight.shape[1:]
    step = 64 if part % 64 == 0 else 32
    anywhere = pl.BlockSpec(memory_space=pl.ANY)
    half = jax.ShapeDtypeStruct((part, width // 2), jnp.bfloat16)
    got = pl.pallas_call(
        functools.partial(normalize_kernel, step, other, taken),
        out_shape=[half] * 2 + [jax.ShapeDtypeStruct(piece, jnp.bfloat16)] * len(taken),
        in_specs=[anywhere, pl.BlockSpec(memory_space=pltpu.VMEM), anywhere],
        out_specs=[anywhere] * (2 + len(taken)),
        scratch_shapes=[
            pltpu.VMEM((part, width), jnp.bfloat16),
            *[pltpu.VMEM((part, width // 2), jnp.bfloat16)] * 2,
            *[pltpu.VMEM(piece, jnp.bfloat16)] * len(taken),
            pltpu.SemaphoreType.DMA((part // step,)),
            pltpu.SemaphoreType.DMA((part // step, 2)),
            pltpu.SemaphoreType.DMA((max(len(taken), 1), 2)),
        ],
        compiler_params=pltpu.CompilerParams(vmem_limit_bytes=62 << 20),
        cost_estimate=pl.CostEstimate(
            flops=8 * part * width, bytes_accessed=4 * part * width, transcendentals=part
        ),
    )(tokens, ln_gain[None], weight)
    return got[:2], got[2:]


def attend_rows(projected_ref, parts, column):
    width = projected_ref.shape[1] // 3
    key_rows = projected_ref[:, width : 2 * width]
    value_rows = projected_ref[:, 2 * width :]
    value_rows = jnp.concatenate([value_rows, jnp.ones_like(value_rows)], axis=1)
    begin = 0
    for part in parts:
        step = part.shape[0]
        queries = projected_ref[begin : begin + step, :width]
        scores = lax.dot_general(
            queries, key_rows, (((1,), (1,)), ((), ())), preferred_element_type=jnp.float32
        )
        highest = jnp.max(scores, axis=-1, keepdims=True)
        expo = jnp.exp((scores - highest) * (1.0 / math.sqrt(width)))
        mixed = jnp.dot(expo.astype(jnp.bfloat16), value_rows, preferred_element_type=jnp.float32)
        mixed = mixed[:, :width] / mixed[:, width:]
        part[:, column : column + width] = mixed.astype(jnp.bfloat16)
        begin += step


class Jobs:
    def __init__(self, **numbers):
        self.__dict__.update(numbers)

    def jobs(self, image):
        return sorted({j for use in self.uses[image] if use for j in range(*use)})


def job_kernel(plan, role_ref, *refs):
    refs = list(refs)
    take = lambda n: [refs.pop(0) for _ in range(n)]
    images, ns = range(len(plan.uses)), range(len(plan.slots))
    pieces = [[[take(2) for _ in place] for place in image] for image in plan.origins]
    weights = [[take(1) * 2 if alike else take(2) for alike in row] for row in plan.same]
    partials = [{j: take(1)[0] for j in plan.added[i]} for i in images]
    carried = [[take(plan.carried[i]) for _ in range(2)] for i in images]
    outs = [
        {j: take(2) if j in plan.finished[i] else take(1)[0] for j in plan.jobs(i)} for i in images
    ]
    features_ref, weight_ref, total_ref, projected_ref = take(4)
    token_sems, weight_sems, sum_sems, out_sems, carry_sems = take(5)
    core, inner = role_ref[0], role_ref[1]
    slab = pieces[0][0][0][0].shape[1] // 2
    tokens, wide = projected_ref.shape[1:]
    part = tokens // 4

    def features(i, n):
        return features_ref.at[pl.ds(i * tokens, tokens), pl.ds(n * slab, slab)]

    def weight(n, j):
        return weight_ref.at[pl.ds(n * slab, slab), pl.ds(j * wide, wide)]

    def total(i, j):
        return total_ref.at[pl.ds(i * tokens, tokens), pl.ds(j * wide, wide)]

    def start_tokens(i, n):
        cut, begin = plan.slots[n] // 2, plan.slots[n] % 2 * slab
        for place in range(2):
            split = len(plan.origins[i][place])
            for owner in range(split):
                row = i * tokens + 2 * place * part
                if split == 2:
                    row += (1 - core if owner else core) * part
                count = 2 * part // split
                from_rows = pl.ds(plan.origins[i][place][owner][cut], count)
                rows = pl.ds(pl.multiple_of(row, 32), count)
                pltpu.make_async_copy(
                    pieces[i][place][owner][cut].at[from_rows, pl.ds(begin, slab)],
                    features_ref.at[rows, pl.ds(n * slab, slab)],
                    token_sems.at[i, n],
                ).start()

    def start_weight(n, j, role):
        source = weights[n][j - plan.first[n]][role]
        if source.shape[0] == slab:
            pltpu.make_async_copy(source, weight(n, j), weight_sems.at[n, j]).start()
            return
        for b in range(source.shape[1] // wide):
            pltpu.make_async_copy(
                source.at[:, pl.ds(b * wide, wide)],
                weight_ref.at[pl.ds(n * slab + b * part, part), pl.ds(j * wide, wide)],
                weight_sems.at[n, j],
            ).start()

    def start_role_weight(n, j):
        if plan.same[n][j - plan.first[n]]:
            start_weight(n, j, 0)
            return

        @pl.when(inner == 1)
        def _():
            start_weight(n, j, 0)

        @pl.when(inner != 1)
        def _():
            start_weight(n, j, 1)

    def partial_copy(i, j):
        return pltpu.make_async_copy(partials[i][j], total(i, j), sum_sems.at[i, j])

    def out_copy(i, j):
        return pltpu.make_async_copy(total(i, j), outs[i][j], out_sems.at[i, j])

    def carry_copies():
        for i in images:
            for place in range(2):
                for k in range(plan.carried[i]):
                    (finished,) = plan.finished[i]
                    target = outs[i][finished][place].at[:, pl.ds(k * wide // 3, wide // 3)]
                    yield pltpu.make_async_copy(
                        carried[i][place][k], target, carry_sems.at[i, place, k]
                    )

    stages = [(i, n) for i in images for n in ns if plan.uses[i][n]]
    held = set()

    def start_stage(i, n):
        start_tokens(i, n)
        for j in range(*plan.uses[i][n]):
            if (n, j) not in held:
                held.add((n, j))
                start_role_weight(n, j)
        if not any((i, n) > (i, m) and plan.uses[i][m] for m in ns):
            for j in plan.added[i]:
                partial_copy(i, j).start()

    ahead = 3
    for stage in stages[:ahead]:
        start_stage(*stage)
    for copy in carry_copies():
        copy.start()
    ready, waiting, step = set(), [], plan.step
    for index, (i, n) in enumerate(stages):
        low, high = plan.uses[i][n]
        pltpu.make_async_copy(features(i, n), features(i, n), token_sems.at[i, n]).wait()
        for j in range(low, high):
            if (n, j) not in ready:
                ready.add((n, j))
                pltpu.make_async_copy(weight(n, j), weight(n, j), weight_sems.at[n, j]).wait()
        if index + ahead < len(stages):
            start_stage(*stages[index + ahead])
        mine = {
            j: [m for m in ns if plan.uses[i][m] and j in range(*plan.uses[i][m])]
            for j in range(low, high)
        }
        for j in range(low, high):
            if n == mine[j][0] and j in plan.added[i]:
                partial_copy(i, j).wait()

        def project(r):
            local = pl.ds(pl.multiple_of(r * step, step), step)
            rows = pl.ds(pl.multiple_of(i * tokens + r * step, step), step)
            term = jnp.dot(
                features_ref[rows, n * slab : (n + 1) * slab],
                weight_ref[n * slab : (n + 1) * slab, low * wide : high * wide],
                preferred_element_type=jnp.float32,
            )
            for j in range(low, high):
                value = term[:, (j - low) * wide : (j - low + 1) * wide]
                if n != mine[j][0] or j in plan.added[i]:
                    value += total_ref[rows, j * wide : (j + 1) * wide]
                if n == mine[j][-1] and j in plan.finished[i]:
                    projected_ref[i % 2, local, :] = value.astype(jnp.bfloat16)
                else:
                    total_ref[rows, j * wide : (j + 1) * wide] = value

        if step == tokens:
            project(0)
        else:
            pl.loop(0, tokens // step)(project)

        for j in range(low, high):
            if n != mine[j][-1]:
                continue
            if j in plan.finished[i]:
                if waiting:
                    attend_rows(*waiting.pop())
                column = plan.carried[i] * wide // 3
                waiting.append((projected_ref.at[i % 2], outs[i][j], column))
            else:
                out_copy(i, j).start()
    if waiting:
        attend_rows(*waiting.pop())
    for copy in carry_copies():
        copy.wait()
    for i in images:
        for j in plan.jobs(i):
            if j not in plan.finished[i]:
                out_copy(i, j).wait()


def run_jobs(role, tokens, wide, images, weights, step=384):
    images = [
        dict(
            image,
            pieces=[
                [[x if isinstance(x, tuple) else (x, 0) for x in owner] for owner in place]
                for place in image["pieces"]
            ],
            sums=image.get("sums", {}),
            finish=image.get("finish", ()),
            carry=image.get("carry", ((), ())),
        )
        for image in images
    ]
    plan = Jobs(
        origins=[[[[r for _, r in o] for o in p] for p in image["pieces"]] for image in images],
        slots=[slot for slot, _, _ in weights],
        first=[first for _, first, _ in weights],
        same=[[not isinstance(w, tuple) for w in row] for _, _, row in weights],
        uses=[image["uses"] for image in images],
        added=[tuple(image["sums"]) for image in images],
        finished=[image["finish"] for image in images],
        carried=[len(image["carry"][0]) for image in images],
        step=step,
    )
    operands = [x for i in images for place in i["pieces"] for owner in place for x, _ in owner]
    slab = operands[0].shape[1] // 2
    for _, _, row in weights:
        for w in row:
            operands += list(w) if isinstance(w, tuple) else [w]
    operands += [x for image in images for x in image["sums"].values()]
    operands += [x for image in images for place in image["carry"] for x in place]
    anywhere, vmem = pl.BlockSpec(memory_space=pl.ANY), pl.BlockSpec(memory_space=pltpu.VMEM)
    head = wide // 3
    shapes, specs = [], []
    for i in range(len(images)):
        for j in plan.jobs(i):
            if j in plan.finished[i]:
                shape = (tokens // 2, head * (plan.carried[i] + 1))
                shapes += [jax.ShapeDtypeStruct(shape, jnp.bfloat16)] * 2
                specs += [vmem] * 2
            else:
                shapes.append(jax.ShapeDtypeStruct((tokens, wide), jnp.float32))
                specs.append(anywhere)
    jobs = 1 + max(j for i in range(len(images)) for j in plan.jobs(i))
    count, depth, total = len(images), len(weights) * slab, len(images) * tokens
    added = sum(high - low for uses in plan.uses for low, high in filter(None, uses))
    got = pl.pallas_call(
        functools.partial(job_kernel, plan),
        out_shape=shapes,
        in_specs=[pl.BlockSpec(memory_space=pltpu.SMEM)] + [anywhere] * len(operands),
        out_specs=specs,
        scratch_shapes=[
            pltpu.VMEM((total, depth), jnp.bfloat16),
            pltpu.VMEM((depth, jobs * wide), jnp.bfloat16),
            pltpu.VMEM((total, jobs * wide), jnp.float32),
            pltpu.VMEM((2, tokens, wide), jnp.bfloat16),
            pltpu.SemaphoreType.DMA((count, len(weights))),
            pltpu.SemaphoreType.DMA((len(weights), jobs)),
            pltpu.SemaphoreType.DMA((count, jobs)),
            pltpu.SemaphoreType.DMA((count, jobs)),
            pltpu.SemaphoreType.DMA((count, 2, max(*plan.carried, 1))),
        ],
        compiler_params=pltpu.CompilerParams(vmem_limit_bytes=62 << 20),
        cost_estimate=pl.CostEstimate(
            flops=2 * tokens * slab * wide * added, bytes_accessed=0, transcendentals=0
        ),
    )(role, *operands)
    got = list(got)
    return [
        {
            j: (got.pop(0), got.pop(0)) if j in plan.finished[i] else got.pop(0)
            for j in plan.jobs(i)
        }
        for i in range(count)
    ]


def join_kernel(place_ref, *refs):
    *parts, out_ref, sems = refs
    count = len(parts) // 2
    inner = place_ref[count]
    wide, head = parts[0].shape[1], parts[count].shape[1]

    def copies(i, role):
        begin = pl.multiple_of(place_ref[i] * wide, wide)
        if role:
            yield parts[i], out_ref.at[:, pl.ds(begin, wide)], sems.at[i, 0]
            return
        kept = wide - head
        yield parts[i].at[:, pl.ds(head, kept)], out_ref.at[:, pl.ds(begin, kept)], sems.at[i, 0]
        last = pl.multiple_of(begin + kept, head)
        yield parts[count + i], out_ref.at[:, pl.ds(last, head)], sems.at[i, 1]

    for role in (1, 0):

        @pl.when((inner == 1) == (role == 1))
        def _():
            every = [pltpu.make_async_copy(*c) for i in range(count) for c in copies(i, role)]
            for copy in every:
                copy.start()
            for copy in every:
                copy.wait()


def join(places, inner, parts, back):
    rows, wide = parts[0].shape
    anywhere = pl.BlockSpec(memory_space=pl.ANY)
    return pl.pallas_call(
        join_kernel,
        out_shape=jax.ShapeDtypeStruct((rows, wide * len(parts)), jnp.bfloat16),
        in_specs=[pl.BlockSpec(memory_space=pltpu.SMEM)] + [anywhere] * (2 * len(parts)),
        out_specs=pl.BlockSpec(memory_space=pltpu.VMEM),
        scratch_shapes=[pltpu.SemaphoreType.DMA((len(parts), 2))],
        cost_estimate=pl.CostEstimate(
            flops=0, bytes_accessed=4 * rows * wide * len(parts), transcendentals=0
        ),
    )(jnp.stack([*places, inner]).astype(jnp.int32), *parts, *back)


def shared(tokens, ln_gain, qkv_weight):
    groups, planes, seqs, cores = (lax.axis_size(a) for a in ("groups", "dp", "seq", "head"))
    group, plane, seq, core = (lax.axis_index(a) for a in ("groups", "dp", "seq", "head"))
    _, rows, _ = tokens.shape
    slab, heads, columns = qkv_weight.shape
    heads, part = heads // groups, rows // cores
    inner = (plane == 1) | (plane == 2)
    wait = lax.optimization_barrier

    def fold(piece):
        piece = piece.reshape(-1, part, columns).transpose(1, 0, 2)
        return piece.reshape(part, -1)

    def pick(for_inner, for_ends):
        return jnp.where(inner, for_inner, for_ends)

    def pair(value):
        return lax.ppermute(value, "dp", [(0, 1), (1, 0), (2, 3), (3, 2)])

    def outward(value):
        return lax.ppermute(value, "dp", [(1, 0), (2, 3)])

    def middle(value):
        return lax.ppermute(value, "dp", [(1, 2), (2, 1)])

    swap = [(0, 1), (1, 0)]
    beside = lambda value: lax.ppermute(value, "seq", swap)
    across = lambda value: lax.ppermute(value, "groups", swap)

    def others(*values):
        got = []
        for value in values:
            if got:
                value, got[-1] = wait((value, got[-1]))
            got.append(lax.ppermute(value, "head", swap))
        return got


    def exchange(mixed):
        got = []
        for a in range(groups):
            for b in range(seqs):
                sent = mixed[a * seqs + b]
                if a or b:
                    steps = [
                        (g * seqs + s, (g + a) % groups * seqs + (s + b) % seqs)
                        for g in range(groups)
                        for s in range(seqs)
                    ]
                    sent = lax.ppermute(sent, ("groups", "seq"), steps)
                got.append(sent)
        return got

    weight = qkv_weight.transpose(1, 0, 2)
    normed, (own0,) = normalize_part(tokens, ln_gain, weight, part, False, (0,))
    normed, own0, later_weight = wait((normed, own0, weight))
    cut0, cut1 = normed
    pair1, middle1 = pair(own0), middle(own0)
    beside1, across1 = beside(cut0), across(cut0)
    own1, own2 = [
        lax.dynamic_index_in_dim(later_weight, group * heads + j, 0, keepdims=False) for j in (1, 2)
    ]
    give = pick(fold(own1), cut0)
    role = jnp.stack([core, inner]).astype(jnp.int32)
    beside1, across1, own1, own2, cut1, tokens, give, role = wait(
        (beside1, across1, own1, own2, cut1, tokens, give, role)
    )
    pair1, middle1, give = wait((pair1, middle1, give))
    run = functools.partial(run_jobs, role, seqs * rows, columns)

    pair2, middle2 = pair(give), middle(pair1)
    beside2, across2 = beside(cut1), across(cut1)
    give = pick(fold(middle1), cut1)
    far_normed, _ = normalize_part(tokens, ln_gain, weight, part, True)
    far1 = others(beside1, across1)
    pair2, middle2, beside2, across2, across1, own1, own2, far_normed, far1, give = wait(
        (pair2, middle2, beside2, across2, across1, own1, own2, far_normed, far1, give)
    )

    pair3, middle3 = pair(give), middle(own1)
    beside3, across3 = beside(across1), across(beside2)
    give = pick(middle2, own1)
    far2 = others(across2, beside2)[::-1]
    pair3, middle3, beside3, across3, pair1, pair2, own2, far2, give = wait(
        (pair3, middle3, beside3, across3, pair1, pair2, own2, far2, give)
    )

    pair4, middle4 = pair(give), middle(own2)
    beside4, across4 = beside(pair2), across(pair2)
    give = pick(middle3, own2)
    pieces0 = ((normed, far_normed), ((beside1, beside2), (far1[0], far2[0])))
    owns = [own0, (own1, own0), (own2, own1)]
    ((head0, sum20, sum30),) = [
        tuple(got.values())
        for got in run(
            [dict(pieces=pieces0, uses=[(0, 3), (0, 2), (0, 1), (0, 1)], finish=(0,))],
            [(0, 0, owns), (2, 0, [middle1, (middle3, pair1)]), (1, 0, [pair1]), (3, 0, [middle2])],
        )
    ]
    far3 = others(beside3, across3)
    lent = jnp.concatenate([pair2, pair3])
    pair4, middle4, beside4, across4, own2, pair3, lent, head0, sum20, sum30, far3, give = wait(
        (pair4, middle4, beside4, across4, own2, pair3, lent, head0, sum20, sum30, far3, give)
    )

    pair5, middle5 = pair(give), middle(pair4)
    beside5, across5 = beside(pair3), across(pair3)
    pieces1 = (((across1, across2), (far1[1], far2[1])), ((beside3, across3), far3))
    image1, image0 = run(
        [
            dict(pieces=pieces1, uses=[(0, 3), (0, 3), (0, 2), (0, 1)], finish=(0,)),
            dict(pieces=pieces0, uses=[None, (2, 3), (1, 2), None], sums={1: sum20, 2: sum30}),
        ],
        [
            (0, 0, owns),
            (2, 0, [middle1, (middle3, pair1), (middle4, pair2)]),
            (1, 0, [pair1, (pair4, pair3)]),
            (3, 0, [middle2]),
        ],
    )
    far_lent, far4 = others(lent, beside4)
    pair5, middle5, beside5, across5, across4, image0, image1, far_lent, far4 = wait(
        (
            *(pair5, middle5, beside5, across5, across4),
            *(image0, image1, far_lent, far4),
        )
    )

    pair6, middle6 = outward(middle5), middle(pair5)
    beside6, across6 = beside(across4), across(beside5)
    far5, far_across4 = others(beside5, across4)
    ahead0, ahead1 = run(
        [
            dict(
                pieces=pieces,
                uses=[(0, 1), (1, 2)],
                sums={0: image[1], 1: image[2]},
                finish=(0,),
            )
            for pieces, image in ((pieces0, image0), (pieces1, image1))
        ],
        [(3, 0, [(middle5, pair4)]), (1, 1, [pair5])],
    )
    lent0 = (((pair2, pair3), (far_lent, (far_lent, part))), ((beside4, beside5), (far4, far5)))
    lent_weights = [(0, 0, [pair5]), (1, 0, [middle4]), (2, 0, [own2])]
    ((sum4,),) = [
        tuple(got.values()) for got in run([dict(pieces=lent0, uses=[(0, 1)] * 3)], lent_weights)
    ]
    pair6, middle6, beside6, across6, across5, ahead0, ahead1, sum4, far_across4 = wait(
        (pair6, middle6, beside6, across6, across5, ahead0, ahead1, sum4, far_across4)
    )

    far_across5, *far6 = [
        lax.ppermute(value, "head", swap) for value in (across5, beside6, across6)
    ]
    done0, done1, lent0 = run(
        [
            dict(pieces=p, uses=[(0, 1)], sums={0: x[1]}, finish=(0,), carry=tuple(zip(h, x[0])))
            for p, h, x in ((pieces0, head0, ahead0), (pieces1, image1[0], ahead1))
        ]
        + [dict(pieces=lent0, uses=[(0, 1)], sums={0: sum4}, finish=(0,))],
        [(3, 0, [(middle6, pair6)])],
    )
    lent1 = (((across4, across5), (far_across4, far_across5)), ((beside6, across6), far6))
    (lent1,) = run(
        [dict(pieces=lent1, uses=[(0, 1)] * 4, finish=(0,))],
        [*lent_weights, (3, 0, [middle6])],
        step=seqs * rows,
    )

    def hand_back(mixed):
        got = []
        for a in range(groups):
            for b in range(seqs):
                steps = [
                    (
                        (g * planes + z) * seqs + s,
                        ((g + a) % groups * planes + (z ^ 1)) * seqs + (s + b) % seqs,
                    )
                    for g in range(groups)
                    for z in (1, 2)
                    for s in range(seqs)
                ]
                sent = mixed[a * seqs + b]
                got.append(lax.ppermute(sent, ("groups", "dp", "seq"), steps))
        return got

    sent = exchange((*done0[0], *done1[0]))
    back = hand_back((*lent0[0], *lent1[0]))
    places = [
        (seq - b) % seqs * groups + (group - a) % groups
        for a in range(groups)
        for b in range(seqs)
    ]
    return join(places, inner, sent, back)[None]


def per_device(tokens, ln_gain, qkv_weight):
    groups, planes, seqs, cores = (lax.axis_size(a) for a in ("groups", "dp", "seq", "head"))
    images, rows, width = tokens.shape
    slab, heads, _ = qkv_weight.shape
    if (groups, planes, seqs, cores) == (2, 4, 2, 2) and images == 1 and heads == 3 * groups:
        part = rows // cores
        if rows % (32 * cores) == 0 and slab % part == 0 and 2 * slab == qkv_weight.shape[2] * slab // part:
            return shared(tokens, ln_gain, qkv_weight)
    return plain(tokens, ln_gain, qkv_weight)


def solution(mesh):
    return jax.shard_map(
        per_device,
        mesh=mesh,
        in_specs=(P(("groups", "dp"), "seq", None), P(), P("dp", ("seq", "head"), None)),
        out_specs=P(("groups", "dp"), "seq", "head"),
        check_vma=False,
    )
```

```python
import functools
import math

import jax
import jax.numpy as jnp
from jax import lax
from jax.experimental import pallas as pl
from jax.experimental.pallas import tpu as pltpu
from jax.sharding import PartitionSpec as P


def normalize(array, gain):
    widened = array.astype(jnp.float32)
    centered = widened - jnp.mean(widened, axis=-1, keepdims=True)
    variance = jnp.mean(centered * centered, axis=-1, keepdims=True)
    return (centered * lax.rsqrt(variance + 1e-06) * gain).astype(jnp.bfloat16)


def attend(projected):
    width = projected.shape[2] // 3
    queries = projected[:, :, :width]
    key_rows = projected[:, :, width : 2 * width]
    value_rows = projected[:, :, 2 * width :]
    scores = jnp.einsum("qhd,khd->hqk", queries, key_rows, preferred_element_type=jnp.float32) * (
        1.0 / math.sqrt(width)
    )
    highest = jnp.max(scores, axis=-1, keepdims=True)
    expo = jnp.exp(scores - highest)
    probs = (expo / jnp.sum(expo, axis=-1, keepdims=True)).astype(jnp.bfloat16)
    mixed = jnp.einsum("hqk,khd->qhd", probs, value_rows, preferred_element_type=jnp.float32)
    return mixed.astype(jnp.bfloat16).reshape(projected.shape[0], -1)


def plain(tokens, ln_gain, qkv_weight):
    images = tokens.shape[0]
    width = tokens.shape[2]
    heads_here = qkv_weight.shape[1]
    columns = heads_here * qkv_weight.shape[2]
    source = normalize(tokens, ln_gain)
    half_width = width // lax.axis_size("head")
    core_index = lax.axis_index("head")
    own_half = lax.dynamic_slice_in_dim(source, core_index * half_width, half_width, 2)
    fetched = lax.all_gather(own_half, "seq", axis=1, tiled=True)
    gathered = lax.all_gather(fetched, "head", axis=2, tiled=True)
    full_tokens = gathered.shape[1]
    features = gathered.reshape(images * full_tokens, width)
    piece = lax.all_gather(qkv_weight, "dp", axis=0, tiled=True)
    projected = jnp.dot(
        features, piece.reshape(piece.shape[0], columns), preferred_element_type=jnp.float32
    )
    projected = projected.astype(jnp.bfloat16).reshape(
        images, full_tokens, heads_here, qkv_weight.shape[2]
    )
    mixed = lax.map(attend, projected)
    return lax.all_to_all(mixed, "seq", split_axis=1, concat_axis=2, tiled=True)


def slab_order(plane):
    inner = (plane == 1) | (plane == 2)
    near, far = plane ^ 1, 2 - plane // 2
    return plane, jnp.where(inner, near, far), jnp.where(inner, far, near), 3 - 3 * (plane // 2)


def normalize_kernel(step, other, taken, tokens_ref, gain_ref, weight_ref, *refs):
    refs = list(refs)
    take = lambda n: [refs.pop(0) for _ in range(n)]
    normed_refs, own_refs, (tokens_buf, *normed_bufs) = take(2), take(len(taken)), take(3)
    own_bufs, (in_sems, out_sems, own_sems) = take(len(taken)), take(3)
    part, width = tokens_buf.shape
    lanes = 128
    slab, span = width // 4, width // 2
    core = lax.axis_index("head")
    first = pl.multiple_of((1 - core if other else core) * part, part)
    order = slab_order(lax.axis_index("dp"))
    heads = weight_ref.shape[0] // lax.axis_size("groups")

    def rows_in(i):
        return pltpu.make_async_copy(
            tokens_ref.at[0, pl.ds(pl.multiple_of(first + i * step, step), step)],
            tokens_buf.at[pl.ds(pl.multiple_of(i * step, step), step)],
            in_sems.at[i],
        )

    def rows_out(i):
        rows = pl.ds(pl.multiple_of(i * step, step), step)
        return [
            pltpu.make_async_copy(buf.at[rows], ref.at[rows], out_sems.at[i, cut])
            for cut, (buf, ref) in enumerate(zip(normed_bufs, normed_refs))
        ]

    def own_in(k):
        head = lax.axis_index("groups") * heads + taken[k]
        return pltpu.make_async_copy(weight_ref.at[head], own_bufs[k], own_sems.at[k, 0])

    def own_out(k):
        return pltpu.make_async_copy(own_bufs[k], own_refs[k], own_sems.at[k, 1])

    for i in range(part // step):
        rows_in(i).start()
    for k in range(len(taken)):
        own_in(k).start()

    @pl.loop(0, part // step)
    def _(i):
        rows_in(i).wait()
        rows = pl.ds(pl.multiple_of(i * step, step), step)

        def widened(begin):
            return tokens_buf[rows, pl.ds(begin, lanes)].astype(jnp.float32)

        total = jnp.zeros((step, lanes), jnp.float32)
        for begin in range(0, width, lanes):
            total += widened(begin)
        mean = jnp.sum(total, axis=-1, keepdims=True) / width
        total = jnp.zeros((step, lanes), jnp.float32)
        for begin in range(0, width, lanes):
            centered = widened(begin) - mean
            total += centered * centered
        scale = lax.rsqrt(jnp.sum(total, axis=-1, keepdims=True) / width + 1e-06)
        for k in range(4):
            for begin in range(0, slab, lanes):
                column = pl.multiple_of(order[k] * slab + begin, lanes)
                value = (widened(column) - mean) * scale * gain_ref[:, pl.ds(column, lanes)]
                target = k * slab % span + begin
                normed_bufs[k * slab // span][rows, target : target + lanes] = value.astype(
                    jnp.bfloat16
                )
        for copy in rows_out(i):
            copy.start()

    for k in range(len(taken)):
        own_in(k).wait()
        own_out(k).start()
    for i in range(part // step):
        for copy in rows_out(i):
            copy.wait()
    for k in range(len(taken)):
        own_out(k).wait()


def normalize_part(tokens, ln_gain, weight, part, other, taken=()):
    width = tokens.shape[2]
    piece = weight.shape[1:]
    step = 96 if part % 96 == 0 else 32
    anywhere = pl.BlockSpec(memory_space=pl.ANY)
    half = jax.ShapeDtypeStruct((part, width // 2), jnp.bfloat16)
    got = pl.pallas_call(
        functools.partial(normalize_kernel, step, other, taken),
        out_shape=[half] * 2 + [jax.ShapeDtypeStruct(piece, jnp.bfloat16)] * len(taken),
        in_specs=[anywhere, pl.BlockSpec(memory_space=pltpu.VMEM), anywhere],
        out_specs=[anywhere] * (2 + len(taken)),
        scratch_shapes=[
            pltpu.VMEM((part, width), jnp.bfloat16),
            *[pltpu.VMEM((part, width // 2), jnp.bfloat16)] * 2,
            *[pltpu.VMEM(piece, jnp.bfloat16)] * len(taken),
            pltpu.SemaphoreType.DMA((part // step,)),
            pltpu.SemaphoreType.DMA((part // step, 2)),
            pltpu.SemaphoreType.DMA((max(len(taken), 1), 2)),
        ],
        compiler_params=pltpu.CompilerParams(vmem_limit_bytes=62 << 20),
        cost_estimate=pl.CostEstimate(
            flops=8 * part * width, bytes_accessed=4 * part * width, transcendentals=part
        ),
    )(tokens, ln_gain[None], weight)
    return got[:2], got[2:]


def attend_rows(projected_ref, parts, column):
    width = projected_ref.shape[1] // 3
    key_rows = projected_ref[:, width : 2 * width]
    value_rows = projected_ref[:, 2 * width :]
    value_rows = jnp.concatenate([value_rows, jnp.ones_like(value_rows)], axis=1)
    begin = 0
    for part in parts:
        step = part.shape[0]
        queries = projected_ref[begin : begin + step, :width]
        scores = lax.dot_general(
            queries, key_rows, (((1,), (1,)), ((), ())), preferred_element_type=jnp.float32
        )
        highest = jnp.max(scores, axis=-1, keepdims=True)
        expo = jnp.exp2((scores - highest) * (math.log2(math.e) / math.sqrt(width)))
        mixed = jnp.dot(expo.astype(jnp.bfloat16), value_rows, preferred_element_type=jnp.float32)
        mixed = mixed[:, :width] / mixed[:, width:]
        part[:, column : column + width] = mixed.astype(jnp.bfloat16)
        begin += step


class Jobs:
    def __init__(self, **numbers):
        self.__dict__.update(numbers)

    def jobs(self, image):
        return sorted({j for use in self.uses[image] if use for j in range(*use)})


def job_kernel(plan, role_ref, *refs):
    refs = list(refs)
    take = lambda n: [refs.pop(0) for _ in range(n)]
    images, ns = range(len(plan.uses)), range(len(plan.slots))
    pieces = [[[take(2) for _ in place] for place in image] for image in plan.origins]
    weights = [[take(1) * 2 if alike else take(2) for alike in row] for row in plan.same]
    partials = [{j: take(1)[0] for j in plan.added[i]} for i in images]
    carried = [[take(plan.carried[i]) for _ in range(2)] for i in images]
    outs = [
        {j: take(2) if j in plan.finished[i] else take(1)[0] for j in plan.jobs(i)} for i in images
    ]
    features_ref, weight_ref, total_ref, projected_ref = take(4)
    token_sems, weight_sems, sum_sems, out_sems, carry_sems = take(5)
    core, inner = role_ref[0], role_ref[1]
    slab = pieces[0][0][0][0].shape[1] // 2
    tokens, wide = projected_ref.shape[1:]
    part = tokens // 4

    def features(i, n):
        return features_ref.at[pl.ds(i * tokens, tokens), pl.ds(n * slab, slab)]

    def weight(n, j):
        return weight_ref.at[pl.ds(n * slab, slab), pl.ds(j * wide, wide)]

    def total(i, j):
        return total_ref.at[pl.ds(i * tokens, tokens), pl.ds(j * wide, wide)]

    def start_tokens(i, n):
        cut, begin = plan.slots[n] // 2, plan.slots[n] % 2 * slab
        for place in range(2):
            split = len(plan.origins[i][place])
            for owner in range(split):
                row = i * tokens + 2 * place * part
                if split == 2:
                    row += (1 - core if owner else core) * part
                count = 2 * part // split
                from_rows = pl.ds(plan.origins[i][place][owner][cut], count)
                rows = pl.ds(pl.multiple_of(row, 32), count)
                pltpu.make_async_copy(
                    pieces[i][place][owner][cut].at[from_rows, pl.ds(begin, slab)],
                    features_ref.at[rows, pl.ds(n * slab, slab)],
                    token_sems.at[i, n],
                ).start()

    def start_weight(n, j, role):
        source = weights[n][j - plan.first[n]][role]
        if source.shape[0] == slab:
            pltpu.make_async_copy(source, weight(n, j), weight_sems.at[n, j]).start()
            return
        for b in range(source.shape[1] // wide):
            pltpu.make_async_copy(
                source.at[:, pl.ds(b * wide, wide)],
                weight_ref.at[pl.ds(n * slab + b * part, part), pl.ds(j * wide, wide)],
                weight_sems.at[n, j],
            ).start()

    def start_role_weight(n, j):
        if plan.same[n][j - plan.first[n]]:
            start_weight(n, j, 0)
            return

        @pl.when(inner == 1)
        def _():
            start_weight(n, j, 0)

        @pl.when(inner != 1)
        def _():
            start_weight(n, j, 1)

    def partial_copy(i, j):
        return pltpu.make_async_copy(partials[i][j], total(i, j), sum_sems.at[i, j])

    def out_copy(i, j):
        return pltpu.make_async_copy(total(i, j), outs[i][j], out_sems.at[i, j])

    def carry_copies():
        for i in images:
            for place in range(2):
                for k in range(plan.carried[i]):
                    (finished,) = plan.finished[i]
                    target = outs[i][finished][place].at[:, pl.ds(k * wide // 3, wide // 3)]
                    yield pltpu.make_async_copy(
                        carried[i][place][k], target, carry_sems.at[i, place, k]
                    )

    stages = [(i, n) for i in images for n in ns if plan.uses[i][n]]
    held = set()

    def start_stage(i, n):
        start_tokens(i, n)
        for j in range(*plan.uses[i][n]):
            if (n, j) not in held:
                held.add((n, j))
                start_role_weight(n, j)
        if not any((i, n) > (i, m) and plan.uses[i][m] for m in ns):
            for j in plan.added[i]:
                partial_copy(i, j).start()

    ahead = 1
    for stage in stages[:ahead]:
        start_stage(*stage)
    for copy in carry_copies():
        copy.start()
    ready, waiting, step = set(), [], plan.step
    for index, (i, n) in enumerate(stages):
        low, high = plan.uses[i][n]
        pltpu.make_async_copy(features(i, n), features(i, n), token_sems.at[i, n]).wait()
        for j in range(low, high):
            if (n, j) not in ready:
                ready.add((n, j))
                pltpu.make_async_copy(weight(n, j), weight(n, j), weight_sems.at[n, j]).wait()
        if index + ahead < len(stages):
            start_stage(*stages[index + ahead])
        mine = {
            j: [m for m in ns if plan.uses[i][m] and j in range(*plan.uses[i][m])]
            for j in range(low, high)
        }
        for j in range(low, high):
            if n == mine[j][0] and j in plan.added[i]:
                partial_copy(i, j).wait()

        def project(r):
            local = pl.ds(pl.multiple_of(r * step, step), step)
            rows = pl.ds(pl.multiple_of(i * tokens + r * step, step), step)
            term = jnp.dot(
                features_ref[rows, n * slab : (n + 1) * slab],
                weight_ref[n * slab : (n + 1) * slab, low * wide : high * wide],
                preferred_element_type=jnp.float32,
            )
            for j in range(low, high):
                value = term[:, (j - low) * wide : (j - low + 1) * wide]
                if n != mine[j][0] or j in plan.added[i]:
                    value += total_ref[rows, j * wide : (j + 1) * wide]
                if n == mine[j][-1] and j in plan.finished[i]:
                    projected_ref[i % 2, local, :] = value.astype(jnp.bfloat16)
                else:
                    total_ref[rows, j * wide : (j + 1) * wide] = value

        if step == tokens:
            project(0)
        else:
            pl.loop(0, tokens // step)(project)

        for j in range(low, high):
            if n != mine[j][-1]:
                continue
            if j in plan.finished[i]:
                if waiting:
                    attend_rows(*waiting.pop())
                column = plan.carried[i] * wide // 3
                waiting.append((projected_ref.at[i % 2], outs[i][j], column))
            else:
                out_copy(i, j).start()
    if waiting:
        attend_rows(*waiting.pop())
    for copy in carry_copies():
        copy.wait()
    for i in images:
        for j in plan.jobs(i):
            if j not in plan.finished[i]:
                out_copy(i, j).wait()


def run_jobs(role, tokens, wide, images, weights, step=384):
    images = [
        dict(
            image,
            pieces=[
                [[x if isinstance(x, tuple) else (x, 0) for x in owner] for owner in place]
                for place in image["pieces"]
            ],
            sums=image.get("sums", {}),
            finish=image.get("finish", ()),
            carry=image.get("carry", ((), ())),
        )
        for image in images
    ]
    plan = Jobs(
        origins=[[[[r for _, r in o] for o in p] for p in image["pieces"]] for image in images],
        slots=[slot for slot, _, _ in weights],
        first=[first for _, first, _ in weights],
        same=[[not isinstance(w, tuple) for w in row] for _, _, row in weights],
        uses=[image["uses"] for image in images],
        added=[tuple(image["sums"]) for image in images],
        finished=[image["finish"] for image in images],
        carried=[len(image["carry"][0]) for image in images],
        step=step,
    )
    operands = [x for i in images for place in i["pieces"] for owner in place for x, _ in owner]
    slab = operands[0].shape[1] // 2
    for _, _, row in weights:
        for w in row:
            operands += list(w) if isinstance(w, tuple) else [w]
    operands += [x for image in images for x in image["sums"].values()]
    operands += [x for image in images for place in image["carry"] for x in place]
    anywhere, vmem = pl.BlockSpec(memory_space=pl.ANY), pl.BlockSpec(memory_space=pltpu.VMEM)
    head = wide // 3
    shapes, specs = [], []
    for i in range(len(images)):
        for j in plan.jobs(i):
            if j in plan.finished[i]:
                shape = (tokens // 2, head * (plan.carried[i] + 1))
                shapes += [jax.ShapeDtypeStruct(shape, jnp.bfloat16)] * 2
                specs += [vmem] * 2
            else:
                shapes.append(jax.ShapeDtypeStruct((tokens, wide), jnp.float32))
                specs.append(anywhere)
    jobs = 1 + max(j for i in range(len(images)) for j in plan.jobs(i))
    count, depth, total = len(images), len(weights) * slab, len(images) * tokens
    added = sum(high - low for uses in plan.uses for low, high in filter(None, uses))
    got = pl.pallas_call(
        functools.partial(job_kernel, plan),
        out_shape=shapes,
        in_specs=[pl.BlockSpec(memory_space=pltpu.SMEM)] + [anywhere] * len(operands),
        out_specs=specs,
        scratch_shapes=[
            pltpu.VMEM((total, depth), jnp.bfloat16),
            pltpu.VMEM((depth, jobs * wide), jnp.bfloat16),
            pltpu.VMEM((total, jobs * wide), jnp.float32),
            pltpu.VMEM((2, tokens, wide), jnp.bfloat16),
            pltpu.SemaphoreType.DMA((count, len(weights))),
            pltpu.SemaphoreType.DMA((len(weights), jobs)),
            pltpu.SemaphoreType.DMA((count, jobs)),
            pltpu.SemaphoreType.DMA((count, jobs)),
            pltpu.SemaphoreType.DMA((count, 2, max(*plan.carried, 1))),
        ],
        compiler_params=pltpu.CompilerParams(vmem_limit_bytes=62 << 20),
        cost_estimate=pl.CostEstimate(
            flops=2 * tokens * slab * wide * added, bytes_accessed=0, transcendentals=0
        ),
    )(role, *operands)
    got = list(got)
    return [
        {
            j: (got.pop(0), got.pop(0)) if j in plan.finished[i] else got.pop(0)
            for j in plan.jobs(i)
        }
        for i in range(count)
    ]


def join_kernel(place_ref, *refs):
    *parts, out_ref, sems = refs
    count = len(parts) // 2
    inner = place_ref[count]
    wide, head = parts[0].shape[1], parts[count].shape[1]

    def copies(i, role):
        begin = pl.multiple_of(place_ref[i] * wide, wide)
        if role:
            yield parts[i], out_ref.at[:, pl.ds(begin, wide)], sems.at[i, 0]
            return
        kept = wide - head
        yield parts[i].at[:, pl.ds(head, kept)], out_ref.at[:, pl.ds(begin, kept)], sems.at[i, 0]
        last = pl.multiple_of(begin + kept, head)
        yield parts[count + i], out_ref.at[:, pl.ds(last, head)], sems.at[i, 1]

    for role in (1, 0):

        @pl.when((inner == 1) == (role == 1))
        def _():
            every = [pltpu.make_async_copy(*c) for i in range(count) for c in copies(i, role)]
            for copy in every:
                copy.start()
            for copy in every:
                copy.wait()


def join(places, inner, parts, back):
    rows, wide = parts[0].shape
    anywhere = pl.BlockSpec(memory_space=pl.ANY)
    return pl.pallas_call(
        join_kernel,
        out_shape=jax.ShapeDtypeStruct((rows, wide * len(parts)), jnp.bfloat16),
        in_specs=[pl.BlockSpec(memory_space=pltpu.SMEM)] + [anywhere] * (2 * len(parts)),
        out_specs=pl.BlockSpec(memory_space=pltpu.VMEM),
        scratch_shapes=[pltpu.SemaphoreType.DMA((len(parts), 2))],
        cost_estimate=pl.CostEstimate(
            flops=0, bytes_accessed=4 * rows * wide * len(parts), transcendentals=0
        ),
    )(jnp.stack([*places, inner]).astype(jnp.int32), *parts, *back)


def shared(tokens, ln_gain, qkv_weight):
    groups, planes, seqs, cores = (lax.axis_size(a) for a in ("groups", "dp", "seq", "head"))
    group, plane, seq, core = (lax.axis_index(a) for a in ("groups", "dp", "seq", "head"))
    _, rows, _ = tokens.shape
    slab, heads, columns = qkv_weight.shape
    heads, part = heads // groups, rows // cores
    inner = (plane == 1) | (plane == 2)
    wait = lax.optimization_barrier

    def fold(piece):
        piece = piece.reshape(-1, part, columns).transpose(1, 0, 2)
        return piece.reshape(part, -1)

    def pick(for_inner, for_ends):
        return jnp.where(inner, for_inner, for_ends)

    def pair(value):
        return lax.ppermute(value, "dp", [(0, 1), (1, 0), (2, 3), (3, 2)])

    def outward(value):
        return lax.ppermute(value, "dp", [(1, 0), (2, 3)])

    def middle(value):
        return lax.ppermute(value, "dp", [(1, 2), (2, 1)])

    swap = [(0, 1), (1, 0)]
    beside = lambda value: lax.ppermute(value, "seq", swap)
    across = lambda value: lax.ppermute(value, "groups", swap)

    def others(*values):
        got = []
        for value in values:
            if got:
                value, got[-1] = wait((value, got[-1]))
            got.append(lax.ppermute(value, "head", swap))
        return got


    def exchange(mixed):
        got = []
        for a in range(groups):
            for b in range(seqs):
                sent = mixed[a * seqs + b]
                if a or b:
                    steps = [
                        (g * seqs + s, (g + a) % groups * seqs + (s + b) % seqs)
                        for g in range(groups)
                        for s in range(seqs)
                    ]
                    sent = lax.ppermute(sent, ("groups", "seq"), steps)
                got.append(sent)
        return got

    weight = qkv_weight.transpose(1, 0, 2)
    normed, (own0,) = normalize_part(tokens, ln_gain, weight, part, False, (0,))
    normed, own0, later_weight = wait((normed, own0, weight))
    cut0, cut1 = normed
    pair1, middle1 = pair(own0), middle(own0)
    beside1, across1 = beside(cut0), across(cut0)
    own1, own2 = [
        lax.dynamic_index_in_dim(later_weight, group * heads + j, 0, keepdims=False) for j in (1, 2)
    ]
    give = pick(fold(own1), cut0)
    role = jnp.stack([core, inner]).astype(jnp.int32)
    beside1, across1, own1, own2, cut1, tokens, give, role = wait(
        (beside1, across1, own1, own2, cut1, tokens, give, role)
    )
    pair1, middle1, give = wait((pair1, middle1, give))
    run = functools.partial(run_jobs, role, seqs * rows, columns)

    pair2, middle2 = pair(give), middle(pair1)
    beside2, across2 = beside(cut1), across(cut1)
    give = pick(fold(middle1), cut1)
    far_normed, _ = normalize_part(tokens, ln_gain, weight, part, True)
    far1 = others(beside1, across1)
    pair2, middle2, beside2, across2, across1, own1, own2, far_normed, far1, give = wait(
        (pair2, middle2, beside2, across2, across1, own1, own2, far_normed, far1, give)
    )

    pair3, middle3 = pair(give), middle(own1)
    beside3, across3 = beside(across1), across(beside2)
    give = pick(middle2, own1)
    far2 = others(across2, beside2)[::-1]
    pair3, middle3, beside3, across3, pair1, pair2, own2, far2, give = wait(
        (pair3, middle3, beside3, across3, pair1, pair2, own2, far2, give)
    )

    pair4, middle4 = pair(give), middle(own2)
    beside4, across4 = beside(pair2), across(pair2)
    give = pick(middle3, own2)
    pieces0 = ((normed, far_normed), ((beside1, beside2), (far1[0], far2[0])))
    owns = [own0, (own1, own0), (own2, own1)]
    ((head0, sum20, sum30),) = [
        tuple(got.values())
        for got in run(
            [dict(pieces=pieces0, uses=[(0, 3), (0, 2), (0, 1), (0, 1)], finish=(0,))],
            [(0, 0, owns), (2, 0, [middle1, (middle3, pair1)]), (1, 0, [pair1]), (3, 0, [middle2])],
        )
    ]
    far3 = others(beside3, across3)
    lent = jnp.concatenate([pair2, pair3])
    pair4, middle4, beside4, across4, own2, pair3, lent, head0, sum20, sum30, far3, give = wait(
        (pair4, middle4, beside4, across4, own2, pair3, lent, head0, sum20, sum30, far3, give)
    )

    pair5, middle5 = pair(give), middle(pair4)
    beside5, across5 = beside(pair3), across(pair3)
    pieces1 = (((across1, across2), (far1[1], far2[1])), ((beside3, across3), far3))
    image1, image0 = run(
        [
            dict(pieces=pieces1, uses=[(0, 3), (0, 3), (0, 2), (0, 1)], finish=(0,)),
            dict(pieces=pieces0, uses=[None, (2, 3), (1, 2), None], sums={1: sum20, 2: sum30}),
        ],
        [
            (0, 0, owns),
            (2, 0, [middle1, (middle3, pair1), (middle4, pair2)]),
            (1, 0, [pair1, (pair4, pair3)]),
            (3, 0, [middle2]),
        ],
    )
    far_lent, far4 = others(lent, beside4)
    pair5, middle5, beside5, across5, across4, image0, image1, far_lent, far4 = wait(
        (
            *(pair5, middle5, beside5, across5, across4),
            *(image0, image1, far_lent, far4),
        )
    )

    pair6, middle6 = outward(middle5), middle(pair5)
    beside6, across6 = beside(across4), across(beside5)
    far5, far_across4 = others(beside5, across4)
    ahead0, ahead1 = run(
        [
            dict(
                pieces=pieces,
                uses=[(0, 1), (1, 2)],
                sums={0: image[1], 1: image[2]},
                finish=(0,),
            )
            for pieces, image in ((pieces0, image0), (pieces1, image1))
        ],
        [(3, 0, [(middle5, pair4)]), (1, 1, [pair5])],
    )
    lent0 = (((pair2, pair3), (far_lent, (far_lent, part))), ((beside4, beside5), (far4, far5)))
    lent_weights = [(0, 0, [pair5]), (1, 0, [middle4]), (2, 0, [own2])]
    ((sum4,),) = [
        tuple(got.values()) for got in run([dict(pieces=lent0, uses=[(0, 1)] * 3)], lent_weights)
    ]
    pair6, middle6, beside6, across6, across5, ahead0, ahead1, sum4, far_across4 = wait(
        (pair6, middle6, beside6, across6, across5, ahead0, ahead1, sum4, far_across4)
    )

    far_across5, *far6 = [
        lax.ppermute(value, "head", swap) for value in (across5, beside6, across6)
    ]
    done0, done1, lent0 = run(
        [
            dict(pieces=p, uses=[(0, 1)], sums={0: x[1]}, finish=(0,), carry=tuple(zip(h, x[0])))
            for p, h, x in ((pieces0, head0, ahead0), (pieces1, image1[0], ahead1))
        ]
        + [dict(pieces=lent0, uses=[(0, 1)], sums={0: sum4}, finish=(0,))],
        [(3, 0, [(middle6, pair6)])],
    )
    lent1 = (((across4, across5), (far_across4, far_across5)), ((beside6, across6), far6))
    (lent1,) = run(
        [dict(pieces=lent1, uses=[(0, 1)] * 4, finish=(0,))],
        [*lent_weights, (3, 0, [middle6])],
        step=seqs * rows,
    )

    def hand_back(mixed):
        got = []
        for a in range(groups):
            for b in range(seqs):
                steps = [
                    (
                        (g * planes + z) * seqs + s,
                        ((g + a) % groups * planes + (z ^ 1)) * seqs + (s + b) % seqs,
                    )
                    for g in range(groups)
                    for z in (1, 2)
                    for s in range(seqs)
                ]
                sent = mixed[a * seqs + b]
                got.append(lax.ppermute(sent, ("groups", "dp", "seq"), steps))
        return got

    sent = exchange((*done0[0], *done1[0]))
    back = hand_back((*lent0[0], *lent1[0]))
    places = [
        (seq - b) % seqs * groups + (group - a) % groups
        for a in range(groups)
        for b in range(seqs)
    ]
    return join(places, inner, sent, back)[None]


def per_device(tokens, ln_gain, qkv_weight):
    groups, planes, seqs, cores = (lax.axis_size(a) for a in ("groups", "dp", "seq", "head"))
    images, rows, width = tokens.shape
    slab, heads, _ = qkv_weight.shape
    if (groups, planes, seqs, cores) == (2, 4, 2, 2) and images == 1 and heads == 3 * groups:
        part = rows // cores
        if rows % (32 * cores) == 0 and slab % part == 0 and 2 * slab == qkv_weight.shape[2] * slab // part:
            return shared(tokens, ln_gain, qkv_weight)
    return plain(tokens, ln_gain, qkv_weight)


def solution(mesh):
    return jax.shard_map(
        per_device,
        mesh=mesh,
        in_specs=(P(("groups", "dp"), "seq", None), P(), P("dp", ("seq", "head"), None)),
        out_specs=P(("groups", "dp"), "seq", "head"),
        check_vma=False,
    )
```

```python
import functools
import math

import jax
import jax.numpy as jnp
from jax import lax
from jax.experimental import pallas as pl
from jax.experimental.pallas import tpu as pltpu
from jax.sharding import PartitionSpec as P


def normalize(array, gain):
    widened = array.astype(jnp.float32)
    centered = widened - jnp.mean(widened, axis=-1, keepdims=True)
    variance = jnp.mean(centered * centered, axis=-1, keepdims=True)
    return (centered * lax.rsqrt(variance + 1e-06) * gain).astype(jnp.bfloat16)


def attend(projected):
    width = projected.shape[2] // 3
    queries = projected[:, :, :width]
    key_rows = projected[:, :, width : 2 * width]
    value_rows = projected[:, :, 2 * width :]
    scores = jnp.einsum("qhd,khd->hqk", queries, key_rows, preferred_element_type=jnp.float32) * (
        1.0 / math.sqrt(width)
    )
    highest = jnp.max(scores, axis=-1, keepdims=True)
    expo = jnp.exp(scores - highest)
    probs = (expo / jnp.sum(expo, axis=-1, keepdims=True)).astype(jnp.bfloat16)
    mixed = jnp.einsum("hqk,khd->qhd", probs, value_rows, preferred_element_type=jnp.float32)
    return mixed.astype(jnp.bfloat16).reshape(projected.shape[0], -1)


def plain(tokens, ln_gain, qkv_weight):
    images = tokens.shape[0]
    width = tokens.shape[2]
    heads_here = qkv_weight.shape[1]
    columns = heads_here * qkv_weight.shape[2]
    source = normalize(tokens, ln_gain)
    half_width = width // lax.axis_size("head")
    core_index = lax.axis_index("head")
    own_half = lax.dynamic_slice_in_dim(source, core_index * half_width, half_width, 2)
    fetched = lax.all_gather(own_half, "seq", axis=1, tiled=True)
    gathered = lax.all_gather(fetched, "head", axis=2, tiled=True)
    full_tokens = gathered.shape[1]
    features = gathered.reshape(images * full_tokens, width)
    piece = lax.all_gather(qkv_weight, "dp", axis=0, tiled=True)
    projected = jnp.dot(
        features, piece.reshape(piece.shape[0], columns), preferred_element_type=jnp.float32
    )
    projected = projected.astype(jnp.bfloat16).reshape(
        images, full_tokens, heads_here, qkv_weight.shape[2]
    )
    mixed = lax.map(attend, projected)
    return lax.all_to_all(mixed, "seq", split_axis=1, concat_axis=2, tiled=True)


def slab_order(plane):
    inner = (plane == 1) | (plane == 2)
    near, far = plane ^ 1, 2 - plane // 2
    return plane, jnp.where(inner, near, far), jnp.where(inner, far, near), 3 - 3 * (plane // 2)


def normalize_kernel(step, other, taken, tokens_ref, gain_ref, weight_ref, *refs):
    refs = list(refs)
    take = lambda n: [refs.pop(0) for _ in range(n)]
    normed_refs, own_refs, (tokens_buf, *normed_bufs) = take(2), take(len(taken)), take(3)
    own_bufs, (in_sems, out_sems, own_sems) = take(len(taken)), take(3)
    part, width = tokens_buf.shape
    lanes = 128
    slab, span = width // 4, width // 2
    core = lax.axis_index("head")
    first = pl.multiple_of((1 - core if other else core) * part, part)
    order = slab_order(lax.axis_index("dp"))
    heads = weight_ref.shape[0] // lax.axis_size("groups")

    def rows_in(i):
        return pltpu.make_async_copy(
            tokens_ref.at[0, pl.ds(pl.multiple_of(first + i * step, step), step)],
            tokens_buf.at[pl.ds(pl.multiple_of(i * step, step), step)],
            in_sems.at[i],
        )

    def rows_out(i):
        rows = pl.ds(pl.multiple_of(i * step, step), step)
        return [
            pltpu.make_async_copy(buf.at[rows], ref.at[rows], out_sems.at[i, cut])
            for cut, (buf, ref) in enumerate(zip(normed_bufs, normed_refs))
        ]

    def own_in(k):
        head = lax.axis_index("groups") * heads + taken[k]
        return pltpu.make_async_copy(weight_ref.at[head], own_bufs[k], own_sems.at[k, 0])

    def own_out(k):
        return pltpu.make_async_copy(own_bufs[k], own_refs[k], own_sems.at[k, 1])

    for i in range(part // step):
        rows_in(i).start()
    for k in range(len(taken)):
        own_in(k).start()

    @pl.loop(0, part // step)
    def _(i):
        rows_in(i).wait()
        rows = pl.ds(pl.multiple_of(i * step, step), step)

        def widened(begin):
            return tokens_buf[rows, pl.ds(begin, lanes)].astype(jnp.float32)

        total = jnp.zeros((step, lanes), jnp.float32)
        for begin in range(0, width, lanes):
            total += widened(begin)
        mean = jnp.sum(total, axis=-1, keepdims=True) / width
        total = jnp.zeros((step, lanes), jnp.float32)
        for begin in range(0, width, lanes):
            centered = widened(begin) - mean
            total += centered * centered
        scale = lax.rsqrt(jnp.sum(total, axis=-1, keepdims=True) / width + 1e-06)
        for k in range(4):
            for begin in range(0, slab, lanes):
                column = pl.multiple_of(order[k] * slab + begin, lanes)
                value = (widened(column) - mean) * scale * gain_ref[:, pl.ds(column, lanes)]
                target = k * slab % span + begin
                normed_bufs[k * slab // span][rows, target : target + lanes] = value.astype(
                    jnp.bfloat16
                )
        for copy in rows_out(i):
            copy.start()

    for k in range(len(taken)):
        own_in(k).wait()
        own_out(k).start()
    for i in range(part // step):
        for copy in rows_out(i):
            copy.wait()
    for k in range(len(taken)):
        own_out(k).wait()


def normalize_part(tokens, ln_gain, weight, part, other, taken=()):
    width = tokens.shape[2]
    piece = weight.shape[1:]
    step = 64 if part % 64 == 0 else 32
    anywhere = pl.BlockSpec(memory_space=pl.ANY)
    half = jax.ShapeDtypeStruct((part, width // 2), jnp.bfloat16)
    got = pl.pallas_call(
        functools.partial(normalize_kernel, step, other, taken),
        out_shape=[half] * 2 + [jax.ShapeDtypeStruct(piece, jnp.bfloat16)] * len(taken),
        in_specs=[anywhere, pl.BlockSpec(memory_space=pltpu.VMEM), anywhere],
        out_specs=[anywhere] * (2 + len(taken)),
        scratch_shapes=[
            pltpu.VMEM((part, width), jnp.bfloat16),
            *[pltpu.VMEM((part, width // 2), jnp.bfloat16)] * 2,
            *[pltpu.VMEM(piece, jnp.bfloat16)] * len(taken),
            pltpu.SemaphoreType.DMA((part // step,)),
            pltpu.SemaphoreType.DMA((part // step, 2)),
            pltpu.SemaphoreType.DMA((max(len(taken), 1), 2)),
        ],
        compiler_params=pltpu.CompilerParams(vmem_limit_bytes=62 << 20),
        cost_estimate=pl.CostEstimate(
            flops=8 * part * width, bytes_accessed=4 * part * width, transcendentals=part
        ),
    )(tokens, ln_gain[None], weight)
    return got[:2], got[2:]


def attend_rows(projected_ref, parts, column):
    width = projected_ref.shape[1] // 3
    key_rows = projected_ref[:, width : 2 * width]
    value_rows = projected_ref[:, 2 * width :]
    value_rows = jnp.concatenate([value_rows, jnp.ones_like(value_rows)], axis=1)
    begin = 0
    for part in parts:
        step = part.shape[0]
        queries = projected_ref[begin : begin + step, :width]
        scores = lax.dot_general(
            queries, key_rows, (((1,), (1,)), ((), ())), preferred_element_type=jnp.float32
        )
        highest = jnp.max(scores, axis=-1, keepdims=True)
        expo = jnp.exp2((scores - highest) * (math.log2(math.e) / math.sqrt(width)))
        mixed = jnp.dot(expo.astype(jnp.bfloat16), value_rows, preferred_element_type=jnp.float32)
        mixed = mixed[:, :width] / mixed[:, width:]
        part[:, column : column + width] = mixed.astype(jnp.bfloat16)
        begin += step


class Jobs:
    def __init__(self, **numbers):
        self.__dict__.update(numbers)

    def jobs(self, image):
        return sorted({j for use in self.uses[image] if use for j in range(*use)})


def job_kernel(plan, role_ref, *refs):
    refs = list(refs)
    take = lambda n: [refs.pop(0) for _ in range(n)]
    images, ns = range(len(plan.uses)), range(len(plan.slots))
    pieces = [[[take(2) for _ in place] for place in image] for image in plan.origins]
    weights = [[take(1) * 2 if alike else take(2) for alike in row] for row in plan.same]
    partials = [{j: take(1)[0] for j in plan.added[i]} for i in images]
    carried = [[take(plan.carried[i]) for _ in range(2)] for i in images]
    outs = [
        {j: take(2) if j in plan.finished[i] else take(1)[0] for j in plan.jobs(i)} for i in images
    ]
    features_ref, weight_ref, total_ref, projected_ref = take(4)
    token_sems, weight_sems, sum_sems, out_sems, carry_sems = take(5)
    core, inner = role_ref[0], role_ref[1]
    slab = pieces[0][0][0][0].shape[1] // 2
    tokens, wide = projected_ref.shape[1:]
    part = tokens // 4

    def features(i, n):
        return features_ref.at[pl.ds(i * tokens, tokens), pl.ds(n * slab, slab)]

    def weight(n, j):
        return weight_ref.at[pl.ds(n * slab, slab), pl.ds(j * wide, wide)]

    def total(i, j):
        return total_ref.at[pl.ds(i * tokens, tokens), pl.ds(j * wide, wide)]

    def start_tokens(i, n):
        cut, begin = plan.slots[n] // 2, plan.slots[n] % 2 * slab
        for place in range(2):
            split = len(plan.origins[i][place])
            for owner in range(split):
                row = i * tokens + 2 * place * part
                if split == 2:
                    row += (1 - core if owner else core) * part
                count = 2 * part // split
                from_rows = pl.ds(plan.origins[i][place][owner][cut], count)
                rows = pl.ds(pl.multiple_of(row, 32), count)
                pltpu.make_async_copy(
                    pieces[i][place][owner][cut].at[from_rows, pl.ds(begin, slab)],
                    features_ref.at[rows, pl.ds(n * slab, slab)],
                    token_sems.at[i, n],
                ).start()

    def start_weight(n, j, role):
        source = weights[n][j - plan.first[n]][role]
        if source.shape[0] == slab:
            pltpu.make_async_copy(source, weight(n, j), weight_sems.at[n, j]).start()
            return
        for b in range(source.shape[1] // wide):
            pltpu.make_async_copy(
                source.at[:, pl.ds(b * wide, wide)],
                weight_ref.at[pl.ds(n * slab + b * part, part), pl.ds(j * wide, wide)],
                weight_sems.at[n, j],
            ).start()

    def start_role_weight(n, j):
        if plan.same[n][j - plan.first[n]]:
            start_weight(n, j, 0)
            return

        @pl.when(inner == 1)
        def _():
            start_weight(n, j, 0)

        @pl.when(inner != 1)
        def _():
            start_weight(n, j, 1)

    def partial_copy(i, j):
        return pltpu.make_async_copy(partials[i][j], total(i, j), sum_sems.at[i, j])

    def out_copy(i, j):
        return pltpu.make_async_copy(total(i, j), outs[i][j], out_sems.at[i, j])

    def carry_copies():
        for i in images:
            for place in range(2):
                for k in range(plan.carried[i]):
                    (finished,) = plan.finished[i]
                    target = outs[i][finished][place].at[:, pl.ds(k * wide // 3, wide // 3)]
                    yield pltpu.make_async_copy(
                        carried[i][place][k], target, carry_sems.at[i, place, k]
                    )

    stages = [(i, n) for i in images for n in ns if plan.uses[i][n]]
    held = set()

    def start_stage(i, n):
        start_tokens(i, n)
        for j in range(*plan.uses[i][n]):
            if (n, j) not in held:
                held.add((n, j))
                start_role_weight(n, j)
        if not any((i, n) > (i, m) and plan.uses[i][m] for m in ns):
            for j in plan.added[i]:
                partial_copy(i, j).start()

    ahead = 2
    for stage in stages[:ahead]:
        start_stage(*stage)
    for copy in carry_copies():
        copy.start()
    ready, waiting, step = set(), [], plan.step
    for index, (i, n) in enumerate(stages):
        low, high = plan.uses[i][n]
        pltpu.make_async_copy(features(i, n), features(i, n), token_sems.at[i, n]).wait()
        for j in range(low, high):
            if (n, j) not in ready:
                ready.add((n, j))
                pltpu.make_async_copy(weight(n, j), weight(n, j), weight_sems.at[n, j]).wait()
        if index + ahead < len(stages):
            start_stage(*stages[index + ahead])
        mine = {
            j: [m for m in ns if plan.uses[i][m] and j in range(*plan.uses[i][m])]
            for j in range(low, high)
        }
        for j in range(low, high):
            if n == mine[j][0] and j in plan.added[i]:
                partial_copy(i, j).wait()

        def project(r):
            local = pl.ds(pl.multiple_of(r * step, step), step)
            rows = pl.ds(pl.multiple_of(i * tokens + r * step, step), step)
            term = jnp.dot(
                features_ref[rows, n * slab : (n + 1) * slab],
                weight_ref[n * slab : (n + 1) * slab, low * wide : high * wide],
                preferred_element_type=jnp.float32,
            )
            for j in range(low, high):
                value = term[:, (j - low) * wide : (j - low + 1) * wide]
                if n != mine[j][0] or j in plan.added[i]:
                    value += total_ref[rows, j * wide : (j + 1) * wide]
                if n == mine[j][-1] and j in plan.finished[i]:
                    projected_ref[i % 2, local, :] = value.astype(jnp.bfloat16)
                else:
                    total_ref[rows, j * wide : (j + 1) * wide] = value

        if step == tokens:
            project(0)
        else:
            pl.loop(0, tokens // step)(project)

        for j in range(low, high):
            if n != mine[j][-1]:
                continue
            if j in plan.finished[i]:
                if waiting:
                    attend_rows(*waiting.pop())
                column = plan.carried[i] * wide // 3
                waiting.append((projected_ref.at[i % 2], outs[i][j], column))
            else:
                out_copy(i, j).start()
    if waiting:
        attend_rows(*waiting.pop())
    for copy in carry_copies():
        copy.wait()
    for i in images:
        for j in plan.jobs(i):
            if j not in plan.finished[i]:
                out_copy(i, j).wait()


def run_jobs(role, tokens, wide, images, weights, step=384):
    images = [
        dict(
            image,
            pieces=[
                [[x if isinstance(x, tuple) else (x, 0) for x in owner] for owner in place]
                for place in image["pieces"]
            ],
            sums=image.get("sums", {}),
            finish=image.get("finish", ()),
            carry=image.get("carry", ((), ())),
        )
        for image in images
    ]
    plan = Jobs(
        origins=[[[[r for _, r in o] for o in p] for p in image["pieces"]] for image in images],
        slots=[slot for slot, _, _ in weights],
        first=[first for _, first, _ in weights],
        same=[[not isinstance(w, tuple) for w in row] for _, _, row in weights],
        uses=[image["uses"] for image in images],
        added=[tuple(image["sums"]) for image in images],
        finished=[image["finish"] for image in images],
        carried=[len(image["carry"][0]) for image in images],
        step=step,
    )
    operands = [x for i in images for place in i["pieces"] for owner in place for x, _ in owner]
    slab = operands[0].shape[1] // 2
    for _, _, row in weights:
        for w in row:
            operands += list(w) if isinstance(w, tuple) else [w]
    operands += [x for image in images for x in image["sums"].values()]
    operands += [x for image in images for place in image["carry"] for x in place]
    anywhere, vmem = pl.BlockSpec(memory_space=pl.ANY), pl.BlockSpec(memory_space=pltpu.VMEM)
    head = wide // 3
    shapes, specs = [], []
    for i in range(len(images)):
        for j in plan.jobs(i):
            if j in plan.finished[i]:
                shape = (tokens // 2, head * (plan.carried[i] + 1))
                shapes += [jax.ShapeDtypeStruct(shape, jnp.bfloat16)] * 2
                specs += [vmem] * 2
            else:
                shapes.append(jax.ShapeDtypeStruct((tokens, wide), jnp.float32))
                specs.append(anywhere)
    jobs = 1 + max(j for i in range(len(images)) for j in plan.jobs(i))
    count, depth, total = len(images), len(weights) * slab, len(images) * tokens
    added = sum(high - low for uses in plan.uses for low, high in filter(None, uses))
    got = pl.pallas_call(
        functools.partial(job_kernel, plan),
        out_shape=shapes,
        in_specs=[pl.BlockSpec(memory_space=pltpu.SMEM)] + [anywhere] * len(operands),
        out_specs=specs,
        scratch_shapes=[
            pltpu.VMEM((total, depth), jnp.bfloat16),
            pltpu.VMEM((depth, jobs * wide), jnp.bfloat16),
            pltpu.VMEM((total, jobs * wide), jnp.float32),
            pltpu.VMEM((2, tokens, wide), jnp.bfloat16),
            pltpu.SemaphoreType.DMA((count, len(weights))),
            pltpu.SemaphoreType.DMA((len(weights), jobs)),
            pltpu.SemaphoreType.DMA((count, jobs)),
            pltpu.SemaphoreType.DMA((count, jobs)),
            pltpu.SemaphoreType.DMA((count, 2, max(*plan.carried, 1))),
        ],
        compiler_params=pltpu.CompilerParams(vmem_limit_bytes=62 << 20),
        cost_estimate=pl.CostEstimate(
            flops=2 * tokens * slab * wide * added, bytes_accessed=0, transcendentals=0
        ),
    )(role, *operands)
    got = list(got)
    return [
        {
            j: (got.pop(0), got.pop(0)) if j in plan.finished[i] else got.pop(0)
            for j in plan.jobs(i)
        }
        for i in range(count)
    ]


def join_kernel(place_ref, *refs):
    *parts, out_ref, sems = refs
    count = len(parts) // 2
    inner = place_ref[count]
    wide, head = parts[0].shape[1], parts[count].shape[1]

    def copies(i, role):
        begin = pl.multiple_of(place_ref[i] * wide, wide)
        if role:
            yield parts[i], out_ref.at[:, pl.ds(begin, wide)], sems.at[i, 0]
            return
        kept = wide - head
        yield parts[i].at[:, pl.ds(head, kept)], out_ref.at[:, pl.ds(begin, kept)], sems.at[i, 0]
        last = pl.multiple_of(begin + kept, head)
        yield parts[count + i], out_ref.at[:, pl.ds(last, head)], sems.at[i, 1]

    for role in (1, 0):

        @pl.when((inner == 1) == (role == 1))
        def _():
            every = [pltpu.make_async_copy(*c) for i in range(count) for c in copies(i, role)]
            for copy in every:
                copy.start()
            for copy in every:
                copy.wait()


def join(places, inner, parts, back):
    rows, wide = parts[0].shape
    anywhere = pl.BlockSpec(memory_space=pl.ANY)
    return pl.pallas_call(
        join_kernel,
        out_shape=jax.ShapeDtypeStruct((rows, wide * len(parts)), jnp.bfloat16),
        in_specs=[pl.BlockSpec(memory_space=pltpu.SMEM)] + [anywhere] * (2 * len(parts)),
        out_specs=pl.BlockSpec(memory_space=pltpu.VMEM),
        scratch_shapes=[pltpu.SemaphoreType.DMA((len(parts), 2))],
        cost_estimate=pl.CostEstimate(
            flops=0, bytes_accessed=4 * rows * wide * len(parts), transcendentals=0
        ),
    )(jnp.stack([*places, inner]).astype(jnp.int32), *parts, *back)


def shared(tokens, ln_gain, qkv_weight):
    groups, planes, seqs, cores = (lax.axis_size(a) for a in ("groups", "dp", "seq", "head"))
    group, plane, seq, core = (lax.axis_index(a) for a in ("groups", "dp", "seq", "head"))
    _, rows, _ = tokens.shape
    slab, heads, columns = qkv_weight.shape
    heads, part = heads // groups, rows // cores
    inner = (plane == 1) | (plane == 2)
    wait = lax.optimization_barrier

    def fold(piece):
        piece = piece.reshape(-1, part, columns).transpose(1, 0, 2)
        return piece.reshape(part, -1)

    def pick(for_inner, for_ends):
        return jnp.where(inner, for_inner, for_ends)

    def pair(value):
        return lax.ppermute(value, "dp", [(0, 1), (1, 0), (2, 3), (3, 2)])

    def middle(value):
        return lax.ppermute(value, "dp", [(1, 2), (2, 1)])

    swap = [(0, 1), (1, 0)]
    beside = lambda value: lax.ppermute(value, "seq", swap)
    across = lambda value: lax.ppermute(value, "groups", swap)

    def others(*values):
        got = []
        for value in values:
            if got:
                value, got[-1] = wait((value, got[-1]))
            got.append(lax.ppermute(value, "head", swap))
        return got


    def exchange(mixed):
        got = []
        for a in range(groups):
            for b in range(seqs):
                sent = mixed[a * seqs + b]
                if a or b:
                    steps = [
                        (g * seqs + s, (g + a) % groups * seqs + (s + b) % seqs)
                        for g in range(groups)
                        for s in range(seqs)
                    ]
                    sent = lax.ppermute(sent, ("groups", "seq"), steps)
                got.append(sent)
        return got

    weight = qkv_weight.transpose(1, 0, 2)
    normed, (own0,) = normalize_part(tokens, ln_gain, weight, part, False, (0,))
    normed, own0, later_weight = wait((normed, own0, weight))
    cut0, cut1 = normed
    pair1, middle1 = pair(own0), middle(own0)
    beside1, across1 = beside(cut0), across(cut0)
    own1, own2 = [
        lax.dynamic_index_in_dim(later_weight, group * heads + j, 0, keepdims=False) for j in (1, 2)
    ]
    give = pick(fold(own1), cut0)
    role = jnp.stack([core, inner]).astype(jnp.int32)
    beside1, across1, own1, own2, cut1, tokens, give, role = wait(
        (beside1, across1, own1, own2, cut1, tokens, give, role)
    )
    pair1, middle1, give = wait((pair1, middle1, give))
    run = functools.partial(run_jobs, role, seqs * rows, columns)

    pair2, middle2 = pair(give), middle(pair1)
    beside2, across2 = beside(cut1), across(cut1)
    give = pick(fold(middle1), cut1)
    far_normed, _ = normalize_part(tokens, ln_gain, weight, part, True)
    far1 = others(beside1, across1)
    pair2, middle2, beside2, across2, across1, own1, own2, far_normed, far1, give = wait(
        (pair2, middle2, beside2, across2, across1, own1, own2, far_normed, far1, give)
    )

    pair3, middle3 = pair(give), middle(own1)
    beside3, across3 = beside(across1), across(beside2)
    give = pick(middle2, own1)
    far2 = others(across2, beside2)[::-1]
    pair3, middle3, beside3, across3, pair1, pair2, own2, far2, give = wait(
        (pair3, middle3, beside3, across3, pair1, pair2, own2, far2, give)
    )

    pair4, middle4 = pair(give), middle(own2)
    beside4, across4 = beside(pair2), across(pair2)
    give = pick(middle3, own2)
    pieces0 = ((normed, far_normed), ((beside1, beside2), (far1[0], far2[0])))
    owns = [own0, (own1, own0), (own2, own1)]
    ((head0, sum20, sum30),) = [
        tuple(got.values())
        for got in run(
            [dict(pieces=pieces0, uses=[(0, 3), (0, 2), (0, 1), (0, 1)], finish=(0,))],
            [(0, 0, owns), (2, 0, [middle1, (middle3, pair1)]), (1, 0, [pair1]), (3, 0, [middle2])],
        )
    ]
    far3 = others(beside3, across3)
    lent = jnp.concatenate([pair2, pair3])
    pair4, middle4, beside4, across4, own2, pair3, lent, head0, sum20, sum30, far3, give = wait(
        (pair4, middle4, beside4, across4, own2, pair3, lent, head0, sum20, sum30, far3, give)
    )

    pair5, middle5 = pair(give), middle(pair4)
    beside5, across5 = beside(pair3), across(pair3)
    pieces1 = (((across1, across2), (far1[1], far2[1])), ((beside3, across3), far3))
    image1, image0 = run(
        [
            dict(pieces=pieces1, uses=[(0, 3), (0, 3), (0, 2), (0, 1)], finish=(0,)),
            dict(pieces=pieces0, uses=[None, (2, 3), (1, 2), None], sums={1: sum20, 2: sum30}),
        ],
        [
            (0, 0, owns),
            (2, 0, [middle1, (middle3, pair1), (middle4, pair2)]),
            (1, 0, [pair1, (pair4, pair3)]),
            (3, 0, [middle2]),
        ],
    )
    far_lent, far4 = others(lent, beside4)
    pair5, middle5, beside5, across5, across4, image0, image1, far_lent, far4 = wait(
        (
            *(pair5, middle5, beside5, across5, across4),
            *(image0, image1, far_lent, far4),
        )
    )

    pair6, middle6 = pair(middle5), middle(pair5)
    beside6, across6 = beside(across4), across(beside5)
    far5, far_across4 = others(beside5, across4)
    ahead0, ahead1 = run(
        [
            dict(
                pieces=pieces,
                uses=[(0, 1), (1, 2)],
                sums={0: image[1], 1: image[2]},
                finish=(0,),
            )
            for pieces, image in ((pieces0, image0), (pieces1, image1))
        ],
        [(3, 0, [(middle5, pair4)]), (1, 1, [pair5])],
    )
    lent0 = (((pair2, pair3), (far_lent, (far_lent, part))), ((beside4, beside5), (far4, far5)))
    lent_weights = [(0, 0, [pair5]), (1, 0, [middle4]), (2, 0, [own2])]
    ((sum4,),) = [
        tuple(got.values()) for got in run([dict(pieces=lent0, uses=[(0, 1)] * 3)], lent_weights)
    ]
    pair6, middle6, beside6, across6, across5, ahead0, ahead1, sum4, far_across4 = wait(
        (pair6, middle6, beside6, across6, across5, ahead0, ahead1, sum4, far_across4)
    )

    far_across5, *far6 = [
        lax.ppermute(value, "head", swap) for value in (across5, beside6, across6)
    ]
    done0, done1, lent0 = run(
        [
            dict(pieces=p, uses=[(0, 1)], sums={0: x[1]}, finish=(0,), carry=tuple(zip(h, x[0])))
            for p, h, x in ((pieces0, head0, ahead0), (pieces1, image1[0], ahead1))
        ]
        + [dict(pieces=lent0, uses=[(0, 1)], sums={0: sum4}, finish=(0,))],
        [(3, 0, [(middle6, pair6)])],
    )
    lent1 = (((across4, across5), (far_across4, far_across5)), ((beside6, across6), far6))
    (lent1,) = run(
        [dict(pieces=lent1, uses=[(0, 1)] * 4, finish=(0,))],
        [*lent_weights, (3, 0, [middle6])],
        step=seqs * rows,
    )

    def hand_back(mixed):
        got = []
        for a in range(groups):
            for b in range(seqs):
                steps = [
                    (
                        (g * planes + z) * seqs + s,
                        ((g + a) % groups * planes + (z ^ 1)) * seqs + (s + b) % seqs,
                    )
                    for g in range(groups)
                    for z in (1, 2)
                    for s in range(seqs)
                ]
                sent = mixed[a * seqs + b]
                got.append(lax.ppermute(sent, ("groups", "dp", "seq"), steps))
        return got

    sent = exchange((*done0[0], *done1[0]))
    back = hand_back((*lent0[0], *lent1[0]))
    places = [
        (seq - b) % seqs * groups + (group - a) % groups
        for a in range(groups)
        for b in range(seqs)
    ]
    return join(places, inner, sent, back)[None]


def per_device(tokens, ln_gain, qkv_weight):
    groups, planes, seqs, cores = (lax.axis_size(a) for a in ("groups", "dp", "seq", "head"))
    images, rows, width = tokens.shape
    slab, heads, _ = qkv_weight.shape
    if (groups, planes, seqs, cores) == (2, 4, 2, 2) and images == 1 and heads == 3 * groups:
        part = rows // cores
        if rows % (32 * cores) == 0 and slab % part == 0 and 2 * slab == qkv_weight.shape[2] * slab // part:
            return shared(tokens, ln_gain, qkv_weight)
    return plain(tokens, ln_gain, qkv_weight)


def solution(mesh):
    return jax.shard_map(
        per_device,
        mesh=mesh,
        in_specs=(P(("groups", "dp"), "seq", None), P(), P("dp", ("seq", "head"), None)),
        out_specs=P(("groups", "dp"), "seq", "head"),
        check_vma=False,
    )
```

```python
import functools
import math

import jax
import jax.numpy as jnp
from jax import lax
from jax.experimental import pallas as pl
from jax.experimental.pallas import tpu as pltpu
from jax.sharding import PartitionSpec as P


def normalize(array, gain):
    widened = array.astype(jnp.float32)
    centered = widened - jnp.mean(widened, axis=-1, keepdims=True)
    variance = jnp.mean(centered * centered, axis=-1, keepdims=True)
    return (centered * lax.rsqrt(variance + 1e-06) * gain).astype(jnp.bfloat16)


def attend(projected):
    width = projected.shape[2] // 3
    queries = projected[:, :, :width]
    key_rows = projected[:, :, width : 2 * width]
    value_rows = projected[:, :, 2 * width :]
    scores = jnp.einsum("qhd,khd->hqk", queries, key_rows, preferred_element_type=jnp.float32) * (
        1.0 / math.sqrt(width)
    )
    highest = jnp.max(scores, axis=-1, keepdims=True)
    expo = jnp.exp(scores - highest)
    probs = (expo / jnp.sum(expo, axis=-1, keepdims=True)).astype(jnp.bfloat16)
    mixed = jnp.einsum("hqk,khd->qhd", probs, value_rows, preferred_element_type=jnp.float32)
    return mixed.astype(jnp.bfloat16).reshape(projected.shape[0], -1)


def plain(tokens, ln_gain, qkv_weight):
    images = tokens.shape[0]
    width = tokens.shape[2]
    heads_here = qkv_weight.shape[1]
    columns = heads_here * qkv_weight.shape[2]
    source = normalize(tokens, ln_gain)
    half_width = width // lax.axis_size("head")
    core_index = lax.axis_index("head")
    own_half = lax.dynamic_slice_in_dim(source, core_index * half_width, half_width, 2)
    fetched = lax.all_gather(own_half, "seq", axis=1, tiled=True)
    gathered = lax.all_gather(fetched, "head", axis=2, tiled=True)
    full_tokens = gathered.shape[1]
    features = gathered.reshape(images * full_tokens, width)
    piece = lax.all_gather(qkv_weight, "dp", axis=0, tiled=True)
    projected = jnp.dot(
        features, piece.reshape(piece.shape[0], columns), preferred_element_type=jnp.float32
    )
    projected = projected.astype(jnp.bfloat16).reshape(
        images, full_tokens, heads_here, qkv_weight.shape[2]
    )
    mixed = lax.map(attend, projected)
    return lax.all_to_all(mixed, "seq", split_axis=1, concat_axis=2, tiled=True)


def slab_order(plane):
    inner = (plane == 1) | (plane == 2)
    near, far = plane ^ 1, 2 - plane // 2
    return plane, jnp.where(inner, near, far), jnp.where(inner, far, near), 3 - 3 * (plane // 2)


def normalize_kernel(step, other, taken, tokens_ref, gain_ref, weight_ref, *refs):
    refs = list(refs)
    take = lambda n: [refs.pop(0) for _ in range(n)]
    normed_refs, own_refs, (tokens_buf, *normed_bufs) = take(2), take(len(taken)), take(3)
    own_bufs, (in_sems, out_sems, own_sems) = take(len(taken)), take(3)
    part, width = tokens_buf.shape
    lanes = 128
    slab, span = width // 4, width // 2
    core = lax.axis_index("head")
    first = pl.multiple_of((1 - core if other else core) * part, part)
    order = slab_order(lax.axis_index("dp"))
    heads = weight_ref.shape[0] // lax.axis_size("groups")

    def rows_in(i):
        return pltpu.make_async_copy(
            tokens_ref.at[0, pl.ds(pl.multiple_of(first + i * step, step), step)],
            tokens_buf.at[pl.ds(pl.multiple_of(i * step, step), step)],
            in_sems.at[i],
        )

    def rows_out(i):
        rows = pl.ds(pl.multiple_of(i * step, step), step)
        return [
            pltpu.make_async_copy(buf.at[rows], ref.at[rows], out_sems.at[i, cut])
            for cut, (buf, ref) in enumerate(zip(normed_bufs, normed_refs))
        ]

    def own_in(k):
        head = lax.axis_index("groups") * heads + taken[k]
        return pltpu.make_async_copy(weight_ref.at[head], own_bufs[k], own_sems.at[k, 0])

    def own_out(k):
        return pltpu.make_async_copy(own_bufs[k], own_refs[k], own_sems.at[k, 1])

    for i in range(part // step):
        rows_in(i).start()
    for k in range(len(taken)):
        own_in(k).start()

    @pl.loop(0, part // step)
    def _(i):
        rows_in(i).wait()
        rows = pl.ds(pl.multiple_of(i * step, step), step)

        def widened(begin):
            return tokens_buf[rows, pl.ds(begin, lanes)].astype(jnp.float32)

        total = jnp.zeros((step, lanes), jnp.float32)
        for begin in range(0, width, lanes):
            total += widened(begin)
        mean = jnp.sum(total, axis=-1, keepdims=True) / width
        total = jnp.zeros((step, lanes), jnp.float32)
        for begin in range(0, width, lanes):
            centered = widened(begin) - mean
            total += centered * centered
        scale = lax.rsqrt(jnp.sum(total, axis=-1, keepdims=True) / width + 1e-06)
        for k in range(4):
            for begin in range(0, slab, lanes):
                column = pl.multiple_of(order[k] * slab + begin, lanes)
                value = (widened(column) - mean) * scale * gain_ref[:, pl.ds(column, lanes)]
                target = k * slab % span + begin
                normed_bufs[k * slab // span][rows, target : target + lanes] = value.astype(
                    jnp.bfloat16
                )
        for copy in rows_out(i):
            copy.start()

    for k in range(len(taken)):
        own_in(k).wait()
        own_out(k).start()
    for i in range(part // step):
        for copy in rows_out(i):
            copy.wait()
    for k in range(len(taken)):
        own_out(k).wait()


def normalize_part(tokens, ln_gain, weight, part, other, taken=()):
    width = tokens.shape[2]
    piece = weight.shape[1:]
    step = 64 if part % 64 == 0 else 32
    anywhere = pl.BlockSpec(memory_space=pl.ANY)
    half = jax.ShapeDtypeStruct((part, width // 2), jnp.bfloat16)
    got = pl.pallas_call(
        functools.partial(normalize_kernel, step, other, taken),
        out_shape=[half] * 2 + [jax.ShapeDtypeStruct(piece, jnp.bfloat16)] * len(taken),
        in_specs=[anywhere, pl.BlockSpec(memory_space=pltpu.VMEM), anywhere],
        out_specs=[anywhere] * (2 + len(taken)),
        scratch_shapes=[
            pltpu.VMEM((part, width), jnp.bfloat16),
            *[pltpu.VMEM((part, width // 2), jnp.bfloat16)] * 2,
            *[pltpu.VMEM(piece, jnp.bfloat16)] * len(taken),
            pltpu.SemaphoreType.DMA((part // step,)),
            pltpu.SemaphoreType.DMA((part // step, 2)),
            pltpu.SemaphoreType.DMA((max(len(taken), 1), 2)),
        ],
        compiler_params=pltpu.CompilerParams(vmem_limit_bytes=62 << 20),
        cost_estimate=pl.CostEstimate(
            flops=8 * part * width, bytes_accessed=4 * part * width, transcendentals=part
        ),
    )(tokens, ln_gain[None], weight)
    return got[:2], got[2:]


def attend_rows(projected_ref, parts, column):
    width = projected_ref.shape[1] // 3
    key_rows = projected_ref[:, width : 2 * width]
    value_rows = projected_ref[:, 2 * width :]
    value_rows = jnp.concatenate([value_rows, jnp.ones_like(value_rows)], axis=1)
    begin = 0
    for part in parts:
        step = part.shape[0]
        queries = projected_ref[begin : begin + step, :width]
        scores = lax.dot_general(
            queries, key_rows, (((1,), (1,)), ((), ())), preferred_element_type=jnp.float32
        )
        highest = jnp.max(scores, axis=-1, keepdims=True)
        expo = jnp.exp2((scores - highest) * (math.log2(math.e) / math.sqrt(width)))
        mixed = jnp.dot(expo.astype(jnp.bfloat16), value_rows, preferred_element_type=jnp.float32)
        mixed = mixed[:, :width] / mixed[:, width:]
        part[:, column : column + width] = mixed.astype(jnp.bfloat16)
        begin += step


class Jobs:
    def __init__(self, **numbers):
        self.__dict__.update(numbers)

    def jobs(self, image):
        return sorted({j for use in self.uses[image] if use for j in range(*use)})


def job_kernel(plan, role_ref, *refs):
    refs = list(refs)
    take = lambda n: [refs.pop(0) for _ in range(n)]
    images, ns = range(len(plan.uses)), range(len(plan.slots))
    pieces = [[[take(2) for _ in place] for place in image] for image in plan.origins]
    weights = [[take(1) * 2 if alike else take(2) for alike in row] for row in plan.same]
    partials = [{j: take(1)[0] for j in plan.added[i]} for i in images]
    carried = [[take(plan.carried[i]) for _ in range(2)] for i in images]
    outs = [
        {j: take(2) if j in plan.finished[i] else take(1)[0] for j in plan.jobs(i)} for i in images
    ]
    features_ref, weight_ref, total_ref, projected_ref = take(4)
    token_sems, weight_sems, sum_sems, out_sems, carry_sems = take(5)
    core, inner = role_ref[0], role_ref[1]
    slab = pieces[0][0][0][0].shape[1] // 2
    tokens, wide = projected_ref.shape[1:]
    part = tokens // 4

    def features(i, n):
        return features_ref.at[pl.ds(i * tokens, tokens), pl.ds(n * slab, slab)]

    def weight(n, j):
        return weight_ref.at[pl.ds(n * slab, slab), pl.ds(j * wide, wide)]

    def total(i, j):
        return total_ref.at[pl.ds(i * tokens, tokens), pl.ds(j * wide, wide)]

    def start_tokens(i, n):
        cut, begin = plan.slots[n] // 2, plan.slots[n] % 2 * slab
        for place in range(2):
            split = len(plan.origins[i][place])
            for owner in range(split):
                row = i * tokens + 2 * place * part
                if split == 2:
                    row += (1 - core if owner else core) * part
                count = 2 * part // split
                from_rows = pl.ds(plan.origins[i][place][owner][cut], count)
                rows = pl.ds(pl.multiple_of(row, 32), count)
                pltpu.make_async_copy(
                    pieces[i][place][owner][cut].at[from_rows, pl.ds(begin, slab)],
                    features_ref.at[rows, pl.ds(n * slab, slab)],
                    token_sems.at[i, n],
                ).start()

    def start_weight(n, j, role):
        source = weights[n][j - plan.first[n]][role]
        if source.shape[0] == slab:
            pltpu.make_async_copy(source, weight(n, j), weight_sems.at[n, j]).start()
            return
        for b in range(source.shape[1] // wide):
            pltpu.make_async_copy(
                source.at[:, pl.ds(b * wide, wide)],
                weight_ref.at[pl.ds(n * slab + b * part, part), pl.ds(j * wide, wide)],
                weight_sems.at[n, j],
            ).start()

    def start_role_weight(n, j):
        if plan.same[n][j - plan.first[n]]:
            start_weight(n, j, 0)
            return

        @pl.when(inner == 1)
        def _():
            start_weight(n, j, 0)

        @pl.when(inner != 1)
        def _():
            start_weight(n, j, 1)

    def partial_copy(i, j):
        return pltpu.make_async_copy(partials[i][j], total(i, j), sum_sems.at[i, j])

    def out_copy(i, j):
        return pltpu.make_async_copy(total(i, j), outs[i][j], out_sems.at[i, j])

    def carry_copies():
        for i in images:
            for place in range(2):
                for k in range(plan.carried[i]):
                    (finished,) = plan.finished[i]
                    target = outs[i][finished][place].at[:, pl.ds(k * wide // 3, wide // 3)]
                    yield pltpu.make_async_copy(
                        carried[i][place][k], target, carry_sems.at[i, place, k]
                    )

    stages = [(i, n) for i in images for n in ns if plan.uses[i][n]]
    held = set()

    def start_stage(i, n):
        start_tokens(i, n)
        for j in range(*plan.uses[i][n]):
            if (n, j) not in held:
                held.add((n, j))
                start_role_weight(n, j)
        if not any((i, n) > (i, m) and plan.uses[i][m] for m in ns):
            for j in plan.added[i]:
                partial_copy(i, j).start()

    ahead = 2
    for stage in stages[:ahead]:
        start_stage(*stage)
    for copy in carry_copies():
        copy.start()
    ready, waiting, step = set(), [], plan.step
    for index, (i, n) in enumerate(stages):
        low, high = plan.uses[i][n]
        pltpu.make_async_copy(features(i, n), features(i, n), token_sems.at[i, n]).wait()
        for j in range(low, high):
            if (n, j) not in ready:
                ready.add((n, j))
                pltpu.make_async_copy(weight(n, j), weight(n, j), weight_sems.at[n, j]).wait()
        if index + ahead < len(stages):
            start_stage(*stages[index + ahead])
        mine = {
            j: [m for m in ns if plan.uses[i][m] and j in range(*plan.uses[i][m])]
            for j in range(low, high)
        }
        for j in range(low, high):
            if n == mine[j][0] and j in plan.added[i]:
                partial_copy(i, j).wait()

        def project(r):
            local = pl.ds(pl.multiple_of(r * step, step), step)
            rows = pl.ds(pl.multiple_of(i * tokens + r * step, step), step)
            term = jnp.dot(
                features_ref[rows, n * slab : (n + 1) * slab],
                weight_ref[n * slab : (n + 1) * slab, low * wide : high * wide],
                preferred_element_type=jnp.float32,
            )
            for j in range(low, high):
                value = term[:, (j - low) * wide : (j - low + 1) * wide]
                if n != mine[j][0] or j in plan.added[i]:
                    value += total_ref[rows, j * wide : (j + 1) * wide]
                if n == mine[j][-1] and j in plan.finished[i]:
                    projected_ref[i % 2, local, :] = value.astype(jnp.bfloat16)
                else:
                    total_ref[rows, j * wide : (j + 1) * wide] = value

        if step == tokens:
            project(0)
        else:
            pl.loop(0, tokens // step)(project)

        for j in range(low, high):
            if n != mine[j][-1]:
                continue
            if j in plan.finished[i]:
                if waiting:
                    attend_rows(*waiting.pop())
                column = plan.carried[i] * wide // 3
                waiting.append((projected_ref.at[i % 2], outs[i][j], column))
            else:
                out_copy(i, j).start()
    if waiting:
        attend_rows(*waiting.pop())
    for copy in carry_copies():
        copy.wait()
    for i in images:
        for j in plan.jobs(i):
            if j not in plan.finished[i]:
                out_copy(i, j).wait()


def run_jobs(role, tokens, wide, images, weights, step=384):
    images = [
        dict(
            image,
            pieces=[
                [[x if isinstance(x, tuple) else (x, 0) for x in owner] for owner in place]
                for place in image["pieces"]
            ],
            sums=image.get("sums", {}),
            finish=image.get("finish", ()),
            carry=image.get("carry", ((), ())),
        )
        for image in images
    ]
    plan = Jobs(
        origins=[[[[r for _, r in o] for o in p] for p in image["pieces"]] for image in images],
        slots=[slot for slot, _, _ in weights],
        first=[first for _, first, _ in weights],
        same=[[not isinstance(w, tuple) for w in row] for _, _, row in weights],
        uses=[image["uses"] for image in images],
        added=[tuple(image["sums"]) for image in images],
        finished=[image["finish"] for image in images],
        carried=[len(image["carry"][0]) for image in images],
        step=step,
    )
    operands = [x for i in images for place in i["pieces"] for owner in place for x, _ in owner]
    slab = operands[0].shape[1] // 2
    for _, _, row in weights:
        for w in row:
            operands += list(w) if isinstance(w, tuple) else [w]
    operands += [x for image in images for x in image["sums"].values()]
    operands += [x for image in images for place in image["carry"] for x in place]
    anywhere, vmem = pl.BlockSpec(memory_space=pl.ANY), pl.BlockSpec(memory_space=pltpu.VMEM)
    head = wide // 3
    shapes, specs = [], []
    for i in range(len(images)):
        for j in plan.jobs(i):
            if j in plan.finished[i]:
                shape = (tokens // 2, head * (plan.carried[i] + 1))
                shapes += [jax.ShapeDtypeStruct(shape, jnp.bfloat16)] * 2
                specs += [vmem] * 2
            else:
                shapes.append(jax.ShapeDtypeStruct((tokens, wide), jnp.float32))
                specs.append(anywhere)
    jobs = 1 + max(j for i in range(len(images)) for j in plan.jobs(i))
    count, depth, total = len(images), len(weights) * slab, len(images) * tokens
    added = sum(high - low for uses in plan.uses for low, high in filter(None, uses))
    got = pl.pallas_call(
        functools.partial(job_kernel, plan),
        out_shape=shapes,
        in_specs=[pl.BlockSpec(memory_space=pltpu.SMEM)] + [anywhere] * len(operands),
        out_specs=specs,
        scratch_shapes=[
            pltpu.VMEM((total, depth), jnp.bfloat16),
            pltpu.VMEM((depth, jobs * wide), jnp.bfloat16),
            pltpu.VMEM((total, jobs * wide), jnp.float32),
            pltpu.VMEM((2, tokens, wide), jnp.bfloat16),
            pltpu.SemaphoreType.DMA((count, len(weights))),
            pltpu.SemaphoreType.DMA((len(weights), jobs)),
            pltpu.SemaphoreType.DMA((count, jobs)),
            pltpu.SemaphoreType.DMA((count, jobs)),
            pltpu.SemaphoreType.DMA((count, 2, max(*plan.carried, 1))),
        ],
        compiler_params=pltpu.CompilerParams(vmem_limit_bytes=62 << 20),
        cost_estimate=pl.CostEstimate(
            flops=2 * tokens * slab * wide * added, bytes_accessed=0, transcendentals=0
        ),
    )(role, *operands)
    got = list(got)
    return [
        {
            j: (got.pop(0), got.pop(0)) if j in plan.finished[i] else got.pop(0)
            for j in plan.jobs(i)
        }
        for i in range(count)
    ]


def join_kernel(place_ref, *refs):
    *parts, out_ref, sems = refs
    count = len(parts) // 2
    inner = place_ref[count]
    wide, head = parts[0].shape[1], parts[count].shape[1]

    def copies(i, role):
        begin = pl.multiple_of(place_ref[i] * wide, wide)
        if role:
            yield parts[i], out_ref.at[:, pl.ds(begin, wide)], sems.at[i, 0]
            return
        kept = wide - head
        yield parts[i].at[:, pl.ds(head, kept)], out_ref.at[:, pl.ds(begin, kept)], sems.at[i, 0]
        last = pl.multiple_of(begin + kept, head)
        yield parts[count + i], out_ref.at[:, pl.ds(last, head)], sems.at[i, 1]

    for role in (1, 0):

        @pl.when((inner == 1) == (role == 1))
        def _():
            every = [pltpu.make_async_copy(*c) for i in range(count) for c in copies(i, role)]
            for copy in every:
                copy.start()
            for copy in every:
                copy.wait()


def join(places, inner, parts, back):
    rows, wide = parts[0].shape
    anywhere = pl.BlockSpec(memory_space=pl.ANY)
    return pl.pallas_call(
        join_kernel,
        out_shape=jax.ShapeDtypeStruct((rows, wide * len(parts)), jnp.bfloat16),
        in_specs=[pl.BlockSpec(memory_space=pltpu.SMEM)] + [anywhere] * (2 * len(parts)),
        out_specs=pl.BlockSpec(memory_space=pltpu.VMEM),
        scratch_shapes=[pltpu.SemaphoreType.DMA((len(parts), 2))],
        cost_estimate=pl.CostEstimate(
            flops=0, bytes_accessed=4 * rows * wide * len(parts), transcendentals=0
        ),
    )(jnp.stack([*places, inner]).astype(jnp.int32), *parts, *back)


def shared(tokens, ln_gain, qkv_weight):
    groups, planes, seqs, cores = (lax.axis_size(a) for a in ("groups", "dp", "seq", "head"))
    group, plane, seq, core = (lax.axis_index(a) for a in ("groups", "dp", "seq", "head"))
    _, rows, _ = tokens.shape
    slab, heads, columns = qkv_weight.shape
    heads, part = heads // groups, rows // cores
    inner = (plane == 1) | (plane == 2)
    wait = lax.optimization_barrier

    def fold(piece):
        piece = piece.reshape(-1, part, columns).transpose(1, 0, 2)
        return piece.reshape(part, -1)

    def pick(for_inner, for_ends):
        return jnp.where(inner, for_inner, for_ends)

    def pair(value):
        return lax.ppermute(value, "dp", [(0, 1), (1, 0), (2, 3), (3, 2)])

    def middle(value):
        return lax.ppermute(value, "dp", [(1, 2), (2, 1)])

    swap = [(0, 1), (1, 0)]
    beside = lambda value: lax.ppermute(value, "seq", swap)
    across = lambda value: lax.ppermute(value, "groups", swap)

    def others(*values):
        got = []
        for value in values:
            if got:
                value, got[-1] = wait((value, got[-1]))
            got.append(lax.ppermute(value, "head", swap))
        return got


    def exchange(mixed):
        got = []
        for a in range(groups):
            for b in range(seqs):
                sent = mixed[a * seqs + b]
                if a or b:
                    steps = [
                        (g * seqs + s, (g + a) % groups * seqs + (s + b) % seqs)
                        for g in range(groups)
                        for s in range(seqs)
                    ]
                    sent = lax.ppermute(sent, ("groups", "seq"), steps)
                got.append(sent)
        return got

    weight = qkv_weight.transpose(1, 0, 2)
    normed, (own0,) = normalize_part(tokens, ln_gain, weight, part, False, (0,))
    normed, own0, later_weight = wait((normed, own0, weight))
    cut0, cut1 = normed
    pair1, middle1 = pair(own0), middle(own0)
    beside1, across1 = beside(cut0), across(cut0)
    own1, own2 = [
        lax.dynamic_index_in_dim(later_weight, group * heads + j, 0, keepdims=False) for j in (1, 2)
    ]
    give = pick(fold(own1), cut0)
    role = jnp.stack([core, inner]).astype(jnp.int32)
    beside1, across1, own1, own2, cut1, tokens, give, role = wait(
        (beside1, across1, own1, own2, cut1, tokens, give, role)
    )
    pair1, middle1, give = wait((pair1, middle1, give))
    run = functools.partial(run_jobs, role, seqs * rows, columns)

    pair2, middle2 = pair(give), middle(pair1)
    beside2, across2 = beside(cut1), across(cut1)
    give = pick(fold(middle1), cut1)
    far_normed, _ = normalize_part(tokens, ln_gain, weight, part, True)
    far1 = others(beside1, across1)
    pair2, middle2, beside2, across2, across1, own1, own2, far_normed, far1, give = wait(
        (pair2, middle2, beside2, across2, across1, own1, own2, far_normed, far1, give)
    )

    pair3, middle3 = pair(give), middle(own1)
    beside3, across3 = beside(across1), across(beside2)
    give = pick(middle2, own1)
    far2 = others(across2, beside2)[::-1]
    pair3, middle3, beside3, across3, pair1, pair2, own2, far2, give = wait(
        (pair3, middle3, beside3, across3, pair1, pair2, own2, far2, give)
    )

    pair4, middle4 = pair(give), middle(own2)
    beside4, across4 = beside(pair2), across(pair2)
    give = pick(middle3, own2)
    pieces0 = ((normed, far_normed), ((beside1, beside2), (far1[0], far2[0])))
    owns = [own0, (own1, own0), (own2, own1)]
    ((head0, sum20, sum30),) = [
        tuple(got.values())
        for got in run(
            [dict(pieces=pieces0, uses=[(0, 3), (0, 2), (0, 1), (0, 1)], finish=(0,))],
            [(0, 0, owns), (2, 0, [middle1, (middle3, pair1)]), (1, 0, [pair1]), (3, 0, [middle2])],
        )
    ]
    far3 = others(beside3, across3)
    lent = jnp.concatenate([pair2, pair3])
    pair4, middle4, beside4, across4, own2, pair3, lent, head0, sum20, sum30, far3, give = wait(
        (pair4, middle4, beside4, across4, own2, pair3, lent, head0, sum20, sum30, far3, give)
    )

    pair5, middle5 = pair(give), middle(pair4)
    beside5, across5 = beside(pair3), across(pair3)
    pieces1 = (((across1, across2), (far1[1], far2[1])), ((beside3, across3), far3))
    image1, image0 = run(
        [
            dict(pieces=pieces1, uses=[(0, 3), (0, 3), (0, 2), (0, 1)], finish=(0,)),
            dict(pieces=pieces0, uses=[None, (2, 3), (1, 2), None], sums={1: sum20, 2: sum30}),
        ],
        [
            (0, 0, owns),
            (2, 0, [middle1, (middle3, pair1), (middle4, pair2)]),
            (1, 0, [pair1, (pair4, pair3)]),
            (3, 0, [middle2]),
        ],
    )
    far_lent, far4 = others(lent, beside4)
    pair5, middle5, beside5, across5, across4, image0, image1, far_lent, far4 = wait(
        (
            *(pair5, middle5, beside5, across5, across4),
            *(image0, image1, far_lent, far4),
        )
    )

    pair6, middle6 = pair(middle5), middle(pair5)
    beside6, across6 = beside(across4), across(beside5)
    far5, far_across4 = others(beside5, across4)
    ahead0, ahead1 = run(
        [
            dict(
                pieces=pieces,
                uses=[(0, 1), (1, 2)],
                sums={0: image[1], 1: image[2]},
                finish=(0,),
            )
            for pieces, image in ((pieces0, image0), (pieces1, image1))
        ],
        [(3, 0, [(middle5, pair4)]), (1, 1, [pair5])],
    )
    lent0 = (((pair2, pair3), (far_lent, (far_lent, part))), ((beside4, beside5), (far4, far5)))
    lent_weights = [(0, 0, [pair5]), (1, 0, [middle4]), (2, 0, [own2])]
    ((sum4,),) = [
        tuple(got.values()) for got in run([dict(pieces=lent0, uses=[(0, 1)] * 3)], lent_weights)
    ]
    pair6, middle6, across5, ahead0, ahead1, sum4, far_across4 = wait(
        (pair6, middle6, across5, ahead0, ahead1, sum4, far_across4)
    )

    far_across5 = lax.ppermute(across5, "head", swap)
    done0, done1, lent0 = run(
        [
            dict(pieces=p, uses=[(0, 1)], sums={0: x[1]}, finish=(0,), carry=tuple(zip(h, x[0])))
            for p, h, x in ((pieces0, head0, ahead0), (pieces1, image1[0], ahead1))
        ]
        + [dict(pieces=lent0, uses=[(0, 1)], sums={0: sum4}, finish=(0,))],
        [(3, 0, [(middle6, pair6)])],
    )
    beside6, across6, done0, done1, lent0 = wait((beside6, across6, done0, done1, lent0))
    far6 = [lax.ppermute(value, "head", swap) for value in (beside6, across6)]
    lent1 = (((across4, across5), (far_across4, far_across5)), ((beside6, across6), far6))
    (lent1,) = run(
        [dict(pieces=lent1, uses=[(0, 1)] * 4, finish=(0,))],
        [*lent_weights, (3, 0, [middle6])],
        step=seqs * rows,
    )

    def hand_back(mixed):
        got = []
        for a in range(groups):
            for b in range(seqs):
                steps = [
                    (
                        (g * planes + z) * seqs + s,
                        ((g + a) % groups * planes + (z ^ 1)) * seqs + (s + b) % seqs,
                    )
                    for g in range(groups)
                    for z in (1, 2)
                    for s in range(seqs)
                ]
                sent = mixed[a * seqs + b]
                got.append(lax.ppermute(sent, ("groups", "dp", "seq"), steps))
        return got

    sent = exchange((*done0[0], *done1[0]))
    back = hand_back((*lent0[0], *lent1[0]))
    places = [
        (seq - b) % seqs * groups + (group - a) % groups
        for a in range(groups)
        for b in range(seqs)
    ]
    return join(places, inner, sent, back)[None]


def per_device(tokens, ln_gain, qkv_weight):
    groups, planes, seqs, cores = (lax.axis_size(a) for a in ("groups", "dp", "seq", "head"))
    images, rows, width = tokens.shape
    slab, heads, _ = qkv_weight.shape
    if (groups, planes, seqs, cores) == (2, 4, 2, 2) and images == 1 and heads == 3 * groups:
        part = rows // cores
        if rows % (32 * cores) == 0 and slab % part == 0 and 2 * slab == qkv_weight.shape[2] * slab // part:
            return shared(tokens, ln_gain, qkv_weight)
    return plain(tokens, ln_gain, qkv_weight)


def solution(mesh):
    return jax.shard_map(
        per_device,
        mesh=mesh,
        in_specs=(P(("groups", "dp"), "seq", None), P(), P("dp", ("seq", "head"), None)),
        out_specs=P(("groups", "dp"), "seq", "head"),
        check_vma=False,
    )
```
